32 devices in a mesh: dp: 16 (over z, x, core), mp: 2 (over y).
Axes of the slice: x: 2, y: 2, z: 4, core: 2. Of those that a mesh axis runs over, the one named last changes fastest.
Arguments:
- image_tokens: bfloat16 [65536, 768], P('dp'), may hold values from -6 to 6
- norm1_gain: bfloat16 [768], replicated, may hold values from 0.5 to 1.5
- norm1_shift: bfloat16 [768], replicated, may hold values from -4 to 4
- qkv_weight: bfloat16 [3, 768, 768], P(None, None, 'mp'), may hold values from -0.21875 to 0.21875
- qv_bias: bfloat16 [2, 768], P(None, 'mp'), may hold values from -4 to 4
- rel_rows: bfloat16 [27, 64], replicated, may hold values from -2 to 2
- rel_cols: bfloat16 [27, 64], replicated, may hold values from -2 to 2
- proj_weight: bfloat16 [768, 768], P('mp'), may hold values from -0.875 to 0.875
- proj_bias: bfloat16 [768], replicated, may hold values from -4 to 4
- norm2_gain: bfloat16 [768], replicated, may hold values from 0.5 to 1.5
- norm2_shift: bfloat16 [768], replicated, may hold values from -4 to 4
- fc1_weight: bfloat16 [768, 3072], P(None, 'mp'), may hold values from -0.21875 to 0.21875
- fc1_bias: bfloat16 [3072], P('mp'), may hold values from -4 to 4
- fc2_weight: bfloat16 [3072, 768], P('mp'), may hold values from -0.109375 to 0.109375
- fc2_bias: bfloat16 [768], replicated, may hold values from -4 to 4
- out_cotangent: bfloat16 [65536, 768], P(('dp', 'mp')), may hold values from -6 to 6
Outputs:
- block_out: bfloat16 [65536, 768], P(('dp', 'mp'))
- input_grad: bfloat16 [65536, 768], P(('dp', 'mp'))
- norm1_gain_grad: float32 [768], replicated
- norm1_shift_grad: float32 [768], replicated
- qkv_weight_grad: float32 [3, 768, 768], P(None, None, 'mp')
- qv_bias_grad: float32 [2, 768], P(None, 'mp')
- rel_rows_grad: float32 [27, 64], replicated
- rel_cols_grad: float32 [27, 64], replicated
- proj_weight_grad: float32 [768, 768], P('mp')
- proj_bias_grad: float32 [768], replicated
- norm2_gain_grad: float32 [768], replicated
- norm2_shift_grad: float32 [768], replicated
- fc1_weight_grad: float32 [768, 3072], P(None, 'mp')
- fc1_bias_grad: float32 [3072], P('mp')
- fc2_weight_grad: float32 [3072, 768], P('mp')
- fc2_bias_grad: float32 [768], replicated
The draws below stay inside these ranges and needn't reach their ends.
All inputs are finite; a program needn't handle non-finite values.
Results may differ from the reference program's by a relative error of at most 0.017.
Values may be sent and summed in bfloat16 or wider, within the bound.
A program may use at most 320 MiB of HBM per device.

```python
import jax
import jax.numpy as jnp
from jax import lax

D = 768
HEADS = 12
HD = 64
FF = 3072
WIN = 14
SIDE = 64
NWIN = 5
PAD = 70
RELS = 27
IMAGES = 16
TOKENS = 65536


def block_scale(key, shape, shards, smallest, top_value):
    loudness, own = 1.0, jax.random.fold_in(key, 6)
    for axis_at, shards_of in shards:
        heights = jnp.exp(jax.random.uniform(jax.random.fold_in(own, axis_at), (shards_of,), jnp.float32, smallest / len(shards), top_value / len(shards)))
        loudness = loudness * jnp.repeat(heights, shape[axis_at] // shards_of).reshape([-1 if axis == axis_at else 1 for axis in range(len(shape))])
    return loudness


def bell_draw(key, extent, deviation, most, cuts=(), held_as=jnp.bfloat16):
    entries = deviation * jax.random.normal(key, extent, jnp.float32)
    if cuts:
        entries = entries * block_scale(key, extent, cuts, -0.22, 0.18)
    return jnp.clip(entries, -most, most).astype(held_as)


def setup_inputs(seed: int = 0) -> dict:
    streams_of = jax.random.split(jax.random.key(seed), 17)
    image_tokens = bell_draw(streams_of[0], (TOKENS, D), 1.0, 6.0, ((0, 16),))
    norm1_gain = jnp.clip(1.0 + 0.1 * jax.random.normal(streams_of[1], (D,), jnp.float32), 0.5, 1.5).astype(jnp.bfloat16)
    norm1_shift = bell_draw(streams_of[2], (D,), 0.3, 4.0)
    qkv_weight = bell_draw(streams_of[3], (3, D, D), D ** -0.5, 0.21875, ((2, 2),))
    qv_bias = bell_draw(streams_of[4], (2, D), 0.3, 4.0, ((1, 2),))
    rel_rows = bell_draw(streams_of[5], (RELS, HD), 0.125, 2.0)
    rel_cols = bell_draw(streams_of[6], (RELS, HD), 0.125, 2.0)
    proj_weight = bell_draw(streams_of[7], (D, D), (D // 14) ** -0.5, 0.875, ((0, 2),))
    proj_bias = bell_draw(streams_of[8], (D,), 0.3, 4.0)
    norm2_gain = jnp.clip(1.0 + 0.1 * jax.random.normal(streams_of[9], (D,), jnp.float32), 0.5, 1.5).astype(jnp.bfloat16)
    norm2_shift = bell_draw(streams_of[10], (D,), 0.3, 4.0)
    fc1_weight = bell_draw(streams_of[11], (D, FF), D ** -0.5, 0.21875, ((1, 2),))
    fc1_bias = bell_draw(streams_of[12], (FF,), 0.3, 4.0, ((0, 2),))
    fc2_weight = bell_draw(streams_of[13], (FF, D), FF ** -0.5, 0.109375, ((0, 2),))
    fc2_bias = bell_draw(streams_of[14], (D,), 0.3, 4.0)
    out_cotangent = bell_draw(streams_of[15], (TOKENS, D), 1.0, 6.0, ((0, 32),))
    return dict(image_tokens=image_tokens, norm1_gain=norm1_gain, norm1_shift=norm1_shift, qkv_weight=qkv_weight, qv_bias=qv_bias, rel_rows=rel_rows, rel_cols=rel_cols, proj_weight=proj_weight, proj_bias=proj_bias, norm2_gain=norm2_gain, norm2_shift=norm2_shift, fc1_weight=fc1_weight, fc1_bias=fc1_bias, fc2_weight=fc2_weight, fc2_bias=fc2_bias, out_cotangent=out_cotangent)


EPSILON = 1e-06
PRECISE = lax.Precision.HIGHEST

@jax.custom_vjp
def low(v):
    return lax.optimization_barrier(v.astype(jnp.bfloat16)).astype(jnp.float32)

@jax.custom_vjp
def low_back(v):
    return v

def low_keep(v):
    return (low(v), None)

def low_pass(kept, grad):
    return (grad,)

def back_keep(v):
    return (v, None)

def back_low(kept, grad):
    return (low(grad),)
low.defvjp(low_keep, low_pass)
low_back.defvjp(back_keep, back_low)

def matmul(left, right):
    return jnp.dot(left, right, precision=PRECISE)

def layer_norm(values, gain_vec, shift_vec):
    average = lax.optimization_barrier(jnp.mean(values, axis=-1, keepdims=True))
    centred = values - average
    spread = lax.optimization_barrier(jnp.mean(centred * centred, axis=-1, keepdims=True))
    return centred * lax.rsqrt(spread + EPSILON) * gain_vec + shift_vec

def offsets_table(rel_table):
    coords = jnp.arange(WIN, dtype=jnp.int32)
    offset_index = (coords[:, None] - coords[None, :] + WIN - 1).astype(jnp.int32)
    return rel_table[offset_index]

def to_windows(token_rows):
    channels = token_rows.shape[-1]
    layout = token_rows.reshape(SIDE, SIDE, channels)
    layout = jnp.pad(layout, ((0, PAD - SIDE), (0, PAD - SIDE), (0, 0)))
    layout = layout.reshape(NWIN, WIN, NWIN, WIN, channels).transpose(0, 2, 1, 3, 4)
    return layout.reshape(NWIN, NWIN, WIN * WIN, channels)

def from_windows(blocks):
    channels = blocks.shape[-1]
    layout = blocks.reshape(NWIN, NWIN, WIN, WIN, channels).transpose(0, 2, 1, 3, 4)
    layout = layout.reshape(PAD, PAD, channels)[:SIDE, :SIDE]
    return layout.reshape(SIDE * SIDE, channels)

def window_row(rows_table, cols_table, window_block):
    queries, key_rows, values = window_block
    length = queries.shape[0]
    query_heads = queries.reshape(length, WIN * WIN, HEADS, HD)
    key_heads = key_rows.reshape(length, WIN * WIN, HEADS, HD)
    value_heads = values.reshape(length, WIN * WIN, HEADS, HD)
    score_scale = HD ** (-0.5)
    base = jnp.einsum('nthe,nshe->nhts', query_heads, key_heads, precision=PRECISE) * score_scale
    query_grid = queries.reshape(length, WIN, WIN, HEADS, HD)
    along_high = jnp.einsum('nyxhe,yke->nhyxk', query_grid, rows_table, precision=PRECISE)
    along_wide = jnp.einsum('nyxhe,xke->nhyxk', query_grid, cols_table, precision=PRECISE)
    scores = base.reshape(length, HEADS, WIN, WIN, WIN, WIN) + along_high[..., :, None] + along_wide[..., None, :]
    scores = low_back(scores.reshape(length, HEADS, WIN * WIN, WIN * WIN))
    probs = low(jax.nn.softmax(scores, axis=-1))
    context = jnp.einsum('nhts,nshe->nthe', probs, value_heads, precision=PRECISE)
    return context.reshape(length, WIN * WIN, HEADS * HD)

def forward(one_image, norm1_gain, norm1_shift, qkv_weight, qv_bias, rel_rows, rel_cols, proj_weight, proj_bias, norm2_gain, norm2_shift, fc1_weight, fc1_bias, fc2_weight, fc2_bias):
    normed_one = low(layer_norm(one_image, norm1_gain, norm1_shift))
    windows = to_windows(normed_one)
    queries = low(low_back(jnp.einsum('rctd,de->rcte', windows, qkv_weight[0], precision=PRECISE) + qv_bias[0]))
    key_rows = low(low_back(jnp.einsum('rctd,de->rcte', windows, qkv_weight[1], precision=PRECISE)))
    values = low(low_back(jnp.einsum('rctd,de->rcte', windows, qkv_weight[2], precision=PRECISE) + qv_bias[1]))
    rows_table = offsets_table(rel_rows)
    cols_table = offsets_table(rel_cols)
    saved_rows = jax.checkpoint(window_row)
    context = lax.map(lambda window_block: saved_rows(rows_table, cols_table, window_block), (queries, key_rows, values))
    context = low(low_back(from_windows(context)))
    projected = low_back(matmul(context, proj_weight) + proj_bias)
    middle = one_image + projected
    normed_two = low(layer_norm(middle, norm2_gain, norm2_shift))
    pre_gelu = low_back(matmul(normed_two, fc1_weight) + fc1_bias)
    hidden = low(jax.nn.gelu(pre_gelu, approximate=False))
    mlp_out = low_back(matmul(hidden, fc2_weight) + fc2_bias)
    return middle + mlp_out

def reference(image_tokens, norm1_gain, norm1_shift, qkv_weight, qv_bias, rel_rows, rel_cols, proj_weight, proj_bias, norm2_gain, norm2_shift, fc1_weight, fc1_bias, fc2_weight, fc2_bias, out_cotangent):
    params = tuple((item.astype(jnp.float32) for item in (norm1_gain, norm1_shift, qkv_weight, qv_bias, rel_rows, rel_cols, proj_weight, proj_bias, norm2_gain, norm2_shift, fc1_weight, fc1_bias, fc2_weight, fc2_bias)))
    images = image_tokens.astype(jnp.float32).reshape(IMAGES, SIDE * SIDE, D)
    cotangents = out_cotangent.astype(jnp.float32).reshape(IMAGES, SIDE * SIDE, D)

    def per_image(totals, image_pair):
        one_image, one_cotangent = image_pair
        result, pullback = jax.vjp(forward, one_image, *params)
        gradients = pullback(one_cotangent)
        totals = tuple((first_item + second_item for first_item, second_item in zip(totals, gradients[1:])))
        return (totals, (result.astype(jnp.bfloat16), gradients[0].astype(jnp.bfloat16)))
    starting = tuple((jnp.zeros_like(item) for item in params))
    totals, outputs = lax.scan(per_image, starting, (images, cotangents))
    block_out = outputs[0].reshape(TOKENS, D)
    input_grad = outputs[1].reshape(TOKENS, D)
    return (block_out, input_grad, totals[0], totals[1], totals[2], totals[3], totals[4], totals[5], totals[6], totals[7], totals[8], totals[9], totals[10], totals[11], totals[12], totals[13])
```

```python
import jax
import jax.numpy as jnp
import numpy as np
from jax import lax
from jax.experimental import pallas as pl
from jax.experimental.pallas import tpu as pltpu
from jax.sharding import PartitionSpec as P

D = 768
HEADS = 12
HD = 64
FF = 3072
WIN = 14
SIDE = 64
NWIN = 5
RELS = 27
EPSILON = 1e-06
F32 = jnp.float32
BF = jnp.bfloat16

SLOTS = 256
KEYS = WIN * 16
PAIR = 2 * SIDE
GREL = 80
OWN = SIDE * SIDE // 2

NN = (((1,), (0,)), ((), ()))
NT = (((1,), (1,)), ((), ()))
TN = (((0,), (0,)), ((), ()))


def dot(left, right, dims=NN):
    return lax.dot_general(left, right, dims, preferred_element_type=F32)


def params(limit=60):
    return pltpu.CompilerParams(vmem_limit_bytes=limit * 2**20)


def whole(shape):
    return pl.BlockSpec(shape, lambda *_: (0,) * len(shape), pipeline_mode=pl.Buffered(1))


STARTS = np.array([[0, 14, 28], [42, 28, 56]], np.int32)


def pair_tables(place):
    block = np.zeros((2, 24), np.int32)
    valid = np.zeros((2, 24), np.int32)
    local = np.zeros((2, 24), np.int32)
    owned = np.zeros((2, 24), np.int32)
    band_of = np.zeros((2, 16), np.int32)
    step_of = np.zeros((2, 16), np.int32)
    for m in range(2):
        for s in range(3):
            for t in range(7):
                row = STARTS[m, s] + 2 * t
                at = s * 8 + t
                block[m, at] = min(row // 2, 31)
                valid[m, at] = row < SIDE
                if 32 * m <= row < 32 * m + 32:
                    local[m, at] = (row - 32 * m) // 2
                    owned[m, at] = 1
                    band_of[m, local[m, at]] = s
                    step_of[m, local[m, at]] = t
            block[m, s * 8 + 7] = block[m, s * 8 + 6]
    pick = lambda table: jnp.where(place == 0, jnp.asarray(table[0]), jnp.asarray(table[1]))
    return tuple(pick(t) for t in (block, valid, local, owned, band_of, step_of))


def spread_rows():
    table = np.zeros((NWIN, 2, 16, PAIR), np.float32)
    for w in range(NWIN):
        for r in range(2):
            for j in range(WIN):
                if WIN * w + j < SIDE:
                    table[w, r, j, r * SIDE + WIN * w + j] = 1
    return table.reshape(NWIN * 32, PAIR)


def rel_order():
    rows = np.full(GREL, -1)
    for m in range(21):
        rows[m] = 26 - (m + 6)
        rows[24 + m] = 26 - m
    cols = np.full(GREL, -1)
    for m in range(RELS):
        cols[48 + m] = 26 - m
    return rows, cols


def rel_onehots():
    rows, cols = rel_order()
    high = (rows[:, None] == np.arange(RELS)[None, :]).astype(np.float32)
    wide = (cols[:, None] == np.arange(RELS)[None, :]).astype(np.float32)
    return high, wide


def norm_parts(values):
    average = jnp.mean(values, axis=-1, keepdims=True)
    centred = values - average
    inverse = lax.rsqrt(jnp.mean(centred * centred, axis=-1, keepdims=True) + EPSILON)
    return centred * inverse, inverse


def window_kernel(block, valid, x, gain, shift, spread, out):
    at = pl.program_id(0) * 8 + pl.program_id(1)

    @pl.when(valid[at] == 1)
    def _():
        scaled, _ = norm_parts(x[...].astype(F32))
        normed = (scaled * gain[...] + shift[...]).astype(BF)
        out[...] = dot(spread[...], normed).astype(BF).reshape(1, NWIN, 32, D)

    @pl.when(valid[at] == 0)
    def _():
        out[...] = jnp.zeros_like(out)


def windows_of(x, gain, shift, spread, block, valid):
    return pl.pallas_call(
        window_kernel,
        grid_spec=pltpu.PrefetchScalarGridSpec(
            num_scalar_prefetch=2,
            grid=(3, 8),
            in_specs=[
                pl.BlockSpec((PAIR, D), lambda s, t, block, valid: (block[s * 8 + t], 0)),
                whole((1, D)),
                whole((1, D)),
                whole((NWIN * 32, PAIR)),
            ],
            out_specs=pl.BlockSpec((1, NWIN, 32, D), lambda s, t, block, valid: (s, 0, t, 0)),
        ),
        out_shape=jax.ShapeDtypeStruct((3, NWIN, SLOTS, D), BF),
        compiler_params=params(),
    )(block, valid, x, gain, shift, spread)


def shift_masks(lanes_from):
    lane = lax.broadcasted_iota(jnp.int32, (1, 128), 1) + lanes_from
    high = lane // 16
    row_shift = jnp.where(lane < 128, 7 - high, jnp.maximum(13 - high, 0))
    col_shift = jnp.maximum(13 - lane % 16, 0)
    return row_shift, col_shift


def skew(table, shift, bits):
    size = table.shape[0]
    for bit in bits:
        moved = pltpu.roll(table, size - bit, 0)
        table = jnp.where((shift & bit) != 0, moved, table)
    return table


def unskew(table, shift, bits):
    for bit in bits:
        moved = pltpu.roll(table, bit, 0)
        table = jnp.where((shift & bit) != 0, moved, table)
    return table


def attend_kernel(x, weights, biases, rel_even, rel_odd, q_out, k_out, v_out, p_out, ctx_out, xt_out, vt):
    band = pl.program_id(0)
    block = x[...].reshape(SLOTS, D)
    xt_out[...] = block.T
    q_out[...] = (dot(block, weights[0]) + biases[0:1, :]).astype(BF).reshape(1, 1, SLOTS, D)
    k_out[...] = dot(block, weights[1]).astype(BF).reshape(1, 1, SLOTS, D)
    values = (dot(block, weights[2]) + biases[2:3, :]).astype(BF)
    v_out[...] = values.reshape(1, 1, SLOTS, D)
    vt[...] = values.T

    def pair_step(pair, lanes):
        cols = pl.ds(pl.multiple_of(pair * 128, 128), 128)
        queries = q_out[0, 0, 0:lanes, cols]
        keys = k_out[0, 0, 0:KEYS, cols]
        even = lax.broadcasted_iota(jnp.int32, (1, 128), 1) < HD
        contexts = []
        for odd in range(2):
            rel = rel_odd if odd else rel_even
            kept = jnp.where(even != (odd == 1), keys, jnp.zeros_like(keys))
            raw = dot(jnp.concatenate([kept, rel[...]], axis=0), queries, NT)
            parts = []
            for tile in range(lanes // 128):
                row_shift, col_shift = shift_masks(tile * 128)
                raw_t = raw[:, tile * 128 : tile * 128 + 128]
                base = raw_t[0:KEYS]
                high = skew(raw_t[KEYS + 24 * tile : KEYS + 24 * tile + 24], row_shift, (4, 2, 1))[0:16]
                wide = skew(raw_t[KEYS + 48 : KEYS + 80], col_shift, (8, 4, 2, 1))[0:16]
                place = lax.broadcasted_iota(jnp.int32, (16, 128), 0)
                wide = jnp.where(place < WIN, wide, -1e30)
                scores = base.reshape(WIN, 16, 128) + wide[None] + high[0:WIN][:, None, :]
                scores = scores.reshape(KEYS, 128)
                peak = jnp.max(scores, axis=0, keepdims=True)
                grown = jnp.exp(scores - peak)
                total = jnp.sum(grown, axis=0, keepdims=True)
                parts.append((grown * (1.0 / total)).astype(BF))
            probs = parts[0] if len(parts) == 1 else jnp.concatenate(parts, axis=1)
            p_out[0, 0, pair * 2 + odd, :, 0:lanes] = probs
            rows = pl.ds(pl.multiple_of(pair * 128 + odd * HD, HD), HD)
            contexts.append(dot(vt[rows, 0:KEYS], probs).astype(BF))
        ctx_out[0, 0, 0:lanes, cols] = jnp.concatenate(contexts, axis=0).T

    @pl.when(band < 2)
    def _():
        for pair in range(HEADS // 2):
            pair_step(pair, 256)

    @pl.when(band == 2)
    def _():
        for pair in range(HEADS // 2):
            pair_step(pair, 128)


def attend(x, weights, biases, rel_even, rel_odd):
    one = pl.BlockSpec((1, 1, SLOTS, D), lambda s, w: (s, w, 0, 0))
    full = jax.ShapeDtypeStruct((3, NWIN, SLOTS, D), BF)
    return pl.pallas_call(
        attend_kernel,
        grid=(3, NWIN),
        in_specs=[one, whole((3, D, D)), whole((8, D)), whole((GREL, 128)), whole((GREL, 128))],
        out_specs=[
            one,
            one,
            one,
            pl.BlockSpec((1, 1, HEADS, KEYS, SLOTS), lambda s, w: (s, w, 0, 0, 0)),
            one,
            pl.BlockSpec((D, SLOTS), lambda s, w: (0, s * NWIN + w)),
        ],
        out_shape=[
            full,
            full,
            full,
            jax.ShapeDtypeStruct((3, NWIN, HEADS, KEYS, SLOTS), BF),
            full,
            jax.ShapeDtypeStruct((D, 3 * NWIN * SLOTS), BF),
        ],
        scratch_shapes=[pltpu.VMEM((D, SLOTS), BF)],
        compiler_params=params(),
    )(x, weights, biases, rel_even, rel_odd)


def middle_kernel(
    band_of, step_of, offset, ctx_a, ctx_b, x, cot, proj, bias, gain, shift, gather,
    middle, normed, normed_t, cot_t, ctx_out,
):
    pieces = [dot(gather[...], c[...].reshape(NWIN * 32, D)).astype(BF) for c in (ctx_a, ctx_b)]
    context = jnp.concatenate(pieces, axis=0)
    ctx_out[...] = context
    value = x[...].astype(F32) + (dot(context, proj[...]) + bias[...])
    middle[...] = value
    scaled, _ = norm_parts(value)
    low = (scaled * gain[...] + shift[...]).astype(BF)
    normed[...] = low
    normed_t[...] = low.T
    cot_t[...] = cot[...].T


def middle_of(ctx, x, cot, proj, bias, gain, shift, gather, band_of, step_of, offset):
    rows = 2 * PAIR
    at = lambda k: lambda i, band_of, step_of, offset: (band_of[2 * i + k], 0, step_of[2 * i + k], 0)
    row_block = pl.BlockSpec((rows, D), lambda i, *_: (i, 0))
    col_block = pl.BlockSpec((D, rows), lambda i, *_: (0, i))
    return pl.pallas_call(
        middle_kernel,
        grid_spec=pltpu.PrefetchScalarGridSpec(
            num_scalar_prefetch=3,
            grid=(OWN // rows,),
            in_specs=[
                pl.BlockSpec((1, NWIN, 32, D), at(0)),
                pl.BlockSpec((1, NWIN, 32, D), at(1)),
                pl.BlockSpec((rows, D), lambda i, band_of, step_of, offset: (offset[0] + i, 0)),
                row_block,
                whole((D, D)),
                whole((1, D)),
                whole((1, D)),
                whole((1, D)),
                whole((PAIR, NWIN * 32)),
            ],
            out_specs=[row_block, row_block, col_block, col_block, row_block],
        ),
        out_shape=[
            jax.ShapeDtypeStruct((OWN, D), F32),
            jax.ShapeDtypeStruct((OWN, D), BF),
            jax.ShapeDtypeStruct((D, OWN), BF),
            jax.ShapeDtypeStruct((D, OWN), BF),
            jax.ShapeDtypeStruct((OWN, D), BF),
        ],
        compiler_params=params(),
    )(band_of, step_of, offset, ctx, ctx, x, cot, proj, bias, gain, shift, gather)


CHUNK = 512
CHUNKS = FF // CHUNK


def feed_kernel(
    normed, normed_t, cot, cot_t, one_a, one_b, bias, two_a, two_b,
    forward, back, one_own, one_other, two_own, two_other, sums, one, two, hidden, grads,
):
    step = pl.program_id(0)

    @pl.when(step == 0)
    def _():
        forward[...] = jnp.zeros_like(forward)
        back[...] = jnp.zeros_like(back)

    @pl.when(step < CHUNKS // 2)
    def _():
        one[...] = one_a[...]
        two[...] = two_a[...]

    @pl.when(step >= CHUNKS // 2)
    def _():
        one[...] = one_b[...]
        two[...] = two_b[...]

    total = jnp.zeros((1, CHUNK), F32)
    for t in range(OWN // 512):
        rows = slice(t * 512, t * 512 + 512)
        pre = dot(normed[rows, :], one[...]) + bias[...]
        phi = 0.5 * (1.0 + lax.erf(pre * 0.7071067811865476))
        slope = phi + pre * (jnp.exp(-0.5 * pre * pre) * 0.3989422804014327)
        low = (pre * phi).astype(BF)
        grad = (dot(cot[rows, :], two[...], NT) * slope).astype(BF)
        hidden[rows, :] = low
        grads[rows, :] = grad
        total += jnp.sum(grad.astype(F32), axis=0, keepdims=True)
        forward[rows, :] += dot(low, two[...])
        back[rows, :] += dot(grad, one[...], NT)
    sums[...] = total

    one_grad = dot(normed_t[...], grads[...]).astype(BF)
    two_grad = dot(cot_t[...], hidden[...]).astype(BF)

    @pl.when(step < CHUNKS // 2)
    def _():
        one_own[...] = one_grad
        two_own[...] = two_grad

    @pl.when(step >= CHUNKS // 2)
    def _():
        one_other[...] = one_grad
        two_other[...] = two_grad


def feed(normed, normed_t, cot, cot_t, one_a, one_b, bias, two_a, two_b):
    half = CHUNKS // 2
    own = lambda j: jnp.minimum(j, half - 1)
    other = lambda j: jnp.maximum(j - half, 0)
    grad_shape = jax.ShapeDtypeStruct((D, FF // 2), BF)
    wide_own = pl.BlockSpec((D, CHUNK), lambda j: (0, own(j)))
    wide_other = pl.BlockSpec((D, CHUNK), lambda j: (0, other(j)))
    return pl.pallas_call(
        feed_kernel,
        grid=(CHUNKS,),
        in_specs=[
            whole((OWN, D)),
            whole((D, OWN)),
            whole((OWN, D)),
            whole((D, OWN)),
            wide_own,
            wide_other,
            pl.BlockSpec((1, CHUNK), lambda j: (0, j)),
            pl.BlockSpec((CHUNK, D), lambda j: (own(j), 0)),
            pl.BlockSpec((CHUNK, D), lambda j: (other(j), 0)),
        ],
        out_specs=[
            pl.BlockSpec((OWN, D), lambda j: (0, 0)),
            pl.BlockSpec((OWN, D), lambda j: (0, 0)),
            wide_own,
            wide_other,
            wide_own,
            wide_other,
            pl.BlockSpec((1, CHUNK), lambda j: (0, j)),
        ],
        out_shape=[
            jax.ShapeDtypeStruct((OWN, D), F32),
            jax.ShapeDtypeStruct((OWN, D), F32),
            grad_shape,
            grad_shape,
            grad_shape,
            grad_shape,
            jax.ShapeDtypeStruct((1, FF), F32),
        ],
        scratch_shapes=[
            pltpu.VMEM((D, CHUNK), BF),
            pltpu.VMEM((CHUNK, D), BF),
            pltpu.VMEM((OWN, CHUNK), BF),
            pltpu.VMEM((OWN, CHUNK), BF),
        ],
        compiler_params=params(62),
    )(normed, normed_t, cot, cot_t, one_a, one_b, bias, two_a, two_b)


def add_row(sums, row, values):
    sums[row : row + 1, :] += jnp.sum(values, axis=0, keepdims=True)


def resid_kernel(middle, forward, back, cot, context, proj, bias, gain, block_out, grad_out, ctx_grad, proj_grad, sums):
    step = pl.program_id(0)

    @pl.when(step == 0)
    def _():
        proj_grad[...] = jnp.zeros_like(proj_grad)
        sums[...] = jnp.zeros_like(sums)

    value = middle[...]
    block_out[...] = (value + (forward[...] + bias[...])).astype(BF)
    scaled, inverse = norm_parts(value)
    upstream = back[...]
    scaled_up = upstream * gain[...]
    first = jnp.mean(scaled_up, axis=-1, keepdims=True)
    second = jnp.mean(scaled_up * scaled, axis=-1, keepdims=True)
    cotangent = cot[...].astype(F32)
    grad = cotangent + inverse * (scaled_up - first - scaled * second)
    grad_out[...] = grad
    low = grad.astype(BF)
    ctx_grad[...] = dot(low, proj[...], NT).astype(BF)
    proj_grad[...] += dot(context[...], low, TN)
    add_row(sums, 0, upstream * scaled)
    add_row(sums, 1, upstream)
    add_row(sums, 2, cotangent)
    add_row(sums, 3, low.astype(F32))


def resid_of(middle, forward, back, cot, context, proj, bias, gain):
    rows = 512
    row_block = pl.BlockSpec((rows, D), lambda i: (i, 0))
    return pl.pallas_call(
        resid_kernel,
        grid=(OWN // rows,),
        in_specs=[row_block] * 5 + [whole((D, D)), whole((1, D)), whole((1, D))],
        out_specs=[
            row_block,
            row_block,
            row_block,
            pl.BlockSpec((D, D), lambda i: (0, 0)),
            pl.BlockSpec((8, D), lambda i: (0, 0)),
        ],
        out_shape=[
            jax.ShapeDtypeStruct((OWN, D), BF),
            jax.ShapeDtypeStruct((OWN, D), F32),
            jax.ShapeDtypeStruct((OWN, D), BF),
            jax.ShapeDtypeStruct((D, D), F32),
            jax.ShapeDtypeStruct((8, D), F32),
        ],
        compiler_params=params(),
    )(middle, forward, back, cot, context, proj, bias, gain)


def attend_back_kernel(
    local, owned, q, k, v, p, ctx_grad, spread, rel_even, rel_odd, fold,
    dq, dk, dv, rel_grad, sums, upstream, kt,
):
    band = pl.program_id(0)
    window = pl.program_id(1)

    @pl.when((band == 0) & (window == 0))
    def _():
        rel_grad[...] = jnp.zeros_like(rel_grad)
        sums[...] = jnp.zeros_like(sums)

    @pl.when(window == 0)
    def _():
        for t in range(7):
            at = band * 8 + t
            rows = pl.ds(pl.multiple_of(local[at] * PAIR, PAIR), PAIR)
            moved = dot(spread[...], ctx_grad[rows, :])
            moved = moved * owned[at].astype(F32)
            upstream[:, 32 * t : 32 * t + 32, :] = moved.astype(BF).reshape(NWIN, 32, D)
        upstream[:, 224:256, :] = jnp.zeros((NWIN, 32, D), BF)

    kt[...] = k[...].reshape(SLOTS, D).T
    even = lax.broadcasted_iota(jnp.int32, (1, 128), 1) < HD

    def pair_step(pair, lanes):
        cols = pl.ds(pl.multiple_of(pair * 128, 128), 128)
        queries = q[0, 0, 0:lanes, cols]
        values = v[0, 0, 0:KEYS, cols]
        ups = upstream[window, 0:lanes, cols]
        dvs, dks, dqs, drs = [], [], [], []
        for odd in range(2):
            rel = rel_odd if odd else rel_even
            kept = jnp.where(even != (odd == 1), values, jnp.zeros_like(values))
            prob_grad = dot(kept, ups, NT)
            probs_low = p[0, 0, pair * 2 + odd, :, 0:lanes]
            probs = probs_low.astype(F32)
            total = jnp.sum(prob_grad * probs, axis=0, keepdims=True)
            score_grad = (probs * (prob_grad - total)).astype(BF)
            dvs.append(dot(probs_low, ups))
            rows = pl.ds(pl.multiple_of(pair * 128 + odd * HD, HD), HD)
            left = jnp.concatenate([kt[rows, 0:KEYS], fold[...]], axis=0)
            both = dot(left, score_grad)
            tables = []
            zero8 = jnp.zeros((8, 128), F32)
            zero24 = jnp.zeros((24, 128), F32)
            zero16 = jnp.zeros((16, 128), F32)
            for tile in range(lanes // 128):
                row_shift, col_shift = shift_masks(tile * 128)
                part = both[:, tile * 128 : tile * 128 + 128]
                high = jnp.concatenate([part[HD : HD + 16], zero8], axis=0)
                wide = jnp.concatenate([part[HD + 16 : HD + 32], zero16], axis=0)
                high = unskew(high, row_shift, (1, 2, 4))
                wide = unskew(wide, col_shift, (1, 2, 4, 8))
                stack = [high, zero24, wide] if tile == 0 else [zero24, high, wide]
                tables.append(jnp.concatenate(stack, axis=0))
            table = tables[0] if len(tables) == 1 else jnp.concatenate(tables, axis=1)
            table = table.astype(BF)
            grads = dot(jnp.concatenate([score_grad, table], axis=0), queries)
            dks.append(grads[0:KEYS])
            drs.append(grads[KEYS:])
            from_rel = dot(rel[...], table, TN)
            dqs.append(both[0:HD] + from_rel[odd * HD : odd * HD + HD])
        dv[0, 0, 0:KEYS, cols] = jnp.where(even, dvs[0], dvs[1]).astype(BF)
        dk[0, 0, 0:KEYS, cols] = (jnp.where(even, dks[0], dks[1]) * HD ** (-0.5)).astype(BF)
        rel_grad[...] += jnp.where(even, drs[0], drs[1])
        dq[0, 0, 0:lanes, cols] = jnp.concatenate(dqs, axis=0).astype(BF).T

    dk[0, 0, KEYS:, :] = jnp.zeros((SLOTS - KEYS, D), BF)
    dv[0, 0, KEYS:, :] = jnp.zeros((SLOTS - KEYS, D), BF)

    @pl.when(band < 2)
    def _():
        for pair in range(HEADS // 2):
            pair_step(pair, 256)

    @pl.when(band == 2)
    def _():
        for pair in range(HEADS // 2):
            pair_step(pair, 128)
        dq[0, 0, 128:, :] = jnp.zeros((128, D), BF)

    sums[0:1, :] += jnp.sum(dq[...].reshape(SLOTS, D).astype(F32), axis=0, keepdims=True)
    sums[1:2, :] += jnp.sum(dv[...].reshape(SLOTS, D).astype(F32), axis=0, keepdims=True)


def fold_table():
    table = np.zeros((32, WIN, 16), np.float32)
    for k in range(WIN):
        for l in range(WIN):
            table[k, k, l] = 1
            table[16 + l, k, l] = 1
    return table.reshape(32, KEYS)


def attend_back(q, k, v, p, ctx_grad, spread, rel_even, rel_odd, fold, local, owned):
    one = pl.BlockSpec((1, 1, SLOTS, D), lambda s, w, *_: (s, w, 0, 0))
    full = jax.ShapeDtypeStruct((3, NWIN, SLOTS, D), BF)
    return pl.pallas_call(
        attend_back_kernel,
        grid_spec=pltpu.PrefetchScalarGridSpec(
            num_scalar_prefetch=2,
            grid=(3, NWIN),
            in_specs=[
                one,
                one,
                one,
                pl.BlockSpec((1, 1, HEADS, KEYS, SLOTS), lambda s, w, *_: (s, w, 0, 0, 0)),
                whole((OWN, D)),
                whole((NWIN * 32, PAIR)),
                whole((GREL, 128)),
                whole((GREL, 128)),
                whole((32, KEYS)),
            ],
            out_specs=[
                one,
                one,
                one,
                pl.BlockSpec((GREL, 128), lambda s, w, *_: (0, 0)),
                pl.BlockSpec((8, D), lambda s, w, *_: (0, 0)),
            ],
            scratch_shapes=[pltpu.VMEM((NWIN, SLOTS, D), BF), pltpu.VMEM((D, SLOTS), BF)],
        ),
        out_shape=[
            full,
            full,
            full,
            jax.ShapeDtypeStruct((GREL, 128), F32),
            jax.ShapeDtypeStruct((8, D), F32),
        ],
        compiler_params=params(),
    )(local, owned, q, k, v, p, ctx_grad, spread, rel_even, rel_odd, fold)


def norm_grad_kernel(dq, dk, dv, weights, gather, out):
    flat = lambda ref: ref[...].reshape(NWIN * 32, D)
    total = dot(flat(dq), weights[0], NT) + dot(flat(dk), weights[1], NT) + dot(flat(dv), weights[2], NT)
    out[...] = dot(gather[...], total.astype(BF)).astype(BF).reshape(1, PAIR, D)


def norm_grad(dq, dk, dv, weights, gather):
    one = pl.BlockSpec((1, NWIN, 32, D), lambda s, t: (s, 0, t, 0))
    return pl.pallas_call(
        norm_grad_kernel,
        grid=(3, 7),
        in_specs=[one, one, one, whole((3, D, D)), whole((PAIR, NWIN * 32))],
        out_specs=pl.BlockSpec((1, PAIR, D), lambda s, t: (s, t, 0)),
        out_shape=jax.ShapeDtypeStruct((3, 7 * PAIR, D), BF),
        compiler_params=params(),
    )(dq, dk, dv, weights, gather)


def qkv_grad_kernel(xt, d, own, other):
    total = dot(xt[...], d[...]).astype(BF)
    own[...] = total[:, : D // 2]
    other[...] = total[:, D // 2 :]


def qkv_grad(xt, d):
    rows = 3 * NWIN * SLOTS
    shape = jax.ShapeDtypeStruct((D, D // 2), BF)
    block = pl.BlockSpec((D // 3, D // 2), lambda i: (i, 0))
    return pl.pallas_call(
        qkv_grad_kernel,
        grid=(3,),
        in_specs=[pl.BlockSpec((D // 3, rows), lambda i: (i, 0)), whole((rows, D))],
        out_specs=[block, block],
        out_shape=[shape, shape],
        compiler_params=params(),
    )(xt, d)


def input_kernel(offset, x, middle_grad, up_a, up_b, gain, out, sums):
    step = pl.program_id(0)

    @pl.when(step == 0)
    def _():
        sums[...] = jnp.zeros_like(sums)

    scaled, inverse = norm_parts(x[...].astype(F32))
    upstream = up_a[...].astype(F32) + up_b[...].astype(F32)
    scaled_up = upstream * gain[...]
    first = jnp.mean(scaled_up, axis=-1, keepdims=True)
    second = jnp.mean(scaled_up * scaled, axis=-1, keepdims=True)
    out[...] = (middle_grad[...] + inverse * (scaled_up - first - scaled * second)).astype(BF)
    add_row(sums, 0, upstream * scaled)
    add_row(sums, 1, upstream)


def input_of(x, middle_grad, up_a, up_b, gain, offset):
    rows = 256
    row_block = pl.BlockSpec((rows, D), lambda i, *_: (i, 0))
    return pl.pallas_call(
        input_kernel,
        grid_spec=pltpu.PrefetchScalarGridSpec(
            num_scalar_prefetch=1,
            grid=(OWN // rows,),
            in_specs=[
                pl.BlockSpec((rows, D), lambda i, offset: (offset[0] + i, 0)),
                row_block,
                row_block,
                row_block,
                whole((1, D)),
            ],
            out_specs=[row_block, pl.BlockSpec((8, D), lambda i, *_: (0, 0))],
        ),
        out_shape=[jax.ShapeDtypeStruct((OWN, D), BF), jax.ShapeDtypeStruct((8, D), F32)],
        compiler_params=params(),
    )(offset, x, middle_grad, up_a, up_b, gain)


def on_device(
    image_tokens,
    norm1_gain,
    norm1_shift,
    qkv_weight,
    qv_bias,
    rel_rows,
    rel_cols,
    proj_weight,
    proj_bias,
    norm2_gain,
    norm2_shift,
    fc1_weight,
    fc1_bias,
    fc2_weight,
    fc2_bias,
    out_cotangent,
):
    place = lax.axis_index("mp")
    swap = lambda value: lax.ppermute(value, "mp", [(0, 1), (1, 0)])
    block, valid, local, owned, band_of, step_of = pair_tables(place)
    offset = (place * (OWN // (2 * PAIR))).astype(jnp.int32).reshape(1)
    row = lambda vector: vector.astype(F32).reshape(1, -1)
    spread = jnp.asarray(spread_rows(), BF)
    gather = jnp.asarray(spread_rows().T, BF)
    fold = jnp.asarray(fold_table(), BF)
    high_hot, wide_hot = (jnp.asarray(t, F32) for t in rel_onehots())
    precise = lax.Precision.HIGHEST
    table = jnp.dot(high_hot, rel_rows.astype(F32), precision=precise)
    table += jnp.dot(wide_hot, rel_cols.astype(F32), precision=precise)
    table = table.astype(BF)
    blank = jnp.zeros_like(table)
    rel_even = jnp.concatenate([table, blank], axis=1)
    rel_odd = jnp.concatenate([blank, table], axis=1)

    scale = jnp.asarray([1.0, HD ** (-0.5), 1.0], BF).reshape(3, 1, 1)
    qkv_all = jnp.concatenate([qkv_weight, swap(qkv_weight)], axis=2) * scale
    small = swap((qv_bias, fc1_bias))
    bias_q = jnp.concatenate([qv_bias[0], small[0][0]])
    bias_v = jnp.concatenate([qv_bias[1], small[0][1]])
    biases = jnp.zeros((8, D), F32).at[0].set(bias_q.astype(F32)).at[2].set(bias_v.astype(F32))
    proj_all = jnp.concatenate([proj_weight, swap(proj_weight)], axis=0)
    fc1_other = swap(fc1_weight)
    fc2_other = swap(fc2_weight)
    fc1_bias_all = row(jnp.concatenate([fc1_bias, small[1]]))

    x_windows = windows_of(image_tokens, row(norm1_gain), row(norm1_shift), spread, block, valid)
    q, k, v, p, ctx, xt = attend(x_windows, qkv_all, biases, rel_even, rel_odd)
    middle, normed, normed_t, cot_t, context = middle_of(
        ctx, image_tokens, out_cotangent, proj_all, row(proj_bias), row(norm2_gain), row(norm2_shift),
        gather, band_of, step_of, offset,
    )
    forward, back, one_own, one_other, two_own, two_other, fc1_sums = feed(
        normed, normed_t, out_cotangent, cot_t, fc1_weight, fc1_other, fc1_bias_all, fc2_weight, fc2_other
    )
    block_out, middle_grad, ctx_grad, proj_grad, two_sums = resid_of(
        middle, forward, back, out_cotangent, context, proj_all, row(fc2_bias), row(norm2_gain)
    )
    dq, dk, dv, rel_grad, qv_sums = attend_back(
        q, k, v, p, ctx_grad, spread, rel_even, rel_odd, fold, local, owned
    )
    back_weights = qkv_all * jnp.asarray([1.0, HD**0.5, 1.0], BF).reshape(3, 1, 1)
    up = norm_grad(dq, dk, dv, back_weights, gather)
    flat = lambda value: value.reshape(3 * NWIN * SLOTS, D)
    wgrads = [qkv_grad(xt, flat(value)) for value in (dq, dk, dv)]

    tokens = lambda band, first, count: up[band, first * SIDE : (first + count) * SIDE]
    zeros = lambda count: jnp.zeros((count * SIDE, D), BF)
    sent = jnp.where(place == 0, tokens(2, 4, 10), jnp.concatenate([tokens(1, 0, 4), zeros(6)]))
    taken = swap(sent)
    up_own = jnp.where(
        place == 0,
        jnp.concatenate([tokens(0, 0, 14), tokens(1, 0, 14), tokens(2, 0, 4)]),
        jnp.concatenate([tokens(1, 4, 10), tokens(0, 0, 14), tokens(2, 0, 8)]),
    )
    up_taken = jnp.where(
        place == 0,
        jnp.concatenate([zeros(28), taken[: 4 * SIDE]]),
        jnp.concatenate([taken, zeros(22)]),
    )
    input_grad, one_sums = input_of(
        image_tokens, middle_grad, up_own, up_taken, row(norm1_gain), offset
    )

    rel_grad = rel_grad[:, :HD] + rel_grad[:, HD:]
    rows_grad = jnp.dot(high_hot.T, rel_grad, precision=precise)
    cols_grad = jnp.dot(wide_hot.T, rel_grad, precision=precise)
    shared = lax.psum(
        (one_sums[0], one_sums[1], rows_grad, cols_grad, two_sums[3], two_sums[0], two_sums[1], two_sums[2]),
        ("dp", "mp"),
    )
    half = D // 2
    proj_low = proj_grad.astype(BF)
    others = swap(
        (
            jnp.stack([g[1] for g in wgrads]),
            proj_low[half:],
            one_other,
            two_other,
            qv_sums[0:2, half:],
            fc1_sums[0, FF // 2 :],
        )
    )
    mine = (
        jnp.stack([g[0] for g in wgrads]),
        proj_low[:half],
        one_own,
        two_own,
        qv_sums[0:2, :half],
        fc1_sums[0, : FF // 2],
    )
    sums = lax.psum(tuple(a + b for a, b in zip(mine, others)), "dp")
    qkv_sum, proj_sum, one_sum, two_sum, qv_sum, fc1_bias_sum = sums
    return (
        block_out,
        input_grad,
        shared[0],
        shared[1],
        qkv_sum.astype(F32),
        qv_sum,
        shared[2],
        shared[3],
        proj_sum.astype(F32),
        shared[4],
        shared[5],
        shared[6],
        one_sum.astype(F32),
        fc1_bias_sum,
        two_sum.astype(F32).T,
        shared[7],
    )


def solution(mesh):
    in_specs = (
        P("dp", None),
        P(),
        P(),
        P(None, None, "mp"),
        P(None, "mp"),
        P(),
        P(),
        P("mp", None),
        P(),
        P(),
        P(),
        P(None, "mp"),
        P("mp"),
        P("mp", None),
        P(),
        P(("dp", "mp"), None),
    )
    out_specs = (
        P(("dp", "mp"), None),
        P(("dp", "mp"), None),
        P(),
        P(),
        P(None, None, "mp"),
        P(None, "mp"),
        P(),
        P(),
        P("mp", None),
        P(),
        P(),
        P(),
        P(None, "mp"),
        P("mp"),
        P("mp", None),
        P(),
    )
    return jax.shard_map(
        on_device, mesh=mesh, in_specs=in_specs, out_specs=out_specs, check_vma=False
    )
```

```python
import jax
import jax.numpy as jnp
import numpy as np
from jax import lax
from jax.experimental import pallas as pl
from jax.experimental.pallas import tpu as pltpu
from jax.sharding import PartitionSpec as P

D = 768
HEADS = 12
HD = 64
FF = 3072
WIN = 14
SIDE = 64
NWIN = 5
RELS = 27
EPSILON = 1e-06
F32 = jnp.float32
BF = jnp.bfloat16

SLOTS = 256
KEYS = WIN * 16
PAIR = 2 * SIDE
GREL = 80
OWN = SIDE * SIDE // 2

HALF = D // 2
TRIO = 3 * HALF
PAIRS = HEADS // 4

NN = (((1,), (0,)), ((), ()))
NT = (((1,), (1,)), ((), ()))
TN = (((0,), (0,)), ((), ()))


def dot(left, right, dims=NN):
    return lax.dot_general(left, right, dims, preferred_element_type=F32)


def params(limit=60):
    return pltpu.CompilerParams(vmem_limit_bytes=limit * 2**20)


def cost(flops, moved, exps=0):
    return pl.CostEstimate(flops=int(flops), bytes_accessed=int(moved), transcendentals=int(exps))


def whole(shape):
    return pl.BlockSpec(shape, lambda *_: (0,) * len(shape), pipeline_mode=pl.Buffered(1))


STARTS = np.array([[0, 14, 28], [42, 28, 56]], np.int32)


def pair_tables(place):
    block = np.zeros((2, 24), np.int32)
    valid = np.zeros((2, 24), np.int32)
    local = np.zeros((2, 24), np.int32)
    owned = np.zeros((2, 24), np.int32)
    band_of = np.zeros((2, 16), np.int32)
    step_of = np.zeros((2, 16), np.int32)
    taken_of = np.zeros((2, 16), np.int32)
    has_taken = np.zeros((2, 16), np.int32)
    taken_of[0, 14:16], has_taken[0, 14:16] = np.arange(2), 1
    taken_of[1, 0:5], has_taken[1, 0:5] = np.arange(5), 1
    for m in range(2):
        for s in range(3):
            for t in range(7):
                row = STARTS[m, s] + 2 * t
                at = s * 8 + t
                block[m, at] = min(row // 2, 31)
                valid[m, at] = row < SIDE
                if 32 * m <= row < 32 * m + 32:
                    local[m, at] = (row - 32 * m) // 2
                    owned[m, at] = 1
                    band_of[m, local[m, at]] = s
                    step_of[m, local[m, at]] = t
            block[m, s * 8 + 7] = block[m, s * 8 + 6]
    pick = lambda table: jnp.where(place == 0, jnp.asarray(table[0]), jnp.asarray(table[1]))
    return tuple(pick(t) for t in (block, valid, local, owned, band_of, step_of, taken_of, has_taken))


def spread_rows():
    table = np.zeros((NWIN, 2, 16, PAIR), np.float32)
    for w in range(NWIN):
        for r in range(2):
            for j in range(WIN):
                if WIN * w + j < SIDE:
                    table[w, r, j, r * SIDE + WIN * w + j] = 1
    return table.reshape(NWIN * 32, PAIR)


def rel_order():
    rows = np.full(GREL, -1)
    for m in range(21):
        rows[m] = 26 - (m + 6)
        rows[24 + m] = 26 - m
    cols = np.full(GREL, -1)
    for m in range(RELS):
        cols[48 + m] = 26 - m
    return rows, cols


def rel_onehots():
    rows, cols = rel_order()
    high = (rows[:, None] == np.arange(RELS)[None, :]).astype(np.float32)
    wide = (cols[:, None] == np.arange(RELS)[None, :]).astype(np.float32)
    return high, wide


GAIN_ONE, SHIFT_ONE, PROJ_BIAS, GAIN_TWO, SHIFT_TWO, FC2_BIAS = range(6)


def norm_parts(values):
    average = jnp.mean(values, axis=-1, keepdims=True)
    centred = values - average
    inverse = lax.rsqrt(jnp.mean(centred * centred, axis=-1, keepdims=True) + EPSILON)
    return centred * inverse, inverse


def vec(table, row):
    return table[row : row + 1, :]


def window_kernel(block, valid, *refs):
    xs, (vectors, spread, out) = refs[:7], refs[7:]
    band = pl.program_id(0)
    for t in range(7):
        scaled, _ = norm_parts(xs[t][...].astype(F32))
        normed = scaled * vec(vectors, GAIN_ONE) + vec(vectors, SHIFT_ONE)
        normed = (normed * valid[band * 8 + t].astype(F32)).astype(BF)
        moved = dot(spread[...], normed).astype(BF)
        out[:, :, 32 * t : 32 * t + 32, :] = moved.reshape(1, NWIN, 32, D)
    out[:, :, 224:, :] = jnp.zeros((1, NWIN, 32, D), BF)


def windows_of(x, vectors, spread, block, valid):
    at = lambda t: lambda s, block, valid: (block[s * 8 + t], 0)
    return pl.pallas_call(
        window_kernel,
        grid_spec=pltpu.PrefetchScalarGridSpec(
            num_scalar_prefetch=2,
            grid=(3,),
            in_specs=[pl.BlockSpec((PAIR, D), at(t)) for t in range(7)]
            + [whole((8, D)), whole((NWIN * 32, PAIR))],
            out_specs=pl.BlockSpec((1, NWIN, SLOTS, D), lambda s, *_: (s, 0, 0, 0)),
        ),
        out_shape=jax.ShapeDtypeStruct((3, NWIN, SLOTS, D), BF),
        compiler_params=params(),
        cost_estimate=cost(3 * 7 * 160 * 128 * 768 * 2, 10e6),
    )(block, valid, *([x] * 7), vectors, spread)


def shift_masks(lanes_from):
    lane = lax.broadcasted_iota(jnp.int32, (1, 128), 1) + lanes_from
    high = lane // 16
    row_shift = jnp.where(lane < 128, 7 - high, jnp.maximum(13 - high, 0))
    col_shift = jnp.maximum(13 - lane % 16, 0)
    return row_shift, col_shift


def skew(table, shift, bits):
    size = table.shape[0]
    for bit in bits:
        moved = pltpu.roll(table, size - bit, 0)
        table = jnp.where((shift & bit) != 0, moved, table)
    return table


def unskew(table, shift, bits):
    for bit in bits:
        moved = pltpu.roll(table, bit, 0)
        table = jnp.where((shift & bit) != 0, moved, table)
    return table


def attend_kernel(x, weights, biases, rel_even, rel_odd, qkv_out, p_out, ctx_out, xt_out, joined, vt):
    band = pl.program_id(0)

    @pl.when((band == 0) & (pl.program_id(1) == 0))
    def _():
        for s in range(3):
            joined[:, s * HALF : s * HALF + HALF] = weights[s]

    block = x[...].reshape(SLOTS, D)
    if xt_out is not None:
        xt_out[...] = block.T
    scales = jnp.where(lax.broadcasted_iota(jnp.int32, (1, TRIO), 1) // HALF == 1, HD ** (-0.5), 1.0)
    low = ((dot(block, joined[...]) + biases[...]) * scales).astype(BF)
    qkv_out[0, 0] = low
    vt[...] = low[:, 2 * HALF :].T

    def pair_step(pair, lanes):
        cols = slice(pair * 128, pair * 128 + 128)
        queries = qkv_out[0, 0, 0:lanes, cols]
        keys = qkv_out[0, 0, 0:KEYS, HALF + pair * 128 : HALF + pair * 128 + 128]
        even = lax.broadcasted_iota(jnp.int32, (1, 128), 1) < HD
        contexts = []
        for odd in range(2):
            rel = rel_odd if odd else rel_even
            kept = jnp.where(even != (odd == 1), keys, jnp.zeros_like(keys))
            raw = dot(jnp.concatenate([kept, rel[...]], axis=0), queries, NT)
            parts = []
            for tile in range(lanes // 128):
                row_shift, col_shift = shift_masks(tile * 128)
                raw_t = raw[:, tile * 128 : tile * 128 + 128]
                base = raw_t[0:KEYS]
                high = skew(raw_t[KEYS + 24 * tile : KEYS + 24 * tile + 24], row_shift, (4, 2, 1))[0:16]
                wide = skew(raw_t[KEYS + 48 : KEYS + 80], col_shift, (8, 4, 2, 1))[0:16]
                place = lax.broadcasted_iota(jnp.int32, (16, 128), 0)
                wide = jnp.where(place < WIN, wide, -1e30)
                scores = base.reshape(WIN, 16, 128) + wide[None] + high[0:WIN][:, None, :]
                scores = scores.reshape(KEYS, 128)
                peak = jnp.max(scores, axis=0, keepdims=True)
                grown = jnp.exp(scores - peak)
                total = jnp.sum(grown, axis=0, keepdims=True)
                parts.append((grown * (1.0 / total)).astype(BF))
            probs = parts[0] if len(parts) == 1 else jnp.concatenate(parts, axis=1)
            p_out[0, 0, pair * 2 + odd, :, 0:lanes] = probs
            rows = slice(pair * 128 + odd * HD, pair * 128 + odd * HD + HD)
            contexts.append(dot(vt[rows, 0:KEYS], probs).astype(BF))
        ctx_out[0, 0, 0:lanes, cols] = jnp.concatenate(contexts, axis=0).T

    @pl.when(band < 2)
    def _():
        for pair in range(PAIRS):
            pair_step(pair, 256)

    @pl.when(band == 2)
    def _():
        for pair in range(PAIRS):
            pair_step(pair, 128)


def attend_plain(x, weights, biases, rel_even, rel_odd, qkv_out, p_out, ctx_out, joined, vt):
    attend_kernel(x, weights, biases, rel_even, rel_odd, qkv_out, p_out, ctx_out, None, joined, vt)


def attend(x, weights, biases, rel_even, rel_odd, first):
    block = lambda width: pl.BlockSpec((1, 1, SLOTS, width), lambda s, w: (s, w, 0, 0))
    shape = lambda width: jax.ShapeDtypeStruct((3, NWIN, SLOTS, width), BF)
    out_specs = [
        block(TRIO),
        pl.BlockSpec((1, 1, HEADS // 2, KEYS, SLOTS), lambda s, w: (s, w, 0, 0, 0)),
        block(HALF),
    ]
    out_shape = [
        shape(TRIO),
        jax.ShapeDtypeStruct((3, NWIN, HEADS // 2, KEYS, SLOTS), BF),
        shape(HALF),
    ]
    if first:
        out_specs.append(pl.BlockSpec((D, SLOTS), lambda s, w: (0, s * NWIN + w)))
        out_shape.append(jax.ShapeDtypeStruct((D, 3 * NWIN * SLOTS), BF))
    return pl.pallas_call(
        attend_kernel if first else attend_plain,
        grid=(3, NWIN),
        in_specs=[block(D), whole((3, D, HALF)), whole((1, TRIO)), whole((GREL, 128)), whole((GREL, 128))],
        out_specs=out_specs,
        out_shape=out_shape,
        scratch_shapes=[pltpu.VMEM((D, TRIO), BF), pltpu.VMEM((HALF, SLOTS), BF)],
        compiler_params=params(),
        cost_estimate=cost(15e9, 45e6, 4e6),
    )(x, weights, biases, rel_even, rel_odd)


def middle_kernel(
    band_of, step_of, offset, own_a, own_b, other_a, other_b, x, cot, proj_own, proj_other, vectors, gather,
    middle, normed, normed_t, cot_t, ctx_out, proj,
):
    @pl.when(pl.program_id(0) == 0)
    def _():
        proj[0:HALF, :] = proj_own[...]
        proj[HALF:, :] = proj_other[...]

    for row, parts in ((0, (own_a, other_a)), (PAIR, (own_b, other_b))):
        for side in range(2):
            moved = dot(gather[...], parts[side][...].reshape(NWIN * 32, HALF)).astype(BF)
            ctx_out[row : row + PAIR, side * HALF : side * HALF + HALF] = moved
    value = x[...].astype(F32) + (dot(ctx_out[...], proj[...]) + vec(vectors, PROJ_BIAS))
    middle[...] = value
    scaled, _ = norm_parts(value)
    low = (scaled * vec(vectors, GAIN_TWO) + vec(vectors, SHIFT_TWO)).astype(BF)
    normed[...] = low
    normed_t[...] = low.T
    cot_t[...] = cot[...].T


def middle_of(ctx_own, ctx_other, x, cot, proj_own, proj_other, vectors, gather, band_of, step_of, offset):
    rows = 2 * PAIR
    at = lambda k: lambda i, band_of, step_of, offset: (band_of[2 * i + k], 0, step_of[2 * i + k], 0)
    row_block = pl.BlockSpec((rows, D), lambda i, *_: (i, 0))
    col_block = pl.BlockSpec((D, rows), lambda i, *_: (0, i))
    return pl.pallas_call(
        middle_kernel,
        grid_spec=pltpu.PrefetchScalarGridSpec(
            num_scalar_prefetch=3,
            grid=(OWN // rows,),
            in_specs=[
                pl.BlockSpec((1, NWIN, 32, HALF), at(0)),
                pl.BlockSpec((1, NWIN, 32, HALF), at(1)),
                pl.BlockSpec((1, NWIN, 32, HALF), at(0)),
                pl.BlockSpec((1, NWIN, 32, HALF), at(1)),
                pl.BlockSpec((rows, D), lambda i, band_of, step_of, offset: (offset[0] + i, 0)),
                row_block,
                whole((HALF, D)),
                whole((HALF, D)),
                whole((8, D)),
                whole((PAIR, NWIN * 32)),
            ],
            out_specs=[row_block, row_block, col_block, col_block, row_block],
            scratch_shapes=[pltpu.VMEM((D, D), BF)],
        ),
        out_shape=[
            jax.ShapeDtypeStruct((OWN, D), F32),
            jax.ShapeDtypeStruct((OWN, D), BF),
            jax.ShapeDtypeStruct((D, OWN), BF),
            jax.ShapeDtypeStruct((D, OWN), BF),
            jax.ShapeDtypeStruct((OWN, D), BF),
        ],
        compiler_params=params(),
        cost_estimate=cost(3e9, 30e6),
    )(band_of, step_of, offset, ctx_own, ctx_own, ctx_other, ctx_other, x, cot, proj_own, proj_other, vectors, gather)


CHUNK = 512
CHUNKS = FF // CHUNK


def feed_kernel(
    normed, normed_t, cot, cot_t, one_a, one_b, bias, two_a, two_b,
    forward, back, one_grad, two_grad, sums, one, two, hidden, grads,
):
    step = pl.program_id(0)

    @pl.when(step == 0)
    def _():
        forward[...] = jnp.zeros_like(forward)
        back[...] = jnp.zeros_like(back)

    @pl.when(step < CHUNKS // 2)
    def _():
        one[...] = one_a[...]
        two[...] = two_a[...]

    @pl.when(step >= CHUNKS // 2)
    def _():
        one[...] = one_b[...]
        two[...] = two_b[...]

    total = jnp.zeros((1, CHUNK), F32)
    for t in range(OWN // 512):
        rows = slice(t * 512, t * 512 + 512)
        pre = dot(normed[rows, :], one[...]) + bias[...]
        phi = 0.5 * (1.0 + lax.erf(pre * 0.7071067811865476))
        slope = phi + pre * (jnp.exp(-0.5 * pre * pre) * 0.3989422804014327)
        low = (pre * phi).astype(BF)
        grad = (dot(cot[rows, :], two[...], NT) * slope).astype(BF)
        hidden[rows, :] = low
        grads[rows, :] = grad
        total += jnp.sum(grad.astype(F32), axis=0, keepdims=True)
        forward[rows, :] += dot(low, two[...])
        back[rows, :] += dot(grad, one[...], NT)
    sums[...] = total

    one_grad[0] = dot(normed_t[...], grads[...]).astype(BF)
    two_grad[0] = dot(cot_t[...], hidden[...]).astype(BF).T


def feed(normed, normed_t, cot, cot_t, one_a, one_b, bias, two_a, two_b):
    half = CHUNKS // 2
    own = lambda j: jnp.minimum(j, half - 1)
    other = lambda j: jnp.maximum(j - half, 0)
    grad_shape = jax.ShapeDtypeStruct((2, D, FF // 2), BF)
    grad_block = pl.BlockSpec((1, D, CHUNK), lambda j: (j // half, 0, j % half))
    return pl.pallas_call(
        feed_kernel,
        grid=(CHUNKS,),
        in_specs=[
            whole((OWN, D)),
            whole((D, OWN)),
            whole((OWN, D)),
            whole((D, OWN)),
            pl.BlockSpec((D, CHUNK), lambda j: (0, own(j))),
            pl.BlockSpec((D, CHUNK), lambda j: (0, other(j))),
            pl.BlockSpec((1, CHUNK), lambda j: (0, j)),
            pl.BlockSpec((CHUNK, D), lambda j: (own(j), 0)),
            pl.BlockSpec((CHUNK, D), lambda j: (other(j), 0)),
        ],
        out_specs=[
            pl.BlockSpec((OWN, D), lambda j: (0, 0)),
            pl.BlockSpec((OWN, D), lambda j: (0, 0)),
            grad_block,
            pl.BlockSpec((1, CHUNK, D), lambda j: (j // half, j % half, 0)),
            pl.BlockSpec((1, CHUNK), lambda j: (0, j)),
        ],
        out_shape=[
            jax.ShapeDtypeStruct((OWN, D), F32),
            jax.ShapeDtypeStruct((OWN, D), F32),
            grad_shape,
            jax.ShapeDtypeStruct((2, FF // 2, D), BF),
            jax.ShapeDtypeStruct((1, FF), F32),
        ],
        scratch_shapes=[
            pltpu.VMEM((D, CHUNK), BF),
            pltpu.VMEM((CHUNK, D), BF),
            pltpu.VMEM((OWN, CHUNK), BF),
            pltpu.VMEM((OWN, CHUNK), BF),
        ],
        compiler_params=params(62),
        cost_estimate=cost(58e9, 60e6, 12e6),
    )(normed, normed_t, cot, cot_t, one_a, one_b, bias, two_a, two_b)


def add_row(sums, row, values):
    sums[row : row + 1, :] += jnp.sum(values, axis=0, keepdims=True)


def resid_kernel(
    middle, forward, back, cot, context, proj_own, proj_other, vectors,
    block_out, grad_out, ctx_grad, grad_own, grad_other, sums, proj, proj_grad,
):
    step = pl.program_id(0)

    @pl.when(step == 0)
    def _():
        proj[0:HALF, :] = proj_own[...]
        proj[HALF:, :] = proj_other[...]
        proj_grad[...] = jnp.zeros_like(proj_grad)
        sums[...] = jnp.zeros_like(sums)

    value = middle[...]
    block_out[...] = (value + (forward[...] + vec(vectors, FC2_BIAS))).astype(BF)
    scaled, inverse = norm_parts(value)
    upstream = back[...]
    scaled_up = upstream * vec(vectors, GAIN_TWO)
    first = jnp.mean(scaled_up, axis=-1, keepdims=True)
    second = jnp.mean(scaled_up * scaled, axis=-1, keepdims=True)
    cotangent = cot[...].astype(F32)
    grad = cotangent + inverse * (scaled_up - first - scaled * second)
    grad_out[...] = grad
    low = grad.astype(BF)
    ctx_grad[...] = dot(low, proj[...], NT).astype(BF)
    proj_grad[...] += dot(context[...], low, TN)
    add_row(sums, 0, upstream * scaled)
    add_row(sums, 1, upstream)
    add_row(sums, 2, cotangent)
    add_row(sums, 3, low.astype(F32))

    @pl.when(step == pl.num_programs(0) - 1)
    def _():
        for out, row in ((grad_own, 0), (grad_other, HALF)):
            for col in (0, HALF):
                out[col : col + HALF, :] = proj_grad[row : row + HALF, col : col + HALF].astype(BF)


def resid_of(middle, forward, back, cot, context, proj_own, proj_other, vectors):
    rows = 512
    row_block = pl.BlockSpec((rows, D), lambda i: (i, 0))
    half_block = pl.BlockSpec((D, HALF), lambda i: (0, 0))
    return pl.pallas_call(
        resid_kernel,
        grid=(OWN // rows,),
        in_specs=[row_block] * 5 + [whole((HALF, D)), whole((HALF, D)), whole((8, D))],
        out_specs=[
            row_block,
            row_block,
            row_block,
            half_block,
            half_block,
            pl.BlockSpec((8, D), lambda i: (0, 0)),
        ],
        out_shape=[
            jax.ShapeDtypeStruct((OWN, D), BF),
            jax.ShapeDtypeStruct((OWN, D), F32),
            jax.ShapeDtypeStruct((OWN, D), BF),
            jax.ShapeDtypeStruct((D, HALF), BF),
            jax.ShapeDtypeStruct((D, HALF), BF),
            jax.ShapeDtypeStruct((8, D), F32),
        ],
        scratch_shapes=[pltpu.VMEM((D, D), BF), pltpu.VMEM((D, D), F32)],
        compiler_params=params(),
        cost_estimate=cost(5e9, 40e6),
    )(middle, forward, back, cot, context, proj_own, proj_other, vectors)


def attend_back_kernel(first, local, owned, qkv, p, ctx_grad, spread, rel_even, rel_odd, fold, *refs):
    d_out, rel_grad, sums, upstream, kt = refs[-5:]
    band = pl.program_id(0) + first
    window = pl.program_id(1)

    @pl.when((band == first) & (window == 0))
    def _():
        rel_grad[...] = jnp.zeros_like(rel_grad)
        sums[...] = jnp.zeros_like(sums)

    @pl.when(window == 0)
    def _():
        for t in range(7):
            at = band * 8 + t
            rows = pl.ds(pl.multiple_of(local[at] * PAIR, PAIR), PAIR)
            moved = dot(spread[...], ctx_grad[rows, :])
            moved = moved * owned[at].astype(F32)
            upstream[:, 32 * t : 32 * t + 32, :] = moved.astype(BF).reshape(NWIN, 32, HALF)
        upstream[:, 224:256, :] = jnp.zeros((NWIN, 32, HALF), BF)

    kt[...] = qkv[0, 0, :, HALF : 2 * HALF].T
    even = lax.broadcasted_iota(jnp.int32, (1, 128), 1) < HD

    def pair_step(pair, lanes):
        cols = slice(pair * 128, pair * 128 + 128)
        shifted = lambda by: slice(by * HALF + pair * 128, by * HALF + pair * 128 + 128)
        queries = qkv[0, 0, 0:lanes, shifted(0)]
        values = qkv[0, 0, 0:KEYS, shifted(2)]
        ups = upstream[window, 0:lanes, cols]
        dvs, dks, dqs, drs = [], [], [], []
        for odd in range(2):
            rel = rel_odd if odd else rel_even
            kept = jnp.where(even != (odd == 1), values, jnp.zeros_like(values))
            prob_grad = dot(kept, ups, NT)
            probs_low = p[0, 0, pair * 2 + odd, :, 0:lanes]
            probs = probs_low.astype(F32)
            total = jnp.sum(prob_grad * probs, axis=0, keepdims=True)
            score_grad = (probs * (prob_grad - total)).astype(BF)
            dvs.append(dot(probs_low, ups))
            rows = slice(pair * 128 + odd * HD, pair * 128 + odd * HD + HD)
            left = jnp.concatenate([kt[rows, 0:KEYS], fold[...]], axis=0)
            both = dot(left, score_grad)
            tables = []
            zero8 = jnp.zeros((8, 128), F32)
            zero24 = jnp.zeros((24, 128), F32)
            zero16 = jnp.zeros((16, 128), F32)
            for tile in range(lanes // 128):
                row_shift, col_shift = shift_masks(tile * 128)
                part = both[:, tile * 128 : tile * 128 + 128]
                high = jnp.concatenate([part[HD : HD + 16], zero8], axis=0)
                wide = jnp.concatenate([part[HD + 16 : HD + 32], zero16], axis=0)
                high = unskew(high, row_shift, (1, 2, 4))
                wide = unskew(wide, col_shift, (1, 2, 4, 8))
                stack = [high, zero24, wide] if tile == 0 else [zero24, high, wide]
                tables.append(jnp.concatenate(stack, axis=0))
            table = tables[0] if len(tables) == 1 else jnp.concatenate(tables, axis=1)
            table = table.astype(BF)
            grads = dot(jnp.concatenate([score_grad, table], axis=0), queries)
            dks.append(grads[0:KEYS])
            drs.append(grads[KEYS:])
            from_rel = dot(rel[...], table, TN)
            dqs.append(both[0:HD] + from_rel[odd * HD : odd * HD + HD])
        d_out[0, 0, 0:lanes, shifted(0)] = jnp.concatenate(dqs, axis=0).astype(BF).T
        d_out[0, 0, 0:KEYS, shifted(1)] = (jnp.where(even, dks[0], dks[1]) * HD ** (-0.5)).astype(BF)
        d_out[0, 0, 0:KEYS, shifted(2)] = jnp.where(even, dvs[0], dvs[1]).astype(BF)
        rel_grad[...] += jnp.where(even, drs[0], drs[1])

    d_out[0, 0, KEYS:, HALF:] = jnp.zeros((SLOTS - KEYS, 2 * HALF), BF)

    @pl.when(band < 2)
    def _():
        for pair in range(PAIRS):
            pair_step(pair, 256)

    @pl.when(band == 2)
    def _():
        for pair in range(PAIRS):
            pair_step(pair, 128)
        d_out[0, 0, 128:, 0:HALF] = jnp.zeros((128, HALF), BF)

    sums[0:1, :] += jnp.sum(d_out[...].reshape(SLOTS, TRIO).astype(F32), axis=0, keepdims=True)


def fold_table():
    table = np.zeros((32, WIN, 16), np.float32)
    for k in range(WIN):
        for l in range(WIN):
            table[k, k, l] = 1
            table[16 + l, k, l] = 1
    return table.reshape(32, KEYS)


def attend_back(qkv, p, ctx_grad, side, spread, rel_even, rel_odd, fold, local, owned, bands, *d_in):
    first, last = bands
    block = pl.BlockSpec((1, 1, SLOTS, TRIO), lambda s, w, *_: (s + first, w, 0, 0))
    share = (last - first) / 3
    return pl.pallas_call(
        lambda *refs: attend_back_kernel(first, *refs),
        grid_spec=pltpu.PrefetchScalarGridSpec(
            num_scalar_prefetch=2,
            grid=(last - first, NWIN),
            in_specs=[
                block,
                pl.BlockSpec((1, 1, HEADS // 2, KEYS, SLOTS), lambda s, w, *_: (s + first, w, 0, 0, 0)),
                pl.BlockSpec((OWN, HALF), lambda *_: (0, side), pipeline_mode=pl.Buffered(1)),
                whole((NWIN * 32, PAIR)),
                whole((GREL, 128)),
                whole((GREL, 128)),
                whole((32, KEYS)),
            ]
            + [pl.BlockSpec(memory_space=pl.ANY)] * len(d_in),
            out_specs=[
                block,
                pl.BlockSpec((GREL, 128), lambda s, w, *_: (0, 0)),
                pl.BlockSpec((8, TRIO), lambda s, w, *_: (0, 0)),
            ],
            scratch_shapes=[pltpu.VMEM((NWIN, SLOTS, HALF), BF), pltpu.VMEM((HALF, SLOTS), BF)],
        ),
        out_shape=[
            jax.ShapeDtypeStruct((3, NWIN, SLOTS, TRIO), BF),
            jax.ShapeDtypeStruct((GREL, 128), F32),
            jax.ShapeDtypeStruct((8, TRIO), F32),
        ],
        input_output_aliases={9: 0} if d_in else {},
        compiler_params=params(),
        cost_estimate=cost(20e9 * share, 45e6 * share),
    )(local, owned, qkv, p, ctx_grad, spread, rel_even, rel_odd, fold, *d_in)


def norm_grad_kernel(own, other, weights_own, weights_other, gather, *refs):
    out, joined = refs[-2:]

    @pl.when((pl.program_id(0) == 0) & (pl.program_id(1) == 0))
    def _():
        for s in range(3):
            joined[:, s * HALF : s * HALF + HALF] = weights_own[s]
            joined[:, TRIO + s * HALF : TRIO + s * HALF + HALF] = weights_other[s]

    rows = NWIN * 128
    left = jnp.concatenate([own[...].reshape(rows, TRIO), other[...].reshape(rows, TRIO)], axis=1)
    total = dot(left, joined[...], NT).astype(BF).reshape(NWIN, 4, 32, D)
    for t in range(4):
        moved = dot(gather[...], total[:, t].reshape(NWIN * 32, D)).astype(BF)
        out[:, t * PAIR : t * PAIR + PAIR, :] = moved.reshape(1, PAIR, D)


def norm_grad(own, other, weights_own, weights_other, gather, bands, *before):
    first, last = bands
    share = (last - first) / 3
    block = pl.BlockSpec((1, NWIN, 128, TRIO), lambda s, t: (s + first, 0, t, 0))
    return pl.pallas_call(
        norm_grad_kernel,
        grid=(last - first, 2),
        in_specs=[block, block, whole((3, D, HALF)), whole((3, D, HALF)), whole((PAIR, NWIN * 32))]
        + [pl.BlockSpec(memory_space=pl.ANY)] * len(before),
        out_specs=pl.BlockSpec((1, 4 * PAIR, D), lambda s, t: (s + first, t, 0)),
        out_shape=jax.ShapeDtypeStruct((3, 8 * PAIR, D), BF),
        input_output_aliases={5: 0} if before else {},
        scratch_shapes=[pltpu.VMEM((D, 2 * TRIO), BF)],
        compiler_params=params(),
        cost_estimate=cost(14e9 * share, 30e6 * share),
    )(own, other, weights_own, weights_other, gather, *before)


def qkv_grad_kernel(xt, d, out, total):
    step = pl.program_id(0)
    part = dot(xt[...], d[...])

    @pl.when(step == 0)
    def _():
        total[...] = part

    @pl.when(step > 0)
    def _():
        total[...] += part

    @pl.when(step == pl.num_programs(0) - 1)
    def _():
        for s in range(3):
            out[s] = total[:, s * HALF : s * HALF + HALF].astype(BF)


def qkv_grad(xt, d):
    rows = NWIN * SLOTS
    return pl.pallas_call(
        qkv_grad_kernel,
        grid=(3,),
        in_specs=[pl.BlockSpec((D, rows), lambda i: (0, i)), pl.BlockSpec((rows, TRIO), lambda i: (i, 0))],
        out_specs=pl.BlockSpec((3, D, HALF), lambda i: (0, 0, 0)),
        out_shape=jax.ShapeDtypeStruct((3, D, HALF), BF),
        scratch_shapes=[pltpu.VMEM((D, TRIO), F32)],
        compiler_params=params(),
        cost_estimate=cost(7e9, 16e6),
    )(xt, d.reshape(3 * rows, TRIO))


def input_kernel(
    band_of, step_of, taken_of, has_taken, offset, x, middle_grad, up_a, up_b, taken_a, taken_b, vectors, out, sums
):
    step = pl.program_id(0)

    @pl.when(step == 0)
    def _():
        sums[...] = jnp.zeros_like(sums)

    for k, (up, taken) in enumerate(((up_a, taken_a), (up_b, taken_b))):
        rows = slice(k * PAIR, k * PAIR + PAIR)
        scaled, inverse = norm_parts(x[rows, :].astype(F32))
        shared = taken[...].astype(F32) * has_taken[2 * step + k].astype(F32)
        upstream = up[0].astype(F32) + shared
        scaled_up = upstream * vec(vectors, GAIN_ONE)
        first = jnp.mean(scaled_up, axis=-1, keepdims=True)
        second = jnp.mean(scaled_up * scaled, axis=-1, keepdims=True)
        out[rows, :] = (middle_grad[rows, :] + inverse * (scaled_up - first - scaled * second)).astype(BF)
        add_row(sums, 0, upstream * scaled)
        add_row(sums, 1, upstream)


def input_of(x, middle_grad, up, taken, vectors, band_of, step_of, taken_of, has_taken, offset):
    rows = 2 * PAIR
    row_block = pl.BlockSpec((rows, D), lambda i, *_: (i, 0))
    up_at = lambda k: lambda i, band_of, step_of, *_: (band_of[2 * i + k], step_of[2 * i + k], 0)
    taken_at = lambda k: lambda i, band_of, step_of, taken_of, *_: (taken_of[2 * i + k], 0)
    return pl.pallas_call(
        input_kernel,
        grid_spec=pltpu.PrefetchScalarGridSpec(
            num_scalar_prefetch=5,
            grid=(OWN // rows,),
            in_specs=[
                pl.BlockSpec((rows, D), lambda i, b, s, t, h, offset: (offset[0] + i, 0)),
                row_block,
                pl.BlockSpec((1, PAIR, D), up_at(0)),
                pl.BlockSpec((1, PAIR, D), up_at(1)),
                pl.BlockSpec((PAIR, D), taken_at(0)),
                pl.BlockSpec((PAIR, D), taken_at(1)),
                whole((8, D)),
            ],
            out_specs=[row_block, pl.BlockSpec((8, D), lambda i, *_: (0, 0))],
        ),
        out_shape=[jax.ShapeDtypeStruct((OWN, D), BF), jax.ShapeDtypeStruct((8, D), F32)],
        compiler_params=params(),
        cost_estimate=cost(1e8, 20e6),
    )(band_of, step_of, taken_of, has_taken, offset, x, middle_grad, up, up, taken, taken, vectors)


MESH = pl.DeviceIdType.MESH
SMALL = 24


def bits_of(size):
    return size.bit_length() - 1


def line_plan(order, rows):
    plan, doubles = [], [("double", order[0], 2 * rows)]
    for bit in order[1:]:
        if rows % 32 == 0:
            doubles.append(("double", bit, rows))
            rows //= 2
            plan.append(("halve", bit, rows))
        else:
            plan.append(("both", bit, rows))
    return plan + doubles[::-1]


def last_kernel(bits, plans, orders, *refs):
    (line_a, line_b, one_sums, two_sums, fc1_sums, sums_a, sums_c, sums_b, sums_d) = refs[:9]
    rel_a, rel_b, rel_c, rel_d, hots, out, small, rel = refs[9:17]
    result, core_landed, small_landed, rel_landed, sends, recvs = refs[17:23]
    rooms = refs[23:]
    dp, mp = lax.axis_index("dp"), lax.axis_index("mp")
    bit_at = lambda bit: mp if bit == 0 else (dp // bit) % 2

    def partner(bit):
        if bit == 0:
            return (dp, 1 - mp)
        return (jnp.where(bit_at(bit) == 0, dp + bit, dp - bit), mp)

    barrier = pltpu.get_barrier_semaphore()
    every = [1] + bits + [0]
    for bit in every:
        pl.semaphore_signal(barrier, inc=1, device_id=partner(bit), device_id_type=MESH)

    small[...] = jnp.zeros_like(small)
    small[0:2, :] = one_sums[0:2, :]
    small[2:6, :] = two_sums[0:4, :]
    first = mp == 0
    own = [sums_a[0:1, :] + sums_c[0:1, :], fc1_sums[0:1, 0 : FF // 2]]
    other = [sums_b[0:1, :] + sums_d[0:1, :], fc1_sums[0:1, FF // 2 :]]
    for row, flip in ((6, False), (9, True)):
        picked = [jnp.where(first != flip, a, b) for a, b in zip(own, other)]
        small[row : row + 1, 0:HALF] = picked[0][:, 0:HALF]
        small[row : row + 1, HALF:] = picked[0][:, 2 * HALF :]
        small[row + 1 : row + 2, :] = picked[1][:, 0:D]
        small[row + 2 : row + 3, :] = picked[1][:, D:]
    table = rel_a[...] + rel_b[...] + rel_c[...] + rel_d[...]
    table = lax.dot_general(hots[...], table, TN, precision=lax.Precision.HIGHEST, preferred_element_type=F32)
    rel[...] = table + pltpu.roll(table, HD, 1)
    pl.semaphore_wait(barrier, len(every))

    count = [0]

    def send(src, dst, bit):
        at = count[0]
        count[0] += 1
        copy = pltpu.make_async_remote_copy(
            src_ref=src,
            dst_ref=dst,
            send_sem=sends.at[at],
            recv_sem=recvs.at[at],
            device_id=partner(bit),
            device_id_type=MESH,
        )
        copy.start()
        return copy

    values = [line_a, line_b]
    starts = [bit_at(order[0]) * (D // 2) for order in orders]
    sizes = [D // 2 for _ in orders]
    placed = [False, False]
    small_bits = bits + [0, 1]
    used = 0
    for at in range(max([len(small_bits)] + [len(plan) for plan in plans])):
        copies, adds = [], []
        if at < len(small_bits):
            copies.append(send(small, small_landed.at[at], small_bits[at]))
            copies.append(send(rel, rel_landed.at[at], small_bits[at]))
        for k, plan in enumerate(plans):
            if at >= len(plan):
                continue
            kind, bit, after = plan[at]
            if kind == "double":
                here = pl.ds(pl.multiple_of(starts[k], 16), sizes[k])
                if not placed[k]:
                    result[k, here, :] = values[k][...]
                    placed[k] = True
                copies.append(send(result.at[k, here], result.at[k, here], bit))
                starts[k] = starts[k] - bit_at(bit) * sizes[k]
            else:
                mine = bit_at(bit) if kind == "halve" else 0
                gone = 1 - mine if kind == "halve" else 0
                room, total = rooms[used], rooms[used + 1]
                used += 2
                gone = pl.ds(pl.multiple_of(gone * after, 16), after)
                copies.append(send(values[k].at[gone], room, bit))
                adds.append((k, pl.ds(pl.multiple_of(mine * after, 16), after), room, total))
                starts[k] = starts[k] + mine * after
            sizes[k] = after
        for copy in copies:
            copy.wait()
        for k, rows, room, total in adds:
            total[...] = (values[k][rows, :].astype(F32) + room[...].astype(F32)).astype(BF)
            values[k] = total
        if at < len(small_bits):
            small[...] += small_landed[at]
            rel[...] += rel_landed[at]
    copy = send(result, core_landed, 1)
    mine = pl.ds(pl.multiple_of(dp % 2 * 2, 2), 2)
    theirs = pl.ds(pl.multiple_of((1 - dp % 2) * 2, 2), 2)
    out[mine] = result[...]
    copy.wait()
    out[theirs] = core_landed[...]


def last_sums(bits, orders, lines, sums, rels, hots):
    vmem = pl.BlockSpec(memory_space=pltpu.VMEM)
    rounds = len(bits) + 2
    copies = 2 * rounds + 4 * len(bits) + 1
    plans = [line_plan(order, D // 2) for order in orders]
    rooms = []
    for at in range(len(plans[0])):
        for plan in plans:
            if plan[at][0] != "double":
                rooms += [pltpu.VMEM((plan[at][2], HALF), BF)] * 2
    return pl.pallas_call(
        lambda *refs: last_kernel(bits, plans, orders, *refs),
        in_specs=[vmem] * (2 + len(sums) + len(rels) + 1),
        out_specs=[vmem] * 3,
        out_shape=[
            jax.ShapeDtypeStruct((4, D, HALF), BF),
            jax.ShapeDtypeStruct((SMALL, D), F32),
            jax.ShapeDtypeStruct((56, 128), F32),
        ],
        scratch_shapes=[
            pltpu.VMEM((2, D, HALF), BF),
            pltpu.VMEM((2, D, HALF), BF),
            pltpu.VMEM((rounds, SMALL, D), F32),
            pltpu.VMEM((rounds, 56, 128), F32),
            pltpu.SemaphoreType.DMA((copies,)),
            pltpu.SemaphoreType.DMA((copies,)),
        ]
        + rooms,
        compiler_params=pltpu.CompilerParams(
            collective_id=0, has_side_effects=True, vmem_limit_bytes=40 * 2**20
        ),
    )(*lines, *sums, *rels, hots)


CORE, PAIRED = 1, 0


def bit_of(bit):
    return lax.axis_index("mp") if bit == PAIRED else (lax.axis_index("dp") // bit) % 2


def exchange(value, bit):
    if bit == PAIRED:
        return lax.ppermute(value, "mp", [(0, 1), (1, 0)])
    return lax.ppermute(value, "dp", [(i, i ^ bit) for i in range(lax.axis_size("dp"))])


class Line:
    def __init__(self, value, places, order, back):
        self.value = value
        self.places = list(places)
        self.steps = [("halve", bit) for bit in order] + [("double", bit) for bit in back]
        self.rank = {bit: at for at, bit in enumerate(places)}
        self.sent = self.kept = self.taken = None

    def prepare(self):
        kind, bit = self.steps[0]
        if kind != "halve":
            self.sent = self.value
            return
        axis = self.places.index(bit)
        if bit == PAIRED:
            part = lambda at: lax.index_in_dim(self.value, at, axis, keepdims=False)
            self.kept, self.sent = part(0), part(1)
        else:
            mine = bit_of(bit)
            part = lambda at: lax.dynamic_index_in_dim(self.value, at, axis, keepdims=False)
            self.kept, self.sent = part(mine), part(1 - mine)

    def launch(self):
        self.taken = exchange(self.sent, self.steps[0][1])

    def land(self):
        kind, bit = self.steps.pop(0)
        if kind == "halve":
            self.places.remove(bit)
            self.value = self.kept + self.taken
        elif kind == "pass":
            self.value = self.taken
        else:
            self.places = sorted(self.places + [bit], key=self.rank.get)
            first = bit_of(bit) == 0
            ends = (lambda v: v.astype(F32)) if not self.steps else (lambda v: v)
            low = ends(jnp.where(first, self.value, self.taken))
            high = ends(jnp.where(first, self.taken, self.value))
            self.value = jnp.stack([low, high], axis=self.places.index(bit))
        self.taken = None


def advance(anchor, lines):
    flying = [line for line in lines if line.taken is not None]
    anchor, taken = lax.optimization_barrier((anchor, [line.taken for line in flying]))
    for line, value in zip(flying, taken):
        line.taken = value
        line.land()
    going = [line for line in lines if line.steps]
    for line in going:
        line.prepare()
    anchor, sent = lax.optimization_barrier((anchor, [line.sent for line in going]))
    for line, value in zip(going, sent):
        line.sent = value
        line.launch()
    return anchor


def finish(lines):
    while any(line.steps for line in lines):
        for line in lines:
            if not line.steps:
                continue
            if line.taken is None:
                line.prepare()
                line.launch()
        for line in lines:
            if line.taken is not None:
                line.land()


def on_device(
    image_tokens,
    norm1_gain,
    norm1_shift,
    qkv_weight,
    qv_bias,
    rel_rows,
    rel_cols,
    proj_weight,
    proj_bias,
    norm2_gain,
    norm2_shift,
    fc1_weight,
    fc1_bias,
    fc2_weight,
    fc2_bias,
    out_cotangent,
):
    place = lax.axis_index("mp")
    core = lax.axis_index("dp") % 2
    swap = lambda value: lax.ppermute(value, "mp", [(0, 1), (1, 0)])
    size = lax.axis_size("dp")
    core_swap = lambda value: lax.ppermute(value, "dp", [(i, i ^ 1) for i in range(size)])

    def from_partner(weight):
        rows = weight.shape[-2] // 2
        half = lax.dynamic_slice_in_dim(weight, core * rows, rows, weight.ndim - 2)
        mine = swap(half)
        theirs = core_swap(mine)
        low = jnp.where(core == 0, mine, theirs)
        high = jnp.where(core == 0, theirs, mine)
        return jnp.concatenate([low, high], axis=weight.ndim - 2)

    block, valid, local, owned, band_of, step_of, taken_of, has_taken = pair_tables(place)
    offset = (place * (OWN // (2 * PAIR))).astype(jnp.int32).reshape(1)
    zero_row = jnp.zeros((D,), BF)
    vectors = jnp.stack(
        [norm1_gain, norm1_shift, proj_bias, norm2_gain, norm2_shift, fc2_bias, zero_row, zero_row]
    ).astype(F32)
    spread = jnp.asarray(spread_rows(), BF)
    gather = jnp.asarray(spread_rows().T, BF)
    fold = jnp.asarray(fold_table(), BF)
    high_hot, wide_hot = (jnp.asarray(t, F32) for t in rel_onehots())
    precise = lax.Precision.HIGHEST
    hots = jnp.concatenate([high_hot, wide_hot], axis=1)
    rels = jnp.concatenate([rel_rows, rel_cols], axis=0)
    table = jnp.dot(hots.astype(BF), rels, preferred_element_type=F32).astype(BF)
    blank = jnp.zeros_like(table)
    rel_even = jnp.concatenate([table, blank], axis=1)
    rel_odd = jnp.concatenate([blank, table], axis=1)

    trio = lambda q, v: jnp.concatenate([q, jnp.zeros((HALF,), BF), v]).astype(F32).reshape(1, TRIO)
    bias_own = trio(qv_bias[0], qv_bias[1])
    qkv_other = from_partner(qkv_weight)

    x_windows = windows_of(image_tokens, vectors, spread, block, valid)
    biases, x_windows = lax.optimization_barrier((jnp.concatenate([qv_bias.reshape(-1), fc1_bias]), x_windows))
    small = swap(biases)
    qkv_a, p_a, ctx_a, xt = attend(x_windows, qkv_weight, bias_own, rel_even, rel_odd, True)
    bias_other = trio(small[:HALF], small[HALF:D])
    fc1_bias_all = jnp.concatenate([fc1_bias, small[D:]]).astype(F32).reshape(1, FF)
    late = lax.optimization_barrier((qkv_other, proj_weight, fc1_weight, fc2_weight))
    qkv_other = late[0]
    proj_other, fc1_other, fc2_other = (from_partner(w) for w in late[1:])
    qkv_b, p_b, ctx_b = attend(x_windows, qkv_other, bias_other, rel_even, rel_odd, False)
    middle, normed, normed_t, cot_t, context = middle_of(
        ctx_a, ctx_b, image_tokens, out_cotangent, proj_weight, proj_other, vectors,
        gather, band_of, step_of, offset,
    )
    forward, back, one_grad, two_grad, fc1_sums = feed(
        normed, normed_t, out_cotangent, cot_t, fc1_weight, fc1_other, fc1_bias_all, fc2_weight, fc2_other
    )
    bits = [2**k for k in range(1, bits_of(size))]
    turned = bits[1:2] + bits[0:1] + bits[2:]
    count = 2 ** (len(bits) + 1)
    places = [CORE] + bits

    def feed_line(value, order, back):
        value = value.reshape((2,) * (len(bits) + 2) + (value.shape[1] // count, value.shape[2]))
        return Line(value, [PAIRED] + places, [CORE] + order, back + [CORE])

    one_line = feed_line(one_grad, [PAIRED] + bits, bits[::-1])
    two_line = feed_line(two_grad, bits[:2] + [PAIRED] + bits[2:], turned[::-1])
    feed_lines = [one_line, two_line]

    middle = advance(middle, feed_lines)
    block_out, middle_grad, ctx_grad, proj_own, proj_oth, two_sums = resid_of(
        middle, forward, back, out_cotangent, context, proj_weight, proj_other, vectors
    )
    back_of = lambda qkv, p, side, grad, bands, *d: attend_back(
        qkv, p, grad, side, spread, rel_even, rel_odd, fold, local, owned, bands, *d
    )
    joined = lambda qkv, proj: jnp.concatenate([qkv.reshape(3 * D, HALF), proj], axis=0).reshape(
        (2,) * (len(bits) + 1) + (4 * D // count, HALF)
    )
    ctx_grad = advance(ctx_grad, feed_lines)
    d_b, rel_b, sums_b = back_of(qkv_b, p_b, 1, ctx_grad, (1, 3))
    d_b = advance(d_b, feed_lines)
    d_b, rel_b0, sums_b0 = back_of(qkv_b, p_b, 1, ctx_grad, (0, 1), d_b)
    d_b = advance(d_b, feed_lines)
    grad_b = qkv_grad(xt, d_b)
    line_b = Line(joined(grad_b, proj_oth), places, [CORE], [])
    line_b.steps.append(("pass", PAIRED))
    lines = feed_lines + [line_b]
    ctx_grad, grad_b = lax.optimization_barrier((ctx_grad, grad_b))
    ctx_grad = advance(ctx_grad, lines)
    d_a, rel_a, sums_a = back_of(qkv_a, p_a, 0, ctx_grad, (1, 3))
    d_a = advance(d_a, lines)
    up = norm_grad(d_a, d_b, qkv_weight, qkv_other, gather, (1, 3))
    tokens = lambda band, first, count: up[band, first * SIDE : (first + count) * SIDE]
    fill = jnp.zeros((6 * SIDE, D), BF)
    sent = jnp.where(place == 0, tokens(2, 4, 10), jnp.concatenate([tokens(1, 0, 4), fill]))
    shared_line = Line(sent, [], [], [])
    shared_line.steps.append(("pass", PAIRED))
    d_a = advance(d_a, [shared_line])
    d_a, rel_a0, sums_a0 = back_of(qkv_a, p_a, 0, ctx_grad, (0, 1), d_a)
    d_a = advance(d_a, lines + [shared_line])
    taken = shared_line.value
    grad_a = qkv_grad(xt, d_a)
    line_a = Line(joined(grad_a, proj_own), places, [CORE], [])
    lines = feed_lines + [line_a]
    grad_a, d_a = lax.optimization_barrier((grad_a, d_a))
    d_a = advance(d_a, lines)
    up = norm_grad(d_a, d_b, qkv_weight, qkv_other, gather, (0, 1), up)
    up = advance(up, lines)
    both = (line_a.value + line_b.value).reshape(2, 2, D // 2, HALF)
    q_lines = [Line(both[0], bits[:1], bits[:1], []), Line(both[1], turned[:1], turned[:1], [])]
    up = advance(up, q_lines)
    input_grad, one_sums = input_of(
        image_tokens, middle_grad, up, taken, vectors, band_of, step_of, taken_of, has_taken, offset
    )
    one_sums = advance(one_sums, feed_lines + q_lines)
    finish(feed_lines)
    four, small, rel = last_sums(
        bits,
        [bits, turned],
        [line.value for line in q_lines],
        [one_sums, two_sums, fc1_sums, sums_a, sums_a0, sums_b, sums_b0],
        [rel_a, rel_a0, rel_b, rel_b0],
        jnp.pad(hots, ((0, 0), (0, 2))),
    )
    one_sum = one_line.value.reshape(D, FF // 2)
    two_sum = two_line.value.reshape(FF // 2, D)
    mine = jnp.where(place == 0, small[6:9], small[9:12])
    return (
        block_out,
        input_grad,
        small[0],
        small[1],
        four[0:3].astype(F32),
        mine[0].reshape(2, HALF),
        rel[:RELS, :HD],
        rel[RELS : 2 * RELS, :HD],
        jnp.concatenate([four[3, :HALF], four[3, HALF:]], axis=1).astype(F32),
        small[5],
        small[2],
        small[3],
        one_sum,
        mine[1:3].reshape(-1),
        two_sum,
        small[4],
    )


def solution(mesh):
    in_specs = (
        P("dp", None),
        P(),
        P(),
        P(None, None, "mp"),
        P(None, "mp"),
        P(),
        P(),
        P("mp", None),
        P(),
        P(),
        P(),
        P(None, "mp"),
        P("mp"),
        P("mp", None),
        P(),
        P(("dp", "mp"), None),
    )
    out_specs = (
        P(("dp", "mp"), None),
        P(("dp", "mp"), None),
        P(),
        P(),
        P(None, None, "mp"),
        P(None, "mp"),
        P(),
        P(),
        P("mp", None),
        P(),
        P(),
        P(),
        P(None, "mp"),
        P("mp"),
        P("mp", None),
        P(),
    )
    return jax.shard_map(
        on_device, mesh=mesh, in_specs=in_specs, out_specs=out_specs, check_vma=False
    )
```

```python
import jax
import jax.numpy as jnp
import numpy as np
from jax import lax
from jax.experimental import pallas as pl
from jax.experimental.pallas import tpu as pltpu
from jax.sharding import PartitionSpec as P

D = 768
HEADS = 12
HD = 64
FF = 3072
WIN = 14
SIDE = 64
NWIN = 5
RELS = 27
EPSILON = 1e-06
F32 = jnp.float32
BF = jnp.bfloat16

SLOTS = 256
KEYS = WIN * 16
PAIR = 2 * SIDE
GREL = 80
OWN = SIDE * SIDE // 2

HALF = D // 2
TRIO = 3 * HALF
PAIRS = HEADS // 4

NN = (((1,), (0,)), ((), ()))
NT = (((1,), (1,)), ((), ()))
TN = (((0,), (0,)), ((), ()))


def dot(left, right, dims=NN):
    return lax.dot_general(left, right, dims, preferred_element_type=F32)


def params(limit=60):
    return pltpu.CompilerParams(vmem_limit_bytes=limit * 2**20)


def cost(flops, moved, exps=0):
    return pl.CostEstimate(flops=int(flops), bytes_accessed=int(moved), transcendentals=int(exps))


def whole(shape):
    return pl.BlockSpec(shape, lambda *_: (0,) * len(shape), pipeline_mode=pl.Buffered(1))


STARTS = np.array([[0, 14, 28], [42, 28, 56]], np.int32)


def pair_tables(place):
    block = np.zeros((2, 24), np.int32)
    valid = np.zeros((2, 24), np.int32)
    local = np.zeros((2, 24), np.int32)
    owned = np.zeros((2, 24), np.int32)
    band_of = np.zeros((2, 16), np.int32)
    step_of = np.zeros((2, 16), np.int32)
    taken_of = np.zeros((2, 16), np.int32)
    has_taken = np.zeros((2, 16), np.int32)
    taken_of[0, 14:16], has_taken[0, 14:16] = np.arange(2), 1
    taken_of[1, 0:5], has_taken[1, 0:5] = np.arange(5), 1
    for m in range(2):
        for s in range(3):
            for t in range(7):
                row = STARTS[m, s] + 2 * t
                at = s * 8 + t
                block[m, at] = min(row // 2, 31)
                valid[m, at] = row < SIDE
                if 32 * m <= row < 32 * m + 32:
                    local[m, at] = (row - 32 * m) // 2
                    owned[m, at] = 1
                    band_of[m, local[m, at]] = s
                    step_of[m, local[m, at]] = t
            block[m, s * 8 + 7] = block[m, s * 8 + 6]
    pick = lambda table: jnp.where(place == 0, jnp.asarray(table[0]), jnp.asarray(table[1]))
    return tuple(pick(t) for t in (block, valid, local, owned, band_of, step_of, taken_of, has_taken))


def spread_rows():
    table = np.zeros((NWIN, 2, 16, PAIR), np.float32)
    for w in range(NWIN):
        for r in range(2):
            for j in range(WIN):
                if WIN * w + j < SIDE:
                    table[w, r, j, r * SIDE + WIN * w + j] = 1
    return table.reshape(NWIN * 32, PAIR)


def rel_order():
    rows = np.full(GREL, -1)
    for m in range(21):
        rows[m] = 26 - (m + 6)
        rows[24 + m] = 26 - m
    cols = np.full(GREL, -1)
    for m in range(RELS):
        cols[48 + m] = 26 - m
    return rows, cols


def rel_onehots():
    rows, cols = rel_order()
    high = (rows[:, None] == np.arange(RELS)[None, :]).astype(np.float32)
    wide = (cols[:, None] == np.arange(RELS)[None, :]).astype(np.float32)
    return high, wide


def norm_parts(values):
    average = jnp.mean(values, axis=-1, keepdims=True)
    centred = values - average
    inverse = lax.rsqrt(jnp.mean(centred * centred, axis=-1, keepdims=True) + EPSILON)
    return centred * inverse, inverse


def vec(ref):
    return ref[...].astype(F32).reshape(1, D)


def window_kernel(block, valid, *refs):
    xs, (gain, shift, spread, out) = refs[:7], refs[7:]
    band = pl.program_id(0)
    for t in range(7):
        scaled, _ = norm_parts(xs[t][...].astype(F32))
        normed = scaled * vec(gain) + vec(shift)
        normed = (normed * valid[band * 8 + t].astype(F32)).astype(BF)
        moved = dot(spread[...], normed).astype(BF)
        out[:, :, 32 * t : 32 * t + 32, :] = moved.reshape(1, NWIN, 32, D)
    out[:, :, 224:, :] = jnp.zeros((1, NWIN, 32, D), BF)


def windows_of(x, gain, shift, spread, block, valid):
    at = lambda t: lambda s, block, valid: (block[s * 8 + t], 0)
    return pl.pallas_call(
        window_kernel,
        grid_spec=pltpu.PrefetchScalarGridSpec(
            num_scalar_prefetch=2,
            grid=(3,),
            in_specs=[pl.BlockSpec((PAIR, D), at(t)) for t in range(7)]
            + [whole((D,)), whole((D,)), whole((NWIN * 32, PAIR))],
            out_specs=pl.BlockSpec((1, NWIN, SLOTS, D), lambda s, *_: (s, 0, 0, 0)),
        ),
        out_shape=jax.ShapeDtypeStruct((3, NWIN, SLOTS, D), BF),
        compiler_params=params(),
        cost_estimate=cost(3 * 7 * 160 * 128 * 768 * 2, 10e6),
    )(block, valid, *([x] * 7), gain, shift, spread)


def shift_masks(lanes_from):
    lane = lax.broadcasted_iota(jnp.int32, (1, 128), 1) + lanes_from
    high = lane // 16
    row_shift = jnp.where(lane < 128, 7 - high, jnp.maximum(13 - high, 0))
    col_shift = jnp.maximum(13 - lane % 16, 0)
    return row_shift, col_shift


def skew(table, shift, bits):
    size = table.shape[0]
    for bit in bits:
        moved = pltpu.roll(table, size - bit, 0)
        table = jnp.where((shift & bit) != 0, moved, table)
    return table


def unskew(table, shift, bits):
    for bit in bits:
        moved = pltpu.roll(table, bit, 0)
        table = jnp.where((shift & bit) != 0, moved, table)
    return table


def start_own(weights, bias, high_hot, wide_hot, rel_rows, rel_cols, rel_even, rel_odd, joined):
    for s in range(3):
        joined[:, s * HALF : s * HALF + HALF] = weights[s]
    table = (dot(high_hot[...], rel_rows[...]) + dot(wide_hot[...], rel_cols[...])).astype(BF)
    blank = jnp.zeros_like(table)
    rel_even[...] = jnp.concatenate([table, blank], axis=1)
    rel_odd[...] = jnp.concatenate([blank, table], axis=1)


def join_pieces(core, mine, theirs, joined, col):
    for piece, at in ((mine, core), (theirs, 1 - core)):
        rows = pl.ds(pl.multiple_of(at * HALF, HALF), HALF)
        for s in range(3):
            joined[rows, col + s * HALF : col + s * HALF + HALF] = piece[s]


def attend_own(
    x, bias, weights, high_hot, wide_hot, rel_rows, rel_cols,
    qkv_out, p_out, ctx_out, xt_out, rel_even, rel_odd, joined, vt,
):
    @pl.when((pl.program_id(0) == 0) & (pl.program_id(1) == 0))
    def _():
        start_own(weights, bias, high_hot, wide_hot, rel_rows, rel_cols, rel_even, rel_odd, joined)

    attend_window(x, bias, rel_even, rel_odd, qkv_out, p_out, ctx_out, xt_out, joined, vt)


def attend_other(x, bias, core, mine, theirs, rel_even, rel_odd, qkv_out, p_out, ctx_out, joined, vt):
    @pl.when((pl.program_id(0) == 0) & (pl.program_id(1) == 0))
    def _():
        join_pieces(core[0], mine, theirs, joined, 0)

    attend_window(x, bias, rel_even, rel_odd, qkv_out, p_out, ctx_out, None, joined, vt)


def attend_window(x, bias, rel_even, rel_odd, qkv_out, p_out, ctx_out, xt_out, joined, vt):
    band = pl.program_id(0)
    biases = bias[...].astype(F32)
    biases = jnp.concatenate([biases[0:1], jnp.zeros((1, HALF), F32), biases[1:2]], axis=1)
    block = x[...].reshape(SLOTS, D)
    if xt_out is not None:
        xt_out[...] = block.T
    scales = jnp.where(lax.broadcasted_iota(jnp.int32, (1, TRIO), 1) // HALF == 1, HD ** (-0.5), 1.0)
    low = ((dot(block, joined[...]) + biases) * scales).astype(BF)
    qkv_out[0, 0] = low
    vt[...] = low[:, 2 * HALF :].T

    even = lax.broadcasted_iota(jnp.int32, (1, 128), 1) < HD

    def raw_scores(head, lanes):
        col = head // 2 * 128
        keys = qkv_out[0, 0, 0:KEYS, HALF + col : HALF + col + 128]
        kept = jnp.where(even != (head % 2 == 1), keys, jnp.zeros_like(keys))
        rel = rel_odd if head % 2 else rel_even
        left = jnp.concatenate([kept, rel[...]], axis=0)
        return dot(left, qkv_out[0, 0, 0:lanes, col : col + 128], NT)

    def soft(head, raw, lanes):
        parts = []
        for tile in range(lanes // 128):
            row_shift, col_shift = shift_masks(tile * 128)
            raw_t = raw[:, tile * 128 : tile * 128 + 128]
            base = raw_t[0:KEYS]
            high = skew(raw_t[KEYS + 24 * tile : KEYS + 24 * tile + 24], row_shift, (4, 2, 1))[0:16]
            wide = skew(raw_t[KEYS + 48 : KEYS + 80], col_shift, (8, 4, 2, 1))[0:16]
            place = lax.broadcasted_iota(jnp.int32, (16, 128), 0)
            wide = jnp.where(place < WIN, wide, -1e30)
            scores = base.reshape(WIN, 16, 128) + wide[None] + high[0:WIN][:, None, :]
            scores = scores.reshape(KEYS, 128)
            peak = jnp.max(scores, axis=0, keepdims=True)
            grown = jnp.exp(scores - peak)
            total = jnp.sum(grown, axis=0, keepdims=True)
            parts.append((grown * (1.0 / total)).astype(BF))
        probs = parts[0] if len(parts) == 1 else jnp.concatenate(parts, axis=1)
        p_out[0, 0, head, :, 0:lanes] = probs
        return probs

    def all_heads(lanes):
        count = HEADS // 2
        raw = raw_scores(0, lanes)
        contexts = []
        for head in range(count):
            ahead = raw_scores(head + 1, lanes) if head + 1 < count else None
            probs = soft(head, raw, lanes)
            if head:
                contexts.append(dot(vt[(head - 1) * HD : head * HD, 0:KEYS], before).astype(BF))
            if head and head % 2 == 0:
                col = (head - 2) * HD
                ctx_out[0, 0, 0:lanes, col : col + 128] = jnp.concatenate(contexts[-2:], axis=0).T
            before, raw = probs, ahead
        contexts.append(dot(vt[(count - 1) * HD :, 0:KEYS], before).astype(BF))
        ctx_out[0, 0, 0:lanes, HALF - 128 :] = jnp.concatenate(contexts[-2:], axis=0).T

    @pl.when(band < 2)
    def _():
        all_heads(256)

    @pl.when(band == 2)
    def _():
        all_heads(128)


SCALAR = pl.BlockSpec(memory_space=pltpu.SMEM)


def attend(x, bias, first, *operands):
    block = lambda width: pl.BlockSpec((1, 1, SLOTS, width), lambda s, w: (s, w, 0, 0))
    shape = lambda width: jax.ShapeDtypeStruct((3, NWIN, SLOTS, width), BF)
    out_specs = [
        block(TRIO),
        pl.BlockSpec((1, 1, HEADS // 2, KEYS, SLOTS), lambda s, w: (s, w, 0, 0, 0)),
        block(HALF),
    ]
    out_shape = [
        shape(TRIO),
        jax.ShapeDtypeStruct((3, NWIN, HEADS // 2, KEYS, SLOTS), BF),
        shape(HALF),
    ]
    rel = pl.BlockSpec((GREL, 128), lambda s, w: (0, 0))
    if first:
        in_specs = [whole((3, D, HALF)), whole((GREL, RELS)), whole((GREL, RELS)), whole((RELS, HD)), whole((RELS, HD))]
        out_specs += [pl.BlockSpec((D, SLOTS), lambda s, w: (0, s * NWIN + w)), rel, rel]
        out_shape += [jax.ShapeDtypeStruct((D, 3 * NWIN * SLOTS), BF)] + [jax.ShapeDtypeStruct((GREL, 128), BF)] * 2
    else:
        in_specs = [SCALAR, whole((3, HALF, HALF)), whole((3, HALF, HALF)), whole((GREL, 128)), whole((GREL, 128))]
    return pl.pallas_call(
        attend_own if first else attend_other,
        grid=(3, NWIN),
        in_specs=[block(D), whole((2, HALF))] + in_specs,
        out_specs=out_specs,
        out_shape=out_shape,
        scratch_shapes=[pltpu.VMEM((D, TRIO), BF), pltpu.VMEM((HALF, SLOTS), BF)],
        compiler_params=params(),
        cost_estimate=cost(15e9, 45e6, 4e6),
    )(x, bias, *operands)


def middle_kernel(
    band_of, step_of, offset, own_a, own_b, other_a, other_b, x, cot, proj_own, proj_other, bias, gain, shift, gather,
    middle, normed, normed_t, cot_t, ctx_out, proj,
):
    @pl.when(pl.program_id(0) == 0)
    def _():
        proj[0:HALF, :] = proj_own[...]
        proj[HALF:, :] = proj_other[...]

    for row, parts in ((0, (own_a, other_a)), (PAIR, (own_b, other_b))):
        for side in range(2):
            moved = dot(gather[...], parts[side][...].reshape(NWIN * 32, HALF)).astype(BF)
            ctx_out[row : row + PAIR, side * HALF : side * HALF + HALF] = moved
    value = x[...].astype(F32) + (dot(ctx_out[...], proj[...]) + vec(bias))
    middle[...] = value
    scaled, _ = norm_parts(value)
    low = (scaled * vec(gain) + vec(shift)).astype(BF)
    normed[...] = low
    normed_t[...] = low.T
    cot_t[...] = cot[...].T


def middle_of(ctx_own, ctx_other, x, cot, proj_own, proj_other, bias, gain, shift, gather, band_of, step_of, offset):
    rows = 2 * PAIR
    at = lambda k: lambda i, band_of, step_of, offset: (band_of[2 * i + k], 0, step_of[2 * i + k], 0)
    row_block = pl.BlockSpec((rows, D), lambda i, *_: (i, 0))
    col_block = pl.BlockSpec((D, rows), lambda i, *_: (0, i))
    return pl.pallas_call(
        middle_kernel,
        grid_spec=pltpu.PrefetchScalarGridSpec(
            num_scalar_prefetch=3,
            grid=(OWN // rows,),
            in_specs=[
                pl.BlockSpec((1, NWIN, 32, HALF), at(0)),
                pl.BlockSpec((1, NWIN, 32, HALF), at(1)),
                pl.BlockSpec((1, NWIN, 32, HALF), at(0)),
                pl.BlockSpec((1, NWIN, 32, HALF), at(1)),
                pl.BlockSpec((rows, D), lambda i, band_of, step_of, offset: (offset[0] + i, 0)),
                row_block,
                whole((HALF, D)),
                whole((HALF, D)),
                whole((D,)),
                whole((D,)),
                whole((D,)),
                whole((PAIR, NWIN * 32)),
            ],
            out_specs=[row_block, row_block, col_block, col_block, row_block],
            scratch_shapes=[pltpu.VMEM((D, D), BF)],
        ),
        out_shape=[
            jax.ShapeDtypeStruct((OWN, D), F32),
            jax.ShapeDtypeStruct((OWN, D), BF),
            jax.ShapeDtypeStruct((D, OWN), BF),
            jax.ShapeDtypeStruct((D, OWN), BF),
            jax.ShapeDtypeStruct((OWN, D), BF),
        ],
        compiler_params=params(),
        cost_estimate=cost(3e9, 30e6),
    )(band_of, step_of, offset, ctx_own, ctx_own, ctx_other, ctx_other, x, cot, proj_own, proj_other, bias, gain, shift, gather)


CHUNK = 512
CHUNKS = FF // CHUNK


def feed_kernel(
    core, normed, normed_t, cot, cot_t, one_a, one_b, one_c, bias_a, bias_b, two_a, two_b, two_c,
    forward, back, one_kept, one_sent, two_kept, two_sent, sums, one, two, bias, hidden, grads,
):
    step = pl.program_id(0)

    @pl.when(step == 0)
    def _():
        forward[...] = jnp.zeros_like(forward)
        back[...] = jnp.zeros_like(back)

    @pl.when(step < CHUNKS // 2)
    def _():
        bias[...] = bias_a[...].astype(F32).reshape(1, CHUNK)
        one[...] = one_a[...]
        two[...] = two_a[...]

    @pl.when(step >= CHUNKS // 2)
    def _():
        bias[...] = bias_b[...].astype(F32).reshape(1, CHUNK)
        mine = pl.multiple_of(core[0] * HALF, HALF)
        theirs = pl.multiple_of((1 - core[0]) * HALF, HALF)
        one[pl.ds(mine, HALF), :] = one_b[...]
        one[pl.ds(theirs, HALF), :] = one_c[...]
        two[:, pl.ds(mine, HALF)] = two_b[...]
        two[:, pl.ds(theirs, HALF)] = two_c[...]

    total = jnp.zeros((1, CHUNK), F32)
    for t in range(OWN // 256):
        rows = slice(t * 256, t * 256 + 256)
        pre = dot(normed[rows, :], one[...]) + bias[...]
        phi = 0.5 * (1.0 + lax.erf(pre * 0.7071067811865476))
        slope = phi + pre * (jnp.exp(-0.5 * pre * pre) * 0.3989422804014327)
        low = (pre * phi).astype(BF)
        grad = (dot(cot[rows, :], two[...], NT) * slope).astype(BF)
        hidden[rows, :] = low
        grads[rows, :] = grad
        total += jnp.sum(grad.astype(F32), axis=0, keepdims=True)
        forward[rows, :] += dot(low, two[...])
        back[rows, :] += dot(grad, one[...], NT)
    sums[...] = total

    first = core[0] == 0
    one_grad = dot(normed_t[...], grads[...]).astype(BF)
    low, high = one_grad[:HALF], one_grad[HALF:]
    one_kept[0] = jnp.where(first, low, high)
    one_sent[0] = jnp.where(first, high, low)
    two_grad = dot(cot_t[...], hidden[...]).astype(BF)
    low, high = two_grad[:HALF], two_grad[HALF:]
    two_kept[0] = jnp.where(first, low, high).T
    two_sent[0] = jnp.where(first, high, low).T


def feed(core, normed, normed_t, cot, cot_t, one_a, ones, bias_a, bias_b, two_a, twos):
    half = CHUNKS // 2
    own = lambda j: jnp.minimum(j, half - 1)
    other = lambda j: jnp.maximum(j - half, 0)
    one_block = pl.BlockSpec((1, HALF, CHUNK), lambda j, *_: (j // half, 0, j % half))
    two_block = pl.BlockSpec((1, CHUNK, HALF), lambda j, *_: (j // half, j % half, 0))
    one_piece = pl.BlockSpec((HALF, CHUNK), lambda j, *_: (0, other(j)))
    two_piece = pl.BlockSpec((CHUNK, HALF), lambda j, *_: (other(j), 0))
    one_shape = jax.ShapeDtypeStruct((2, HALF, FF // 2), BF)
    two_shape = jax.ShapeDtypeStruct((2, FF // 2, HALF), BF)
    sum_block = pl.BlockSpec((OWN, D), lambda j, *_: (0, 0))
    bias_block = pl.BlockSpec((1, CHUNK), lambda j, *_: (0, j))
    return pl.pallas_call(
        feed_kernel,
        grid_spec=pltpu.PrefetchScalarGridSpec(
            num_scalar_prefetch=1,
            grid=(CHUNKS,),
            in_specs=[
                whole((OWN, D)),
                whole((D, OWN)),
                whole((OWN, D)),
                whole((D, OWN)),
                pl.BlockSpec((D, CHUNK), lambda j, *_: (0, own(j))),
                one_piece,
                one_piece,
                pl.BlockSpec((CHUNK,), lambda j, *_: (own(j),)),
                pl.BlockSpec((CHUNK,), lambda j, *_: (other(j),)),
                pl.BlockSpec((CHUNK, D), lambda j, *_: (own(j), 0)),
                two_piece,
                two_piece,
            ],
            out_specs=[sum_block, sum_block, one_block, one_block, two_block, two_block, bias_block],
            scratch_shapes=[
                pltpu.VMEM((D, CHUNK), BF),
                pltpu.VMEM((CHUNK, D), BF),
                pltpu.VMEM((1, CHUNK), F32),
                pltpu.VMEM((OWN, CHUNK), BF),
                pltpu.VMEM((OWN, CHUNK), BF),
            ],
        ),
        out_shape=[
            jax.ShapeDtypeStruct((OWN, D), F32),
            jax.ShapeDtypeStruct((OWN, D), F32),
            one_shape,
            one_shape,
            two_shape,
            two_shape,
            jax.ShapeDtypeStruct((1, FF), F32),
        ],
        compiler_params=params(62),
        cost_estimate=cost(58e9, 60e6, 12e6),
    )(core, normed, normed_t, cot, cot_t, one_a, *ones, bias_a, bias_b, two_a, *twos)


def add_row(sums, row, values):
    sums[row : row + 1, :] += jnp.sum(values, axis=0, keepdims=True)


def resid_kernel(
    middle, forward, back, cot, context, proj_own, proj_other, bias, gain,
    block_out, grad_out, ctx_grad, grad_own, grad_other, sums, proj, proj_grad,
):
    step = pl.program_id(0)

    @pl.when(step == 0)
    def _():
        proj[0:HALF, :] = proj_own[...]
        proj[HALF:, :] = proj_other[...]
        proj_grad[...] = jnp.zeros_like(proj_grad)
        sums[...] = jnp.zeros_like(sums)

    value = middle[...]
    block_out[...] = (value + (forward[...] + vec(bias))).astype(BF)
    scaled, inverse = norm_parts(value)
    upstream = back[...]
    scaled_up = upstream * vec(gain)
    first = jnp.mean(scaled_up, axis=-1, keepdims=True)
    second = jnp.mean(scaled_up * scaled, axis=-1, keepdims=True)
    cotangent = cot[...].astype(F32)
    grad = cotangent + inverse * (scaled_up - first - scaled * second)
    grad_out[...] = grad
    low = grad.astype(BF)
    ctx_grad[...] = dot(low, proj[...], NT).astype(BF)
    proj_grad[...] += dot(context[...], low, TN)
    add_row(sums, 0, upstream * scaled)
    add_row(sums, 1, upstream)
    add_row(sums, 2, cotangent)
    add_row(sums, 3, low.astype(F32))

    @pl.when(step == pl.num_programs(0) - 1)
    def _():
        for out, row in ((grad_own, 0), (grad_other, HALF)):
            for col in (0, HALF):
                out[col : col + HALF, :] = proj_grad[row : row + HALF, col : col + HALF].astype(BF)


def resid_of(middle, forward, back, cot, context, proj_own, proj_other, bias, gain):
    rows = 512
    row_block = pl.BlockSpec((rows, D), lambda i: (i, 0))
    half_block = pl.BlockSpec((D, HALF), lambda i: (0, 0))
    return pl.pallas_call(
        resid_kernel,
        grid=(OWN // rows,),
        in_specs=[row_block] * 5 + [whole((HALF, D)), whole((HALF, D)), whole((D,)), whole((D,))],
        out_specs=[
            row_block,
            row_block,
            row_block,
            half_block,
            half_block,
            pl.BlockSpec((8, D), lambda i: (0, 0)),
        ],
        out_shape=[
            jax.ShapeDtypeStruct((OWN, D), BF),
            jax.ShapeDtypeStruct((OWN, D), F32),
            jax.ShapeDtypeStruct((OWN, D), BF),
            jax.ShapeDtypeStruct((D, HALF), BF),
            jax.ShapeDtypeStruct((D, HALF), BF),
            jax.ShapeDtypeStruct((8, D), F32),
        ],
        scratch_shapes=[pltpu.VMEM((D, D), BF), pltpu.VMEM((D, D), F32)],
        compiler_params=params(),
        cost_estimate=cost(5e9, 40e6),
    )(middle, forward, back, cot, context, proj_own, proj_other, bias, gain)


def attend_back_kernel(first, local, owned, qkv, p, ctx_grad, spread, rel_even, rel_odd, fold, *refs):
    d_out, rel_grad, sums, upstream, kt = refs[-5:]
    band = pl.program_id(0) + first
    window = pl.program_id(1)

    @pl.when((band == first) & (window == 0))
    def _():
        rel_grad[...] = jnp.zeros_like(rel_grad)
        sums[...] = jnp.zeros_like(sums)

    @pl.when(window == 0)
    def _():
        for t in range(7):
            at = band * 8 + t
            rows = pl.ds(pl.multiple_of(local[at] * PAIR, PAIR), PAIR)
            moved = dot(spread[...], ctx_grad[rows, :])
            moved = moved * owned[at].astype(F32)
            upstream[:, 32 * t : 32 * t + 32, :] = moved.astype(BF).reshape(NWIN, 32, HALF)
        upstream[:, 224:256, :] = jnp.zeros((NWIN, 32, HALF), BF)

    kt[...] = qkv[0, 0, :, HALF : 2 * HALF].T
    even = lax.broadcasted_iota(jnp.int32, (1, 128), 1) < HD

    def shifted(head, by):
        return slice(by * HALF + head // 2 * 128, by * HALF + head // 2 * 128 + 128)

    def prob_grads(head, lanes):
        values = qkv[0, 0, 0:KEYS, shifted(head, 2)]
        kept = jnp.where(even != (head % 2 == 1), values, jnp.zeros_like(values))
        return dot(kept, upstream[window, 0:lanes, shifted(head, 0)], NT)

    def rel_table(both, lanes):
        tables = []
        zero8 = jnp.zeros((8, 128), F32)
        zero24 = jnp.zeros((24, 128), F32)
        zero16 = jnp.zeros((16, 128), F32)
        for tile in range(lanes // 128):
            row_shift, col_shift = shift_masks(tile * 128)
            part = both[:, tile * 128 : tile * 128 + 128]
            high = jnp.concatenate([part[HD : HD + 16], zero8], axis=0)
            wide = jnp.concatenate([part[HD + 16 : HD + 32], zero16], axis=0)
            high = unskew(high, row_shift, (1, 2, 4))
            wide = unskew(wide, col_shift, (1, 2, 4, 8))
            stack = [high, zero24, wide] if tile == 0 else [zero24, high, wide]
            tables.append(jnp.concatenate(stack, axis=0))
        table = tables[0] if len(tables) == 1 else jnp.concatenate(tables, axis=1)
        return table.astype(BF)

    def all_heads(lanes):
        count = HEADS // 2
        dvs, dks, dqs, drs = [], [], [], []

        def last_part(head, score_grad, both):
            rel = rel_odd if head % 2 else rel_even
            table = rel_table(both, lanes)
            queries = qkv[0, 0, 0:lanes, shifted(head, 0)]
            grads = dot(jnp.concatenate([score_grad, table], axis=0), queries)
            dks.append(grads[0:KEYS])
            drs.append(grads[KEYS:])
            from_rel = dot(rel[...], table, TN)
            side = head % 2 * HD
            dqs.append(both[0:HD] + from_rel[side : side + HD])
            if head % 2:
                d_out[0, 0, 0:lanes, shifted(head, 0)] = jnp.concatenate(dqs[-2:], axis=0).astype(BF).T
                d_out[0, 0, 0:KEYS, shifted(head, 1)] = (jnp.where(even, dks[-2], dks[-1]) * HD ** (-0.5)).astype(BF)

        prob_grad = prob_grads(0, lanes)
        before = None
        for head in range(count):
            ahead = prob_grads(head + 1, lanes) if head + 1 < count else None
            probs_low = p[0, 0, head, :, 0:lanes]
            probs = probs_low.astype(F32)
            total = jnp.sum(prob_grad * probs, axis=0, keepdims=True)
            score_grad = (probs * (prob_grad - total)).astype(BF)
            dvs.append(dot(probs_low, upstream[window, 0:lanes, shifted(head, 0)]))
            left = jnp.concatenate([kt[head * HD : head * HD + HD, 0:KEYS], fold[...]], axis=0)
            both = dot(left, score_grad)
            if head % 2:
                d_out[0, 0, 0:KEYS, shifted(head, 2)] = jnp.where(even, dvs[-2], dvs[-1]).astype(BF)
            if before is not None:
                last_part(head - 1, *before)
            before, prob_grad = (score_grad, both), ahead
        last_part(count - 1, *before)
        evens = drs[0] + drs[2] + drs[4]
        odds = drs[1] + drs[3] + drs[5]
        rel_grad[...] += jnp.where(even, evens, odds)

    d_out[0, 0, KEYS:, HALF:] = jnp.zeros((SLOTS - KEYS, 2 * HALF), BF)

    @pl.when(band < 2)
    def _():
        all_heads(256)

    @pl.when(band == 2)
    def _():
        all_heads(128)
        d_out[0, 0, 128:, 0:HALF] = jnp.zeros((128, HALF), BF)

    sums[0:1, :] += jnp.sum(d_out[...].reshape(SLOTS, TRIO).astype(F32), axis=0, keepdims=True)


def fold_table():
    table = np.zeros((32, WIN, 16), np.float32)
    for k in range(WIN):
        for l in range(WIN):
            table[k, k, l] = 1
            table[16 + l, k, l] = 1
    return table.reshape(32, KEYS)


def attend_back(qkv, p, ctx_grad, side, spread, rel_even, rel_odd, fold, local, owned, bands, *d_in):
    first, last = bands
    block = pl.BlockSpec((1, 1, SLOTS, TRIO), lambda s, w, *_: (s + first, w, 0, 0))
    share = (last - first) / 3
    return pl.pallas_call(
        lambda *refs: attend_back_kernel(first, *refs),
        grid_spec=pltpu.PrefetchScalarGridSpec(
            num_scalar_prefetch=2,
            grid=(last - first, NWIN),
            in_specs=[
                block,
                pl.BlockSpec((1, 1, HEADS // 2, KEYS, SLOTS), lambda s, w, *_: (s + first, w, 0, 0, 0)),
                pl.BlockSpec((OWN, HALF), lambda *_: (0, side), pipeline_mode=pl.Buffered(1)),
                whole((NWIN * 32, PAIR)),
                whole((GREL, 128)),
                whole((GREL, 128)),
                whole((32, KEYS)),
            ]
            + [pl.BlockSpec(memory_space=pl.ANY)] * len(d_in),
            out_specs=[
                block,
                pl.BlockSpec((GREL, 128), lambda s, w, *_: (0, 0)),
                pl.BlockSpec((8, TRIO), lambda s, w, *_: (0, 0)),
            ],
            scratch_shapes=[pltpu.VMEM((NWIN, SLOTS, HALF), BF), pltpu.VMEM((HALF, SLOTS), BF)],
        ),
        out_shape=[
            jax.ShapeDtypeStruct((3, NWIN, SLOTS, TRIO), BF),
            jax.ShapeDtypeStruct((GREL, 128), F32),
            jax.ShapeDtypeStruct((8, TRIO), F32),
        ],
        input_output_aliases={9: 0} if d_in else {},
        compiler_params=params(),
        cost_estimate=cost(20e9 * share, 45e6 * share),
    )(local, owned, qkv, p, ctx_grad, spread, rel_even, rel_odd, fold, *d_in)


def norm_grad_kernel(own, other, weights_own, core, mine, theirs, gather, *refs):
    out, joined = refs[-2:]

    @pl.when((pl.program_id(0) == 0) & (pl.program_id(1) == 0))
    def _():
        for s in range(3):
            joined[:, s * HALF : s * HALF + HALF] = weights_own[s]
        join_pieces(core[0], mine, theirs, joined, TRIO)

    rows = NWIN * 128
    left = jnp.concatenate([own[...].reshape(rows, TRIO), other[...].reshape(rows, TRIO)], axis=1)
    total = dot(left, joined[...], NT).astype(BF).reshape(NWIN, 4, 32, D)
    for t in range(4):
        moved = dot(gather[...], total[:, t].reshape(NWIN * 32, D)).astype(BF)
        out[:, t * PAIR : t * PAIR + PAIR, :] = moved.reshape(1, PAIR, D)


def norm_grad(own, other, weights_own, core, mine, theirs, gather, bands, *before):
    first, last = bands
    share = (last - first) / 3
    block = pl.BlockSpec((1, NWIN, 128, TRIO), lambda s, t: (s + first, 0, t, 0))
    return pl.pallas_call(
        norm_grad_kernel,
        grid=(last - first, 2),
        in_specs=[block, block, whole((3, D, HALF)), SCALAR]
        + [whole((3, HALF, HALF)), whole((3, HALF, HALF)), whole((PAIR, NWIN * 32))]
        + [pl.BlockSpec(memory_space=pl.ANY)] * len(before),
        out_specs=pl.BlockSpec((1, 4 * PAIR, D), lambda s, t: (s + first, t, 0)),
        out_shape=jax.ShapeDtypeStruct((3, 8 * PAIR, D), BF),
        input_output_aliases={7: 0} if before else {},
        scratch_shapes=[pltpu.VMEM((D, 2 * TRIO), BF)],
        compiler_params=params(),
        cost_estimate=cost(14e9 * share, 30e6 * share),
    )(own, other, weights_own, core, mine, theirs, gather, *before)


def qkv_grad_kernel(core, xt, d, proj, kept, sent, total):
    step = pl.program_id(0)
    part = dot(xt[...], d[...])

    @pl.when(step == 0)
    def _():
        total[...] = part

    @pl.when(step > 0)
    def _():
        total[...] += part

    @pl.when(step == pl.num_programs(0) - 1)
    def _():
        first = core[0] == 0
        values = [total[:, s * HALF : s * HALF + HALF].astype(BF) for s in range(3)] + [proj[...]]
        for k in range(2):
            kept[k] = jnp.where(first, values[k], values[2 + k])
            sent[k] = jnp.where(first, values[2 + k], values[k])


def qkv_grad(core, xt, d, proj):
    rows = NWIN * SLOTS
    block = pl.BlockSpec((2, D, HALF), lambda i: (0, 0, 0))
    shape = jax.ShapeDtypeStruct((2, D, HALF), BF)
    return pl.pallas_call(
        qkv_grad_kernel,
        grid=(3,),
        in_specs=[
            SCALAR,
            pl.BlockSpec((D, rows), lambda i: (0, i)),
            pl.BlockSpec((rows, TRIO), lambda i: (i, 0)),
            whole((D, HALF)),
        ],
        out_specs=[block, block],
        out_shape=[shape, shape],
        scratch_shapes=[pltpu.VMEM((D, TRIO), F32)],
        compiler_params=params(),
        cost_estimate=cost(7e9, 16e6),
    )(core, xt, d.reshape(3 * rows, TRIO), proj)


def input_kernel(
    band_of, step_of, taken_of, has_taken, offset, core, x, middle_grad, up_a, up_b, taken_a, taken_b, gain,
    one_mine, one_theirs, two_mine, two_theirs, out, sums, one_out, two_out,
):
    step = pl.program_id(0)
    first = core[0] == 0
    mine, theirs = one_mine[...].astype(F32), one_theirs[...].astype(F32)
    one_out[0] = jnp.where(first, mine, theirs)
    one_out[1] = jnp.where(first, theirs, mine)
    mine, theirs = two_mine[...].astype(F32), two_theirs[...].astype(F32)
    two_out[:, 0:HALF] = jnp.where(first, mine, theirs)
    two_out[:, HALF:] = jnp.where(first, theirs, mine)

    @pl.when(step == 0)
    def _():
        sums[...] = jnp.zeros_like(sums)

    for k, (up, taken) in enumerate(((up_a, taken_a), (up_b, taken_b))):
        rows = slice(k * PAIR, k * PAIR + PAIR)
        scaled, inverse = norm_parts(x[rows, :].astype(F32))
        shared = taken[...].astype(F32) * has_taken[2 * step + k].astype(F32)
        upstream = up[0].astype(F32) + shared
        scaled_up = upstream * vec(gain)
        mean = jnp.mean(scaled_up, axis=-1, keepdims=True)
        second = jnp.mean(scaled_up * scaled, axis=-1, keepdims=True)
        out[rows, :] = (middle_grad[rows, :] + inverse * (scaled_up - mean - scaled * second)).astype(BF)
        add_row(sums, 0, upstream * scaled)
        add_row(sums, 1, upstream)


def input_of(x, middle_grad, up, taken, gain, ones, twos, band_of, step_of, taken_of, has_taken, offset, core):
    rows = 2 * PAIR
    row_block = pl.BlockSpec((rows, D), lambda i, *_: (i, 0))
    steps = OWN // rows
    one_rows, two_rows = HALF // steps, FF // 2 // steps
    up_at = lambda k: lambda i, band_of, step_of, *_: (band_of[2 * i + k], step_of[2 * i + k], 0)
    taken_at = lambda k: lambda i, band_of, step_of, taken_of, *_: (taken_of[2 * i + k], 0)
    return pl.pallas_call(
        input_kernel,
        grid_spec=pltpu.PrefetchScalarGridSpec(
            num_scalar_prefetch=6,
            grid=(steps,),
            in_specs=[
                pl.BlockSpec((rows, D), lambda i, b, s, t, h, offset, core: (offset[0] + i, 0)),
                row_block,
                pl.BlockSpec((1, PAIR, D), up_at(0)),
                pl.BlockSpec((1, PAIR, D), up_at(1)),
                pl.BlockSpec((PAIR, D), taken_at(0)),
                pl.BlockSpec((PAIR, D), taken_at(1)),
                whole((D,)),
            ]
            + [pl.BlockSpec((one_rows, FF // 2), lambda i, *_: (i, 0))] * 2
            + [pl.BlockSpec((two_rows, HALF), lambda i, *_: (i, 0))] * 2,
            out_specs=[
                row_block,
                pl.BlockSpec((8, D), lambda i, *_: (0, 0)),
                pl.BlockSpec((2, one_rows, FF // 2), lambda i, *_: (0, i, 0)),
                pl.BlockSpec((two_rows, D), lambda i, *_: (i, 0)),
            ],
        ),
        out_shape=[
            jax.ShapeDtypeStruct((OWN, D), BF),
            jax.ShapeDtypeStruct((8, D), F32),
            jax.ShapeDtypeStruct((2, HALF, FF // 2), F32),
            jax.ShapeDtypeStruct((FF // 2, D), F32),
        ],
        compiler_params=params(),
        cost_estimate=cost(1e8, 35e6),
    )(band_of, step_of, taken_of, has_taken, offset, core, x, middle_grad, up, up, taken, taken, gain, *ones, *twos)


MESH = pl.DeviceIdType.MESH
SMALL = 24


def bits_of(size):
    return size.bit_length() - 1


def line_plan(order, rows):
    plan, doubles = [], [("double", order[0], rows)]
    for bit in order[1:]:
        if rows % 32 == 0:
            doubles.append(("double", bit, rows))
            rows //= 2
            plan.append(("halve", bit, rows))
        else:
            plan.append(("both", bit, rows))
    return plan + doubles[::-1]


PARTS = 2
PART_ROWS = D // 2 // PARTS


def last_kernel(bits, plans, orders, *refs):
    (line_a, line_b, one_sums, two_sums, fc1_sums, sums_a, sums_c, sums_b, sums_d) = refs[:9]
    rel_a, rel_b, rel_c, rel_d, hots, out, small, rel = refs[9:17]
    small_landed, rel_landed, sends, recvs = refs[17:21]
    rooms = list(refs[21:])
    dp, mp = lax.axis_index("dp"), lax.axis_index("mp")
    bit_at = lambda bit: mp if bit == 0 else (dp // bit) % 2

    def partner(bit):
        if bit == 0:
            return (dp, 1 - mp)
        return (jnp.where(bit_at(bit) == 0, dp + bit, dp - bit), mp)

    barrier = pltpu.get_barrier_semaphore()
    every = [1] + bits + [0]
    for bit in every:
        pl.semaphore_signal(barrier, inc=1, device_id=partner(bit), device_id_type=MESH)

    count = [0]

    def send(src, dst, bit):
        at = count[0]
        count[0] += 1
        copy = pltpu.make_async_remote_copy(
            src_ref=src,
            dst_ref=dst,
            send_sem=sends.at[at],
            recv_sem=recvs.at[at],
            device_id=partner(bit),
            device_id_type=MESH,
        )
        copy.start()
        return copy

    def line(k, part):
        order, value = orders[k], (line_a, line_b)[k].at[pl.ds(part * PART_ROWS, PART_ROWS)]
        slot = dp % 2 * 2 + k
        first = bit_at(order[0]) * (D // 2) + part * PART_ROWS
        start, size, placed = first, PART_ROWS, False
        for kind, bit, after in plans[k]:
            if kind == "double":
                here = pl.ds(pl.multiple_of(start, 16), size)
                if not placed:
                    out[slot, here, :] = value[...]
                    placed = True
                copy = send(out.at[slot, here], out.at[slot, here], bit)
                yield
                copy.wait()
                if after != size or bit != order[0]:
                    start, size = start - bit_at(bit) * size, 2 * size
                continue
            mine = bit_at(bit) if kind == "halve" else 0
            gone = 1 - mine if kind == "halve" else 0
            room, total = rooms.pop(0), rooms.pop(0)
            copy = send(value.at[pl.ds(pl.multiple_of(gone * after, 16), after)], room, bit)
            yield
            copy.wait()
            rows = pl.ds(pl.multiple_of(mine * after, 16), after)
            total[...] = (value[rows, :].astype(F32) + room[...].astype(F32)).astype(BF)
            value = total
            start, size = start + mine * after, after
        copies = []
        for half in range(2):
            rows = pl.ds(half * (D // 2) + part * PART_ROWS, PART_ROWS)
            copies.append(send(out.at[slot, rows], out.at[slot, rows], 1))
        yield
        for copy in copies:
            copy.wait()

    def vectors():
        for at, bit in enumerate(bits + [0, 1]):
            copies = [send(small, small_landed.at[at], bit), send(rel, rel_landed.at[at], bit)]
            yield
            for copy in copies:
                copy.wait()
            small[...] += small_landed[at]
            rel[...] += rel_landed[at]

    lines = [line(k, part) for part in range(PARTS) for k in range(2)]
    pl.semaphore_wait(barrier, len(every))
    for one in lines:
        next(one)

    small[...] = jnp.zeros_like(small)
    small[0:2, :] = one_sums[0:2, :]
    small[2:6, :] = two_sums[0:4, :]
    first = mp == 0
    own = [sums_a[0:1, :] + sums_c[0:1, :], fc1_sums[0:1, 0 : FF // 2]]
    other = [sums_b[0:1, :] + sums_d[0:1, :], fc1_sums[0:1, FF // 2 :]]
    for row, flip in ((6, False), (9, True)):
        picked = [jnp.where(first != flip, a, b) for a, b in zip(own, other)]
        small[row : row + 1, 0:HALF] = picked[0][:, 0:HALF]
        small[row : row + 1, HALF:] = picked[0][:, 2 * HALF :]
        small[row + 1 : row + 2, :] = picked[1][:, 0:D]
        small[row + 2 : row + 3, :] = picked[1][:, D:]
    table = rel_a[...] + rel_b[...] + rel_c[...] + rel_d[...]
    table = lax.dot_general(hots[...], table, TN, precision=lax.Precision.HIGHEST, preferred_element_type=F32)
    rel[...] = table + pltpu.roll(table, HD, 1)

    active = lines + [vectors()]
    while active:
        for one in list(active):
            if next(one, "end") == "end":
                active.remove(one)


def last_sums(bits, orders, lines, sums, rels, hots):
    vmem = pl.BlockSpec(memory_space=pltpu.VMEM)
    rounds = len(bits) + 2
    copies = 2 * rounds + 2 * PARTS * (2 * len(bits) + 2)
    plans = [line_plan(order, PART_ROWS) for order in orders]
    rooms = []
    for at in range(len(plans[0])):
        for part in range(PARTS):
            for plan in plans:
                if plan[at][0] != "double":
                    rooms += [pltpu.VMEM((plan[at][2], HALF), BF)] * 2
    return pl.pallas_call(
        lambda *refs: last_kernel(bits, plans, orders, *refs),
        in_specs=[vmem] * (2 + len(sums) + len(rels) + 1),
        out_specs=[vmem] * 3,
        out_shape=[
            jax.ShapeDtypeStruct((4, D, HALF), BF),
            jax.ShapeDtypeStruct((SMALL, D), F32),
            jax.ShapeDtypeStruct((56, 128), F32),
        ],
        scratch_shapes=[
            pltpu.VMEM((rounds, SMALL, D), F32),
            pltpu.VMEM((rounds, 56, 128), F32),
            pltpu.SemaphoreType.DMA((copies,)),
            pltpu.SemaphoreType.DMA((copies,)),
        ]
        + rooms,
        compiler_params=pltpu.CompilerParams(
            collective_id=0, has_side_effects=True, vmem_limit_bytes=40 * 2**20
        ),
    )(*lines, *sums, *rels, hots)


CORE, PAIRED = 1, 0


def bit_of(bit):
    return lax.axis_index("mp") if bit == PAIRED else (lax.axis_index("dp") // bit) % 2


def exchange(value, bit):
    if bit == PAIRED:
        return lax.ppermute(value, "mp", [(0, 1), (1, 0)])
    return lax.ppermute(value, "dp", [(i, i ^ bit) for i in range(lax.axis_size("dp"))])


class Line:
    def __init__(self, value, places, rank, steps, sent=None):
        self.terms = [(value, tuple(places))]
        self.fixed = {}
        self.rank = list(rank)
        self.steps = list(steps)
        self.sent, self.taken = sent, None
        self.value = None

    def part(self, changes):
        fixed = {**self.fixed, **changes}
        total = None
        for term, places in self.terms:
            starts, sizes, shape = [], [], []
            for bit in places:
                starts.append(fixed.get(bit, 0))
                sizes.append(1 if bit in fixed else 2)
                if bit not in fixed:
                    shape.append(2)
            rest = term.shape[len(places) :]
            if places:
                starts = [jnp.asarray(at, jnp.int32) for at in starts + [0] * len(rest)]
                term = lax.dynamic_slice(term, starts, tuple(sizes) + rest).reshape(tuple(shape) + rest)
            total = term.astype(F32) if total is None else total + term.astype(F32)
        return total.astype(BF)

    def prepare(self):
        kind, bit = self.steps[0]
        if kind == "halve":
            mine = 0 if bit == PAIRED else bit_of(bit)
            self.sent = self.part({bit: 1 - mine})
            self.fixed[bit] = mine
        elif kind == "double":
            if self.value is None:
                self.value, self.done = self.part({}), []
            self.sent = self.value
        elif kind == "pass":
            self.sent = self.part({})

    def launch(self):
        self.taken = exchange(self.sent, self.steps[0][1])

    def land(self):
        kind, bit = self.steps.pop(0)
        if kind in ("halve", "give"):
            places = [p for p in self.terms[0][1] if p not in self.fixed]
            self.terms.append((self.taken, tuple(places)))
        elif kind == "pass":
            self.terms = [(self.taken, tuple(p for p in self.terms[0][1] if p not in self.fixed))]
        else:
            if not self.steps:
                self.taken_last, self.taken = self.taken, None
                return
            self.done = sorted(self.done + [bit], key=self.rank.index)
            axis = self.done.index(bit)
            shape = [1] * (self.value.ndim + 1)
            shape[axis] = 2
            mine = jnp.arange(2).reshape(shape) == bit_of(bit)
            wide = lambda v: jnp.expand_dims(v, axis)
            self.value = jnp.where(mine, wide(self.value), wide(self.taken))
        self.taken = None


def advance(anchor, lines):
    flying = [line for line in lines if line.taken is not None]
    anchor, taken = lax.optimization_barrier((anchor, [line.taken for line in flying]))
    for line, value in zip(flying, taken):
        line.taken = value
        line.land()
    going = [line for line in lines if line.steps]
    for line in going:
        line.prepare()
    anchor, sent = lax.optimization_barrier((anchor, [line.sent for line in going]))
    for line, value in zip(going, sent):
        line.sent = value
        line.launch()
    return anchor


def finish(lines):
    while any(line.steps for line in lines):
        for line in lines:
            if not line.steps:
                continue
            if line.taken is None:
                line.prepare()
                line.launch()
        for line in lines:
            if line.taken is not None:
                line.land()


def on_device(
    image_tokens,
    norm1_gain,
    norm1_shift,
    qkv_weight,
    qv_bias,
    rel_rows,
    rel_cols,
    proj_weight,
    proj_bias,
    norm2_gain,
    norm2_shift,
    fc1_weight,
    fc1_bias,
    fc2_weight,
    fc2_bias,
    out_cotangent,
):
    place = lax.axis_index("mp")
    core = lax.axis_index("dp") % 2
    swap = lambda value: lax.ppermute(value, "mp", [(0, 1), (1, 0)])
    size = lax.axis_size("dp")
    core_swap = lambda value: lax.ppermute(value, "dp", [(i, i ^ 1) for i in range(size)])

    def by_core(weight, axis, mine):
        return lax.dynamic_slice_in_dim(weight, (core if mine else 1 - core) * HALF, HALF, axis)

    block, valid, local, owned, band_of, step_of, taken_of, has_taken = pair_tables(place)
    offset = (place * (OWN // (2 * PAIR))).astype(jnp.int32).reshape(1)
    spread = jnp.asarray(spread_rows(), BF)
    gather = jnp.asarray(spread_rows().T, BF)
    fold = jnp.asarray(fold_table(), BF)
    high_hot, wide_hot = rel_onehots()
    hots = jnp.asarray(np.pad(np.concatenate([high_hot, wide_hot], axis=1), ((0, 0), (0, 2))), F32)
    high_hot, wide_hot = jnp.asarray(high_hot, BF), jnp.asarray(wide_hot, BF)
    core_at = core.astype(jnp.int32).reshape(1)
    qkv_mine = swap(by_core(qkv_weight, 1, True))
    bias_other = swap(qv_bias)
    fc1_bias_other = swap(fc1_bias)
    x_windows = windows_of(image_tokens, norm1_gain, norm1_shift, spread, block, valid)
    x_windows, qkv_mine = lax.optimization_barrier((x_windows, qkv_mine))
    late = (by_core(fc1_weight, 0, True), by_core(fc2_weight, 1, True), proj_weight)
    x_windows, qkv_mine, late = lax.optimization_barrier((x_windows, qkv_mine, late))
    qkv_theirs = exchange(qkv_mine, CORE)
    one_mine, two_mine, proj_other = (swap(w) for w in late)
    qkv_a, p_a, ctx_a, xt, rel_even, rel_odd = attend(
        x_windows, qv_bias, True, qkv_weight, high_hot, wide_hot, rel_rows, rel_cols
    )
    qkv_b, p_b, ctx_b = attend(
        x_windows, bias_other, False, core_at, qkv_mine, qkv_theirs, rel_even, rel_odd
    )
    ctx_b, one_mine, two_mine, proj_other = lax.optimization_barrier((ctx_b, one_mine, two_mine, proj_other))
    one_theirs, two_theirs = exchange(one_mine, CORE), exchange(two_mine, CORE)
    middle, normed, normed_t, cot_t, context = middle_of(
        ctx_a, ctx_b, image_tokens, out_cotangent, proj_weight, proj_other, proj_bias, norm2_gain,
        norm2_shift, gather, band_of, step_of, offset,
    )
    forward, back, one_kept, one_sent, two_kept, two_sent, fc1_sums = feed(
        core_at, normed, normed_t, out_cotangent, cot_t, fc1_weight, (one_mine, one_theirs), fc1_bias,
        fc1_bias_other, fc2_weight, (two_mine, two_theirs),
    )
    bits = [2**k for k in range(1, bits_of(size))]
    turned = bits[1:2] + bits[0:1] + bits[2:]
    halves = lambda order: [("halve", bit) for bit in order]
    doubles = lambda order: [("double", bit) for bit in order]

    def cut(value, axis, places):
        shape = value.shape[:axis] + (2,) * len(places) + (value.shape[axis] // 2 ** len(places),)
        return value.reshape(shape + value.shape[axis + 1 :])

    def feed_line(kept, sent, order, back):
        steps = [("give", CORE)] + halves(order) + doubles(back) + [("double", CORE)]
        rank = [CORE] + bits
        return Line(cut(kept, 1, bits), [PAIRED] + bits, rank, steps, cut(sent, 1, bits))

    one_line = feed_line(one_kept, one_sent, [PAIRED] + bits, bits[::-1])
    two_line = feed_line(two_kept, two_sent, bits[:2] + [PAIRED] + bits[2:], turned[::-1])
    feed_lines = [one_line, two_line]

    middle = advance(middle, feed_lines)
    block_out, middle_grad, ctx_grad, proj_own, proj_oth, two_sums = resid_of(
        middle, forward, back, out_cotangent, context, proj_weight, proj_other, fc2_bias, norm2_gain
    )
    back_of = lambda qkv, p, side, grad, bands, *d: attend_back(
        qkv, p, grad, side, spread, rel_even, rel_odd, fold, local, owned, bands, *d
    )
    ctx_grad = advance(ctx_grad, feed_lines)
    d_b, rel_b, sums_b = back_of(qkv_b, p_b, 1, ctx_grad, (1, 3))
    d_b = advance(d_b, feed_lines)
    d_b, rel_b0, sums_b0 = back_of(qkv_b, p_b, 1, ctx_grad, (0, 1), d_b)
    d_b = advance(d_b, feed_lines)
    kept_b, sent_b = qkv_grad(core_at, xt, d_b, proj_oth)
    line_b = Line(kept_b, [], [], [("give", CORE), ("pass", PAIRED)], sent_b)
    lines = feed_lines + [line_b]
    ctx_grad, kept_b = lax.optimization_barrier((ctx_grad, kept_b))
    ctx_grad = advance(ctx_grad, lines)
    d_a, rel_a, sums_a = back_of(qkv_a, p_a, 0, ctx_grad, (1, 3))
    d_a = advance(d_a, lines)
    up = norm_grad(d_a, d_b, qkv_weight, core_at, qkv_mine, qkv_theirs, gather, (1, 3))
    at = [2 - place, (1 - place) * 4 * SIDE, jnp.zeros_like(place)]
    sent = lax.dynamic_slice(up, at, (1, 10 * SIDE, D)).reshape(10 * SIDE, D)
    shared_line = Line(sent, [], [], [("pass", PAIRED)])
    d_a = advance(d_a, [shared_line])
    d_a, rel_a0, sums_a0 = back_of(qkv_a, p_a, 0, ctx_grad, (0, 1), d_a)
    d_a = advance(d_a, feed_lines + [line_b])
    kept_a, sent_a = qkv_grad(core_at, xt, d_a, proj_own)
    line_a = Line(kept_a, [], [], [("give", CORE)], sent_a)
    kept_a, d_a = lax.optimization_barrier((kept_a, d_a))
    d_a = advance(d_a, feed_lines + [line_a, shared_line])
    up = norm_grad(d_a, d_b, qkv_weight, core_at, qkv_mine, qkv_theirs, gather, (0, 1), up)
    up = advance(up, feed_lines + [line_a])
    taken = shared_line.terms[0][0]
    q_lines = []
    for k, order in enumerate((bits, turned)):
        line = Line(None, [], [], halves(order[:1]))
        parts = [term for term, _ in line_a.terms] + [term for term, _ in line_b.terms]
        line.terms = [(part.reshape(2, 2, D // 2, HALF), ("line", order[0])) for part in parts]
        line.fixed = {"line": k}
        q_lines.append(line)
    up = advance(up, q_lines)
    finish(feed_lines)
    flat = lambda line, rows: (line.value.reshape(rows, -1), line.taken_last.reshape(rows, -1))
    input_grad, one_sums, one_sum, two_sum = input_of(
        image_tokens, middle_grad, up, taken, norm1_gain, flat(one_line, HALF), flat(two_line, FF // 2),
        band_of, step_of, taken_of, has_taken, offset, core_at,
    )
    one_sums = advance(one_sums, q_lines)
    four, small, rel = last_sums(
        bits,
        [bits, turned],
        [line.part({}) for line in q_lines],
        [one_sums, two_sums, fc1_sums, sums_a, sums_a0, sums_b, sums_b0],
        [rel_a, rel_a0, rel_b, rel_b0],
        hots,
    )
    one_sum = one_sum.reshape(D, FF // 2)
    mine = jnp.where(place == 0, small[6:9], small[9:12])
    return (
        block_out,
        input_grad,
        small[0],
        small[1],
        four[0:3].astype(F32),
        mine[0].reshape(2, HALF),
        rel[:RELS, :HD],
        rel[RELS : 2 * RELS, :HD],
        jnp.concatenate([four[3, :HALF], four[3, HALF:]], axis=1).astype(F32),
        small[5],
        small[2],
        small[3],
        one_sum,
        mine[1:3].reshape(-1),
        two_sum,
        small[4],
    )


def solution(mesh):
    in_specs = (
        P("dp", None),
        P(),
        P(),
        P(None, None, "mp"),
        P(None, "mp"),
        P(),
        P(),
        P("mp", None),
        P(),
        P(),
        P(),
        P(None, "mp"),
        P("mp"),
        P("mp", None),
        P(),
        P(("dp", "mp"), None),
    )
    out_specs = (
        P(("dp", "mp"), None),
        P(("dp", "mp"), None),
        P(),
        P(),
        P(None, None, "mp"),
        P(None, "mp"),
        P(),
        P(),
        P("mp", None),
        P(),
        P(),
        P(),
        P(None, "mp"),
        P("mp"),
        P("mp", None),
        P(),
    )
    return jax.shard_map(
        on_device, mesh=mesh, in_specs=in_specs, out_specs=out_specs, check_vma=False
    )
```

```python
import jax
import jax.numpy as jnp
import numpy as np
from jax import lax
from jax.experimental import pallas as pl
from jax.experimental.pallas import tpu as pltpu
from jax.sharding import PartitionSpec as P

D = 768
HEADS = 12
HD = 64
FF = 3072
WIN = 14
SIDE = 64
NWIN = 5
RELS = 27
EPSILON = 1e-06
F32 = jnp.float32
BF = jnp.bfloat16

SLOTS = 256
KEYS = WIN * 16
PAIR = 2 * SIDE
GREL = 80
OWN = SIDE * SIDE // 2

HALF = D // 2
TRIO = 3 * HALF
PAIRS = HEADS // 4

NN = (((1,), (0,)), ((), ()))
NT = (((1,), (1,)), ((), ()))
TN = (((0,), (0,)), ((), ()))


def dot(left, right, dims=NN):
    return lax.dot_general(left, right, dims, preferred_element_type=F32)


def params(limit=60):
    return pltpu.CompilerParams(vmem_limit_bytes=limit * 2**20)


def cost(flops, moved, exps=0):
    return pl.CostEstimate(flops=int(flops), bytes_accessed=int(moved), transcendentals=int(exps))


def whole(shape):
    return pl.BlockSpec(shape, lambda *_: (0,) * len(shape), pipeline_mode=pl.Buffered(1))


def band_start(place, band):
    return (1 - place) * (14 * band) + place * (42 - 14 * band + 21 * band * (band - 1))


def image_pair(place, band, step):
    pair = band_start(place, band) // 2 + step
    return jnp.minimum(pair, SIDE // 2 - 1), pair < SIDE // 2


def owned_pair(place, band, step):
    pair = band_start(place, band) // 2 + step - 16 * place
    return jnp.clip(pair, 0, 15), (pair >= 0) & (pair < 16)


def band_step(place, pair):
    first = pair // 7, pair % 7
    band = jnp.where(pair < 5, 1, jnp.where(pair < 12, 0, 2))
    second = band, jnp.where(pair < 5, pair + 2, jnp.where(pair < 12, pair - 5, pair - 12))
    return tuple(jnp.where(place == 0, a, b) for a, b in zip(first, second))


def taken_pair(place, pair):
    return (
        jnp.where(place == 0, jnp.maximum(pair - 14, 0), jnp.minimum(pair, 4)),
        jnp.where(place == 0, pair >= 14, pair < 5),
    )


def spread_rows():
    table = np.zeros((NWIN, 2, 16, PAIR), np.float32)
    for w in range(NWIN):
        for r in range(2):
            for j in range(WIN):
                if WIN * w + j < SIDE:
                    table[w, r, j, r * SIDE + WIN * w + j] = 1
    return table.reshape(NWIN * 32, PAIR)


def rel_order():
    rows = np.full(GREL, -1)
    for m in range(21):
        rows[m] = 26 - (m + 6)
        rows[24 + m] = 26 - m
    cols = np.full(GREL, -1)
    for m in range(RELS):
        cols[48 + m] = 26 - m
    return rows, cols


def rel_onehots():
    rows, cols = rel_order()
    high = (rows[:, None] == np.arange(RELS)[None, :]).astype(np.float32)
    wide = (cols[:, None] == np.arange(RELS)[None, :]).astype(np.float32)
    return high, wide


def norm_parts(values):
    average = jnp.mean(values, axis=-1, keepdims=True)
    centred = values - average
    inverse = lax.rsqrt(jnp.mean(centred * centred, axis=-1, keepdims=True) + EPSILON)
    return centred * inverse, inverse


def vec(ref):
    return ref[...].astype(F32).reshape(1, D)


def window_kernel(spot, *refs):
    xs, (gain, shift, spread, out) = refs[:7], refs[7:]
    band = pl.program_id(0)
    for t in range(7):
        scaled, _ = norm_parts(xs[t][...].astype(F32))
        normed = scaled * vec(gain) + vec(shift)
        valid = image_pair(spot[0], band, t)[1]
        normed = (normed * valid.astype(F32)).astype(BF)
        moved = dot(spread[...], normed).astype(BF)
        out[:, :, 32 * t : 32 * t + 32, :] = moved.reshape(1, NWIN, 32, D)
    out[:, :, 224:, :] = jnp.zeros((1, NWIN, 32, D), BF)


def windows_of(spot, x, gain, shift, spread):
    at = lambda t: lambda s, spot: (image_pair(spot[0], s, t)[0], 0)
    return pl.pallas_call(
        window_kernel,
        grid_spec=pltpu.PrefetchScalarGridSpec(
            num_scalar_prefetch=1,
            grid=(3,),
            in_specs=[pl.BlockSpec((PAIR, D), at(t)) for t in range(7)]
            + [whole((D,)), whole((D,)), whole((NWIN * 32, PAIR))],
            out_specs=pl.BlockSpec((1, NWIN, SLOTS, D), lambda s, *_: (s, 0, 0, 0)),
        ),
        out_shape=jax.ShapeDtypeStruct((3, NWIN, SLOTS, D), BF),
        compiler_params=params(),
        cost_estimate=cost(3 * 7 * 160 * 128 * 768 * 2, 10e6),
    )(spot, *([x] * 7), gain, shift, spread)


def shift_masks(lanes_from):
    lane = lax.broadcasted_iota(jnp.int32, (1, 128), 1) + lanes_from
    high = lane // 16
    row_shift = jnp.where(lane < 128, 7 - high, jnp.maximum(13 - high, 0))
    col_shift = jnp.maximum(13 - lane % 16, 0)
    return row_shift, col_shift


def skew(table, shift, bits):
    size = table.shape[0]
    for bit in bits:
        moved = pltpu.roll(table, size - bit, 0)
        table = jnp.where((shift & bit) != 0, moved, table)
    return table


def unskew(table, shift, bits):
    for bit in bits:
        moved = pltpu.roll(table, bit, 0)
        table = jnp.where((shift & bit) != 0, moved, table)
    return table


def start_own(weights, bias, high_hot, wide_hot, rel_rows, rel_cols, rel_even, rel_odd, joined):
    for s in range(3):
        joined[:, s * HALF : s * HALF + HALF] = weights[s]
    table = (dot(high_hot[...], rel_rows[...]) + dot(wide_hot[...], rel_cols[...])).astype(BF)
    blank = jnp.zeros_like(table)
    rel_even[...] = jnp.concatenate([table, blank], axis=1)
    rel_odd[...] = jnp.concatenate([blank, table], axis=1)


def join_pieces(core, mine, theirs, joined, col):
    for piece, at in ((mine, core), (theirs, 1 - core)):
        rows = pl.ds(pl.multiple_of(at * HALF, HALF), HALF)
        for s in range(3):
            joined[rows, col + s * HALF : col + s * HALF + HALF] = piece[s]


def attend_own(
    x, bias, weights, high_hot, wide_hot, rel_rows, rel_cols,
    qkv_out, p_out, ctx_out, xt_out, rel_even, rel_odd, joined, vt,
):
    @pl.when((pl.program_id(0) == 0) & (pl.program_id(1) == 0))
    def _():
        start_own(weights, bias, high_hot, wide_hot, rel_rows, rel_cols, rel_even, rel_odd, joined)

    attend_window(x, bias, rel_even, rel_odd, qkv_out, p_out, ctx_out, xt_out, joined, vt)


def attend_other(x, bias, spot, mine, theirs, rel_even, rel_odd, qkv_out, p_out, ctx_out, joined, vt):
    @pl.when((pl.program_id(0) == 0) & (pl.program_id(1) == 0))
    def _():
        join_pieces(spot[1], mine, theirs, joined, 0)

    attend_window(x, bias, rel_even, rel_odd, qkv_out, p_out, ctx_out, None, joined, vt)


def attend_window(x, bias, rel_even, rel_odd, qkv_out, p_out, ctx_out, xt_out, joined, vt):
    band = pl.program_id(0)
    biases = bias[...].astype(F32)
    biases = jnp.concatenate([biases[0:1], jnp.zeros((1, HALF), F32), biases[1:2]], axis=1)
    block = x[...].reshape(SLOTS, D)
    if xt_out is not None:
        xt_out[...] = block.T
    scales = jnp.where(lax.broadcasted_iota(jnp.int32, (1, TRIO), 1) // HALF == 1, HD ** (-0.5), 1.0)
    low = ((dot(block, joined[...]) + biases) * scales).astype(BF)
    qkv_out[0, 0] = low
    vt[...] = low[:, 2 * HALF :].T

    even = lax.broadcasted_iota(jnp.int32, (1, 128), 1) < HD

    def raw_scores(head, lanes):
        col = head // 2 * 128
        keys = qkv_out[0, 0, 0:KEYS, HALF + col : HALF + col + 128]
        kept = jnp.where(even != (head % 2 == 1), keys, jnp.zeros_like(keys))
        rel = rel_odd if head % 2 else rel_even
        left = jnp.concatenate([kept, rel[...]], axis=0)
        return dot(left, qkv_out[0, 0, 0:lanes, col : col + 128], NT)

    def soft(head, raw, lanes):
        parts = []
        for tile in range(lanes // 128):
            row_shift, col_shift = shift_masks(tile * 128)
            raw_t = raw[:, tile * 128 : tile * 128 + 128]
            base = raw_t[0:KEYS]
            high = skew(raw_t[KEYS + 24 * tile : KEYS + 24 * tile + 24], row_shift, (4, 2, 1))[0:16]
            wide = skew(raw_t[KEYS + 48 : KEYS + 80], col_shift, (8, 4, 2, 1))[0:16]
            place = lax.broadcasted_iota(jnp.int32, (16, 128), 0)
            wide = jnp.where(place < WIN, wide, -1e30)
            scores = base.reshape(WIN, 16, 128) + wide[None] + high[0:WIN][:, None, :]
            scores = scores.reshape(KEYS, 128)
            peak = jnp.max(scores, axis=0, keepdims=True)
            grown = jnp.exp(scores - peak)
            total = jnp.sum(grown, axis=0, keepdims=True)
            parts.append((grown * (1.0 / total)).astype(BF))
        probs = parts[0] if len(parts) == 1 else jnp.concatenate(parts, axis=1)
        p_out[0, 0, head, :, 0:lanes] = probs
        return probs

    def all_heads(lanes):
        count = HEADS // 2
        raw = raw_scores(0, lanes)
        contexts = []
        for head in range(count):
            ahead = raw_scores(head + 1, lanes) if head + 1 < count else None
            probs = soft(head, raw, lanes)
            if head:
                contexts.append(dot(vt[(head - 1) * HD : head * HD, 0:KEYS], before).astype(BF))
            if head and head % 2 == 0:
                col = (head - 2) * HD
                ctx_out[0, 0, 0:lanes, col : col + 128] = jnp.concatenate(contexts[-2:], axis=0).T
            before, raw = probs, ahead
        contexts.append(dot(vt[(count - 1) * HD :, 0:KEYS], before).astype(BF))
        ctx_out[0, 0, 0:lanes, HALF - 128 :] = jnp.concatenate(contexts[-2:], axis=0).T

    @pl.when(band < 2)
    def _():
        all_heads(256)

    @pl.when(band == 2)
    def _():
        all_heads(128)


SCALAR = pl.BlockSpec(memory_space=pltpu.SMEM)


def attend(x, bias, first, *operands):
    block = lambda width: pl.BlockSpec((1, 1, SLOTS, width), lambda s, w: (s, w, 0, 0))
    shape = lambda width: jax.ShapeDtypeStruct((3, NWIN, SLOTS, width), BF)
    out_specs = [
        block(TRIO),
        pl.BlockSpec((1, 1, HEADS // 2, KEYS, SLOTS), lambda s, w: (s, w, 0, 0, 0)),
        block(HALF),
    ]
    out_shape = [
        shape(TRIO),
        jax.ShapeDtypeStruct((3, NWIN, HEADS // 2, KEYS, SLOTS), BF),
        shape(HALF),
    ]
    rel = pl.BlockSpec((GREL, 128), lambda s, w: (0, 0))
    if first:
        in_specs = [whole((3, D, HALF)), whole((GREL, RELS)), whole((GREL, RELS)), whole((RELS, HD)), whole((RELS, HD))]
        out_specs += [pl.BlockSpec((D, SLOTS), lambda s, w: (0, s * NWIN + w)), rel, rel]
        out_shape += [jax.ShapeDtypeStruct((D, 3 * NWIN * SLOTS), BF)] + [jax.ShapeDtypeStruct((GREL, 128), BF)] * 2
    else:
        in_specs = [SCALAR, whole((3, HALF, HALF)), whole((3, HALF, HALF)), whole((GREL, 128)), whole((GREL, 128))]
    return pl.pallas_call(
        attend_own if first else attend_other,
        grid=(3, NWIN),
        in_specs=[block(D), whole((2, HALF))] + in_specs,
        out_specs=out_specs,
        out_shape=out_shape,
        scratch_shapes=[pltpu.VMEM((D, TRIO), BF), pltpu.VMEM((HALF, SLOTS), BF)],
        compiler_params=params(),
        cost_estimate=cost(15e9, 45e6, 4e6),
    )(x, bias, *operands)


def middle_kernel(
    spot, own_a, own_b, other_a, other_b, x, proj_own, proj_other, bias, gain, shift, gather,
    middle, normed, normed_t, ctx_out, proj,
):
    @pl.when(pl.program_id(0) == 0)
    def _():
        proj[0:HALF, :] = proj_own[...]
        proj[HALF:, :] = proj_other[...]

    for row, parts in ((0, (own_a, other_a)), (PAIR, (own_b, other_b))):
        for side in range(2):
            moved = dot(gather[...], parts[side][...].reshape(NWIN * 32, HALF)).astype(BF)
            ctx_out[row : row + PAIR, side * HALF : side * HALF + HALF] = moved
    value = x[...].astype(F32) + (dot(ctx_out[...], proj[...]) + vec(bias))
    middle[...] = value.astype(BF)
    scaled, _ = norm_parts(value)
    low = (scaled * vec(gain) + vec(shift)).astype(BF)
    normed[...] = low
    normed_t[...] = low.T


def middle_of(spot, ctx_own, ctx_other, x, proj_own, proj_other, bias, gain, shift, gather):
    rows = 2 * PAIR

    def at(k):
        def place(i, spot):
            band, step = band_step(spot[0], 2 * i + k)
            return band, 0, step, 0

        return pl.BlockSpec((1, NWIN, 32, HALF), place)

    row_block = pl.BlockSpec((rows, D), lambda i, *_: (i, 0))
    col_block = pl.BlockSpec((D, rows), lambda i, *_: (0, i))
    low = jax.ShapeDtypeStruct((OWN, D), BF)
    return pl.pallas_call(
        middle_kernel,
        grid_spec=pltpu.PrefetchScalarGridSpec(
            num_scalar_prefetch=1,
            grid=(OWN // rows,),
            in_specs=[
                at(0),
                at(1),
                at(0),
                at(1),
                pl.BlockSpec((rows, D), lambda i, spot: (spot[0] * (OWN // rows) + i, 0)),
                whole((HALF, D)),
                whole((HALF, D)),
                whole((D,)),
                whole((D,)),
                whole((D,)),
                whole((PAIR, NWIN * 32)),
            ],
            out_specs=[row_block, row_block, col_block, row_block],
            scratch_shapes=[pltpu.VMEM((D, D), BF)],
        ),
        out_shape=[low, low, jax.ShapeDtypeStruct((D, OWN), BF), low],
        compiler_params=params(),
        cost_estimate=cost(3e9, 25e6),
    )(spot, ctx_own, ctx_own, ctx_other, ctx_other, x, proj_own, proj_other, bias, gain, shift, gather)


def turn_kernel(value, out):
    out[...] = value[...].T


def turned_of(value):
    rows = 512
    return pl.pallas_call(
        turn_kernel,
        grid=(OWN // rows,),
        in_specs=[pl.BlockSpec((rows, D), lambda i: (i, 0))],
        out_specs=pl.BlockSpec((D, rows), lambda i: (0, i)),
        out_shape=jax.ShapeDtypeStruct((D, OWN), BF),
        compiler_params=params(),
        cost_estimate=cost(1e6, 6e6),
    )(value)


CHUNK = 512
CHUNKS = FF // CHUNK


def feed_kernel(
    spot, normed, normed_t, cot, cot_t, one_a, one_b, one_c, bias_a, bias_b, two_a, two_b, two_c,
    forward_out, back_out, one_kept, one_sent, two_kept, two_sent, sums,
    forward, back, one, two, bias, hidden, grads,
):
    step = pl.program_id(0)

    @pl.when(step == 0)
    def _():
        forward[...] = jnp.zeros_like(forward)
        back[...] = jnp.zeros_like(back)

    @pl.when(step < CHUNKS // 2)
    def _():
        bias[...] = bias_a[...].astype(F32).reshape(1, CHUNK)
        one[...] = one_a[...]
        two[...] = two_a[...]

    @pl.when(step >= CHUNKS // 2)
    def _():
        bias[...] = bias_b[...].astype(F32).reshape(1, CHUNK)
        mine = pl.multiple_of(spot[1] * HALF, HALF)
        theirs = pl.multiple_of((1 - spot[1]) * HALF, HALF)
        one[pl.ds(mine, HALF), :] = one_b[...]
        one[pl.ds(theirs, HALF), :] = one_c[...]
        two[:, pl.ds(mine, HALF)] = two_b[...]
        two[:, pl.ds(theirs, HALF)] = two_c[...]

    total = jnp.zeros((1, CHUNK), F32)
    for t in range(OWN // 256):
        rows = slice(t * 256, t * 256 + 256)
        pre = dot(normed[rows, :], one[...]) + bias[...]
        phi = 0.5 * (1.0 + lax.erf(pre * 0.7071067811865476))
        slope = phi + pre * (jnp.exp(-0.5 * pre * pre) * 0.3989422804014327)
        low = (pre * phi).astype(BF)
        grad = (dot(cot[rows, :], two[...], NT) * slope).astype(BF)
        hidden[rows, :] = low
        grads[rows, :] = grad
        total += jnp.sum(grad.astype(F32), axis=0, keepdims=True)
        forward[rows, :] += dot(low, two[...])
        back[rows, :] += dot(grad, one[...], NT)
    sums[...] = total

    first = spot[1] == 0
    one_grad = dot(normed_t[...], grads[...]).astype(BF)
    low, high = one_grad[:HALF], one_grad[HALF:]
    one_kept[0] = jnp.where(first, low, high)
    one_sent[0] = jnp.where(first, high, low)
    two_grad = dot(cot_t[...], hidden[...]).astype(BF)
    low, high = two_grad[:HALF], two_grad[HALF:]
    two_kept[0] = jnp.where(first, low, high).T
    two_sent[0] = jnp.where(first, high, low).T

    @pl.when(step == pl.num_programs(0) - 1)
    def _():
        forward_out[...] = forward[...].astype(BF)
        back_out[...] = back[...].astype(BF)


def feed(spot, normed, normed_t, cot, cot_t, one_a, ones, bias_a, bias_b, two_a, twos):
    half = CHUNKS // 2
    own = lambda j: jnp.minimum(j, half - 1)
    other = lambda j: jnp.maximum(j - half, 0)
    one_block = pl.BlockSpec((1, HALF, CHUNK), lambda j, *_: (j // half, 0, j % half))
    two_block = pl.BlockSpec((1, CHUNK, HALF), lambda j, *_: (j // half, j % half, 0))
    one_piece = pl.BlockSpec((HALF, CHUNK), lambda j, *_: (0, other(j)))
    two_piece = pl.BlockSpec((CHUNK, HALF), lambda j, *_: (other(j), 0))
    one_shape = jax.ShapeDtypeStruct((2, HALF, FF // 2), BF)
    two_shape = jax.ShapeDtypeStruct((2, FF // 2, HALF), BF)
    sum_block = pl.BlockSpec((OWN, D), lambda j, *_: (0, 0))
    bias_block = pl.BlockSpec((1, CHUNK), lambda j, *_: (0, j))
    return pl.pallas_call(
        feed_kernel,
        grid_spec=pltpu.PrefetchScalarGridSpec(
            num_scalar_prefetch=1,
            grid=(CHUNKS,),
            in_specs=[
                whole((OWN, D)),
                whole((D, OWN)),
                whole((OWN, D)),
                whole((D, OWN)),
                pl.BlockSpec((D, CHUNK), lambda j, *_: (0, own(j))),
                one_piece,
                one_piece,
                pl.BlockSpec((CHUNK,), lambda j, *_: (own(j),)),
                pl.BlockSpec((CHUNK,), lambda j, *_: (other(j),)),
                pl.BlockSpec((CHUNK, D), lambda j, *_: (own(j), 0)),
                two_piece,
                two_piece,
            ],
            out_specs=[sum_block, sum_block, one_block, one_block, two_block, two_block, bias_block],
            scratch_shapes=[
                pltpu.VMEM((OWN, D), F32),
                pltpu.VMEM((OWN, D), F32),
                pltpu.VMEM((D, CHUNK), BF),
                pltpu.VMEM((CHUNK, D), BF),
                pltpu.VMEM((1, CHUNK), F32),
                pltpu.VMEM((OWN, CHUNK), BF),
                pltpu.VMEM((OWN, CHUNK), BF),
            ],
        ),
        out_shape=[
            jax.ShapeDtypeStruct((OWN, D), BF),
            jax.ShapeDtypeStruct((OWN, D), BF),
            one_shape,
            one_shape,
            two_shape,
            two_shape,
            jax.ShapeDtypeStruct((1, FF), F32),
        ],
        compiler_params=params(62),
        cost_estimate=cost(58e9, 60e6, 12e6),
    )(spot, normed, normed_t, cot, cot_t, one_a, *ones, bias_a, bias_b, two_a, *twos)


def add_row(sums, row, values):
    sums[row : row + 1, :] += jnp.sum(values, axis=0, keepdims=True)


def resid_kernel(
    middle, forward, back, cot, context, proj_own, proj_other, bias, gain,
    block_out, grad_out, ctx_grad, grad_own, grad_other, sums, proj, proj_grad,
):
    step = pl.program_id(0)

    @pl.when(step == 0)
    def _():
        proj[0:HALF, :] = proj_own[...]
        proj[HALF:, :] = proj_other[...]
        proj_grad[...] = jnp.zeros_like(proj_grad)
        sums[...] = jnp.zeros_like(sums)

    value = middle[...].astype(F32)
    block_out[...] = (value + (forward[...].astype(F32) + vec(bias))).astype(BF)
    scaled, inverse = norm_parts(value)
    upstream = back[...].astype(F32)
    scaled_up = upstream * vec(gain)
    first = jnp.mean(scaled_up, axis=-1, keepdims=True)
    second = jnp.mean(scaled_up * scaled, axis=-1, keepdims=True)
    cotangent = cot[...].astype(F32)
    grad = cotangent + inverse * (scaled_up - first - scaled * second)
    low = grad.astype(BF)
    grad_out[...] = low
    ctx_grad[...] = dot(low, proj[...], NT).astype(BF)
    proj_grad[...] += dot(context[...], low, TN)
    add_row(sums, 0, upstream * scaled)
    add_row(sums, 1, upstream)
    add_row(sums, 2, cotangent)
    add_row(sums, 3, low.astype(F32))

    @pl.when(step == pl.num_programs(0) - 1)
    def _():
        for out, row in ((grad_own, 0), (grad_other, HALF)):
            for col in (0, HALF):
                out[col : col + HALF, :] = proj_grad[row : row + HALF, col : col + HALF].astype(BF)


def resid_of(middle, forward, back, cot, context, proj_own, proj_other, bias, gain):
    rows = 512
    row_block = pl.BlockSpec((rows, D), lambda i: (i, 0))
    half_block = pl.BlockSpec((D, HALF), lambda i: (0, 0))
    return pl.pallas_call(
        resid_kernel,
        grid=(OWN // rows,),
        in_specs=[row_block] * 5 + [whole((HALF, D)), whole((HALF, D)), whole((D,)), whole((D,))],
        out_specs=[
            row_block,
            row_block,
            row_block,
            half_block,
            half_block,
            pl.BlockSpec((8, D), lambda i: (0, 0)),
        ],
        out_shape=[
            jax.ShapeDtypeStruct((OWN, D), BF),
            jax.ShapeDtypeStruct((OWN, D), BF),
            jax.ShapeDtypeStruct((OWN, D), BF),
            jax.ShapeDtypeStruct((D, HALF), BF),
            jax.ShapeDtypeStruct((D, HALF), BF),
            jax.ShapeDtypeStruct((8, D), F32),
        ],
        scratch_shapes=[pltpu.VMEM((D, D), BF), pltpu.VMEM((D, D), F32)],
        compiler_params=params(),
        cost_estimate=cost(5e9, 40e6),
    )(middle, forward, back, cot, context, proj_own, proj_other, bias, gain)


def attend_back_kernel(first, spot, qkv, p, ctx_grad, spread, rel_even, rel_odd, fold, *refs):
    d_out, rel_grad, sums, upstream, kt = refs[-5:]
    band = pl.program_id(0) + first
    window = pl.program_id(1)

    @pl.when((band == first) & (window == 0))
    def _():
        rel_grad[...] = jnp.zeros_like(rel_grad)
        sums[...] = jnp.zeros_like(sums)

    @pl.when(window == 0)
    def _():
        for t in range(7):
            at, owned = owned_pair(spot[0], band, t)
            rows = pl.ds(pl.multiple_of(at * PAIR, PAIR), PAIR)
            moved = dot(spread[...], ctx_grad[rows, :])
            moved = moved * owned.astype(F32)
            upstream[:, 32 * t : 32 * t + 32, :] = moved.astype(BF).reshape(NWIN, 32, HALF)
        upstream[:, 224:256, :] = jnp.zeros((NWIN, 32, HALF), BF)

    kt[...] = qkv[0, 0, :, HALF : 2 * HALF].T
    even = lax.broadcasted_iota(jnp.int32, (1, 128), 1) < HD

    def shifted(head, by):
        return slice(by * HALF + head // 2 * 128, by * HALF + head // 2 * 128 + 128)

    def prob_grads(head, lanes):
        values = qkv[0, 0, 0:KEYS, shifted(head, 2)]
        kept = jnp.where(even != (head % 2 == 1), values, jnp.zeros_like(values))
        return dot(kept, upstream[window, 0:lanes, shifted(head, 0)], NT)

    def rel_table(both, lanes):
        tables = []
        zero8 = jnp.zeros((8, 128), F32)
        zero24 = jnp.zeros((24, 128), F32)
        zero16 = jnp.zeros((16, 128), F32)
        for tile in range(lanes // 128):
            row_shift, col_shift = shift_masks(tile * 128)
            part = both[:, tile * 128 : tile * 128 + 128]
            high = jnp.concatenate([part[HD : HD + 16], zero8], axis=0)
            wide = jnp.concatenate([part[HD + 16 : HD + 32], zero16], axis=0)
            high = unskew(high, row_shift, (1, 2, 4))
            wide = unskew(wide, col_shift, (1, 2, 4, 8))
            stack = [high, zero24, wide] if tile == 0 else [zero24, high, wide]
            tables.append(jnp.concatenate(stack, axis=0))
        table = tables[0] if len(tables) == 1 else jnp.concatenate(tables, axis=1)
        return table.astype(BF)

    def all_heads(lanes):
        count = HEADS // 2
        dvs, dks, dqs, drs = [], [], [], []

        def last_part(head, score_grad, both):
            rel = rel_odd if head % 2 else rel_even
            table = rel_table(both, lanes)
            queries = qkv[0, 0, 0:lanes, shifted(head, 0)]
            grads = dot(jnp.concatenate([score_grad, table], axis=0), queries)
            dks.append(grads[0:KEYS])
            drs.append(grads[KEYS:])
            from_rel = dot(rel[...], table, TN)
            side = head % 2 * HD
            dqs.append(both[0:HD] + from_rel[side : side + HD])
            if head % 2:
                d_out[0, 0, 0:lanes, shifted(head, 0)] = jnp.concatenate(dqs[-2:], axis=0).astype(BF).T
                d_out[0, 0, 0:KEYS, shifted(head, 1)] = (jnp.where(even, dks[-2], dks[-1]) * HD ** (-0.5)).astype(BF)

        prob_grad = prob_grads(0, lanes)
        before = None
        for head in range(count):
            ahead = prob_grads(head + 1, lanes) if head + 1 < count else None
            probs_low = p[0, 0, head, :, 0:lanes]
            probs = probs_low.astype(F32)
            total = jnp.sum(prob_grad * probs, axis=0, keepdims=True)
            score_grad = (probs * (prob_grad - total)).astype(BF)
            dvs.append(dot(probs_low, upstream[window, 0:lanes, shifted(head, 0)]))
            left = jnp.concatenate([kt[head * HD : head * HD + HD, 0:KEYS], fold[...]], axis=0)
            both = dot(left, score_grad)
            if head % 2:
                d_out[0, 0, 0:KEYS, shifted(head, 2)] = jnp.where(even, dvs[-2], dvs[-1]).astype(BF)
            if before is not None:
                last_part(head - 1, *before)
            before, prob_grad = (score_grad, both), ahead
        last_part(count - 1, *before)
        evens = drs[0] + drs[2] + drs[4]
        odds = drs[1] + drs[3] + drs[5]
        rel_grad[...] += jnp.where(even, evens, odds)

    d_out[0, 0, KEYS:, HALF:] = jnp.zeros((SLOTS - KEYS, 2 * HALF), BF)

    @pl.when(band < 2)
    def _():
        all_heads(256)

    @pl.when(band == 2)
    def _():
        all_heads(128)
        d_out[0, 0, 128:, 0:HALF] = jnp.zeros((128, HALF), BF)

    sums[0:1, :] += jnp.sum(d_out[...].reshape(SLOTS, TRIO).astype(F32), axis=0, keepdims=True)


def fold_table():
    table = np.zeros((32, WIN, 16), np.float32)
    for k in range(WIN):
        for l in range(WIN):
            table[k, k, l] = 1
            table[16 + l, k, l] = 1
    return table.reshape(32, KEYS)


def attend_back(spot, qkv, p, ctx_grad, side, spread, rel_even, rel_odd, fold, bands, *d_in):
    first, last = bands
    block = pl.BlockSpec((1, 1, SLOTS, TRIO), lambda s, w, *_: (s + first, w, 0, 0))
    share = (last - first) / 3
    return pl.pallas_call(
        lambda *refs: attend_back_kernel(first, *refs),
        grid_spec=pltpu.PrefetchScalarGridSpec(
            num_scalar_prefetch=1,
            grid=(last - first, NWIN),
            in_specs=[
                block,
                pl.BlockSpec((1, 1, HEADS // 2, KEYS, SLOTS), lambda s, w, *_: (s + first, w, 0, 0, 0)),
                pl.BlockSpec((OWN, HALF), lambda *_: (0, side), pipeline_mode=pl.Buffered(1)),
                whole((NWIN * 32, PAIR)),
                whole((GREL, 128)),
                whole((GREL, 128)),
                whole((32, KEYS)),
            ]
            + [pl.BlockSpec(memory_space=pl.ANY)] * len(d_in),
            out_specs=[
                block,
                pl.BlockSpec((GREL, 128), lambda s, w, *_: (0, 0)),
                pl.BlockSpec((8, TRIO), lambda s, w, *_: (0, 0)),
            ],
            scratch_shapes=[pltpu.VMEM((NWIN, SLOTS, HALF), BF), pltpu.VMEM((HALF, SLOTS), BF)],
        ),
        out_shape=[
            jax.ShapeDtypeStruct((3, NWIN, SLOTS, TRIO), BF),
            jax.ShapeDtypeStruct((GREL, 128), F32),
            jax.ShapeDtypeStruct((8, TRIO), F32),
        ],
        input_output_aliases={8: 0} if d_in else {},
        compiler_params=params(),
        cost_estimate=cost(20e9 * share, 45e6 * share),
    )(spot, qkv, p, ctx_grad, spread, rel_even, rel_odd, fold, *d_in)


def norm_grad_kernel(own, other, weights_own, spot, mine, theirs, gather, *refs):
    out, joined = refs[-2:]

    @pl.when((pl.program_id(0) == 0) & (pl.program_id(1) == 0))
    def _():
        for s in range(3):
            joined[:, s * HALF : s * HALF + HALF] = weights_own[s]
        join_pieces(spot[1], mine, theirs, joined, TRIO)

    rows = NWIN * 128
    left = jnp.concatenate([own[...].reshape(rows, TRIO), other[...].reshape(rows, TRIO)], axis=1)
    total = dot(left, joined[...], NT).astype(BF).reshape(NWIN, 4, 32, D)
    for t in range(4):
        moved = dot(gather[...], total[:, t].reshape(NWIN * 32, D)).astype(BF)
        out[:, t * PAIR : t * PAIR + PAIR, :] = moved.reshape(1, PAIR, D)


def norm_grad(own, other, weights_own, core, mine, theirs, gather, bands, *before):
    first, last = bands
    share = (last - first) / 3
    block = pl.BlockSpec((1, NWIN, 128, TRIO), lambda s, t: (s + first, 0, t, 0))
    return pl.pallas_call(
        norm_grad_kernel,
        grid=(last - first, 2),
        in_specs=[block, block, whole((3, D, HALF)), SCALAR]
        + [whole((3, HALF, HALF)), whole((3, HALF, HALF)), whole((PAIR, NWIN * 32))]
        + [pl.BlockSpec(memory_space=pl.ANY)] * len(before),
        out_specs=pl.BlockSpec((1, 4 * PAIR, D), lambda s, t: (s + first, t, 0)),
        out_shape=jax.ShapeDtypeStruct((3, 8 * PAIR, D), BF),
        input_output_aliases={7: 0} if before else {},
        scratch_shapes=[pltpu.VMEM((D, 2 * TRIO), BF)],
        compiler_params=params(),
        cost_estimate=cost(14e9 * share, 30e6 * share),
    )(own, other, weights_own, core, mine, theirs, gather, *before)


def qkv_grad_kernel(spot, xt, d, proj, kept, sent, total):
    step = pl.program_id(0)
    for col in range(0, TRIO, 256):
        cols = slice(col, min(col + 256, TRIO))
        part = dot(xt[...], d[:, cols])
        total[:, cols] = jnp.where(step == 0, part, total[:, cols] + part)

    @pl.when(step == pl.num_programs(0) - 1)
    def _():
        first = spot[1] == 0
        values = [total[:, s * HALF : s * HALF + HALF].astype(BF) for s in range(3)] + [proj[...]]
        for k in range(2):
            kept[k] = jnp.where(first, values[k], values[2 + k])
            sent[k] = jnp.where(first, values[2 + k], values[k])


def qkv_grad(core, xt, d, proj):
    rows = NWIN * SLOTS
    block = pl.BlockSpec((2, D, HALF), lambda i: (0, 0, 0))
    shape = jax.ShapeDtypeStruct((2, D, HALF), BF)
    return pl.pallas_call(
        qkv_grad_kernel,
        grid=(3,),
        in_specs=[
            SCALAR,
            pl.BlockSpec((D, rows), lambda i: (0, i)),
            pl.BlockSpec((rows, TRIO), lambda i: (i, 0)),
            whole((D, HALF)),
        ],
        out_specs=[block, block],
        out_shape=[shape, shape],
        scratch_shapes=[pltpu.VMEM((D, TRIO), F32)],
        compiler_params=params(),
        cost_estimate=cost(7e9, 16e6),
    )(core, xt, d.reshape(3 * rows, TRIO), proj)


def input_kernel(
    spot, x, middle_grad, up_a, up_b, taken_a, taken_b, gain,
    one_mine, one_theirs, two_mine, two_theirs, out, sums, one_out, two_out,
):
    step = pl.program_id(0)
    first = spot[1] == 0
    mine, theirs = one_mine[...].astype(F32), one_theirs[...].astype(F32)
    one_out[0] = jnp.where(first, mine, theirs)
    one_out[1] = jnp.where(first, theirs, mine)
    mine, theirs = two_mine[...].astype(F32), two_theirs[...].astype(F32)
    two_out[:, 0:HALF] = jnp.where(first, mine, theirs)
    two_out[:, HALF:] = jnp.where(first, theirs, mine)

    @pl.when(step == 0)
    def _():
        sums[...] = jnp.zeros_like(sums)

    for k, (up, taken) in enumerate(((up_a, taken_a), (up_b, taken_b))):
        rows = slice(k * PAIR, k * PAIR + PAIR)
        scaled, inverse = norm_parts(x[rows, :].astype(F32))
        shared = taken[...].astype(F32) * taken_pair(spot[0], 2 * step + k)[1].astype(F32)
        upstream = up[0].astype(F32) + shared
        scaled_up = upstream * vec(gain)
        mean = jnp.mean(scaled_up, axis=-1, keepdims=True)
        second = jnp.mean(scaled_up * scaled, axis=-1, keepdims=True)
        out[rows, :] = (middle_grad[rows, :].astype(F32) + inverse * (scaled_up - mean - scaled * second)).astype(BF)
        add_row(sums, 0, upstream * scaled)
        add_row(sums, 1, upstream)


def input_of(spot, x, middle_grad, up, taken, gain, ones, twos):
    rows = 2 * PAIR
    row_block = pl.BlockSpec((rows, D), lambda i, *_: (i, 0))
    up_at = lambda k: lambda i, spot: band_step(spot[0], 2 * i + k) + (0,)
    taken_at = lambda k: lambda i, spot: (taken_pair(spot[0], 2 * i + k)[0], 0)
    steps = OWN // rows
    one_rows, two_rows = HALF // steps, FF // 2 // steps
    return pl.pallas_call(
        input_kernel,
        grid_spec=pltpu.PrefetchScalarGridSpec(
            num_scalar_prefetch=1,
            grid=(steps,),
            in_specs=[
                pl.BlockSpec((rows, D), lambda i, spot: (spot[0] * steps + i, 0)),
                row_block,
                pl.BlockSpec((1, PAIR, D), up_at(0)),
                pl.BlockSpec((1, PAIR, D), up_at(1)),
                pl.BlockSpec((PAIR, D), taken_at(0)),
                pl.BlockSpec((PAIR, D), taken_at(1)),
                whole((D,)),
            ]
            + [pl.BlockSpec((one_rows, FF // 2), lambda i, *_: (i, 0))] * 2
            + [pl.BlockSpec((two_rows, HALF), lambda i, *_: (i, 0))] * 2,
            out_specs=[
                row_block,
                pl.BlockSpec((8, D), lambda i, *_: (0, 0)),
                pl.BlockSpec((2, one_rows, FF // 2), lambda i, *_: (0, i, 0)),
                pl.BlockSpec((two_rows, D), lambda i, *_: (i, 0)),
            ],
        ),
        out_shape=[
            jax.ShapeDtypeStruct((OWN, D), BF),
            jax.ShapeDtypeStruct((8, D), F32),
            jax.ShapeDtypeStruct((2, HALF, FF // 2), F32),
            jax.ShapeDtypeStruct((FF // 2, D), F32),
        ],
        compiler_params=params(),
        cost_estimate=cost(1e8, 35e6),
    )(spot, x, middle_grad, up, up, taken, taken, gain, *ones, *twos)


MESH = pl.DeviceIdType.MESH
SMALL = 24


def bits_of(size):
    return size.bit_length() - 1


def line_plan(order, rows):
    plan, doubles = [], [("double", order[0], rows)]
    for bit in order[1:]:
        if rows % 32 == 0:
            doubles.append(("double", bit, rows))
            rows //= 2
            plan.append(("halve", bit, rows))
        else:
            plan.append(("both", bit, rows))
    return plan + doubles[::-1]


PARTS = 2
PART_ROWS = D // 2 // PARTS


def last_kernel(bits, plans, orders, *refs):
    (line_a, line_b, one_sums, two_sums, fc1_sums, sums_a, sums_c, sums_b, sums_d) = refs[:9]
    rel_a, rel_b, rel_c, rel_d, hots, out, small, rel = refs[9:17]
    small_landed, rel_landed, sends, recvs = refs[17:21]
    rooms = list(refs[21:])
    dp, mp = lax.axis_index("dp"), lax.axis_index("mp")
    bit_at = lambda bit: mp if bit == 0 else (dp // bit) % 2

    def partner(bit):
        if bit == 0:
            return (dp, 1 - mp)
        return (jnp.where(bit_at(bit) == 0, dp + bit, dp - bit), mp)

    barrier = pltpu.get_barrier_semaphore()
    every = [1] + bits + [0]
    for bit in every:
        pl.semaphore_signal(barrier, inc=1, device_id=partner(bit), device_id_type=MESH)

    count = [0]

    def send(src, dst, bit):
        at = count[0]
        count[0] += 1
        copy = pltpu.make_async_remote_copy(
            src_ref=src,
            dst_ref=dst,
            send_sem=sends.at[at],
            recv_sem=recvs.at[at],
            device_id=partner(bit),
            device_id_type=MESH,
        )
        copy.start()
        return copy

    def line(k, part):
        order, value = orders[k], (line_a, line_b)[k].at[pl.ds(part * PART_ROWS, PART_ROWS)]
        slot = dp % 2 * 2 + k
        first = bit_at(order[0]) * (D // 2) + part * PART_ROWS
        start, size, placed = first, PART_ROWS, False
        for kind, bit, after in plans[k]:
            if kind == "double":
                here = pl.ds(pl.multiple_of(start, 16), size)
                if not placed:
                    out[slot, here, :] = value[...]
                    placed = True
                copy = send(out.at[slot, here], out.at[slot, here], bit)
                yield
                copy.wait()
                if after != size or bit != order[0]:
                    start, size = start - bit_at(bit) * size, 2 * size
                continue
            mine = bit_at(bit) if kind == "halve" else 0
            gone = 1 - mine if kind == "halve" else 0
            room, total = rooms.pop(0), rooms.pop(0)
            copy = send(value.at[pl.ds(pl.multiple_of(gone * after, 16), after)], room, bit)
            yield
            copy.wait()
            rows = pl.ds(pl.multiple_of(mine * after, 16), after)
            total[...] = (value[rows, :].astype(F32) + room[...].astype(F32)).astype(BF)
            value = total
            start, size = start + mine * after, after
        copies = []
        for half in range(2):
            rows = pl.ds(half * (D // 2) + part * PART_ROWS, PART_ROWS)
            copies.append(send(out.at[slot, rows], out.at[slot, rows], 1))
        yield
        for copy in copies:
            copy.wait()

    def vectors():
        for at, bit in enumerate(bits + [0, 1]):
            copies = [send(small, small_landed.at[at], bit), send(rel, rel_landed.at[at], bit)]
            yield
            for copy in copies:
                copy.wait()
            small[...] += small_landed[at]
            rel[...] += rel_landed[at]

    lines = [line(k, part) for part in range(PARTS) for k in range(2)]
    pl.semaphore_wait(barrier, len(every))
    for one in lines:
        next(one)

    small[...] = jnp.zeros_like(small)
    small[0:2, :] = one_sums[0:2, :]
    small[2:6, :] = two_sums[0:4, :]
    first = mp == 0
    own = [sums_a[0:1, :] + sums_c[0:1, :], fc1_sums[0:1, 0 : FF // 2]]
    other = [sums_b[0:1, :] + sums_d[0:1, :], fc1_sums[0:1, FF // 2 :]]
    for row, flip in ((6, False), (9, True)):
        picked = [jnp.where(first != flip, a, b) for a, b in zip(own, other)]
        small[row : row + 1, 0:HALF] = picked[0][:, 0:HALF]
        small[row : row + 1, HALF:] = picked[0][:, 2 * HALF :]
        small[row + 1 : row + 2, :] = picked[1][:, 0:D]
        small[row + 2 : row + 3, :] = picked[1][:, D:]
    table = rel_a[...] + rel_b[...] + rel_c[...] + rel_d[...]
    table = lax.dot_general(hots[...], table, TN, precision=lax.Precision.HIGHEST, preferred_element_type=F32)
    rel[...] = table + pltpu.roll(table, HD, 1)

    active = lines + [vectors()]
    while active:
        for one in list(active):
            if next(one, "end") == "end":
                active.remove(one)


def last_sums(bits, orders, lines, sums, rels, hots):
    vmem = pl.BlockSpec(memory_space=pltpu.VMEM)
    rounds = len(bits) + 2
    copies = 2 * rounds + 2 * PARTS * (2 * len(bits) + 2)
    plans = [line_plan(order, PART_ROWS) for order in orders]
    rooms = []
    for at in range(len(plans[0])):
        for part in range(PARTS):
            for plan in plans:
                if plan[at][0] != "double":
                    rooms += [pltpu.VMEM((plan[at][2], HALF), BF)] * 2
    return pl.pallas_call(
        lambda *refs: last_kernel(bits, plans, orders, *refs),
        in_specs=[vmem] * (2 + len(sums) + len(rels) + 1),
        out_specs=[vmem] * 3,
        out_shape=[
            jax.ShapeDtypeStruct((4, D, HALF), BF),
            jax.ShapeDtypeStruct((SMALL, D), F32),
            jax.ShapeDtypeStruct((56, 128), F32),
        ],
        scratch_shapes=[
            pltpu.VMEM((rounds, SMALL, D), F32),
            pltpu.VMEM((rounds, 56, 128), F32),
            pltpu.SemaphoreType.DMA((copies,)),
            pltpu.SemaphoreType.DMA((copies,)),
        ]
        + rooms,
        compiler_params=pltpu.CompilerParams(
            collective_id=0, has_side_effects=True, vmem_limit_bytes=40 * 2**20
        ),
    )(*lines, *sums, *rels, hots)


CORE, PAIRED = 1, 0


def bit_of(bit):
    return lax.axis_index("mp") if bit == PAIRED else (lax.axis_index("dp") // bit) % 2


def exchange(value, bit):
    if bit == PAIRED:
        return lax.ppermute(value, "mp", [(0, 1), (1, 0)])
    return lax.ppermute(value, "dp", [(i, i ^ bit) for i in range(lax.axis_size("dp"))])


class Line:
    def __init__(self, value, places, rank, steps, sent=None):
        self.terms = [(value, tuple(places))]
        self.fixed = {}
        self.rank = list(rank)
        self.steps = list(steps)
        self.sent, self.taken = sent, None
        self.value = None

    def part(self, changes):
        fixed = {**self.fixed, **changes}
        total = None
        for term, places in self.terms:
            starts, sizes, shape = [], [], []
            for bit in places:
                starts.append(fixed.get(bit, 0))
                sizes.append(1 if bit in fixed else 2)
                if bit not in fixed:
                    shape.append(2)
            rest = term.shape[len(places) :]
            if places:
                starts = [jnp.asarray(at, jnp.int32) for at in starts + [0] * len(rest)]
                term = lax.dynamic_slice(term, starts, tuple(sizes) + rest).reshape(tuple(shape) + rest)
            total = term.astype(F32) if total is None else total + term.astype(F32)
        return total.astype(BF)

    def prepare(self):
        kind, bit = self.steps[0]
        if kind == "halve":
            mine = 0 if bit == PAIRED else bit_of(bit)
            self.sent = self.part({bit: 1 - mine})
            self.fixed[bit] = mine
        elif kind == "double":
            if self.value is None:
                self.value, self.done = self.part({}), []
            self.sent = self.value
        elif kind == "pass":
            self.sent = self.part({})

    def launch(self):
        self.taken = exchange(self.sent, self.steps[0][1])

    def land(self):
        kind, bit = self.steps.pop(0)
        if kind in ("halve", "give"):
            places = [p for p in self.terms[0][1] if p not in self.fixed]
            self.terms.append((self.taken, tuple(places)))
        elif kind == "pass":
            self.terms = [(self.taken, tuple(p for p in self.terms[0][1] if p not in self.fixed))]
        else:
            if not self.steps:
                self.value, self.taken_last, self.taken = self.sent, self.taken, None
                return
            self.done = sorted(self.done + [bit], key=self.rank.index)
            axis = self.done.index(bit)
            shape = [1] * (self.value.ndim + 1)
            shape[axis] = 2
            mine = jnp.arange(2).reshape(shape) == bit_of(bit)
            wide = lambda v: jnp.expand_dims(v, axis)
            self.value = jnp.where(mine, wide(self.sent), wide(self.taken))
        self.taken = None


def advance(anchor, lines):
    flying = [line for line in lines if line.taken is not None]
    anchor, taken = lax.optimization_barrier((anchor, [line.taken for line in flying]))
    for line, value in zip(flying, taken):
        line.taken = value
        line.land()
    going = [line for line in lines if line.steps]
    for line in going:
        line.prepare()
    anchor, sent = lax.optimization_barrier((anchor, [line.sent for line in going]))
    for line, value in zip(going, sent):
        line.sent = value
        line.launch()
    return anchor


def finish(lines):
    while any(line.steps for line in lines):
        for line in lines:
            if not line.steps:
                continue
            if line.taken is None:
                line.prepare()
                line.launch()
        for line in lines:
            if line.taken is not None:
                line.land()


def on_device(
    image_tokens,
    norm1_gain,
    norm1_shift,
    qkv_weight,
    qv_bias,
    rel_rows,
    rel_cols,
    proj_weight,
    proj_bias,
    norm2_gain,
    norm2_shift,
    fc1_weight,
    fc1_bias,
    fc2_weight,
    fc2_bias,
    out_cotangent,
):
    place = lax.axis_index("mp")
    core = lax.axis_index("dp") % 2
    swap = lambda value: lax.ppermute(value, "mp", [(0, 1), (1, 0)])
    size = lax.axis_size("dp")
    core_swap = lambda value: lax.ppermute(value, "dp", [(i, i ^ 1) for i in range(size)])

    def by_core(weight, axis, mine):
        return lax.dynamic_slice_in_dim(weight, (core if mine else 1 - core) * HALF, HALF, axis)

    spot = jnp.stack([place, core]).astype(jnp.int32)
    spread = jnp.asarray(spread_rows(), BF)
    gather = jnp.asarray(spread_rows().T, BF)
    fold = jnp.asarray(fold_table(), BF)
    high_hot, wide_hot = rel_onehots()
    hots = jnp.asarray(np.pad(np.concatenate([high_hot, wide_hot], axis=1), ((0, 0), (0, 2))), F32)
    high_hot, wide_hot = jnp.asarray(high_hot, BF), jnp.asarray(wide_hot, BF)
    qkv_mine = swap(by_core(qkv_weight, 1, True))
    bias_other = swap(qv_bias)
    fc1_bias_other = swap(fc1_bias)
    x_windows = windows_of(spot, image_tokens, norm1_gain, norm1_shift, spread)
    cot_t = turned_of(out_cotangent)
    x_windows, cot_t, qkv_mine = lax.optimization_barrier((x_windows, cot_t, qkv_mine))
    late = (by_core(fc1_weight, 0, True), by_core(fc2_weight, 1, True), proj_weight)
    x_windows, qkv_mine, late = lax.optimization_barrier((x_windows, qkv_mine, late))
    qkv_theirs = exchange(qkv_mine, CORE)
    one_mine, two_mine, proj_other = (swap(w) for w in late)
    qkv_a, p_a, ctx_a, xt, rel_even, rel_odd = attend(
        x_windows, qv_bias, True, qkv_weight, high_hot, wide_hot, rel_rows, rel_cols
    )
    qkv_b, p_b, ctx_b = attend(
        x_windows, bias_other, False, spot, qkv_mine, qkv_theirs, rel_even, rel_odd
    )
    ctx_b, one_mine, two_mine, proj_other = lax.optimization_barrier((ctx_b, one_mine, two_mine, proj_other))
    one_theirs, two_theirs = exchange(one_mine, CORE), exchange(two_mine, CORE)
    middle, normed, normed_t, context = middle_of(
        spot, ctx_a, ctx_b, image_tokens, proj_weight, proj_other, proj_bias, norm2_gain, norm2_shift, gather
    )
    forward, back, one_kept, one_sent, two_kept, two_sent, fc1_sums = feed(
        spot, normed, normed_t, out_cotangent, cot_t, fc1_weight, (one_mine, one_theirs), fc1_bias,
        fc1_bias_other, fc2_weight, (two_mine, two_theirs),
    )
    bits = [2**k for k in range(1, bits_of(size))]
    turned = bits[1:2] + bits[0:1] + bits[2:]
    halves = lambda order: [("halve", bit) for bit in order]
    doubles = lambda order: [("double", bit) for bit in order]

    def cut(value, axis, places):
        shape = value.shape[:axis] + (2,) * len(places) + (value.shape[axis] // 2 ** len(places),)
        return value.reshape(shape + value.shape[axis + 1 :])

    def feed_line(kept, sent, order, back):
        steps = [("give", CORE)] + halves(order) + doubles(back) + [("double", CORE)]
        rank = [CORE] + bits
        return Line(cut(kept, 1, bits), [PAIRED] + bits, rank, steps, cut(sent, 1, bits))

    one_line = feed_line(one_kept, one_sent, [PAIRED] + bits, bits[::-1])
    two_line = feed_line(two_kept, two_sent, bits[:2] + [PAIRED] + bits[2:], turned[::-1])
    feed_lines = [one_line, two_line]

    middle = advance(middle, feed_lines)
    block_out, middle_grad, ctx_grad, proj_own, proj_oth, two_sums = resid_of(
        middle, forward, back, out_cotangent, context, proj_weight, proj_other, fc2_bias, norm2_gain
    )
    back_of = lambda qkv, p, side, grad, bands, *d: attend_back(
        spot, qkv, p, grad, side, spread, rel_even, rel_odd, fold, bands, *d
    )
    ctx_grad = advance(ctx_grad, feed_lines)
    d_b, rel_b, sums_b = back_of(qkv_b, p_b, 1, ctx_grad, (1, 3))
    d_b = advance(d_b, feed_lines)
    d_b, rel_b0, sums_b0 = back_of(qkv_b, p_b, 1, ctx_grad, (0, 1), d_b)
    d_b = advance(d_b, feed_lines)
    kept_b, sent_b = qkv_grad(spot, xt, d_b, proj_oth)
    line_b = Line(kept_b, [], [], [("give", CORE), ("pass", PAIRED)], sent_b)
    lines = feed_lines + [line_b]
    ctx_grad, kept_b = lax.optimization_barrier((ctx_grad, kept_b))
    ctx_grad = advance(ctx_grad, lines)
    d_a, rel_a, sums_a = back_of(qkv_a, p_a, 0, ctx_grad, (1, 3))
    d_a = advance(d_a, lines)
    up = norm_grad(d_a, d_b, qkv_weight, spot, qkv_mine, qkv_theirs, gather, (1, 3))
    at = [2 - place, (1 - place) * 4 * SIDE, jnp.zeros_like(place)]
    sent = lax.dynamic_slice(up, at, (1, 10 * SIDE, D)).reshape(10 * SIDE, D)
    shared_line = Line(sent, [], [], [("pass", PAIRED)])
    d_a = advance(d_a, [shared_line])
    d_a, rel_a0, sums_a0 = back_of(qkv_a, p_a, 0, ctx_grad, (0, 1), d_a)
    d_a = advance(d_a, feed_lines + [line_b])
    kept_a, sent_a = qkv_grad(spot, xt, d_a, proj_own)
    line_a = Line(kept_a, [], [], [("give", CORE)], sent_a)
    kept_a, d_a = lax.optimization_barrier((kept_a, d_a))
    d_a = advance(d_a, feed_lines + [line_a, shared_line])
    up = norm_grad(d_a, d_b, qkv_weight, spot, qkv_mine, qkv_theirs, gather, (0, 1), up)
    up = advance(up, feed_lines + [line_a])
    taken = shared_line.terms[0][0]
    q_lines = []
    for k, order in enumerate((bits, turned)):
        line = Line(None, [], [], halves(order[:1]))
        parts = [term for term, _ in line_a.terms] + [term for term, _ in line_b.terms]
        line.terms = [(part.reshape(2, 2, D // 2, HALF), ("line", order[0])) for part in parts]
        line.fixed = {"line": k}
        q_lines.append(line)
    up = advance(up, q_lines)
    finish(feed_lines)
    flat = lambda line, rows: (line.value.reshape(rows, -1), line.taken_last.reshape(rows, -1))
    input_grad, one_sums, one_sum, two_sum = input_of(
        spot, image_tokens, middle_grad, up, taken, norm1_gain, flat(one_line, HALF), flat(two_line, FF // 2)
    )
    one_sums = advance(one_sums, q_lines)
    four, small, rel = last_sums(
        bits,
        [bits, turned],
        [line.part({}) for line in q_lines],
        [one_sums, two_sums, fc1_sums, sums_a, sums_a0, sums_b, sums_b0],
        [rel_a, rel_a0, rel_b, rel_b0],
        hots,
    )
    one_sum = one_sum.reshape(D, FF // 2)
    mine = jnp.where(place == 0, small[6:9], small[9:12])
    return (
        block_out,
        input_grad,
        small[0],
        small[1],
        four[0:3].astype(F32),
        mine[0].reshape(2, HALF),
        rel[:RELS, :HD],
        rel[RELS : 2 * RELS, :HD],
        jnp.concatenate([four[3, :HALF], four[3, HALF:]], axis=1).astype(F32),
        small[5],
        small[2],
        small[3],
        one_sum,
        mine[1:3].reshape(-1),
        two_sum,
        small[4],
    )


def solution(mesh):
    in_specs = (
        P("dp", None),
        P(),
        P(),
        P(None, None, "mp"),
        P(None, "mp"),
        P(),
        P(),
        P("mp", None),
        P(),
        P(),
        P(),
        P(None, "mp"),
        P("mp"),
        P("mp", None),
        P(),
        P(("dp", "mp"), None),
    )
    out_specs = (
        P(("dp", "mp"), None),
        P(("dp", "mp"), None),
        P(),
        P(),
        P(None, None, "mp"),
        P(None, "mp"),
        P(),
        P(),
        P("mp", None),
        P(),
        P(),
        P(),
        P(None, "mp"),
        P("mp"),
        P("mp", None),
        P(),
    )
    return jax.shard_map(
        on_device, mesh=mesh, in_specs=in_specs, out_specs=out_specs, check_vma=False
    )
```

```python
import jax
import jax.numpy as jnp
import numpy as np
from jax import lax
from jax.experimental import pallas as pl
from jax.experimental.pallas import tpu as pltpu
from jax.sharding import PartitionSpec as P

D = 768
HEADS = 12
HD = 64
FF = 3072
WIN = 14
SIDE = 64
NWIN = 5
RELS = 27
EPSILON = 1e-06
F32 = jnp.float32
BF = jnp.bfloat16

SLOTS = 256
KEYS = WIN * 16
PAIR = 2 * SIDE
GREL = 80
OWN = SIDE * SIDE // 2

HALF = D // 2
TRIO = 3 * HALF
PAIRS = HEADS // 4

NN = (((1,), (0,)), ((), ()))
NT = (((1,), (1,)), ((), ()))
TN = (((0,), (0,)), ((), ()))


def dot(left, right, dims=NN):
    return lax.dot_general(left, right, dims, preferred_element_type=F32)


def params(limit=60):
    return pltpu.CompilerParams(vmem_limit_bytes=limit * 2**20)


def cost(flops, moved, exps=0):
    return pl.CostEstimate(flops=int(flops), bytes_accessed=int(moved), transcendentals=int(exps))


def whole(shape):
    return pl.BlockSpec(shape, lambda *_: (0,) * len(shape), pipeline_mode=pl.Buffered(1))


def band_start(place, band):
    return (1 - place) * (14 * band) + place * (42 - 14 * band + 21 * band * (band - 1))


def image_pair(place, band, step):
    pair = band_start(place, band) // 2 + step
    return jnp.minimum(pair, SIDE // 2 - 1), pair < SIDE // 2


def owned_pair(place, band, step):
    pair = band_start(place, band) // 2 + step - 16 * place
    return jnp.clip(pair, 0, 15), (pair >= 0) & (pair < 16)


def band_step(place, pair):
    first = pair // 7, pair % 7
    band = jnp.where(pair < 5, 1, jnp.where(pair < 12, 0, 2))
    second = band, jnp.where(pair < 5, pair + 2, jnp.where(pair < 12, pair - 5, pair - 12))
    return tuple(jnp.where(place == 0, a, b) for a, b in zip(first, second))


def taken_pair(place, pair):
    return (
        jnp.where(place == 0, jnp.maximum(pair - 14, 0), jnp.minimum(pair, 4)),
        jnp.where(place == 0, pair >= 14, pair < 5),
    )


def spread_rows():
    table = np.zeros((NWIN, 2, 16, PAIR), np.float32)
    for w in range(NWIN):
        for r in range(2):
            for j in range(WIN):
                if WIN * w + j < SIDE:
                    table[w, r, j, r * SIDE + WIN * w + j] = 1
    return table.reshape(NWIN * 32, PAIR)


def rel_order():
    rows = np.full(GREL, -1)
    for m in range(21):
        rows[m] = 26 - (m + 6)
        rows[24 + m] = 26 - m
    cols = np.full(GREL, -1)
    for m in range(RELS):
        cols[48 + m] = 26 - m
    return rows, cols


def rel_onehots():
    rows, cols = rel_order()
    high = (rows[:, None] == np.arange(RELS)[None, :]).astype(np.float32)
    wide = (cols[:, None] == np.arange(RELS)[None, :]).astype(np.float32)
    return high, wide


def norm_parts(values):
    average = jnp.mean(values, axis=-1, keepdims=True)
    centred = values - average
    inverse = lax.rsqrt(jnp.mean(centred * centred, axis=-1, keepdims=True) + EPSILON)
    return centred * inverse, inverse


def vec(ref):
    return ref[...].astype(F32).reshape(1, D)


def window_kernel(spot, *refs):
    xs, (gain, shift, spread, out) = refs[:7], refs[7:]
    band = pl.program_id(0)
    for t in range(7):
        scaled, _ = norm_parts(xs[t][...].astype(F32))
        normed = scaled * vec(gain) + vec(shift)
        valid = image_pair(spot[0], band, t)[1]
        normed = (normed * valid.astype(F32)).astype(BF)
        moved = dot(spread[...], normed).astype(BF)
        out[:, :, 32 * t : 32 * t + 32, :] = moved.reshape(1, NWIN, 32, D)
    out[:, :, 224:, :] = jnp.zeros((1, NWIN, 32, D), BF)


def windows_of(spot, x, gain, shift, spread):
    at = lambda t: lambda s, spot: (image_pair(spot[0], s, t)[0], 0)
    return pl.pallas_call(
        window_kernel,
        grid_spec=pltpu.PrefetchScalarGridSpec(
            num_scalar_prefetch=1,
            grid=(3,),
            in_specs=[pl.BlockSpec((PAIR, D), at(t)) for t in range(7)]
            + [whole((D,)), whole((D,)), whole((NWIN * 32, PAIR))],
            out_specs=pl.BlockSpec((1, NWIN, SLOTS, D), lambda s, *_: (s, 0, 0, 0)),
        ),
        out_shape=jax.ShapeDtypeStruct((3, NWIN, SLOTS, D), BF),
        compiler_params=params(),
        cost_estimate=cost(3 * 7 * 160 * 128 * 768 * 2, 10e6),
    )(spot, *([x] * 7), gain, shift, spread)


def shift_masks(lanes_from):
    lane = lax.broadcasted_iota(jnp.int32, (1, 128), 1) + lanes_from
    high = lane // 16
    row_shift = jnp.where(lane < 128, 7 - high, jnp.maximum(13 - high, 0))
    col_shift = jnp.maximum(13 - lane % 16, 0)
    return row_shift, col_shift


def skew(table, shift, bits):
    size = table.shape[0]
    for bit in bits:
        moved = pltpu.roll(table, size - bit, 0)
        table = jnp.where((shift & bit) != 0, moved, table)
    return table


def unskew(table, shift, bits):
    for bit in bits:
        moved = pltpu.roll(table, bit, 0)
        table = jnp.where((shift & bit) != 0, moved, table)
    return table


def start_own(weights, bias, high_hot, wide_hot, rel_rows, rel_cols, rel_even, rel_odd, joined):
    for s in range(3):
        joined[:, s * HALF : s * HALF + HALF] = weights[s]
    table = (dot(high_hot[...], rel_rows[...]) + dot(wide_hot[...], rel_cols[...])).astype(BF)
    blank = jnp.zeros_like(table)
    rel_even[...] = jnp.concatenate([table, blank], axis=1)
    rel_odd[...] = jnp.concatenate([blank, table], axis=1)


def join_pieces(core, mine, theirs, joined, col):
    for piece, at in ((mine, core), (theirs, 1 - core)):
        rows = pl.ds(pl.multiple_of(at * HALF, HALF), HALF)
        for s in range(3):
            joined[rows, col + s * HALF : col + s * HALF + HALF] = piece[s]


def attend_own(
    x, bias, weights, high_hot, wide_hot, rel_rows, rel_cols,
    qkv_out, p_out, ctx_out, xt_out, rel_even, rel_odd, joined, vt,
):
    @pl.when((pl.program_id(0) == 0) & (pl.program_id(1) == 0))
    def _():
        start_own(weights, bias, high_hot, wide_hot, rel_rows, rel_cols, rel_even, rel_odd, joined)

    attend_window(x, bias, rel_even, rel_odd, qkv_out, p_out, ctx_out, xt_out, joined, vt)


def attend_other(x, bias, spot, mine, theirs, rel_even, rel_odd, qkv_out, p_out, ctx_out, joined, vt):
    @pl.when((pl.program_id(0) == 0) & (pl.program_id(1) == 0))
    def _():
        join_pieces(spot[1], mine, theirs, joined, 0)

    attend_window(x, bias, rel_even, rel_odd, qkv_out, p_out, ctx_out, None, joined, vt)


def attend_window(x, bias, rel_even, rel_odd, qkv_out, p_out, ctx_out, xt_out, joined, vt):
    band = pl.program_id(0)
    biases = bias[...].astype(F32)
    biases = jnp.concatenate([biases[0:1], jnp.zeros((1, HALF), F32), biases[1:2]], axis=1)
    block = x[...].reshape(SLOTS, D)
    if xt_out is not None:
        xt_out[...] = block.T
    scales = jnp.where(lax.broadcasted_iota(jnp.int32, (1, TRIO), 1) // HALF == 1, HD ** (-0.5), 1.0)
    low = ((dot(block, joined[...]) + biases) * scales).astype(BF)
    qkv_out[0, 0] = low
    vt[...] = low[:, 2 * HALF :].T

    even = lax.broadcasted_iota(jnp.int32, (1, 128), 1) < HD

    def raw_scores(head, lanes):
        col = head // 2 * 128
        keys = qkv_out[0, 0, 0:KEYS, HALF + col : HALF + col + 128]
        kept = jnp.where(even != (head % 2 == 1), keys, jnp.zeros_like(keys))
        rel = rel_odd if head % 2 else rel_even
        left = jnp.concatenate([kept, rel[...]], axis=0)
        return dot(left, qkv_out[0, 0, 0:lanes, col : col + 128], NT)

    def soft(head, raw, lanes):
        parts = []
        for tile in range(lanes // 128):
            row_shift, col_shift = shift_masks(tile * 128)
            raw_t = raw[:, tile * 128 : tile * 128 + 128]
            base = raw_t[0:KEYS]
            high = skew(raw_t[KEYS + 24 * tile : KEYS + 24 * tile + 24], row_shift, (4, 2, 1))[0:16]
            wide = skew(raw_t[KEYS + 48 : KEYS + 80], col_shift, (8, 4, 2, 1))[0:16]
            place = lax.broadcasted_iota(jnp.int32, (16, 128), 0)
            wide = jnp.where(place < WIN, wide, -1e30)
            scores = base.reshape(WIN, 16, 128) + wide[None] + high[0:WIN][:, None, :]
            scores = scores.reshape(KEYS, 128)
            peak = jnp.max(scores, axis=0, keepdims=True)
            grown = jnp.exp(scores - peak)
            total = jnp.sum(grown, axis=0, keepdims=True)
            parts.append((grown * (1.0 / total)).astype(BF))
        probs = parts[0] if len(parts) == 1 else jnp.concatenate(parts, axis=1)
        p_out[0, 0, head, :, 0:lanes] = probs
        return probs

    def all_heads(lanes):
        count = HEADS // 2
        raw = raw_scores(0, lanes)
        contexts = []
        for head in range(count):
            ahead = raw_scores(head + 1, lanes) if head + 1 < count else None
            probs = soft(head, raw, lanes)
            if head:
                contexts.append(dot(vt[(head - 1) * HD : head * HD, 0:KEYS], before).astype(BF))
            if head and head % 2 == 0:
                col = (head - 2) * HD
                ctx_out[0, 0, 0:lanes, col : col + 128] = jnp.concatenate(contexts[-2:], axis=0).T
            before, raw = probs, ahead
        contexts.append(dot(vt[(count - 1) * HD :, 0:KEYS], before).astype(BF))
        ctx_out[0, 0, 0:lanes, HALF - 128 :] = jnp.concatenate(contexts[-2:], axis=0).T

    @pl.when(band < 2)
    def _():
        all_heads(256)

    @pl.when(band == 2)
    def _():
        all_heads(128)


SCALAR = pl.BlockSpec(memory_space=pltpu.SMEM)


def attend(x, bias, first, *operands):
    block = lambda width: pl.BlockSpec((1, 1, SLOTS, width), lambda s, w: (s, w, 0, 0))
    shape = lambda width: jax.ShapeDtypeStruct((3, NWIN, SLOTS, width), BF)
    out_specs = [
        block(TRIO),
        pl.BlockSpec((1, 1, HEADS // 2, KEYS, SLOTS), lambda s, w: (s, w, 0, 0, 0)),
        block(HALF),
    ]
    out_shape = [
        shape(TRIO),
        jax.ShapeDtypeStruct((3, NWIN, HEADS // 2, KEYS, SLOTS), BF),
        shape(HALF),
    ]
    rel = pl.BlockSpec((GREL, 128), lambda s, w: (0, 0))
    if first:
        in_specs = [whole((3, D, HALF)), whole((GREL, RELS)), whole((GREL, RELS)), whole((RELS, HD)), whole((RELS, HD))]
        out_specs += [pl.BlockSpec((D, SLOTS), lambda s, w: (0, s * NWIN + w)), rel, rel]
        out_shape += [jax.ShapeDtypeStruct((D, 3 * NWIN * SLOTS), BF)] + [jax.ShapeDtypeStruct((GREL, 128), BF)] * 2
    else:
        in_specs = [SCALAR, whole((3, HALF, HALF)), whole((3, HALF, HALF)), whole((GREL, 128)), whole((GREL, 128))]
    return pl.pallas_call(
        attend_own if first else attend_other,
        grid=(3, NWIN),
        in_specs=[block(D), whole((2, HALF))] + in_specs,
        out_specs=out_specs,
        out_shape=out_shape,
        scratch_shapes=[pltpu.VMEM((D, TRIO), BF), pltpu.VMEM((HALF, SLOTS), BF)],
        compiler_params=params(),
        cost_estimate=cost(15e9, 45e6, 4e6),
    )(x, bias, *operands)


def middle_kernel(
    spot, own_a, own_b, other_a, other_b, x, proj_own, proj_other, bias, gain, shift, gather,
    middle, normed, normed_t, ctx_out, proj,
):
    @pl.when(pl.program_id(0) == 0)
    def _():
        proj[0:HALF, :] = proj_own[...]
        proj[HALF:, :] = proj_other[...]

    for row, parts in ((0, (own_a, other_a)), (PAIR, (own_b, other_b))):
        for side in range(2):
            moved = dot(gather[...], parts[side][...].reshape(NWIN * 32, HALF)).astype(BF)
            ctx_out[row : row + PAIR, side * HALF : side * HALF + HALF] = moved
    value = x[...].astype(F32) + (dot(ctx_out[...], proj[...]) + vec(bias))
    middle[...] = value.astype(BF)
    scaled, _ = norm_parts(value)
    low = (scaled * vec(gain) + vec(shift)).astype(BF)
    normed[...] = low
    normed_t[...] = low.T


def middle_of(spot, ctx_own, ctx_other, x, proj_own, proj_other, bias, gain, shift, gather):
    rows = 2 * PAIR

    def at(k):
        def place(i, spot):
            band, step = band_step(spot[0], 2 * i + k)
            return band, 0, step, 0

        return pl.BlockSpec((1, NWIN, 32, HALF), place)

    row_block = pl.BlockSpec((rows, D), lambda i, *_: (i, 0))
    col_block = pl.BlockSpec((D, rows), lambda i, *_: (0, i))
    low = jax.ShapeDtypeStruct((OWN, D), BF)
    return pl.pallas_call(
        middle_kernel,
        grid_spec=pltpu.PrefetchScalarGridSpec(
            num_scalar_prefetch=1,
            grid=(OWN // rows,),
            in_specs=[
                at(0),
                at(1),
                at(0),
                at(1),
                pl.BlockSpec((rows, D), lambda i, spot: (spot[0] * (OWN // rows) + i, 0)),
                whole((HALF, D)),
                whole((HALF, D)),
                whole((D,)),
                whole((D,)),
                whole((D,)),
                whole((PAIR, NWIN * 32)),
            ],
            out_specs=[row_block, row_block, col_block, row_block],
            scratch_shapes=[pltpu.VMEM((D, D), BF)],
        ),
        out_shape=[low, low, jax.ShapeDtypeStruct((D, OWN), BF), low],
        compiler_params=params(),
        cost_estimate=cost(3e9, 25e6),
    )(spot, ctx_own, ctx_own, ctx_other, ctx_other, x, proj_own, proj_other, bias, gain, shift, gather)


def turn_kernel(value, out):
    out[...] = value[...].T


def turned_of(value):
    rows = 512
    return pl.pallas_call(
        turn_kernel,
        grid=(OWN // rows,),
        in_specs=[pl.BlockSpec((rows, D), lambda i: (i, 0))],
        out_specs=pl.BlockSpec((D, rows), lambda i: (0, i)),
        out_shape=jax.ShapeDtypeStruct((D, OWN), BF),
        compiler_params=params(),
        cost_estimate=cost(1e6, 6e6),
    )(value)


CHUNK = 512
CHUNKS = FF // CHUNK


def feed_kernel(
    spot, normed, normed_t, cot, cot_t, one_a, one_b, one_c, bias_a, bias_b, two_a, two_b, two_c,
    forward_out, back_out, one_kept, one_sent, two_kept, two_sent, sums,
    forward, back, one, two, bias, hidden, grads,
):
    step = pl.program_id(0)

    @pl.when(step == 0)
    def _():
        forward[...] = jnp.zeros_like(forward)
        back[...] = jnp.zeros_like(back)

    @pl.when(step < CHUNKS // 2)
    def _():
        bias[...] = bias_a[...].astype(F32).reshape(1, CHUNK)
        one[...] = one_a[...]
        two[...] = two_a[...]

    @pl.when(step >= CHUNKS // 2)
    def _():
        bias[...] = bias_b[...].astype(F32).reshape(1, CHUNK)
        mine = pl.multiple_of(spot[1] * HALF, HALF)
        theirs = pl.multiple_of((1 - spot[1]) * HALF, HALF)
        one[pl.ds(mine, HALF), :] = one_b[...]
        one[pl.ds(theirs, HALF), :] = one_c[...]
        two[:, pl.ds(mine, HALF)] = two_b[...]
        two[:, pl.ds(theirs, HALF)] = two_c[...]

    total = jnp.zeros((1, CHUNK), F32)
    for t in range(OWN // 256):
        rows = slice(t * 256, t * 256 + 256)
        pre = dot(normed[rows, :], one[...]) + bias[...]
        phi = 0.5 * (1.0 + lax.erf(pre * 0.7071067811865476))
        slope = phi + pre * (jnp.exp(-0.5 * pre * pre) * 0.3989422804014327)
        low = (pre * phi).astype(BF)
        grad = (dot(cot[rows, :], two[...], NT) * slope).astype(BF)
        hidden[rows, :] = low
        grads[rows, :] = grad
        total += jnp.sum(grad.astype(F32), axis=0, keepdims=True)
        forward[rows, :] += dot(low, two[...])
        back[rows, :] += dot(grad, one[...], NT)
    sums[...] = total

    first = spot[1] == 0
    one_grad = dot(normed_t[...], grads[...]).astype(BF)
    low, high = one_grad[:HALF], one_grad[HALF:]
    one_kept[0] = jnp.where(first, low, high)
    one_sent[0] = jnp.where(first, high, low)
    two_grad = dot(cot_t[...], hidden[...]).astype(BF)
    low, high = two_grad[:HALF], two_grad[HALF:]
    two_kept[0] = jnp.where(first, low, high).T
    two_sent[0] = jnp.where(first, high, low).T

    @pl.when(step == pl.num_programs(0) - 1)
    def _():
        forward_out[...] = forward[...].astype(BF)
        back_out[...] = back[...].astype(BF)


def feed(spot, normed, normed_t, cot, cot_t, one_a, ones, bias_a, bias_b, two_a, twos):
    half = CHUNKS // 2
    own = lambda j: jnp.minimum(j, half - 1)
    other = lambda j: jnp.maximum(j - half, 0)
    one_block = pl.BlockSpec((1, HALF, CHUNK), lambda j, *_: (j // half, 0, j % half))
    two_block = pl.BlockSpec((1, CHUNK, HALF), lambda j, *_: (j // half, j % half, 0))
    one_piece = pl.BlockSpec((HALF, CHUNK), lambda j, *_: (0, other(j)))
    two_piece = pl.BlockSpec((CHUNK, HALF), lambda j, *_: (other(j), 0))
    one_shape = jax.ShapeDtypeStruct((2, HALF, FF // 2), BF)
    two_shape = jax.ShapeDtypeStruct((2, FF // 2, HALF), BF)
    sum_block = pl.BlockSpec((OWN, D), lambda j, *_: (0, 0))
    bias_block = pl.BlockSpec((1, CHUNK), lambda j, *_: (0, j))
    return pl.pallas_call(
        feed_kernel,
        grid_spec=pltpu.PrefetchScalarGridSpec(
            num_scalar_prefetch=1,
            grid=(CHUNKS,),
            in_specs=[
                whole((OWN, D)),
                whole((D, OWN)),
                whole((OWN, D)),
                whole((D, OWN)),
                pl.BlockSpec((D, CHUNK), lambda j, *_: (0, own(j))),
                one_piece,
                one_piece,
                pl.BlockSpec((CHUNK,), lambda j, *_: (own(j),)),
                pl.BlockSpec((CHUNK,), lambda j, *_: (other(j),)),
                pl.BlockSpec((CHUNK, D), lambda j, *_: (own(j), 0)),
                two_piece,
                two_piece,
            ],
            out_specs=[sum_block, sum_block, one_block, one_block, two_block, two_block, bias_block],
            scratch_shapes=[
                pltpu.VMEM((OWN, D), F32),
                pltpu.VMEM((OWN, D), F32),
                pltpu.VMEM((D, CHUNK), BF),
                pltpu.VMEM((CHUNK, D), BF),
                pltpu.VMEM((1, CHUNK), F32),
                pltpu.VMEM((OWN, CHUNK), BF),
                pltpu.VMEM((OWN, CHUNK), BF),
            ],
        ),
        out_shape=[
            jax.ShapeDtypeStruct((OWN, D), BF),
            jax.ShapeDtypeStruct((OWN, D), BF),
            one_shape,
            one_shape,
            two_shape,
            two_shape,
            jax.ShapeDtypeStruct((1, FF), F32),
        ],
        compiler_params=params(62),
        cost_estimate=cost(58e9, 60e6, 12e6),
    )(spot, normed, normed_t, cot, cot_t, one_a, *ones, bias_a, bias_b, two_a, *twos)


def add_row(sums, row, values):
    sums[row : row + 1, :] += jnp.sum(values, axis=0, keepdims=True)


def resid_kernel(
    middle, forward, back, cot, context, proj_own, proj_other, bias, gain,
    block_out, grad_out, ctx_grad, grad_own, grad_other, sums, proj, proj_grad,
):
    step = pl.program_id(0)

    @pl.when(step == 0)
    def _():
        proj[0:HALF, :] = proj_own[...]
        proj[HALF:, :] = proj_other[...]
        proj_grad[...] = jnp.zeros_like(proj_grad)
        sums[...] = jnp.zeros_like(sums)

    value = middle[...].astype(F32)
    block_out[...] = (value + (forward[...].astype(F32) + vec(bias))).astype(BF)
    scaled, inverse = norm_parts(value)
    upstream = back[...].astype(F32)
    scaled_up = upstream * vec(gain)
    first = jnp.mean(scaled_up, axis=-1, keepdims=True)
    second = jnp.mean(scaled_up * scaled, axis=-1, keepdims=True)
    cotangent = cot[...].astype(F32)
    grad = cotangent + inverse * (scaled_up - first - scaled * second)
    low = grad.astype(BF)
    grad_out[...] = low
    ctx_grad[...] = dot(low, proj[...], NT).astype(BF)
    proj_grad[...] += dot(context[...], low, TN)
    add_row(sums, 0, upstream * scaled)
    add_row(sums, 1, upstream)
    add_row(sums, 2, cotangent)
    add_row(sums, 3, low.astype(F32))

    @pl.when(step == pl.num_programs(0) - 1)
    def _():
        for out, row in ((grad_own, 0), (grad_other, HALF)):
            for col in (0, HALF):
                out[col : col + HALF, :] = proj_grad[row : row + HALF, col : col + HALF].astype(BF)


def resid_of(middle, forward, back, cot, context, proj_own, proj_other, bias, gain):
    rows = 512
    row_block = pl.BlockSpec((rows, D), lambda i: (i, 0))
    half_block = pl.BlockSpec((D, HALF), lambda i: (0, 0))
    return pl.pallas_call(
        resid_kernel,
        grid=(OWN // rows,),
        in_specs=[row_block] * 5 + [whole((HALF, D)), whole((HALF, D)), whole((D,)), whole((D,))],
        out_specs=[
            row_block,
            row_block,
            row_block,
            half_block,
            half_block,
            pl.BlockSpec((8, D), lambda i: (0, 0)),
        ],
        out_shape=[
            jax.ShapeDtypeStruct((OWN, D), BF),
            jax.ShapeDtypeStruct((OWN, D), BF),
            jax.ShapeDtypeStruct((OWN, D), BF),
            jax.ShapeDtypeStruct((D, HALF), BF),
            jax.ShapeDtypeStruct((D, HALF), BF),
            jax.ShapeDtypeStruct((8, D), F32),
        ],
        scratch_shapes=[pltpu.VMEM((D, D), BF), pltpu.VMEM((D, D), F32)],
        compiler_params=params(),
        cost_estimate=cost(5e9, 40e6),
    )(middle, forward, back, cot, context, proj_own, proj_other, bias, gain)


def attend_back_kernel(first, spot, qkv, p, ctx_grad, spread, rel_even, rel_odd, fold, *refs):
    d_out, rel_grad, sums, upstream, kt = refs[-5:]
    band = pl.program_id(0) + first
    window = pl.program_id(1)

    @pl.when((band == first) & (window == 0))
    def _():
        rel_grad[...] = jnp.zeros_like(rel_grad)
        sums[...] = jnp.zeros_like(sums)

    @pl.when(window == 0)
    def _():
        for t in range(7):
            at, owned = owned_pair(spot[0], band, t)
            rows = pl.ds(pl.multiple_of(at * PAIR, PAIR), PAIR)
            moved = dot(spread[...], ctx_grad[rows, :])
            moved = moved * owned.astype(F32)
            upstream[:, 32 * t : 32 * t + 32, :] = moved.astype(BF).reshape(NWIN, 32, HALF)
        upstream[:, 224:256, :] = jnp.zeros((NWIN, 32, HALF), BF)

    kt[...] = qkv[0, 0, :, HALF : 2 * HALF].T
    even = lax.broadcasted_iota(jnp.int32, (1, 128), 1) < HD

    def shifted(head, by):
        return slice(by * HALF + head // 2 * 128, by * HALF + head // 2 * 128 + 128)

    def prob_grads(head, lanes):
        values = qkv[0, 0, 0:KEYS, shifted(head, 2)]
        kept = jnp.where(even != (head % 2 == 1), values, jnp.zeros_like(values))
        return dot(kept, upstream[window, 0:lanes, shifted(head, 0)], NT)

    def rel_table(both, lanes):
        tables = []
        zero8 = jnp.zeros((8, 128), F32)
        zero24 = jnp.zeros((24, 128), F32)
        zero16 = jnp.zeros((16, 128), F32)
        for tile in range(lanes // 128):
            row_shift, col_shift = shift_masks(tile * 128)
            part = both[:, tile * 128 : tile * 128 + 128]
            high = jnp.concatenate([part[HD : HD + 16], zero8], axis=0)
            wide = jnp.concatenate([part[HD + 16 : HD + 32], zero16], axis=0)
            high = unskew(high, row_shift, (1, 2, 4))
            wide = unskew(wide, col_shift, (1, 2, 4, 8))
            stack = [high, zero24, wide] if tile == 0 else [zero24, high, wide]
            tables.append(jnp.concatenate(stack, axis=0))
        table = tables[0] if len(tables) == 1 else jnp.concatenate(tables, axis=1)
        return table.astype(BF)

    def all_heads(lanes):
        count = HEADS // 2
        dvs, dks, dqs, drs = [], [], [], []

        def last_part(head, score_grad, both):
            rel = rel_odd if head % 2 else rel_even
            table = rel_table(both, lanes)
            queries = qkv[0, 0, 0:lanes, shifted(head, 0)]
            grads = dot(jnp.concatenate([score_grad, table], axis=0), queries)
            dks.append(grads[0:KEYS])
            drs.append(grads[KEYS:])
            from_rel = dot(rel[...], table, TN)
            side = head % 2 * HD
            dqs.append(both[0:HD] + from_rel[side : side + HD])
            if head % 2:
                d_out[0, 0, 0:lanes, shifted(head, 0)] = jnp.concatenate(dqs[-2:], axis=0).astype(BF).T
                d_out[0, 0, 0:KEYS, shifted(head, 1)] = (jnp.where(even, dks[-2], dks[-1]) * HD ** (-0.5)).astype(BF)

        prob_grad = prob_grads(0, lanes)
        before = None
        for head in range(count):
            ahead = prob_grads(head + 1, lanes) if head + 1 < count else None
            probs_low = p[0, 0, head, :, 0:lanes]
            probs = probs_low.astype(F32)
            total = jnp.sum(prob_grad * probs, axis=0, keepdims=True)
            score_grad = (probs * (prob_grad - total)).astype(BF)
            dvs.append(dot(probs_low, upstream[window, 0:lanes, shifted(head, 0)]))
            left = jnp.concatenate([kt[head * HD : head * HD + HD, 0:KEYS], fold[...]], axis=0)
            both = dot(left, score_grad)
            if head % 2:
                d_out[0, 0, 0:KEYS, shifted(head, 2)] = jnp.where(even, dvs[-2], dvs[-1]).astype(BF)
            if before is not None:
                last_part(head - 1, *before)
            before, prob_grad = (score_grad, both), ahead
        last_part(count - 1, *before)
        evens = drs[0] + drs[2] + drs[4]
        odds = drs[1] + drs[3] + drs[5]
        rel_grad[...] += jnp.where(even, evens, odds)

    d_out[0, 0, KEYS:, HALF:] = jnp.zeros((SLOTS - KEYS, 2 * HALF), BF)

    @pl.when(band < 2)
    def _():
        all_heads(256)

    @pl.when(band == 2)
    def _():
        all_heads(128)
        d_out[0, 0, 128:, 0:HALF] = jnp.zeros((128, HALF), BF)

    sums[0:1, :] += jnp.sum(d_out[...].reshape(SLOTS, TRIO).astype(F32), axis=0, keepdims=True)


def fold_table():
    table = np.zeros((32, WIN, 16), np.float32)
    for k in range(WIN):
        for l in range(WIN):
            table[k, k, l] = 1
            table[16 + l, k, l] = 1
    return table.reshape(32, KEYS)


def attend_back(spot, qkv, p, ctx_grad, side, spread, rel_even, rel_odd, fold, bands, *d_in):
    first, last = bands
    block = pl.BlockSpec((1, 1, SLOTS, TRIO), lambda s, w, *_: (s + first, w, 0, 0))
    share = (last - first) / 3
    return pl.pallas_call(
        lambda *refs: attend_back_kernel(first, *refs),
        grid_spec=pltpu.PrefetchScalarGridSpec(
            num_scalar_prefetch=1,
            grid=(last - first, NWIN),
            in_specs=[
                block,
                pl.BlockSpec((1, 1, HEADS // 2, KEYS, SLOTS), lambda s, w, *_: (s + first, w, 0, 0, 0)),
                pl.BlockSpec((OWN, HALF), lambda *_: (0, side), pipeline_mode=pl.Buffered(1)),
                whole((NWIN * 32, PAIR)),
                whole((GREL, 128)),
                whole((GREL, 128)),
                whole((32, KEYS)),
            ]
            + [pl.BlockSpec(memory_space=pl.ANY)] * len(d_in),
            out_specs=[
                block,
                pl.BlockSpec((GREL, 128), lambda s, w, *_: (0, 0)),
                pl.BlockSpec((8, TRIO), lambda s, w, *_: (0, 0)),
            ],
            scratch_shapes=[pltpu.VMEM((NWIN, SLOTS, HALF), BF), pltpu.VMEM((HALF, SLOTS), BF)],
        ),
        out_shape=[
            jax.ShapeDtypeStruct((3, NWIN, SLOTS, TRIO), BF),
            jax.ShapeDtypeStruct((GREL, 128), F32),
            jax.ShapeDtypeStruct((8, TRIO), F32),
        ],
        input_output_aliases={8: 0} if d_in else {},
        compiler_params=params(),
        cost_estimate=cost(20e9 * share, 45e6 * share),
    )(spot, qkv, p, ctx_grad, spread, rel_even, rel_odd, fold, *d_in)


def norm_grad_kernel(own, other, weights_own, spot, mine, theirs, gather, *refs):
    out, joined = refs[-2:]

    @pl.when((pl.program_id(0) == 0) & (pl.program_id(1) == 0))
    def _():
        for s in range(3):
            joined[:, s * HALF : s * HALF + HALF] = weights_own[s]
        join_pieces(spot[1], mine, theirs, joined, TRIO)

    rows = NWIN * 128
    left = jnp.concatenate([own[...].reshape(rows, TRIO), other[...].reshape(rows, TRIO)], axis=1)
    total = dot(left, joined[...], NT).astype(BF).reshape(NWIN, 4, 32, D)
    for t in range(4):
        moved = dot(gather[...], total[:, t].reshape(NWIN * 32, D)).astype(BF)
        out[:, t * PAIR : t * PAIR + PAIR, :] = moved.reshape(1, PAIR, D)


def norm_grad(own, other, weights_own, core, mine, theirs, gather, bands, *before):
    first, last = bands
    share = (last - first) / 3
    block = pl.BlockSpec((1, NWIN, 128, TRIO), lambda s, t: (s + first, 0, t, 0))
    return pl.pallas_call(
        norm_grad_kernel,
        grid=(last - first, 2),
        in_specs=[block, block, whole((3, D, HALF)), SCALAR]
        + [whole((3, HALF, HALF)), whole((3, HALF, HALF)), whole((PAIR, NWIN * 32))]
        + [pl.BlockSpec(memory_space=pl.ANY)] * len(before),
        out_specs=pl.BlockSpec((1, 4 * PAIR, D), lambda s, t: (s + first, t, 0)),
        out_shape=jax.ShapeDtypeStruct((3, 8 * PAIR, D), BF),
        input_output_aliases={7: 0} if before else {},
        scratch_shapes=[pltpu.VMEM((D, 2 * TRIO), BF)],
        compiler_params=params(),
        cost_estimate=cost(14e9 * share, 30e6 * share),
    )(own, other, weights_own, core, mine, theirs, gather, *before)


def qkv_grad_kernel(spot, xt, d, proj, kept, sent, total):
    step = pl.program_id(0)
    for col in range(0, TRIO, 256):
        cols = slice(col, min(col + 256, TRIO))
        part = dot(xt[...], d[:, cols])
        total[:, cols] = jnp.where(step == 0, part, total[:, cols] + part)

    @pl.when(step == pl.num_programs(0) - 1)
    def _():
        first = spot[1] == 0
        values = [total[:, s * HALF : s * HALF + HALF].astype(BF) for s in range(3)] + [proj[...]]
        for k in range(2):
            kept[k] = jnp.where(first, values[k], values[2 + k])
            sent[k] = jnp.where(first, values[2 + k], values[k])


def qkv_grad(core, xt, d, proj):
    rows = NWIN * SLOTS
    block = pl.BlockSpec((2, D, HALF), lambda i: (0, 0, 0))
    shape = jax.ShapeDtypeStruct((2, D, HALF), BF)
    return pl.pallas_call(
        qkv_grad_kernel,
        grid=(3,),
        in_specs=[
            SCALAR,
            pl.BlockSpec((D, rows), lambda i: (0, i)),
            pl.BlockSpec((rows, TRIO), lambda i: (i, 0)),
            whole((D, HALF)),
        ],
        out_specs=[block, block],
        out_shape=[shape, shape],
        scratch_shapes=[pltpu.VMEM((D, TRIO), F32)],
        compiler_params=params(),
        cost_estimate=cost(7e9, 16e6),
    )(core, xt, d.reshape(3 * rows, TRIO), proj)


def input_kernel(
    spot, x, middle_grad, up_a, up_b, taken_a, taken_b, gain,
    one_mine, one_theirs, two_mine, two_theirs, out, sums, one_out, two_out,
):
    step = pl.program_id(0)
    first = spot[1] == 0
    mine, theirs = one_mine[...].astype(F32), one_theirs[...].astype(F32)
    one_out[0] = jnp.where(first, mine, theirs)
    one_out[1] = jnp.where(first, theirs, mine)
    mine, theirs = two_mine[...].astype(F32), two_theirs[...].astype(F32)
    two_out[:, 0:HALF] = jnp.where(first, mine, theirs)
    two_out[:, HALF:] = jnp.where(first, theirs, mine)

    @pl.when(step == 0)
    def _():
        sums[...] = jnp.zeros_like(sums)

    for k, (up, taken) in enumerate(((up_a, taken_a), (up_b, taken_b))):
        rows = slice(k * PAIR, k * PAIR + PAIR)
        scaled, inverse = norm_parts(x[rows, :].astype(F32))
        shared = taken[...].astype(F32) * taken_pair(spot[0], 2 * step + k)[1].astype(F32)
        upstream = up[0].astype(F32) + shared
        scaled_up = upstream * vec(gain)
        mean = jnp.mean(scaled_up, axis=-1, keepdims=True)
        second = jnp.mean(scaled_up * scaled, axis=-1, keepdims=True)
        out[rows, :] = (middle_grad[rows, :].astype(F32) + inverse * (scaled_up - mean - scaled * second)).astype(BF)
        add_row(sums, 0, upstream * scaled)
        add_row(sums, 1, upstream)


def input_of(spot, x, middle_grad, up, taken, gain, ones, twos):
    rows = 2 * PAIR
    row_block = pl.BlockSpec((rows, D), lambda i, *_: (i, 0))
    up_at = lambda k: lambda i, spot: band_step(spot[0], 2 * i + k) + (0,)
    taken_at = lambda k: lambda i, spot: (taken_pair(spot[0], 2 * i + k)[0], 0)
    steps = OWN // rows
    one_rows, two_rows = HALF // steps, FF // 2 // steps
    return pl.pallas_call(
        input_kernel,
        grid_spec=pltpu.PrefetchScalarGridSpec(
            num_scalar_prefetch=1,
            grid=(steps,),
            in_specs=[
                pl.BlockSpec((rows, D), lambda i, spot: (spot[0] * steps + i, 0)),
                row_block,
                pl.BlockSpec((1, PAIR, D), up_at(0)),
                pl.BlockSpec((1, PAIR, D), up_at(1)),
                pl.BlockSpec((PAIR, D), taken_at(0)),
                pl.BlockSpec((PAIR, D), taken_at(1)),
                whole((D,)),
            ]
            + [pl.BlockSpec((one_rows, FF // 2), lambda i, *_: (i, 0))] * 2
            + [pl.BlockSpec((two_rows, HALF), lambda i, *_: (i, 0))] * 2,
            out_specs=[
                row_block,
                pl.BlockSpec((8, D), lambda i, *_: (0, 0)),
                pl.BlockSpec((2, one_rows, FF // 2), lambda i, *_: (0, i, 0)),
                pl.BlockSpec((two_rows, D), lambda i, *_: (i, 0)),
            ],
        ),
        out_shape=[
            jax.ShapeDtypeStruct((OWN, D), BF),
            jax.ShapeDtypeStruct((8, D), F32),
            jax.ShapeDtypeStruct((2, HALF, FF // 2), F32),
            jax.ShapeDtypeStruct((FF // 2, D), F32),
        ],
        compiler_params=params(),
        cost_estimate=cost(1e8, 35e6),
    )(spot, x, middle_grad, up, up, taken, taken, gain, *ones, *twos)


MESH = pl.DeviceIdType.MESH
SMALL = 24


def bits_of(size):
    return size.bit_length() - 1


def line_plan(order, rows):
    plan, doubles = [], [("double", order[0], rows)]
    for bit in order[1:]:
        if rows % 32 == 0:
            doubles.append(("double", bit, rows))
            rows //= 2
            plan.append(("halve", bit, rows))
        else:
            plan.append(("both", bit, rows))
    return plan + doubles[::-1]


PARTS = 2
PART_ROWS = D // 2 // PARTS


def last_kernel(bits, plans, orders, *refs):
    (line_a, line_b, one_sums, two_sums, fc1_sums, sums_a, sums_c, sums_b, sums_d) = refs[:9]
    rel_a, rel_b, rel_c, rel_d, hots, out, small, rel = refs[9:17]
    small_landed, rel_landed, sends, recvs = refs[17:21]
    rooms = list(refs[21:])
    dp, mp = lax.axis_index("dp"), lax.axis_index("mp")
    bit_at = lambda bit: mp if bit == 0 else (dp // bit) % 2

    def partner(bit):
        if bit == 0:
            return (dp, 1 - mp)
        return (jnp.where(bit_at(bit) == 0, dp + bit, dp - bit), mp)

    barrier = pltpu.get_barrier_semaphore()
    every = [1] + bits + [0]
    for bit in every:
        pl.semaphore_signal(barrier, inc=1, device_id=partner(bit), device_id_type=MESH)

    count = [0]

    def send(src, dst, bit):
        at = count[0]
        count[0] += 1
        copy = pltpu.make_async_remote_copy(
            src_ref=src,
            dst_ref=dst,
            send_sem=sends.at[at],
            recv_sem=recvs.at[at],
            device_id=partner(bit),
            device_id_type=MESH,
        )
        copy.start()
        return copy

    def line(k, part):
        order, value = orders[k], (line_a, line_b)[k].at[pl.ds(part * PART_ROWS, PART_ROWS)]
        slot = dp % 2 * 2 + k
        first = bit_at(order[0]) * (D // 2) + part * PART_ROWS
        start, size, placed = first, PART_ROWS, False
        for kind, bit, after in plans[k]:
            if kind == "double":
                here = pl.ds(pl.multiple_of(start, 16), size)
                if not placed:
                    out[slot, here, :] = value[...]
                    placed = True
                copy = send(out.at[slot, here], out.at[slot, here], bit)
                yield
                copy.wait()
                if after != size or bit != order[0]:
                    start, size = start - bit_at(bit) * size, 2 * size
                continue
            mine = bit_at(bit) if kind == "halve" else 0
            gone = 1 - mine if kind == "halve" else 0
            room, total = rooms.pop(0), rooms.pop(0)
            copy = send(value.at[pl.ds(pl.multiple_of(gone * after, 16), after)], room, bit)
            yield
            copy.wait()
            rows = pl.ds(pl.multiple_of(mine * after, 16), after)
            total[...] = (value[rows, :].astype(F32) + room[...].astype(F32)).astype(BF)
            value = total
            start, size = start + mine * after, after
        copies = []
        for half in range(2):
            rows = pl.ds(half * (D // 2) + part * PART_ROWS, PART_ROWS)
            copies.append(send(out.at[slot, rows], out.at[slot, rows], 1))
        yield
        for copy in copies:
            copy.wait()

    def vectors():
        for at, bit in enumerate(bits + [0, 1]):
            copies = [send(small, small_landed.at[at], bit), send(rel, rel_landed.at[at], bit)]
            yield
            for copy in copies:
                copy.wait()
            small[...] += small_landed[at]
            rel[...] += rel_landed[at]

    lines = [line(k, part) for part in range(PARTS) for k in range(2)]
    pl.semaphore_wait(barrier, len(every))
    for one in lines:
        next(one)

    small[...] = jnp.zeros_like(small)
    small[0:2, :] = one_sums[0:2, :]
    small[2:6, :] = two_sums[0:4, :]
    first = mp == 0
    own = [sums_a[0:1, :] + sums_c[0:1, :], fc1_sums[0:1, 0 : FF // 2]]
    other = [sums_b[0:1, :] + sums_d[0:1, :], fc1_sums[0:1, FF // 2 :]]
    for row, flip in ((6, False), (9, True)):
        picked = [jnp.where(first != flip, a, b) for a, b in zip(own, other)]
        small[row : row + 1, 0:HALF] = picked[0][:, 0:HALF]
        small[row : row + 1, HALF:] = picked[0][:, 2 * HALF :]
        small[row + 1 : row + 2, :] = picked[1][:, 0:D]
        small[row + 2 : row + 3, :] = picked[1][:, D:]
    table = rel_a[...] + rel_b[...] + rel_c[...] + rel_d[...]
    table = lax.dot_general(hots[...], table, TN, precision=lax.Precision.HIGHEST, preferred_element_type=F32)
    rel[...] = table + pltpu.roll(table, HD, 1)

    active = lines + [vectors()]
    while active:
        for one in list(active):
            if next(one, "end") == "end":
                active.remove(one)


def last_sums(bits, orders, lines, sums, rels, hots):
    vmem = pl.BlockSpec(memory_space=pltpu.VMEM)
    rounds = len(bits) + 2
    copies = 2 * rounds + 2 * PARTS * (2 * len(bits) + 2)
    plans = [line_plan(order, PART_ROWS) for order in orders]
    rooms = []
    for at in range(len(plans[0])):
        for part in range(PARTS):
            for plan in plans:
                if plan[at][0] != "double":
                    rooms += [pltpu.VMEM((plan[at][2], HALF), BF)] * 2
    return pl.pallas_call(
        lambda *refs: last_kernel(bits, plans, orders, *refs),
        in_specs=[vmem] * (2 + len(sums) + len(rels) + 1),
        out_specs=[vmem] * 3,
        out_shape=[
            jax.ShapeDtypeStruct((4, D, HALF), BF),
            jax.ShapeDtypeStruct((SMALL, D), F32),
            jax.ShapeDtypeStruct((56, 128), F32),
        ],
        scratch_shapes=[
            pltpu.VMEM((rounds, SMALL, D), F32),
            pltpu.VMEM((rounds, 56, 128), F32),
            pltpu.SemaphoreType.DMA((copies,)),
            pltpu.SemaphoreType.DMA((copies,)),
        ]
        + rooms,
        compiler_params=pltpu.CompilerParams(
            collective_id=0, has_side_effects=True, vmem_limit_bytes=40 * 2**20
        ),
    )(*lines, *sums, *rels, hots)


CORE, PAIRED = 1, 0


def bit_of(bit):
    return lax.axis_index("mp") if bit == PAIRED else (lax.axis_index("dp") // bit) % 2


def exchange(value, bit):
    if bit == PAIRED:
        return lax.ppermute(value, "mp", [(0, 1), (1, 0)])
    return lax.ppermute(value, "dp", [(i, i ^ bit) for i in range(lax.axis_size("dp"))])


class Line:
    def __init__(self, value, places, rank, steps, sent=None):
        self.terms = [(value, tuple(places))]
        self.fixed = {}
        self.rank = list(rank)
        self.steps = list(steps)
        self.sent, self.taken = sent, None
        self.value = None

    def part(self, changes):
        fixed = {**self.fixed, **changes}
        total = None
        for term, places in self.terms:
            starts, sizes, shape = [], [], []
            for bit in places:
                starts.append(fixed.get(bit, 0))
                sizes.append(1 if bit in fixed else 2)
                if bit not in fixed:
                    shape.append(2)
            rest = term.shape[len(places) :]
            if places:
                starts = [jnp.asarray(at, jnp.int32) for at in starts + [0] * len(rest)]
                term = lax.dynamic_slice(term, starts, tuple(sizes) + rest).reshape(tuple(shape) + rest)
            total = term.astype(F32) if total is None else total + term.astype(F32)
        return total.astype(BF)

    def prepare(self):
        kind, bit = self.steps[0]
        if kind == "halve":
            mine = 0 if bit == PAIRED else bit_of(bit)
            self.sent = self.part({bit: 1 - mine})
            self.fixed[bit] = mine
        elif kind == "double":
            if self.value is None:
                self.value, self.done = self.part({}), []
            self.sent = self.value
        elif kind == "pass":
            self.sent = self.part({})

    def launch(self):
        self.taken = exchange(self.sent, self.steps[0][1])

    def land(self):
        kind, bit = self.steps.pop(0)
        if kind in ("halve", "give"):
            places = [p for p in self.terms[0][1] if p not in self.fixed]
            self.terms.append((self.taken, tuple(places)))
        elif kind == "pass":
            self.terms = [(self.taken, tuple(p for p in self.terms[0][1] if p not in self.fixed))]
        else:
            if not self.steps:
                self.value, self.taken_last, self.taken = self.sent, self.taken, None
                return
            self.done = sorted(self.done + [bit], key=self.rank.index)
            axis = self.done.index(bit)
            shape = [1] * (self.value.ndim + 1)
            shape[axis] = 2
            mine = jnp.arange(2).reshape(shape) == bit_of(bit)
            wide = lambda v: jnp.expand_dims(v, axis)
            self.value = jnp.where(mine, wide(self.sent), wide(self.taken))
        self.taken = None


def advance(anchor, lines):
    flying = [line for line in lines if line.taken is not None]
    anchor, taken = lax.optimization_barrier((anchor, [line.taken for line in flying]))
    for line, value in zip(flying, taken):
        line.taken = value
        line.land()
    going = [line for line in lines if line.steps]
    for line in going:
        line.prepare()
    anchor, sent = lax.optimization_barrier((anchor, [line.sent for line in going]))
    for line, value in zip(going, sent):
        line.sent = value
        line.launch()
    return anchor


def finish(lines):
    while any(line.steps for line in lines):
        for line in lines:
            if not line.steps:
                continue
            if line.taken is None:
                line.prepare()
                line.launch()
        for line in lines:
            if line.taken is not None:
                line.land()


def on_device(
    image_tokens,
    norm1_gain,
    norm1_shift,
    qkv_weight,
    qv_bias,
    rel_rows,
    rel_cols,
    proj_weight,
    proj_bias,
    norm2_gain,
    norm2_shift,
    fc1_weight,
    fc1_bias,
    fc2_weight,
    fc2_bias,
    out_cotangent,
):
    place = lax.axis_index("mp")
    core = lax.axis_index("dp") % 2
    swap = lambda value: lax.ppermute(value, "mp", [(0, 1), (1, 0)])
    size = lax.axis_size("dp")
    core_swap = lambda value: lax.ppermute(value, "dp", [(i, i ^ 1) for i in range(size)])

    def by_core(weight, axis, mine):
        return lax.dynamic_slice_in_dim(weight, (core if mine else 1 - core) * HALF, HALF, axis)

    spot = jnp.stack([place, core]).astype(jnp.int32)
    spread = jnp.asarray(spread_rows(), BF)
    gather = jnp.asarray(spread_rows().T, BF)
    fold = jnp.asarray(fold_table(), BF)
    high_hot, wide_hot = rel_onehots()
    hots = jnp.asarray(np.pad(np.concatenate([high_hot, wide_hot], axis=1), ((0, 0), (0, 2))), F32)
    high_hot, wide_hot = jnp.asarray(high_hot, BF), jnp.asarray(wide_hot, BF)
    qkv_mine = swap(by_core(qkv_weight, 1, True))
    bias_other = swap(qv_bias)
    fc1_bias_other = swap(fc1_bias)
    x_windows = windows_of(spot, image_tokens, norm1_gain, norm1_shift, spread)
    cot_t = turned_of(out_cotangent)
    x_windows, cot_t, qkv_mine = lax.optimization_barrier((x_windows, cot_t, qkv_mine))
    late = (by_core(fc1_weight, 0, True), by_core(fc2_weight, 1, True), proj_weight)
    x_windows, qkv_mine, late = lax.optimization_barrier((x_windows, qkv_mine, late))
    qkv_theirs = exchange(qkv_mine, CORE)
    one_mine, two_mine, proj_other = (swap(w) for w in late)
    qkv_a, p_a, ctx_a, xt, rel_even, rel_odd = attend(
        x_windows, qv_bias, True, qkv_weight, high_hot, wide_hot, rel_rows, rel_cols
    )
    qkv_b, p_b, ctx_b = attend(
        x_windows, bias_other, False, spot, qkv_mine, qkv_theirs, rel_even, rel_odd
    )
    ctx_b, one_mine, two_mine, proj_other = lax.optimization_barrier((ctx_b, one_mine, two_mine, proj_other))
    one_theirs, two_theirs = exchange(one_mine, CORE), exchange(two_mine, CORE)
    middle, normed, normed_t, context = middle_of(
        spot, ctx_a, ctx_b, image_tokens, proj_weight, proj_other, proj_bias, norm2_gain, norm2_shift, gather
    )
    forward, back, one_kept, one_sent, two_kept, two_sent, fc1_sums = feed(
        spot, normed, normed_t, out_cotangent, cot_t, fc1_weight, (one_mine, one_theirs), fc1_bias,
        fc1_bias_other, fc2_weight, (two_mine, two_theirs),
    )
    bits = [2**k for k in range(1, bits_of(size))]
    turned = bits[1:2] + bits[0:1] + bits[2:]
    halves = lambda order: [("halve", bit) for bit in order]
    doubles = lambda order: [("double", bit) for bit in order]

    def cut(value, axis, places):
        shape = value.shape[:axis] + (2,) * len(places) + (value.shape[axis] // 2 ** len(places),)
        return value.reshape(shape + value.shape[axis + 1 :])

    def feed_line(kept, sent, order, back):
        steps = [("give", CORE)] + halves(order) + doubles(back) + [("double", CORE)]
        rank = [CORE] + bits
        return Line(cut(kept, 1, bits), [PAIRED] + bits, rank, steps, cut(sent, 1, bits))

    one_line = feed_line(one_kept, one_sent, [PAIRED] + bits, bits[::-1])
    two_line = feed_line(two_kept, two_sent, bits[:2] + [PAIRED] + bits[2:], turned[::-1])
    feed_lines = [one_line, two_line]

    middle = advance(middle, feed_lines)
    block_out, middle_grad, ctx_grad, proj_own, proj_oth, two_sums = resid_of(
        middle, forward, back, out_cotangent, context, proj_weight, proj_other, fc2_bias, norm2_gain
    )
    back_of = lambda qkv, p, side, grad, bands, *d: attend_back(
        spot, qkv, p, grad, side, spread, rel_even, rel_odd, fold, bands, *d
    )
    ctx_grad = advance(ctx_grad, feed_lines)
    d_b, rel_b, sums_b = back_of(qkv_b, p_b, 1, ctx_grad, (1, 3))
    d_b = advance(d_b, feed_lines)
    d_b, rel_b0, sums_b0 = back_of(qkv_b, p_b, 1, ctx_grad, (0, 1), d_b)
    d_b = advance(d_b, feed_lines)
    kept_b, sent_b = qkv_grad(spot, xt, d_b, proj_oth)
    line_b = Line(kept_b, [], [], [("give", CORE)], sent_b)
    lines = feed_lines + [line_b]
    ctx_grad, kept_b = lax.optimization_barrier((ctx_grad, kept_b))
    ctx_grad = advance(ctx_grad, lines)
    d_a, rel_a0, sums_a0 = back_of(qkv_a, p_a, 0, ctx_grad, (0, 1))
    d_a = advance(d_a, lines)
    passes = []
    for k in range(2):
        line = Line(None, [], [], [("pass", PAIRED)])
        line.terms = [(term[k], ()) for term, _ in line_b.terms]
        passes.append(line)
    d_a = advance(d_a, passes[:1])
    d_a, rel_a, sums_a = back_of(qkv_a, p_a, 0, ctx_grad, (1, 3), d_a)
    d_a = advance(d_a, feed_lines + passes[:1])
    d_a = advance(d_a, passes[1:])
    up = norm_grad(d_a, d_b, qkv_weight, spot, qkv_mine, qkv_theirs, gather, (1, 3))
    at = [2 - place, (1 - place) * 4 * SIDE, jnp.zeros_like(place)]
    shares = []
    for first, count in ((0, 6), (6, 4)):
        start = [at[0], at[1] + first * SIDE, at[2]]
        part = lax.dynamic_slice(up, start, (1, count * SIDE, D)).reshape(count * SIDE, D)
        shares.append(Line(part, [], [], [("pass", PAIRED)]))
    d_a = advance(d_a, feed_lines + passes[1:])
    d_a = advance(d_a, shares[:1])
    kept_a, sent_a = qkv_grad(spot, xt, d_a, proj_own)
    line_a = Line(kept_a, [], [], [("give", CORE)], sent_a)
    kept_a, d_a = lax.optimization_barrier((kept_a, d_a))
    d_a = advance(d_a, feed_lines + [line_a] + shares[:1])
    d_a = advance(d_a, shares[1:])
    up = norm_grad(d_a, d_b, qkv_weight, spot, qkv_mine, qkv_theirs, gather, (0, 1), up)
    up = advance(up, feed_lines + [line_a] + shares[1:])
    taken = jnp.concatenate([line.terms[0][0] for line in shares], axis=0)
    q_lines = []
    for k, order in enumerate((bits, turned)):
        line = Line(None, [], [], halves(order[:1]))
        line.terms = [(part.reshape(2, 2, D // 2, HALF), ("line", order[0])) for part, _ in line_a.terms]
        line.terms += [(part.reshape(2, D // 2, HALF), (order[0],)) for part, _ in passes[k].terms]
        line.fixed = {"line": k}
        q_lines.append(line)
    up = advance(up, q_lines)
    finish(feed_lines)
    flat = lambda line, rows: (line.value.reshape(rows, -1), line.taken_last.reshape(rows, -1))
    input_grad, one_sums, one_sum, two_sum = input_of(
        spot, image_tokens, middle_grad, up, taken, norm1_gain, flat(one_line, HALF), flat(two_line, FF // 2)
    )
    one_sums = advance(one_sums, q_lines)
    four, small, rel = last_sums(
        bits,
        [bits, turned],
        [line.part({}) for line in q_lines],
        [one_sums, two_sums, fc1_sums, sums_a, sums_a0, sums_b, sums_b0],
        [rel_a, rel_a0, rel_b, rel_b0],
        hots,
    )
    one_sum = one_sum.reshape(D, FF // 2)
    mine = jnp.where(place == 0, small[6:9], small[9:12])
    return (
        block_out,
        input_grad,
        small[0],
        small[1],
        four[0:3].astype(F32),
        mine[0].reshape(2, HALF),
        rel[:RELS, :HD],
        rel[RELS : 2 * RELS, :HD],
        jnp.concatenate([four[3, :HALF], four[3, HALF:]], axis=1).astype(F32),
        small[5],
        small[2],
        small[3],
        one_sum,
        mine[1:3].reshape(-1),
        two_sum,
        small[4],
    )


def solution(mesh):
    in_specs = (
        P("dp", None),
        P(),
        P(),
        P(None, None, "mp"),
        P(None, "mp"),
        P(),
        P(),
        P("mp", None),
        P(),
        P(),
        P(),
        P(None, "mp"),
        P("mp"),
        P("mp", None),
        P(),
        P(("dp", "mp"), None),
    )
    out_specs = (
        P(("dp", "mp"), None),
        P(("dp", "mp"), None),
        P(),
        P(),
        P(None, None, "mp"),
        P(None, "mp"),
        P(),
        P(),
        P("mp", None),
        P(),
        P(),
        P(),
        P(None, "mp"),
        P("mp"),
        P("mp", None),
        P(),
    )
    return jax.shard_map(
        on_device, mesh=mesh, in_specs=in_specs, out_specs=out_specs, check_vma=False
    )
```

```python
import jax
import jax.numpy as jnp
import numpy as np
from jax import lax
from jax.experimental import pallas as pl
from jax.experimental.pallas import tpu as pltpu
from jax.sharding import PartitionSpec as P

D = 768
HEADS = 12
HD = 64
FF = 3072
WIN = 14
SIDE = 64
NWIN = 5
RELS = 27
EPSILON = 1e-06
F32 = jnp.float32
BF = jnp.bfloat16

SLOTS = 256
KEYS = WIN * 16
PAIR = 2 * SIDE
GREL = 80
OWN = SIDE * SIDE // 2

HALF = D // 2
TRIO = 3 * HALF
PAIRS = HEADS // 4

NN = (((1,), (0,)), ((), ()))
NT = (((1,), (1,)), ((), ()))
TN = (((0,), (0,)), ((), ()))


def dot(left, right, dims=NN):
    return lax.dot_general(left, right, dims, preferred_element_type=F32)


def params(limit=60):
    return pltpu.CompilerParams(vmem_limit_bytes=limit * 2**20)


def cost(flops, moved, exps=0):
    return pl.CostEstimate(flops=int(flops), bytes_accessed=int(moved), transcendentals=int(exps))


def whole(shape):
    return pl.BlockSpec(shape, lambda *_: (0,) * len(shape), pipeline_mode=pl.Buffered(1))


def band_start(place, band):
    return (1 - place) * (14 * band) + place * (42 - 14 * band + 21 * band * (band - 1))


def image_pair(place, band, step):
    pair = band_start(place, band) // 2 + step
    return jnp.minimum(pair, SIDE // 2 - 1), pair < SIDE // 2


def owned_pair(place, band, step):
    pair = band_start(place, band) // 2 + step - 16 * place
    return jnp.clip(pair, 0, 15), (pair >= 0) & (pair < 16)


def band_step(place, pair):
    first = pair // 7, pair % 7
    band = jnp.where(pair < 5, 1, jnp.where(pair < 12, 0, 2))
    second = band, jnp.where(pair < 5, pair + 2, jnp.where(pair < 12, pair - 5, pair - 12))
    return tuple(jnp.where(place == 0, a, b) for a, b in zip(first, second))


def taken_pair(place, pair):
    return (
        jnp.where(place == 0, jnp.maximum(pair - 14, 0), jnp.minimum(pair, 4)),
        jnp.where(place == 0, pair >= 14, pair < 5),
    )


def spread_rows():
    table = np.zeros((NWIN, 2, 16, PAIR), np.float32)
    for w in range(NWIN):
        for r in range(2):
            for j in range(WIN):
                if WIN * w + j < SIDE:
                    table[w, r, j, r * SIDE + WIN * w + j] = 1
    return table.reshape(NWIN * 32, PAIR)


def rel_order():
    rows = np.full(GREL, -1)
    for m in range(21):
        rows[m] = 26 - (m + 6)
        rows[24 + m] = 26 - m
    cols = np.full(GREL, -1)
    for m in range(RELS):
        cols[48 + m] = 26 - m
    return rows, cols


def rel_onehots():
    rows, cols = rel_order()
    high = (rows[:, None] == np.arange(RELS)[None, :]).astype(np.float32)
    wide = (cols[:, None] == np.arange(RELS)[None, :]).astype(np.float32)
    return high, wide


def norm_parts(values):
    average = jnp.mean(values, axis=-1, keepdims=True)
    centred = values - average
    inverse = lax.rsqrt(jnp.mean(centred * centred, axis=-1, keepdims=True) + EPSILON)
    return centred * inverse, inverse


def vec(ref):
    return ref[...].astype(F32).reshape(1, D)


def window_kernel(spot, *refs):
    xs, (gain, shift, spread, out) = refs[:7], refs[7:]
    band = pl.program_id(0)
    for t in range(7):
        scaled, _ = norm_parts(xs[t][...].astype(F32))
        normed = scaled * vec(gain) + vec(shift)
        valid = image_pair(spot[0], band, t)[1]
        normed = (normed * valid.astype(F32)).astype(BF)
        moved = dot(spread[...], normed).astype(BF)
        out[:, :, 32 * t : 32 * t + 32, :] = moved.reshape(1, NWIN, 32, D)
    out[:, :, 224:, :] = jnp.zeros((1, NWIN, 32, D), BF)


def windows_of(spot, x, gain, shift, spread):
    at = lambda t: lambda s, spot: (image_pair(spot[0], s, t)[0], 0)
    return pl.pallas_call(
        window_kernel,
        grid_spec=pltpu.PrefetchScalarGridSpec(
            num_scalar_prefetch=1,
            grid=(3,),
            in_specs=[pl.BlockSpec((PAIR, D), at(t)) for t in range(7)]
            + [whole((D,)), whole((D,)), whole((NWIN * 32, PAIR))],
            out_specs=pl.BlockSpec((1, NWIN, SLOTS, D), lambda s, *_: (s, 0, 0, 0)),
        ),
        out_shape=jax.ShapeDtypeStruct((3, NWIN, SLOTS, D), BF),
        compiler_params=params(),
        cost_estimate=cost(3 * 7 * 160 * 128 * 768 * 2, 10e6),
    )(spot, *([x] * 7), gain, shift, spread)


def shift_masks(lanes_from):
    lane = lax.broadcasted_iota(jnp.int32, (1, 128), 1) + lanes_from
    high = lane // 16
    row_shift = jnp.where(lane < 128, 7 - high, jnp.maximum(13 - high, 0))
    col_shift = jnp.maximum(13 - lane % 16, 0)
    return row_shift, col_shift


def skew(table, shift, bits):
    size = table.shape[0]
    for bit in bits:
        moved = pltpu.roll(table, size - bit, 0)
        table = jnp.where((shift & bit) != 0, moved, table)
    return table


def unskew(table, shift, bits):
    for bit in bits:
        moved = pltpu.roll(table, bit, 0)
        table = jnp.where((shift & bit) != 0, moved, table)
    return table


def start_own(weights, bias, high_hot, wide_hot, rel_rows, rel_cols, rel_even, rel_odd, joined):
    for s in range(3):
        joined[:, s * HALF : s * HALF + HALF] = weights[s]
    table = (dot(high_hot[...], rel_rows[...]) + dot(wide_hot[...], rel_cols[...])).astype(BF)
    blank = jnp.zeros_like(table)
    rel_even[...] = jnp.concatenate([table, blank], axis=1)
    rel_odd[...] = jnp.concatenate([blank, table], axis=1)


def join_pieces(core, mine, theirs, joined, col):
    for piece, at in ((mine, core), (theirs, 1 - core)):
        rows = pl.ds(pl.multiple_of(at * HALF, HALF), HALF)
        for s in range(3):
            joined[rows, col + s * HALF : col + s * HALF + HALF] = piece[s]


def attend_own(
    x, bias, weights, high_hot, wide_hot, rel_rows, rel_cols,
    qkv_out, p_out, ctx_out, xt_out, rel_even, rel_odd, joined, vt,
):
    @pl.when((pl.program_id(0) == 0) & (pl.program_id(1) == 0))
    def _():
        start_own(weights, bias, high_hot, wide_hot, rel_rows, rel_cols, rel_even, rel_odd, joined)

    attend_window(x, bias, rel_even, rel_odd, qkv_out, p_out, ctx_out, xt_out, joined, vt)


def attend_other(x, bias, spot, mine, theirs, rel_even, rel_odd, qkv_out, p_out, ctx_out, joined, vt):
    @pl.when((pl.program_id(0) == 0) & (pl.program_id(1) == 0))
    def _():
        join_pieces(spot[1], mine, theirs, joined, 0)

    attend_window(x, bias, rel_even, rel_odd, qkv_out, p_out, ctx_out, None, joined, vt)


def attend_window(x, bias, rel_even, rel_odd, qkv_out, p_out, ctx_out, xt_out, joined, vt):
    band = pl.program_id(0)
    biases = bias[...].astype(F32)
    biases = jnp.concatenate([biases[0:1], jnp.zeros((1, HALF), F32), biases[1:2]], axis=1)
    block = x[...].reshape(SLOTS, D)
    if xt_out is not None:
        xt_out[...] = block.T
    scales = jnp.where(lax.broadcasted_iota(jnp.int32, (1, TRIO), 1) // HALF == 1, HD ** (-0.5), 1.0)
    low = ((dot(block, joined[...]) + biases) * scales).astype(BF)
    qkv_out[0, 0] = low
    vt[...] = low[:, 2 * HALF :].T

    even = lax.broadcasted_iota(jnp.int32, (1, 128), 1) < HD

    def raw_scores(head, lanes):
        col = head // 2 * 128
        keys = qkv_out[0, 0, 0:KEYS, HALF + col : HALF + col + 128]
        kept = jnp.where(even != (head % 2 == 1), keys, jnp.zeros_like(keys))
        rel = rel_odd if head % 2 else rel_even
        left = jnp.concatenate([kept, rel[...]], axis=0)
        return dot(left, qkv_out[0, 0, 0:lanes, col : col + 128], NT)

    def soft(head, raw, lanes):
        parts = []
        for tile in range(lanes // 128):
            row_shift, col_shift = shift_masks(tile * 128)
            raw_t = raw[:, tile * 128 : tile * 128 + 128]
            base = raw_t[0:KEYS]
            high = skew(raw_t[KEYS + 24 * tile : KEYS + 24 * tile + 24], row_shift, (4, 2, 1))[0:16]
            wide = skew(raw_t[KEYS + 48 : KEYS + 80], col_shift, (8, 4, 2, 1))[0:16]
            place = lax.broadcasted_iota(jnp.int32, (16, 128), 0)
            wide = jnp.where(place < WIN, wide, -1e30)
            scores = base.reshape(WIN, 16, 128) + wide[None] + high[0:WIN][:, None, :]
            scores = scores.reshape(KEYS, 128)
            peak = jnp.max(scores, axis=0, keepdims=True)
            grown = jnp.exp(scores - peak)
            total = jnp.sum(grown, axis=0, keepdims=True)
            parts.append((grown * (1.0 / total)).astype(BF))
        probs = parts[0] if len(parts) == 1 else jnp.concatenate(parts, axis=1)
        p_out[0, 0, head, :, 0:lanes] = probs
        return probs

    def all_heads(lanes):
        count = HEADS // 2
        raw = raw_scores(0, lanes)
        contexts = []
        for head in range(count):
            ahead = raw_scores(head + 1, lanes) if head + 1 < count else None
            probs = soft(head, raw, lanes)
            if head:
                contexts.append(dot(vt[(head - 1) * HD : head * HD, 0:KEYS], before).astype(BF))
            if head and head % 2 == 0:
                col = (head - 2) * HD
                ctx_out[0, 0, 0:lanes, col : col + 128] = jnp.concatenate(contexts[-2:], axis=0).T
            before, raw = probs, ahead
        contexts.append(dot(vt[(count - 1) * HD :, 0:KEYS], before).astype(BF))
        ctx_out[0, 0, 0:lanes, HALF - 128 :] = jnp.concatenate(contexts[-2:], axis=0).T

    @pl.when(band < 2)
    def _():
        all_heads(256)

    @pl.when(band == 2)
    def _():
        all_heads(128)


SCALAR = pl.BlockSpec(memory_space=pltpu.SMEM)


def attend(x, bias, first, *operands):
    block = lambda width: pl.BlockSpec((1, 1, SLOTS, width), lambda s, w: (s, w, 0, 0))
    shape = lambda width: jax.ShapeDtypeStruct((3, NWIN, SLOTS, width), BF)
    out_specs = [
        block(TRIO),
        pl.BlockSpec((1, 1, HEADS // 2, KEYS, SLOTS), lambda s, w: (s, w, 0, 0, 0)),
        block(HALF),
    ]
    out_shape = [
        shape(TRIO),
        jax.ShapeDtypeStruct((3, NWIN, HEADS // 2, KEYS, SLOTS), BF),
        shape(HALF),
    ]
    rel = pl.BlockSpec((GREL, 128), lambda s, w: (0, 0))
    if first:
        in_specs = [whole((3, D, HALF)), whole((GREL, RELS)), whole((GREL, RELS)), whole((RELS, HD)), whole((RELS, HD))]
        out_specs += [pl.BlockSpec((D, SLOTS), lambda s, w: (0, s * NWIN + w)), rel, rel]
        out_shape += [jax.ShapeDtypeStruct((D, 3 * NWIN * SLOTS), BF)] + [jax.ShapeDtypeStruct((GREL, 128), BF)] * 2
    else:
        in_specs = [SCALAR, whole((3, HALF, HALF)), whole((3, HALF, HALF)), whole((GREL, 128)), whole((GREL, 128))]
    return pl.pallas_call(
        attend_own if first else attend_other,
        grid=(3, NWIN),
        in_specs=[block(D), whole((2, HALF))] + in_specs,
        out_specs=out_specs,
        out_shape=out_shape,
        scratch_shapes=[pltpu.VMEM((D, TRIO), BF), pltpu.VMEM((HALF, SLOTS), BF)],
        compiler_params=params(),
        cost_estimate=cost(15e9, 45e6, 4e6),
    )(x, bias, *operands)


def middle_kernel(
    spot, own_a, own_b, other_a, other_b, x, proj_own, proj_other, bias, gain, shift, gather,
    middle, normed, normed_t, ctx_out, proj,
):
    @pl.when(pl.program_id(0) == 0)
    def _():
        proj[0:HALF, :] = proj_own[...]
        proj[HALF:, :] = proj_other[...]

    for row, parts in ((0, (own_a, other_a)), (PAIR, (own_b, other_b))):
        for side in range(2):
            moved = dot(gather[...], parts[side][...].reshape(NWIN * 32, HALF)).astype(BF)
            ctx_out[row : row + PAIR, side * HALF : side * HALF + HALF] = moved
    value = x[...].astype(F32) + (dot(ctx_out[...], proj[...]) + vec(bias))
    middle[...] = value.astype(BF)
    scaled, _ = norm_parts(value)
    low = (scaled * vec(gain) + vec(shift)).astype(BF)
    normed[...] = low
    normed_t[...] = low.T


def middle_of(spot, ctx_own, ctx_other, x, proj_own, proj_other, bias, gain, shift, gather):
    rows = 2 * PAIR

    def at(k):
        def place(i, spot):
            band, step = band_step(spot[0], 2 * i + k)
            return band, 0, step, 0

        return pl.BlockSpec((1, NWIN, 32, HALF), place)

    row_block = pl.BlockSpec((rows, D), lambda i, *_: (i, 0))
    col_block = pl.BlockSpec((D, rows), lambda i, *_: (0, i))
    low = jax.ShapeDtypeStruct((OWN, D), BF)
    return pl.pallas_call(
        middle_kernel,
        grid_spec=pltpu.PrefetchScalarGridSpec(
            num_scalar_prefetch=1,
            grid=(OWN // rows,),
            in_specs=[
                at(0),
                at(1),
                at(0),
                at(1),
                pl.BlockSpec((rows, D), lambda i, spot: (spot[0] * (OWN // rows) + i, 0)),
                whole((HALF, D)),
                whole((HALF, D)),
                whole((D,)),
                whole((D,)),
                whole((D,)),
                whole((PAIR, NWIN * 32)),
            ],
            out_specs=[row_block, row_block, col_block, row_block],
            scratch_shapes=[pltpu.VMEM((D, D), BF)],
        ),
        out_shape=[low, low, jax.ShapeDtypeStruct((D, OWN), BF), low],
        compiler_params=params(),
        cost_estimate=cost(3e9, 25e6),
    )(spot, ctx_own, ctx_own, ctx_other, ctx_other, x, proj_own, proj_other, bias, gain, shift, gather)


def turn_kernel(value, out):
    out[...] = value[...].T


def turned_of(value):
    rows = 512
    return pl.pallas_call(
        turn_kernel,
        grid=(OWN // rows,),
        in_specs=[pl.BlockSpec((rows, D), lambda i: (i, 0))],
        out_specs=pl.BlockSpec((D, rows), lambda i: (0, i)),
        out_shape=jax.ShapeDtypeStruct((D, OWN), BF),
        compiler_params=params(),
        cost_estimate=cost(1e6, 6e6),
    )(value)


CHUNK = 512
CHUNKS = FF // CHUNK


def feed_kernel(
    spot, normed, normed_t, cot, cot_t, one_a, one_b, one_c, bias_a, bias_b, two_a, two_b, two_c,
    forward_out, back_out, one_kept, one_sent, two_kept, two_sent, sums,
    forward, back, one, two, bias, hidden, grads,
):
    step = pl.program_id(0)

    @pl.when(step == 0)
    def _():
        forward[...] = jnp.zeros_like(forward)
        back[...] = jnp.zeros_like(back)

    @pl.when(step < CHUNKS // 2)
    def _():
        bias[...] = bias_a[...].astype(F32).reshape(1, CHUNK)
        one[...] = one_a[...]
        two[...] = two_a[...]

    @pl.when(step >= CHUNKS // 2)
    def _():
        bias[...] = bias_b[...].astype(F32).reshape(1, CHUNK)
        mine = pl.multiple_of(spot[1] * HALF, HALF)
        theirs = pl.multiple_of((1 - spot[1]) * HALF, HALF)
        one[pl.ds(mine, HALF), :] = one_b[...]
        one[pl.ds(theirs, HALF), :] = one_c[...]
        two[:, pl.ds(mine, HALF)] = two_b[...]
        two[:, pl.ds(theirs, HALF)] = two_c[...]

    total = jnp.zeros((1, CHUNK), F32)
    for t in range(OWN // 256):
        rows = slice(t * 256, t * 256 + 256)
        pre = dot(normed[rows, :], one[...]) + bias[...]
        phi = 0.5 * (1.0 + lax.erf(pre * 0.7071067811865476))
        slope = phi + pre * (jnp.exp(-0.5 * pre * pre) * 0.3989422804014327)
        low = (pre * phi).astype(BF)
        grad = (dot(cot[rows, :], two[...], NT) * slope).astype(BF)
        hidden[rows, :] = low
        grads[rows, :] = grad
        total += jnp.sum(grad.astype(F32), axis=0, keepdims=True)
        forward[rows, :] += dot(low, two[...])
        back[rows, :] += dot(grad, one[...], NT)
    sums[...] = total

    first = spot[1] == 0
    one_grad = dot(normed_t[...], grads[...]).astype(BF)
    low, high = one_grad[:HALF], one_grad[HALF:]
    one_kept[0] = jnp.where(first, low, high)
    one_sent[0] = jnp.where(first, high, low)
    two_grad = dot(cot_t[...], hidden[...]).astype(BF)
    low, high = two_grad[:HALF], two_grad[HALF:]
    two_kept[0] = jnp.where(first, low, high).T
    two_sent[0] = jnp.where(first, high, low).T

    @pl.when(step == pl.num_programs(0) - 1)
    def _():
        forward_out[...] = forward[...].astype(BF)
        back_out[...] = back[...].astype(BF)


def feed(spot, normed, normed_t, cot, cot_t, one_a, ones, bias_a, bias_b, two_a, twos):
    half = CHUNKS // 2
    own = lambda j: jnp.minimum(j, half - 1)
    other = lambda j: jnp.maximum(j - half, 0)
    one_block = pl.BlockSpec((1, HALF, CHUNK), lambda j, *_: (j // half, 0, j % half))
    two_block = pl.BlockSpec((1, CHUNK, HALF), lambda j, *_: (j // half, j % half, 0))
    one_piece = pl.BlockSpec((HALF, CHUNK), lambda j, *_: (0, other(j)))
    two_piece = pl.BlockSpec((CHUNK, HALF), lambda j, *_: (other(j), 0))
    one_shape = jax.ShapeDtypeStruct((2, HALF, FF // 2), BF)
    two_shape = jax.ShapeDtypeStruct((2, FF // 2, HALF), BF)
    sum_block = pl.BlockSpec((OWN, D), lambda j, *_: (0, 0))
    bias_block = pl.BlockSpec((1, CHUNK), lambda j, *_: (0, j))
    return pl.pallas_call(
        feed_kernel,
        grid_spec=pltpu.PrefetchScalarGridSpec(
            num_scalar_prefetch=1,
            grid=(CHUNKS,),
            in_specs=[
                whole((OWN, D)),
                whole((D, OWN)),
                whole((OWN, D)),
                whole((D, OWN)),
                pl.BlockSpec((D, CHUNK), lambda j, *_: (0, own(j))),
                one_piece,
                one_piece,
                pl.BlockSpec((CHUNK,), lambda j, *_: (own(j),)),
                pl.BlockSpec((CHUNK,), lambda j, *_: (other(j),)),
                pl.BlockSpec((CHUNK, D), lambda j, *_: (own(j), 0)),
                two_piece,
                two_piece,
            ],
            out_specs=[sum_block, sum_block, one_block, one_block, two_block, two_block, bias_block],
            scratch_shapes=[
                pltpu.VMEM((OWN, D), F32),
                pltpu.VMEM((OWN, D), F32),
                pltpu.VMEM((D, CHUNK), BF),
                pltpu.VMEM((CHUNK, D), BF),
                pltpu.VMEM((1, CHUNK), F32),
                pltpu.VMEM((OWN, CHUNK), BF),
                pltpu.VMEM((OWN, CHUNK), BF),
            ],
        ),
        out_shape=[
            jax.ShapeDtypeStruct((OWN, D), BF),
            jax.ShapeDtypeStruct((OWN, D), BF),
            one_shape,
            one_shape,
            two_shape,
            two_shape,
            jax.ShapeDtypeStruct((1, FF), F32),
        ],
        compiler_params=params(62),
        cost_estimate=cost(58e9, 60e6, 12e6),
    )(spot, normed, normed_t, cot, cot_t, one_a, *ones, bias_a, bias_b, two_a, *twos)


def add_row(sums, row, values):
    sums[row : row + 1, :] += jnp.sum(values, axis=0, keepdims=True)


def resid_kernel(
    middle, forward, back, cot, context, proj_own, proj_other, bias, gain,
    block_out, grad_out, ctx_grad, grad_own, grad_other, sums, proj, proj_grad,
):
    step = pl.program_id(0)

    @pl.when(step == 0)
    def _():
        proj[0:HALF, :] = proj_own[...]
        proj[HALF:, :] = proj_other[...]
        proj_grad[...] = jnp.zeros_like(proj_grad)
        sums[...] = jnp.zeros_like(sums)

    value = middle[...].astype(F32)
    block_out[...] = (value + (forward[...].astype(F32) + vec(bias))).astype(BF)
    scaled, inverse = norm_parts(value)
    upstream = back[...].astype(F32)
    scaled_up = upstream * vec(gain)
    first = jnp.mean(scaled_up, axis=-1, keepdims=True)
    second = jnp.mean(scaled_up * scaled, axis=-1, keepdims=True)
    cotangent = cot[...].astype(F32)
    grad = cotangent + inverse * (scaled_up - first - scaled * second)
    low = grad.astype(BF)
    grad_out[...] = low
    ctx_grad[...] = dot(low, proj[...], NT).astype(BF)
    proj_grad[...] += dot(context[...], low, TN)
    add_row(sums, 0, upstream * scaled)
    add_row(sums, 1, upstream)
    add_row(sums, 2, cotangent)
    add_row(sums, 3, low.astype(F32))

    @pl.when(step == pl.num_programs(0) - 1)
    def _():
        for out, row in ((grad_own, 0), (grad_other, HALF)):
            for col in (0, HALF):
                out[col : col + HALF, :] = proj_grad[row : row + HALF, col : col + HALF].astype(BF)


def resid_of(middle, forward, back, cot, context, proj_own, proj_other, bias, gain):
    rows = 512
    row_block = pl.BlockSpec((rows, D), lambda i: (i, 0))
    half_block = pl.BlockSpec((D, HALF), lambda i: (0, 0))
    return pl.pallas_call(
        resid_kernel,
        grid=(OWN // rows,),
        in_specs=[row_block] * 5 + [whole((HALF, D)), whole((HALF, D)), whole((D,)), whole((D,))],
        out_specs=[
            row_block,
            row_block,
            row_block,
            half_block,
            half_block,
            pl.BlockSpec((8, D), lambda i: (0, 0)),
        ],
        out_shape=[
            jax.ShapeDtypeStruct((OWN, D), BF),
            jax.ShapeDtypeStruct((OWN, D), BF),
            jax.ShapeDtypeStruct((OWN, D), BF),
            jax.ShapeDtypeStruct((D, HALF), BF),
            jax.ShapeDtypeStruct((D, HALF), BF),
            jax.ShapeDtypeStruct((8, D), F32),
        ],
        scratch_shapes=[pltpu.VMEM((D, D), BF), pltpu.VMEM((D, D), F32)],
        compiler_params=params(),
        cost_estimate=cost(5e9, 40e6),
    )(middle, forward, back, cot, context, proj_own, proj_other, bias, gain)


def attend_back_kernel(first, spot, qkv, p, ctx_grad, spread, rel_even, rel_odd, fold, *refs):
    d_out, rel_grad, sums, upstream, kt = refs[-5:]
    band = pl.program_id(0) + first
    window = pl.program_id(1)

    @pl.when((band == first) & (window == 0))
    def _():
        rel_grad[...] = jnp.zeros_like(rel_grad)
        sums[...] = jnp.zeros_like(sums)

    @pl.when(window == 0)
    def _():
        for t in range(7):
            at, owned = owned_pair(spot[0], band, t)
            rows = pl.ds(pl.multiple_of(at * PAIR, PAIR), PAIR)
            moved = dot(spread[...], ctx_grad[rows, :])
            moved = moved * owned.astype(F32)
            upstream[:, 32 * t : 32 * t + 32, :] = moved.astype(BF).reshape(NWIN, 32, HALF)
        upstream[:, 224:256, :] = jnp.zeros((NWIN, 32, HALF), BF)

    kt[...] = qkv[0, 0, :, HALF : 2 * HALF].T
    even = lax.broadcasted_iota(jnp.int32, (1, 128), 1) < HD

    def shifted(head, by):
        return slice(by * HALF + head // 2 * 128, by * HALF + head // 2 * 128 + 128)

    def prob_grads(head, lanes):
        values = qkv[0, 0, 0:KEYS, shifted(head, 2)]
        kept = jnp.where(even != (head % 2 == 1), values, jnp.zeros_like(values))
        return dot(kept, upstream[window, 0:lanes, shifted(head, 0)], NT)

    def rel_table(both, lanes):
        tables = []
        zero8 = jnp.zeros((8, 128), F32)
        zero24 = jnp.zeros((24, 128), F32)
        zero16 = jnp.zeros((16, 128), F32)
        for tile in range(lanes // 128):
            row_shift, col_shift = shift_masks(tile * 128)
            part = both[:, tile * 128 : tile * 128 + 128]
            high = jnp.concatenate([part[HD : HD + 16], zero8], axis=0)
            wide = jnp.concatenate([part[HD + 16 : HD + 32], zero16], axis=0)
            high = unskew(high, row_shift, (1, 2, 4))
            wide = unskew(wide, col_shift, (1, 2, 4, 8))
            stack = [high, zero24, wide] if tile == 0 else [zero24, high, wide]
            tables.append(jnp.concatenate(stack, axis=0))
        table = tables[0] if len(tables) == 1 else jnp.concatenate(tables, axis=1)
        return table.astype(BF)

    def all_heads(lanes):
        count = HEADS // 2
        dvs, dks, dqs, drs = [], [], [], []

        def last_part(head, score_grad, both):
            rel = rel_odd if head % 2 else rel_even
            table = rel_table(both, lanes)
            queries = qkv[0, 0, 0:lanes, shifted(head, 0)]
            grads = dot(jnp.concatenate([score_grad, table], axis=0), queries)
            dks.append(grads[0:KEYS])
            drs.append(grads[KEYS:])
            from_rel = dot(rel[...], table, TN)
            side = head % 2 * HD
            dqs.append(both[0:HD] + from_rel[side : side + HD])
            if head % 2:
                d_out[0, 0, 0:lanes, shifted(head, 0)] = jnp.concatenate(dqs[-2:], axis=0).astype(BF).T
                d_out[0, 0, 0:KEYS, shifted(head, 1)] = (jnp.where(even, dks[-2], dks[-1]) * HD ** (-0.5)).astype(BF)

        prob_grad = prob_grads(0, lanes)
        before = None
        for head in range(count):
            ahead = prob_grads(head + 1, lanes) if head + 1 < count else None
            probs_low = p[0, 0, head, :, 0:lanes]
            probs = probs_low.astype(F32)
            total = jnp.sum(prob_grad * probs, axis=0, keepdims=True)
            score_grad = (probs * (prob_grad - total)).astype(BF)
            dvs.append(dot(probs_low, upstream[window, 0:lanes, shifted(head, 0)]))
            left = jnp.concatenate([kt[head * HD : head * HD + HD, 0:KEYS], fold[...]], axis=0)
            both = dot(left, score_grad)
            if head % 2:
                d_out[0, 0, 0:KEYS, shifted(head, 2)] = jnp.where(even, dvs[-2], dvs[-1]).astype(BF)
            if before is not None:
                last_part(head - 1, *before)
            before, prob_grad = (score_grad, both), ahead
        last_part(count - 1, *before)
        evens = drs[0] + drs[2] + drs[4]
        odds = drs[1] + drs[3] + drs[5]
        rel_grad[...] += jnp.where(even, evens, odds)

    d_out[0, 0, KEYS:, HALF:] = jnp.zeros((SLOTS - KEYS, 2 * HALF), BF)

    @pl.when(band < 2)
    def _():
        all_heads(256)

    @pl.when(band == 2)
    def _():
        all_heads(128)
        d_out[0, 0, 128:, 0:HALF] = jnp.zeros((128, HALF), BF)

    sums[0:1, :] += jnp.sum(d_out[...].reshape(SLOTS, TRIO).astype(F32), axis=0, keepdims=True)


def fold_table():
    table = np.zeros((32, WIN, 16), np.float32)
    for k in range(WIN):
        for l in range(WIN):
            table[k, k, l] = 1
            table[16 + l, k, l] = 1
    return table.reshape(32, KEYS)


def attend_back(spot, qkv, p, ctx_grad, side, spread, rel_even, rel_odd, fold, bands, *d_in):
    first, last = bands
    block = pl.BlockSpec((1, 1, SLOTS, TRIO), lambda s, w, *_: (s + first, w, 0, 0))
    share = (last - first) / 3
    return pl.pallas_call(
        lambda *refs: attend_back_kernel(first, *refs),
        grid_spec=pltpu.PrefetchScalarGridSpec(
            num_scalar_prefetch=1,
            grid=(last - first, NWIN),
            in_specs=[
                block,
                pl.BlockSpec((1, 1, HEADS // 2, KEYS, SLOTS), lambda s, w, *_: (s + first, w, 0, 0, 0)),
                pl.BlockSpec((OWN, HALF), lambda *_: (0, side), pipeline_mode=pl.Buffered(1)),
                whole((NWIN * 32, PAIR)),
                whole((GREL, 128)),
                whole((GREL, 128)),
                whole((32, KEYS)),
            ]
            + [pl.BlockSpec(memory_space=pl.ANY)] * len(d_in),
            out_specs=[
                pl.BlockSpec((1, 1, SLOTS, TRIO), lambda s, w, *_: (s + first, w, 0, side)),
                pl.BlockSpec((GREL, 128), lambda s, w, *_: (0, 0)),
                pl.BlockSpec((8, TRIO), lambda s, w, *_: (0, 0)),
            ],
            scratch_shapes=[pltpu.VMEM((NWIN, SLOTS, HALF), BF), pltpu.VMEM((HALF, SLOTS), BF)],
        ),
        out_shape=[
            jax.ShapeDtypeStruct((3, NWIN, SLOTS, 2 * TRIO), BF),
            jax.ShapeDtypeStruct((GREL, 128), F32),
            jax.ShapeDtypeStruct((8, TRIO), F32),
        ],
        input_output_aliases={8: 0} if d_in else {},
        compiler_params=params(),
        cost_estimate=cost(20e9 * share, 45e6 * share),
    )(spot, qkv, p, ctx_grad, spread, rel_even, rel_odd, fold, *d_in)


def norm_grad_kernel(d, weights_own, spot, mine, theirs, gather, *refs):
    out, joined = refs[-2:]

    @pl.when((pl.program_id(0) == 0) & (pl.program_id(1) == 0))
    def _():
        for s in range(3):
            joined[:, s * HALF : s * HALF + HALF] = weights_own[s]
        join_pieces(spot[1], mine, theirs, joined, TRIO)

    rows = NWIN * 128
    total = dot(d[...].reshape(rows, 2 * TRIO), joined[...], NT).astype(BF).reshape(NWIN, 4, 32, D)
    for t in range(4):
        moved = dot(gather[...], total[:, t].reshape(NWIN * 32, D)).astype(BF)
        out[:, t * PAIR : t * PAIR + PAIR, :] = moved.reshape(1, PAIR, D)


def norm_grad(d, weights_own, core, mine, theirs, gather, bands, *before):
    first, last = bands
    share = (last - first) / 3
    block = pl.BlockSpec((1, NWIN, 128, 2 * TRIO), lambda s, t: (s + first, 0, t, 0))
    return pl.pallas_call(
        norm_grad_kernel,
        grid=(last - first, 2),
        in_specs=[block, whole((3, D, HALF)), SCALAR]
        + [whole((3, HALF, HALF)), whole((3, HALF, HALF)), whole((PAIR, NWIN * 32))]
        + [pl.BlockSpec(memory_space=pl.ANY)] * len(before),
        out_specs=pl.BlockSpec((1, 4 * PAIR, D), lambda s, t: (s + first, t, 0)),
        out_shape=jax.ShapeDtypeStruct((3, 8 * PAIR, D), BF),
        input_output_aliases={6: 0} if before else {},
        scratch_shapes=[pltpu.VMEM((D, 2 * TRIO), BF)],
        compiler_params=params(),
        cost_estimate=cost(14e9 * share, 30e6 * share),
    )(d, weights_own, core, mine, theirs, gather, *before)


def qkv_grad_kernel(spot, xt, d, proj, kept, sent, total):
    step = pl.program_id(0)
    for col in range(0, TRIO, 256):
        cols = slice(col, min(col + 256, TRIO))
        part = dot(xt[...], d[:, cols])
        total[:, cols] = jnp.where(step == 0, part, total[:, cols] + part)

    @pl.when(step == pl.num_programs(0) - 1)
    def _():
        first = spot[1] == 0
        values = [total[:, s * HALF : s * HALF + HALF].astype(BF) for s in range(3)] + [proj[...]]
        for k in range(2):
            kept[k] = jnp.where(first, values[k], values[2 + k])
            sent[k] = jnp.where(first, values[2 + k], values[k])


def qkv_grad(core, xt, d, side, proj):
    rows = NWIN * SLOTS
    block = pl.BlockSpec((2, D, HALF), lambda i: (0, 0, 0))
    shape = jax.ShapeDtypeStruct((2, D, HALF), BF)
    return pl.pallas_call(
        qkv_grad_kernel,
        grid=(3,),
        in_specs=[
            SCALAR,
            pl.BlockSpec((D, rows), lambda i: (0, i)),
            pl.BlockSpec((rows, TRIO), lambda i: (i, side)),
            whole((D, HALF)),
        ],
        out_specs=[block, block],
        out_shape=[shape, shape],
        scratch_shapes=[pltpu.VMEM((D, TRIO), F32)],
        compiler_params=params(),
        cost_estimate=cost(7e9, 16e6),
    )(core, xt, d.reshape(3 * rows, 2 * TRIO), proj)


EARLY = 3


def input_kernel(
    spot, x, middle_grad, up_a, up_b, early_a, early_b, late_a, late_b, gain,
    one_mine, one_theirs, two_mine, two_theirs, out, sums, one_out, two_out,
):
    step = pl.program_id(0)
    first = spot[1] == 0
    mine, theirs = one_mine[...].astype(F32), one_theirs[...].astype(F32)
    one_out[0] = jnp.where(first, mine, theirs)
    one_out[1] = jnp.where(first, theirs, mine)
    mine, theirs = two_mine[...].astype(F32), two_theirs[...].astype(F32)
    two_out[:, 0:HALF] = jnp.where(first, mine, theirs)
    two_out[:, HALF:] = jnp.where(first, theirs, mine)

    @pl.when(step == 0)
    def _():
        sums[...] = jnp.zeros_like(sums)

    for k, (up, early, late) in enumerate(((up_a, early_a, late_a), (up_b, early_b, late_b))):
        rows = slice(k * PAIR, k * PAIR + PAIR)
        scaled, inverse = norm_parts(x[rows, :].astype(F32))
        at, some = taken_pair(spot[0], 2 * step + k)
        shared = jnp.where(at < EARLY, early[...].astype(F32), late[...].astype(F32)) * some.astype(F32)
        upstream = up[0].astype(F32) + shared
        scaled_up = upstream * vec(gain)
        mean = jnp.mean(scaled_up, axis=-1, keepdims=True)
        second = jnp.mean(scaled_up * scaled, axis=-1, keepdims=True)
        out[rows, :] = (middle_grad[rows, :].astype(F32) + inverse * (scaled_up - mean - scaled * second)).astype(BF)
        add_row(sums, 0, upstream * scaled)
        add_row(sums, 1, upstream)


def input_of(spot, x, middle_grad, up, early, late, gain, ones, twos):
    rows = 2 * PAIR
    row_block = pl.BlockSpec((rows, D), lambda i, *_: (i, 0))
    up_at = lambda k: lambda i, spot: band_step(spot[0], 2 * i + k) + (0,)
    early_at = lambda k: lambda i, spot: (jnp.minimum(taken_pair(spot[0], 2 * i + k)[0], EARLY - 1), 0)
    late_at = lambda k: lambda i, spot: (jnp.maximum(taken_pair(spot[0], 2 * i + k)[0] - EARLY, 0), 0)
    steps = OWN // rows
    one_rows, two_rows = HALF // steps, FF // 2 // steps
    return pl.pallas_call(
        input_kernel,
        grid_spec=pltpu.PrefetchScalarGridSpec(
            num_scalar_prefetch=1,
            grid=(steps,),
            in_specs=[
                pl.BlockSpec((rows, D), lambda i, spot: (spot[0] * steps + i, 0)),
                row_block,
                pl.BlockSpec((1, PAIR, D), up_at(0)),
                pl.BlockSpec((1, PAIR, D), up_at(1)),
                pl.BlockSpec((PAIR, D), early_at(0)),
                pl.BlockSpec((PAIR, D), early_at(1)),
                pl.BlockSpec((PAIR, D), late_at(0)),
                pl.BlockSpec((PAIR, D), late_at(1)),
                whole((D,)),
            ]
            + [pl.BlockSpec((one_rows, FF // 2), lambda i, *_: (i, 0))] * 2
            + [pl.BlockSpec((two_rows, HALF), lambda i, *_: (i, 0))] * 2,
            out_specs=[
                row_block,
                pl.BlockSpec((8, D), lambda i, *_: (0, 0)),
                pl.BlockSpec((2, one_rows, FF // 2), lambda i, *_: (0, i, 0)),
                pl.BlockSpec((two_rows, D), lambda i, *_: (i, 0)),
            ],
        ),
        out_shape=[
            jax.ShapeDtypeStruct((OWN, D), BF),
            jax.ShapeDtypeStruct((8, D), F32),
            jax.ShapeDtypeStruct((2, HALF, FF // 2), F32),
            jax.ShapeDtypeStruct((FF // 2, D), F32),
        ],
        compiler_params=params(),
        cost_estimate=cost(1e8, 35e6),
    )(spot, x, middle_grad, up, up, early, early, late, late, gain, *ones, *twos)


MESH = pl.DeviceIdType.MESH
SMALL = 24


def bits_of(size):
    return size.bit_length() - 1


def line_plan(order, rows):
    plan, doubles = [], [("double", order[0], rows)]
    for bit in order[1:]:
        if rows % 32 == 0:
            doubles.append(("double", bit, rows))
            rows //= 2
            plan.append(("halve", bit, rows))
        else:
            plan.append(("both", bit, rows))
    return plan + doubles[::-1]


PARTS = 2
PART_ROWS = D // 2 // PARTS


def last_kernel(bits, plans, orders, *refs):
    (line_a, line_b, one_sums, two_sums, fc1_sums, sums_a, sums_c, sums_b) = refs[:8]
    rel_a, rel_b, rel_c, hots, out, small, rel = refs[8:15]
    small_landed, rel_landed, sends, recvs = refs[15:19]
    rooms = list(refs[19:])
    dp, mp = lax.axis_index("dp"), lax.axis_index("mp")
    bit_at = lambda bit: mp if bit == 0 else (dp // bit) % 2

    def partner(bit):
        if bit == 0:
            return (dp, 1 - mp)
        return (jnp.where(bit_at(bit) == 0, dp + bit, dp - bit), mp)

    barrier = pltpu.get_barrier_semaphore()
    every = [1] + bits + [0]
    for bit in every:
        pl.semaphore_signal(barrier, inc=1, device_id=partner(bit), device_id_type=MESH)

    count = [0]

    def send(src, dst, bit):
        at = count[0]
        count[0] += 1
        copy = pltpu.make_async_remote_copy(
            src_ref=src,
            dst_ref=dst,
            send_sem=sends.at[at],
            recv_sem=recvs.at[at],
            device_id=partner(bit),
            device_id_type=MESH,
        )
        copy.start()
        return copy

    def line(k, part):
        order, value = orders[k], (line_a, line_b)[k].at[pl.ds(part * PART_ROWS, PART_ROWS)]
        slot = dp % 2 * 2 + k
        first = bit_at(order[0]) * (D // 2) + part * PART_ROWS
        start, size, placed = first, PART_ROWS, False
        for kind, bit, after in plans[k]:
            if kind == "double":
                here = pl.ds(pl.multiple_of(start, 16), size)
                if not placed:
                    out[slot, here, :] = value[...]
                    placed = True
                copy = send(out.at[slot, here], out.at[slot, here], bit)
                yield
                copy.wait()
                if after != size or bit != order[0]:
                    start, size = start - bit_at(bit) * size, 2 * size
                continue
            mine = bit_at(bit) if kind == "halve" else 0
            gone = 1 - mine if kind == "halve" else 0
            room, total = rooms.pop(0), rooms.pop(0)
            copy = send(value.at[pl.ds(pl.multiple_of(gone * after, 16), after)], room, bit)
            yield
            copy.wait()
            rows = pl.ds(pl.multiple_of(mine * after, 16), after)
            total[...] = (value[rows, :].astype(F32) + room[...].astype(F32)).astype(BF)
            value = total
            start, size = start + mine * after, after
        copies = []
        for half in range(2):
            rows = pl.ds(half * (D // 2) + part * PART_ROWS, PART_ROWS)
            copies.append(send(out.at[slot, rows], out.at[slot, rows], 1))
        yield
        for copy in copies:
            copy.wait()

    def vectors():
        for at, bit in enumerate(bits + [0, 1]):
            copies = [send(small, small_landed.at[at], bit), send(rel, rel_landed.at[at], bit)]
            yield
            for copy in copies:
                copy.wait()
            small[...] += small_landed[at]
            rel[...] += rel_landed[at]

    lines = [line(k, part) for part in range(PARTS) for k in range(2)]
    pl.semaphore_wait(barrier, len(every))
    for one in lines:
        next(one)

    small[...] = jnp.zeros_like(small)
    small[0:2, :] = one_sums[0:2, :]
    small[2:6, :] = two_sums[0:4, :]
    first = mp == 0
    own = [sums_a[0:1, :] + sums_c[0:1, :], fc1_sums[0:1, 0 : FF // 2]]
    other = [sums_b[0:1, :], fc1_sums[0:1, FF // 2 :]]
    for row, flip in ((6, False), (9, True)):
        picked = [jnp.where(first != flip, a, b) for a, b in zip(own, other)]
        small[row : row + 1, 0:HALF] = picked[0][:, 0:HALF]
        small[row : row + 1, HALF:] = picked[0][:, 2 * HALF :]
        small[row + 1 : row + 2, :] = picked[1][:, 0:D]
        small[row + 2 : row + 3, :] = picked[1][:, D:]
    table = rel_a[...] + rel_b[...] + rel_c[...]
    table = lax.dot_general(hots[...], table, TN, precision=lax.Precision.HIGHEST, preferred_element_type=F32)
    rel[...] = table + pltpu.roll(table, HD, 1)

    active = lines + [vectors()]
    while active:
        for one in list(active):
            if next(one, "end") == "end":
                active.remove(one)


def last_sums(bits, orders, lines, sums, rels, hots):
    vmem = pl.BlockSpec(memory_space=pltpu.VMEM)
    rounds = len(bits) + 2
    copies = 2 * rounds + 2 * PARTS * (2 * len(bits) + 2)
    plans = [line_plan(order, PART_ROWS) for order in orders]
    rooms = []
    for at in range(len(plans[0])):
        for part in range(PARTS):
            for plan in plans:
                if plan[at][0] != "double":
                    rooms += [pltpu.VMEM((plan[at][2], HALF), BF)] * 2
    return pl.pallas_call(
        lambda *refs: last_kernel(bits, plans, orders, *refs),
        in_specs=[vmem] * (2 + len(sums) + len(rels) + 1),
        out_specs=[vmem] * 3,
        out_shape=[
            jax.ShapeDtypeStruct((4, D, HALF), BF),
            jax.ShapeDtypeStruct((SMALL, D), F32),
            jax.ShapeDtypeStruct((56, 128), F32),
        ],
        scratch_shapes=[
            pltpu.VMEM((rounds, SMALL, D), F32),
            pltpu.VMEM((rounds, 56, 128), F32),
            pltpu.SemaphoreType.DMA((copies,)),
            pltpu.SemaphoreType.DMA((copies,)),
        ]
        + rooms,
        compiler_params=pltpu.CompilerParams(
            collective_id=0, has_side_effects=True, vmem_limit_bytes=40 * 2**20
        ),
    )(*lines, *sums, *rels, hots)


CORE, PAIRED = 1, 0


def bit_of(bit):
    return lax.axis_index("mp") if bit == PAIRED else (lax.axis_index("dp") // bit) % 2


def exchange(value, bit):
    if bit == PAIRED:
        return lax.ppermute(value, "mp", [(0, 1), (1, 0)])
    return lax.ppermute(value, "dp", [(i, i ^ bit) for i in range(lax.axis_size("dp"))])


class Line:
    def __init__(self, value, places, rank, steps, sent=None):
        self.terms = [(value, tuple(places))]
        self.fixed = {}
        self.rank = list(rank)
        self.steps = list(steps)
        self.sent, self.taken = sent, None
        self.value = None

    def part(self, changes):
        fixed = {**self.fixed, **changes}
        total = None
        for term, places in self.terms:
            starts, sizes, shape = [], [], []
            for bit in places:
                starts.append(fixed.get(bit, 0))
                sizes.append(1 if bit in fixed else 2)
                if bit not in fixed:
                    shape.append(2)
            rest = term.shape[len(places) :]
            if places:
                starts = [jnp.asarray(at, jnp.int32) for at in starts + [0] * len(rest)]
                term = lax.dynamic_slice(term, starts, tuple(sizes) + rest).reshape(tuple(shape) + rest)
            total = term.astype(F32) if total is None else total + term.astype(F32)
        return total.astype(BF)

    def prepare(self):
        kind, bit = self.steps[0]
        if kind == "halve":
            mine = 0 if bit == PAIRED else bit_of(bit)
            self.sent = self.part({bit: 1 - mine})
            self.fixed[bit] = mine
        elif kind == "double":
            if self.value is None:
                self.value, self.done = self.part({}), []
            self.sent = self.value
        elif kind == "pass":
            self.sent = self.part({})

    def launch(self):
        self.taken = exchange(self.sent, self.steps[0][1])

    def land(self):
        kind, bit = self.steps.pop(0)
        if kind in ("halve", "give"):
            places = [p for p in self.terms[0][1] if p not in self.fixed]
            self.terms.append((self.taken, tuple(places)))
        elif kind == "pass":
            self.terms = [(self.taken, tuple(p for p in self.terms[0][1] if p not in self.fixed))]
        else:
            if not self.steps:
                self.value, self.taken_last, self.taken = self.sent, self.taken, None
                return
            self.done = sorted(self.done + [bit], key=self.rank.index)
            axis = self.done.index(bit)
            shape = [1] * (self.value.ndim + 1)
            shape[axis] = 2
            mine = jnp.arange(2).reshape(shape) == bit_of(bit)
            wide = lambda v: jnp.expand_dims(v, axis)
            self.value = jnp.where(mine, wide(self.sent), wide(self.taken))
        self.taken = None


def advance(anchor, lines):
    flying = [line for line in lines if line.taken is not None]
    anchor, taken = lax.optimization_barrier((anchor, [line.taken for line in flying]))
    for line, value in zip(flying, taken):
        line.taken = value
        line.land()
    going = [line for line in lines if line.steps]
    for line in going:
        line.prepare()
    anchor, sent = lax.optimization_barrier((anchor, [line.sent for line in going]))
    for line, value in zip(going, sent):
        line.sent = value
        line.launch()
    return anchor


def finish(lines):
    while any(line.steps for line in lines):
        for line in lines:
            if not line.steps:
                continue
            if line.taken is None:
                line.prepare()
                line.launch()
        for line in lines:
            if line.taken is not None:
                line.land()


def on_device(
    image_tokens,
    norm1_gain,
    norm1_shift,
    qkv_weight,
    qv_bias,
    rel_rows,
    rel_cols,
    proj_weight,
    proj_bias,
    norm2_gain,
    norm2_shift,
    fc1_weight,
    fc1_bias,
    fc2_weight,
    fc2_bias,
    out_cotangent,
):
    place = lax.axis_index("mp")
    core = lax.axis_index("dp") % 2
    swap = lambda value: lax.ppermute(value, "mp", [(0, 1), (1, 0)])
    size = lax.axis_size("dp")
    core_swap = lambda value: lax.ppermute(value, "dp", [(i, i ^ 1) for i in range(size)])

    def by_core(weight, axis, mine):
        return lax.dynamic_slice_in_dim(weight, (core if mine else 1 - core) * HALF, HALF, axis)

    spot = jnp.stack([place, core]).astype(jnp.int32)
    spread = jnp.asarray(spread_rows(), BF)
    gather = jnp.asarray(spread_rows().T, BF)
    fold = jnp.asarray(fold_table(), BF)
    high_hot, wide_hot = rel_onehots()
    hots = jnp.asarray(np.pad(np.concatenate([high_hot, wide_hot], axis=1), ((0, 0), (0, 2))), F32)
    high_hot, wide_hot = jnp.asarray(high_hot, BF), jnp.asarray(wide_hot, BF)
    qkv_mine = swap(by_core(qkv_weight, 1, True))
    bias_other = swap(qv_bias)
    fc1_bias_other = swap(fc1_bias)
    x_windows = windows_of(spot, image_tokens, norm1_gain, norm1_shift, spread)
    cot_t = turned_of(out_cotangent)
    x_windows, cot_t, qkv_mine = lax.optimization_barrier((x_windows, cot_t, qkv_mine))
    late = (by_core(fc1_weight, 0, True), by_core(fc2_weight, 1, True), proj_weight)
    x_windows, qkv_mine, late = lax.optimization_barrier((x_windows, qkv_mine, late))
    qkv_theirs = exchange(qkv_mine, CORE)
    one_mine, two_mine, proj_other = (swap(w) for w in late)
    qkv_a, p_a, ctx_a, xt, rel_even, rel_odd = attend(
        x_windows, qv_bias, True, qkv_weight, high_hot, wide_hot, rel_rows, rel_cols
    )
    qkv_b, p_b, ctx_b = attend(
        x_windows, bias_other, False, spot, qkv_mine, qkv_theirs, rel_even, rel_odd
    )
    ctx_b, one_mine, two_mine, proj_other = lax.optimization_barrier((ctx_b, one_mine, two_mine, proj_other))
    one_theirs, two_theirs = exchange(one_mine, CORE), exchange(two_mine, CORE)
    middle, normed, normed_t, context = middle_of(
        spot, ctx_a, ctx_b, image_tokens, proj_weight, proj_other, proj_bias, norm2_gain, norm2_shift, gather
    )
    forward, back, one_kept, one_sent, two_kept, two_sent, fc1_sums = feed(
        spot, normed, normed_t, out_cotangent, cot_t, fc1_weight, (one_mine, one_theirs), fc1_bias,
        fc1_bias_other, fc2_weight, (two_mine, two_theirs),
    )
    bits = [2**k for k in range(1, bits_of(size))]
    turned = bits[1:2] + bits[0:1] + bits[2:]
    halves = lambda order: [("halve", bit) for bit in order]
    doubles = lambda order: [("double", bit) for bit in order]

    def cut(value, axis, places):
        shape = value.shape[:axis] + (2,) * len(places) + (value.shape[axis] // 2 ** len(places),)
        return value.reshape(shape + value.shape[axis + 1 :])

    def feed_line(kept, sent, order, back):
        steps = [("give", CORE)] + halves(order) + doubles(back) + [("double", CORE)]
        rank = [CORE] + bits
        return Line(cut(kept, 1, bits), [PAIRED] + bits, rank, steps, cut(sent, 1, bits))

    one_line = feed_line(one_kept, one_sent, [PAIRED] + bits, bits[::-1])
    two_line = feed_line(two_kept, two_sent, bits[:2] + [PAIRED] + bits[2:], turned[::-1])
    feed_lines = [one_line, two_line]

    middle = advance(middle, feed_lines)
    block_out, middle_grad, ctx_grad, proj_own, proj_oth, two_sums = resid_of(
        middle, forward, back, out_cotangent, context, proj_weight, proj_other, fc2_bias, norm2_gain
    )
    back_of = lambda qkv, p, side, grad, bands, *d: attend_back(
        spot, qkv, p, grad, side, spread, rel_even, rel_odd, fold, bands, *d
    )
    ctx_grad = advance(ctx_grad, feed_lines)
    d, rel_b, sums_b = back_of(qkv_b, p_b, 1, ctx_grad, (0, 3))
    d = advance(d, feed_lines)
    kept_b, sent_b = qkv_grad(spot, xt, d, 1, proj_oth)
    line_b = Line(kept_b, [], [], [("give", CORE)], sent_b)
    lines = feed_lines + [line_b]
    ctx_grad, kept_b, d = lax.optimization_barrier((ctx_grad, kept_b, d))
    ctx_grad = advance(ctx_grad, lines)
    d, rel_a0, sums_a0 = back_of(qkv_a, p_a, 0, ctx_grad, (0, 1), d)
    d = advance(d, lines)
    passes = []
    for k in range(2):
        line = Line(None, [], [], [("pass", PAIRED)])
        line.terms = [(term[k], ()) for term, _ in line_b.terms]
        passes.append(line)
    d = advance(d, passes[:1])
    d, rel_a, sums_a = back_of(qkv_a, p_a, 0, ctx_grad, (1, 3), d)
    d = advance(d, feed_lines + passes[:1])
    d = advance(d, passes[1:])
    up = norm_grad(d, qkv_weight, spot, qkv_mine, qkv_theirs, gather, (1, 3))
    at = [2 - place, (1 - place) * 4 * SIDE, jnp.zeros_like(place)]
    shares = []
    for first, count in ((0, 2 * EARLY), (2 * EARLY, 10 - 2 * EARLY)):
        start = [at[0], at[1] + first * SIDE, at[2]]
        part = lax.dynamic_slice(up, start, (1, count * SIDE, D)).reshape(count * SIDE, D)
        shares.append(Line(part, [], [], [("pass", PAIRED)]))
    d = advance(d, feed_lines + passes[1:])
    d = advance(d, shares[:1])
    kept_a, sent_a = qkv_grad(spot, xt, d, 0, proj_own)
    line_a = Line(kept_a, [], [], [("give", CORE)], sent_a)
    kept_a, d = lax.optimization_barrier((kept_a, d))
    d = advance(d, feed_lines + [line_a] + shares[:1])
    d = advance(d, shares[1:])
    up = norm_grad(d, qkv_weight, spot, qkv_mine, qkv_theirs, gather, (0, 1), up)
    up = advance(up, feed_lines + [line_a] + shares[1:])
    early, late = (line.terms[0][0] for line in shares)
    q_lines = []
    for k, order in enumerate((bits, turned)):
        line = Line(None, [], [], halves(order[:1]))
        line.terms = [(part.reshape(2, 2, D // 2, HALF), ("line", order[0])) for part, _ in line_a.terms]
        line.terms += [(part.reshape(2, D // 2, HALF), (order[0],)) for part, _ in passes[k].terms]
        line.fixed = {"line": k}
        q_lines.append(line)
    up = advance(up, q_lines)
    finish(feed_lines)
    flat = lambda line, rows: (line.value.reshape(rows, -1), line.taken_last.reshape(rows, -1))
    input_grad, one_sums, one_sum, two_sum = input_of(
        spot, image_tokens, middle_grad, up, early, late, norm1_gain, flat(one_line, HALF), flat(two_line, FF // 2)
    )
    one_sums = advance(one_sums, q_lines)
    four, small, rel = last_sums(
        bits,
        [bits, turned],
        [line.part({}) for line in q_lines],
        [one_sums, two_sums, fc1_sums, sums_a, sums_a0, sums_b],
        [rel_a, rel_a0, rel_b],
        hots,
    )
    one_sum = one_sum.reshape(D, FF // 2)
    mine = jnp.where(place == 0, small[6:9], small[9:12])
    return (
        block_out,
        input_grad,
        small[0],
        small[1],
        four[0:3].astype(F32),
        mine[0].reshape(2, HALF),
        rel[:RELS, :HD],
        rel[RELS : 2 * RELS, :HD],
        jnp.concatenate([four[3, :HALF], four[3, HALF:]], axis=1).astype(F32),
        small[5],
        small[2],
        small[3],
        one_sum,
        mine[1:3].reshape(-1),
        two_sum,
        small[4],
    )


def solution(mesh):
    in_specs = (
        P("dp", None),
        P(),
        P(),
        P(None, None, "mp"),
        P(None, "mp"),
        P(),
        P(),
        P("mp", None),
        P(),
        P(),
        P(),
        P(None, "mp"),
        P("mp"),
        P("mp", None),
        P(),
        P(("dp", "mp"), None),
    )
    out_specs = (
        P(("dp", "mp"), None),
        P(("dp", "mp"), None),
        P(),
        P(),
        P(None, None, "mp"),
        P(None, "mp"),
        P(),
        P(),
        P("mp", None),
        P(),
        P(),
        P(),
        P(None, "mp"),
        P("mp"),
        P("mp", None),
        P(),
    )
    return jax.shard_map(
        on_device, mesh=mesh, in_specs=in_specs, out_specs=out_specs, check_vma=False
    )
```

```python
import jax
import jax.numpy as jnp
import numpy as np
from jax import lax
from jax.experimental import pallas as pl
from jax.experimental.pallas import tpu as pltpu
from jax.sharding import PartitionSpec as P

D = 768
HEADS = 12
HD = 64
FF = 3072
WIN = 14
SIDE = 64
NWIN = 5
RELS = 27
EPSILON = 1e-06
F32 = jnp.float32
BF = jnp.bfloat16

SLOTS = 256
KEYS = WIN * 16
PAIR = 2 * SIDE
GREL = 80
OWN = SIDE * SIDE // 2

HALF = D // 2
TRIO = 3 * HALF
PAIRS = HEADS // 4

NN = (((1,), (0,)), ((), ()))
NT = (((1,), (1,)), ((), ()))
TN = (((0,), (0,)), ((), ()))


def dot(left, right, dims=NN):
    return lax.dot_general(left, right, dims, preferred_element_type=F32)


def params(limit=60):
    return pltpu.CompilerParams(vmem_limit_bytes=limit * 2**20)


def cost(flops, moved, exps=0):
    return pl.CostEstimate(flops=int(flops), bytes_accessed=int(moved), transcendentals=int(exps))


def whole(shape):
    return pl.BlockSpec(shape, lambda *_: (0,) * len(shape), pipeline_mode=pl.Buffered(1))


def band_start(place, band):
    return (1 - place) * (14 * band) + place * (42 - 14 * band + 21 * band * (band - 1))


def image_pair(place, band, step):
    pair = band_start(place, band) // 2 + step
    return jnp.minimum(pair, SIDE // 2 - 1), pair < SIDE // 2


def owned_pair(place, band, step):
    pair = band_start(place, band) // 2 + step - 16 * place
    return jnp.clip(pair, 0, 15), (pair >= 0) & (pair < 16)


def band_step(place, pair):
    first = pair // 7, pair % 7
    band = jnp.where(pair < 5, 1, jnp.where(pair < 12, 0, 2))
    second = band, jnp.where(pair < 5, pair + 2, jnp.where(pair < 12, pair - 5, pair - 12))
    return tuple(jnp.where(place == 0, a, b) for a, b in zip(first, second))


def taken_pair(place, pair):
    return (
        jnp.where(place == 0, jnp.maximum(pair - 14, 0), jnp.minimum(pair, 4)),
        jnp.where(place == 0, pair >= 14, pair < 5),
    )


def spread_rows():
    table = np.zeros((NWIN, 2, 16, PAIR), np.float32)
    for w in range(NWIN):
        for r in range(2):
            for j in range(WIN):
                if WIN * w + j < SIDE:
                    table[w, r, j, r * SIDE + WIN * w + j] = 1
    return table.reshape(NWIN * 32, PAIR)


def rel_order():
    rows = np.full(GREL, -1)
    for m in range(21):
        rows[m] = 26 - (m + 6)
        rows[24 + m] = 26 - m
    cols = np.full(GREL, -1)
    for m in range(RELS):
        cols[48 + m] = 26 - m
    return rows, cols


def rel_onehots():
    rows, cols = rel_order()
    high = (rows[:, None] == np.arange(RELS)[None, :]).astype(np.float32)
    wide = (cols[:, None] == np.arange(RELS)[None, :]).astype(np.float32)
    return high, wide


def norm_parts(values):
    average = jnp.mean(values, axis=-1, keepdims=True)
    centred = values - average
    inverse = lax.rsqrt(jnp.mean(centred * centred, axis=-1, keepdims=True) + EPSILON)
    return centred * inverse, inverse


def vec(ref):
    return ref[...].astype(F32).reshape(1, D)


def window_kernel(spot, *refs):
    xs, (gain, shift, spread, out) = refs[:7], refs[7:]
    band = pl.program_id(0)
    for t in range(7):
        scaled, _ = norm_parts(xs[t][...].astype(F32))
        normed = scaled * vec(gain) + vec(shift)
        valid = image_pair(spot[0], band, t)[1]
        normed = (normed * valid.astype(F32)).astype(BF)
        moved = dot(spread[...], normed).astype(BF)
        out[:, :, 32 * t : 32 * t + 32, :] = moved.reshape(1, NWIN, 32, D)
    out[:, :, 224:, :] = jnp.zeros((1, NWIN, 32, D), BF)


def windows_of(spot, x, gain, shift, spread):
    at = lambda t: lambda s, spot: (image_pair(spot[0], s, t)[0], 0)
    return pl.pallas_call(
        window_kernel,
        grid_spec=pltpu.PrefetchScalarGridSpec(
            num_scalar_prefetch=1,
            grid=(3,),
            in_specs=[pl.BlockSpec((PAIR, D), at(t)) for t in range(7)]
            + [whole((D,)), whole((D,)), whole((NWIN * 32, PAIR))],
            out_specs=pl.BlockSpec((1, NWIN, SLOTS, D), lambda s, *_: (s, 0, 0, 0)),
        ),
        out_shape=jax.ShapeDtypeStruct((3, NWIN, SLOTS, D), BF),
        compiler_params=params(),
        cost_estimate=cost(3 * 7 * 160 * 128 * 768 * 2, 10e6),
    )(spot, *([x] * 7), gain, shift, spread)


def shift_masks(lanes_from):
    lane = lax.broadcasted_iota(jnp.int32, (1, 128), 1) + lanes_from
    high = lane // 16
    row_shift = jnp.where(lane < 128, 7 - high, jnp.maximum(13 - high, 0))
    col_shift = jnp.maximum(13 - lane % 16, 0)
    return row_shift, col_shift


def skew(table, shift, bits):
    size = table.shape[0]
    for bit in bits:
        moved = pltpu.roll(table, size - bit, 0)
        table = jnp.where((shift & bit) != 0, moved, table)
    return table


def unskew(table, shift, bits):
    for bit in bits:
        moved = pltpu.roll(table, bit, 0)
        table = jnp.where((shift & bit) != 0, moved, table)
    return table


def start_own(weights, bias, high_hot, wide_hot, rel_rows, rel_cols, rel_even, rel_odd, joined):
    for s in range(3):
        joined[:, s * HALF : s * HALF + HALF] = weights[s]
    table = (dot(high_hot[...], rel_rows[...]) + dot(wide_hot[...], rel_cols[...])).astype(BF)
    blank = jnp.zeros_like(table)
    rel_even[...] = jnp.concatenate([table, blank], axis=1)
    rel_odd[...] = jnp.concatenate([blank, table], axis=1)


def join_pieces(core, mine, theirs, joined, col):
    for piece, at in ((mine, core), (theirs, 1 - core)):
        rows = pl.ds(pl.multiple_of(at * HALF, HALF), HALF)
        for s in range(3):
            joined[rows, col + s * HALF : col + s * HALF + HALF] = piece[s]


def attend_own(
    x, bias, weights, high_hot, wide_hot, rel_rows, rel_cols,
    qkv_out, p_out, ctx_out, xt_out, rel_even, rel_odd, joined, vt,
):
    @pl.when((pl.program_id(0) == 0) & (pl.program_id(1) == 0))
    def _():
        start_own(weights, bias, high_hot, wide_hot, rel_rows, rel_cols, rel_even, rel_odd, joined)

    attend_window(x, bias, rel_even, rel_odd, qkv_out, p_out, ctx_out, xt_out, joined, vt)


def attend_other(x, bias, spot, mine, theirs, rel_even, rel_odd, qkv_out, p_out, ctx_out, joined, vt):
    @pl.when((pl.program_id(0) == 0) & (pl.program_id(1) == 0))
    def _():
        join_pieces(spot[1], mine, theirs, joined, 0)

    attend_window(x, bias, rel_even, rel_odd, qkv_out, p_out, ctx_out, None, joined, vt)


def attend_window(x, bias, rel_even, rel_odd, qkv_out, p_out, ctx_out, xt_out, joined, vt):
    band = pl.program_id(0)
    biases = bias[...].astype(F32)
    biases = jnp.concatenate([biases[0:1], jnp.zeros((1, HALF), F32), biases[1:2]], axis=1)
    block = x[...].reshape(SLOTS, D)
    if xt_out is not None:
        xt_out[...] = block.T
    scales = jnp.where(lax.broadcasted_iota(jnp.int32, (1, TRIO), 1) // HALF == 1, HD ** (-0.5), 1.0)
    low = ((dot(block, joined[...]) + biases) * scales).astype(BF)
    qkv_out[0, 0] = low
    vt[...] = low[:, 2 * HALF :].T

    even = lax.broadcasted_iota(jnp.int32, (1, 128), 1) < HD

    def raw_scores(head, lanes):
        col = head // 2 * 128
        keys = qkv_out[0, 0, 0:KEYS, HALF + col : HALF + col + 128]
        kept = jnp.where(even != (head % 2 == 1), keys, jnp.zeros_like(keys))
        rel = rel_odd if head % 2 else rel_even
        left = jnp.concatenate([kept, rel[...]], axis=0)
        return dot(left, qkv_out[0, 0, 0:lanes, col : col + 128], NT)

    def soft(head, raw, lanes):
        parts = []
        for tile in range(lanes // 128):
            row_shift, col_shift = shift_masks(tile * 128)
            raw_t = raw[:, tile * 128 : tile * 128 + 128]
            base = raw_t[0:KEYS]
            high = skew(raw_t[KEYS + 24 * tile : KEYS + 24 * tile + 24], row_shift, (4, 2, 1))[0:16]
            wide = skew(raw_t[KEYS + 48 : KEYS + 80], col_shift, (8, 4, 2, 1))[0:16]
            place = lax.broadcasted_iota(jnp.int32, (16, 128), 0)
            wide = jnp.where(place < WIN, wide, -1e30)
            scores = base.reshape(WIN, 16, 128) + wide[None] + high[0:WIN][:, None, :]
            scores = scores.reshape(KEYS, 128)
            peak = jnp.max(scores, axis=0, keepdims=True)
            grown = jnp.exp(scores - peak)
            total = jnp.sum(grown, axis=0, keepdims=True)
            parts.append((grown * (1.0 / total)).astype(BF))
        probs = parts[0] if len(parts) == 1 else jnp.concatenate(parts, axis=1)
        p_out[0, 0, head, :, 0:lanes] = probs
        return probs

    def all_heads(lanes):
        count = HEADS // 2
        raw = raw_scores(0, lanes)
        contexts = []
        for head in range(count):
            ahead = raw_scores(head + 1, lanes) if head + 1 < count else None
            probs = soft(head, raw, lanes)
            if head:
                contexts.append(dot(vt[(head - 1) * HD : head * HD, 0:KEYS], before).astype(BF))
            if head and head % 2 == 0:
                col = (head - 2) * HD
                ctx_out[0, 0, 0:lanes, col : col + 128] = jnp.concatenate(contexts[-2:], axis=0).T
            before, raw = probs, ahead
        contexts.append(dot(vt[(count - 1) * HD :, 0:KEYS], before).astype(BF))
        ctx_out[0, 0, 0:lanes, HALF - 128 :] = jnp.concatenate(contexts[-2:], axis=0).T

    @pl.when(band < 2)
    def _():
        all_heads(256)

    @pl.when(band == 2)
    def _():
        all_heads(128)


SCALAR = pl.BlockSpec(memory_space=pltpu.SMEM)


def attend(x, bias, first, *operands):
    block = lambda width: pl.BlockSpec((1, 1, SLOTS, width), lambda s, w: (s, w, 0, 0))
    shape = lambda width: jax.ShapeDtypeStruct((3, NWIN, SLOTS, width), BF)
    out_specs = [
        block(TRIO),
        pl.BlockSpec((1, 1, HEADS // 2, KEYS, SLOTS), lambda s, w: (s, w, 0, 0, 0)),
        block(HALF),
    ]
    out_shape = [
        shape(TRIO),
        jax.ShapeDtypeStruct((3, NWIN, HEADS // 2, KEYS, SLOTS), BF),
        shape(HALF),
    ]
    rel = pl.BlockSpec((GREL, 128), lambda s, w: (0, 0))
    if first:
        in_specs = [whole((3, D, HALF)), whole((GREL, RELS)), whole((GREL, RELS)), whole((RELS, HD)), whole((RELS, HD))]
        out_specs += [pl.BlockSpec((D, SLOTS), lambda s, w: (0, s * NWIN + w)), rel, rel]
        out_shape += [jax.ShapeDtypeStruct((D, 3 * NWIN * SLOTS), BF)] + [jax.ShapeDtypeStruct((GREL, 128), BF)] * 2
    else:
        in_specs = [SCALAR, whole((3, HALF, HALF)), whole((3, HALF, HALF)), whole((GREL, 128)), whole((GREL, 128))]
    return pl.pallas_call(
        attend_own if first else attend_other,
        grid=(3, NWIN),
        in_specs=[block(D), whole((2, HALF))] + in_specs,
        out_specs=out_specs,
        out_shape=out_shape,
        scratch_shapes=[pltpu.VMEM((D, TRIO), BF), pltpu.VMEM((HALF, SLOTS), BF)],
        compiler_params=params(),
        cost_estimate=cost(15e9, 45e6, 4e6),
    )(x, bias, *operands)


def middle_kernel(
    spot, own_a, own_b, other_a, other_b, x, proj_own, proj_other, bias, gain, shift, gather,
    middle, normed, normed_t, ctx_out, proj,
):
    @pl.when(pl.program_id(0) == 0)
    def _():
        proj[0:HALF, :] = proj_own[...]
        proj[HALF:, :] = proj_other[...]

    for row, parts in ((0, (own_a, other_a)), (PAIR, (own_b, other_b))):
        for side in range(2):
            moved = dot(gather[...], parts[side][...].reshape(NWIN * 32, HALF)).astype(BF)
            ctx_out[row : row + PAIR, side * HALF : side * HALF + HALF] = moved
    value = x[...].astype(F32) + (dot(ctx_out[...], proj[...]) + vec(bias))
    middle[...] = value.astype(BF)
    scaled, _ = norm_parts(value)
    low = (scaled * vec(gain) + vec(shift)).astype(BF)
    normed[...] = low
    normed_t[...] = low.T


def middle_of(spot, ctx_own, ctx_other, x, proj_own, proj_other, bias, gain, shift, gather):
    rows = 2 * PAIR

    def at(k):
        def place(i, spot):
            band, step = band_step(spot[0], 2 * i + k)
            return band, 0, step, 0

        return pl.BlockSpec((1, NWIN, 32, HALF), place)

    row_block = pl.BlockSpec((rows, D), lambda i, *_: (i, 0))
    col_block = pl.BlockSpec((D, rows), lambda i, *_: (0, i))
    low = jax.ShapeDtypeStruct((OWN, D), BF)
    return pl.pallas_call(
        middle_kernel,
        grid_spec=pltpu.PrefetchScalarGridSpec(
            num_scalar_prefetch=1,
            grid=(OWN // rows,),
            in_specs=[
                at(0),
                at(1),
                at(0),
                at(1),
                pl.BlockSpec((rows, D), lambda i, spot: (spot[0] * (OWN // rows) + i, 0)),
                whole((HALF, D)),
                whole((HALF, D)),
                whole((D,)),
                whole((D,)),
                whole((D,)),
                whole((PAIR, NWIN * 32)),
            ],
            out_specs=[row_block, row_block, col_block, row_block],
            scratch_shapes=[pltpu.VMEM((D, D), BF)],
        ),
        out_shape=[low, low, jax.ShapeDtypeStruct((D, OWN), BF), low],
        compiler_params=params(),
        cost_estimate=cost(3e9, 25e6),
    )(spot, ctx_own, ctx_own, ctx_other, ctx_other, x, proj_own, proj_other, bias, gain, shift, gather)


def turn_kernel(value, out):
    out[...] = value[...].T


def turned_of(value):
    rows = 512
    return pl.pallas_call(
        turn_kernel,
        grid=(OWN // rows,),
        in_specs=[pl.BlockSpec((rows, D), lambda i: (i, 0))],
        out_specs=pl.BlockSpec((D, rows), lambda i: (0, i)),
        out_shape=jax.ShapeDtypeStruct((D, OWN), BF),
        compiler_params=params(),
        cost_estimate=cost(1e6, 6e6),
    )(value)


CHUNK = 512
CHUNKS = FF // CHUNK


def feed_kernel(
    spot, normed, normed_t, cot, cot_t, one_a, one_b, one_c, bias_a, bias_b, two_a, two_b, two_c,
    forward_out, back_out, one_kept, one_sent, two_kept, two_sent, sums,
    forward, back, one, two, bias, hidden, grads,
):
    step = pl.program_id(0)

    @pl.when(step == 0)
    def _():
        forward[...] = jnp.zeros_like(forward)
        back[...] = jnp.zeros_like(back)

    @pl.when(step < CHUNKS // 2)
    def _():
        bias[...] = bias_a[...].astype(F32).reshape(1, CHUNK)
        one[...] = one_a[...]
        two[...] = two_a[...]

    @pl.when(step >= CHUNKS // 2)
    def _():
        bias[...] = bias_b[...].astype(F32).reshape(1, CHUNK)
        mine = pl.multiple_of(spot[1] * HALF, HALF)
        theirs = pl.multiple_of((1 - spot[1]) * HALF, HALF)
        one[pl.ds(mine, HALF), :] = one_b[...]
        one[pl.ds(theirs, HALF), :] = one_c[...]
        two[:, pl.ds(mine, HALF)] = two_b[...]
        two[:, pl.ds(theirs, HALF)] = two_c[...]

    total = jnp.zeros((1, CHUNK), F32)
    def starts(t):
        rows = slice(t * 256, t * 256 + 256)
        return dot(normed[rows, :], one[...]), dot(cot[rows, :], two[...], NT)

    now = starts(0)
    for t in range(OWN // 256):
        rows = slice(t * 256, t * 256 + 256)
        ahead = starts(t + 1) if t + 1 < OWN // 256 else None
        pre = now[0] + bias[...]
        phi = 0.5 * (1.0 + lax.erf(pre * 0.7071067811865476))
        slope = phi + pre * (jnp.exp(-0.5 * pre * pre) * 0.3989422804014327)
        low = (pre * phi).astype(BF)
        grad = (now[1] * slope).astype(BF)
        hidden[rows, :] = low
        grads[rows, :] = grad
        total += jnp.sum(grad.astype(F32), axis=0, keepdims=True)
        if t:
            before = slice(t * 256 - 256, t * 256)
            forward[before, :] += dot(last[0], two[...])
            back[before, :] += dot(last[1], one[...], NT)
        last, now = (low, grad), ahead
    forward[OWN - 256 :, :] += dot(last[0], two[...])
    back[OWN - 256 :, :] += dot(last[1], one[...], NT)
    sums[...] = total

    first = spot[1] == 0
    one_grad = dot(normed_t[...], grads[...]).astype(BF)
    low, high = one_grad[:HALF], one_grad[HALF:]
    one_kept[0] = jnp.where(first, low, high)
    one_sent[0] = jnp.where(first, high, low)
    two_grad = dot(cot_t[...], hidden[...]).astype(BF)
    low, high = two_grad[:HALF], two_grad[HALF:]
    two_kept[0] = jnp.where(first, low, high).T
    two_sent[0] = jnp.where(first, high, low).T

    @pl.when(step == pl.num_programs(0) - 1)
    def _():
        forward_out[...] = forward[...].astype(BF)
        back_out[...] = back[...].astype(BF)


def feed(spot, normed, normed_t, cot, cot_t, one_a, ones, bias_a, bias_b, two_a, twos):
    half = CHUNKS // 2
    own = lambda j: jnp.minimum(j, half - 1)
    other = lambda j: jnp.maximum(j - half, 0)
    one_block = pl.BlockSpec((1, HALF, CHUNK), lambda j, *_: (j // half, 0, j % half))
    two_block = pl.BlockSpec((1, CHUNK, HALF), lambda j, *_: (j // half, j % half, 0))
    one_piece = pl.BlockSpec((HALF, CHUNK), lambda j, *_: (0, other(j)))
    two_piece = pl.BlockSpec((CHUNK, HALF), lambda j, *_: (other(j), 0))
    one_shape = jax.ShapeDtypeStruct((2, HALF, FF // 2), BF)
    two_shape = jax.ShapeDtypeStruct((2, FF // 2, HALF), BF)
    sum_block = pl.BlockSpec((OWN, D), lambda j, *_: (0, 0))
    bias_block = pl.BlockSpec((1, CHUNK), lambda j, *_: (0, j))
    return pl.pallas_call(
        feed_kernel,
        grid_spec=pltpu.PrefetchScalarGridSpec(
            num_scalar_prefetch=1,
            grid=(CHUNKS,),
            in_specs=[
                whole((OWN, D)),
                whole((D, OWN)),
                whole((OWN, D)),
                whole((D, OWN)),
                pl.BlockSpec((D, CHUNK), lambda j, *_: (0, own(j))),
                one_piece,
                one_piece,
                pl.BlockSpec((CHUNK,), lambda j, *_: (own(j),)),
                pl.BlockSpec((CHUNK,), lambda j, *_: (other(j),)),
                pl.BlockSpec((CHUNK, D), lambda j, *_: (own(j), 0)),
                two_piece,
                two_piece,
            ],
            out_specs=[sum_block, sum_block, one_block, one_block, two_block, two_block, bias_block],
            scratch_shapes=[
                pltpu.VMEM((OWN, D), F32),
                pltpu.VMEM((OWN, D), F32),
                pltpu.VMEM((D, CHUNK), BF),
                pltpu.VMEM((CHUNK, D), BF),
                pltpu.VMEM((1, CHUNK), F32),
                pltpu.VMEM((OWN, CHUNK), BF),
                pltpu.VMEM((OWN, CHUNK), BF),
            ],
        ),
        out_shape=[
            jax.ShapeDtypeStruct((OWN, D), BF),
            jax.ShapeDtypeStruct((OWN, D), BF),
            one_shape,
            one_shape,
            two_shape,
            two_shape,
            jax.ShapeDtypeStruct((1, FF), F32),
        ],
        compiler_params=params(62),
        cost_estimate=cost(58e9, 60e6, 12e6),
    )(spot, normed, normed_t, cot, cot_t, one_a, *ones, bias_a, bias_b, two_a, *twos)


def add_row(sums, row, values):
    sums[row : row + 1, :] += jnp.sum(values, axis=0, keepdims=True)


def resid_kernel(
    middle, forward, back, cot, context, proj_own, proj_other, bias, gain,
    block_out, grad_out, ctx_grad, grad_own, grad_other, sums, proj, proj_grad,
):
    step = pl.program_id(0)

    @pl.when(step == 0)
    def _():
        proj[0:HALF, :] = proj_own[...]
        proj[HALF:, :] = proj_other[...]
        proj_grad[...] = jnp.zeros_like(proj_grad)
        sums[...] = jnp.zeros_like(sums)

    value = middle[...].astype(F32)
    block_out[...] = (value + (forward[...].astype(F32) + vec(bias))).astype(BF)
    scaled, inverse = norm_parts(value)
    upstream = back[...].astype(F32)
    scaled_up = upstream * vec(gain)
    first = jnp.mean(scaled_up, axis=-1, keepdims=True)
    second = jnp.mean(scaled_up * scaled, axis=-1, keepdims=True)
    cotangent = cot[...].astype(F32)
    grad = cotangent + inverse * (scaled_up - first - scaled * second)
    low = grad.astype(BF)
    grad_out[...] = low
    ctx_grad[...] = dot(low, proj[...], NT).astype(BF)
    proj_grad[...] += dot(context[...], low, TN)
    add_row(sums, 0, upstream * scaled)
    add_row(sums, 1, upstream)
    add_row(sums, 2, cotangent)
    add_row(sums, 3, low.astype(F32))

    @pl.when(step == pl.num_programs(0) - 1)
    def _():
        for out, row in ((grad_own, 0), (grad_other, HALF)):
            for col in (0, HALF):
                out[col : col + HALF, :] = proj_grad[row : row + HALF, col : col + HALF].astype(BF)


def resid_of(middle, forward, back, cot, context, proj_own, proj_other, bias, gain):
    rows = 512
    row_block = pl.BlockSpec((rows, D), lambda i: (i, 0))
    half_block = pl.BlockSpec((D, HALF), lambda i: (0, 0))
    return pl.pallas_call(
        resid_kernel,
        grid=(OWN // rows,),
        in_specs=[row_block] * 5 + [whole((HALF, D)), whole((HALF, D)), whole((D,)), whole((D,))],
        out_specs=[
            row_block,
            row_block,
            row_block,
            half_block,
            half_block,
            pl.BlockSpec((8, D), lambda i: (0, 0)),
        ],
        out_shape=[
            jax.ShapeDtypeStruct((OWN, D), BF),
            jax.ShapeDtypeStruct((OWN, D), BF),
            jax.ShapeDtypeStruct((OWN, D), BF),
            jax.ShapeDtypeStruct((D, HALF), BF),
            jax.ShapeDtypeStruct((D, HALF), BF),
            jax.ShapeDtypeStruct((8, D), F32),
        ],
        scratch_shapes=[pltpu.VMEM((D, D), BF), pltpu.VMEM((D, D), F32)],
        compiler_params=params(),
        cost_estimate=cost(5e9, 40e6),
    )(middle, forward, back, cot, context, proj_own, proj_other, bias, gain)


def attend_back_kernel(first, spot, qkv, p, ctx_grad, spread, rel_even, rel_odd, fold, *refs):
    d_out, rel_grad, sums, upstream, kt = refs[-5:]
    band = pl.program_id(0) + first
    window = pl.program_id(1)

    @pl.when((band == first) & (window == 0))
    def _():
        rel_grad[...] = jnp.zeros_like(rel_grad)
        sums[...] = jnp.zeros_like(sums)

    @pl.when(window == 0)
    def _():
        for t in range(7):
            at, owned = owned_pair(spot[0], band, t)
            rows = pl.ds(pl.multiple_of(at * PAIR, PAIR), PAIR)
            moved = dot(spread[...], ctx_grad[rows, :])
            moved = moved * owned.astype(F32)
            upstream[:, 32 * t : 32 * t + 32, :] = moved.astype(BF).reshape(NWIN, 32, HALF)
        upstream[:, 224:256, :] = jnp.zeros((NWIN, 32, HALF), BF)

    kt[...] = qkv[0, 0, :, HALF : 2 * HALF].T
    even = lax.broadcasted_iota(jnp.int32, (1, 128), 1) < HD

    def shifted(head, by):
        return slice(by * HALF + head // 2 * 128, by * HALF + head // 2 * 128 + 128)

    def prob_grads(head, lanes):
        values = qkv[0, 0, 0:KEYS, shifted(head, 2)]
        kept = jnp.where(even != (head % 2 == 1), values, jnp.zeros_like(values))
        return dot(kept, upstream[window, 0:lanes, shifted(head, 0)], NT)

    def rel_table(both, lanes):
        tables = []
        zero8 = jnp.zeros((8, 128), F32)
        zero24 = jnp.zeros((24, 128), F32)
        zero16 = jnp.zeros((16, 128), F32)
        for tile in range(lanes // 128):
            row_shift, col_shift = shift_masks(tile * 128)
            part = both[:, tile * 128 : tile * 128 + 128]
            high = jnp.concatenate([part[HD : HD + 16], zero8], axis=0)
            wide = jnp.concatenate([part[HD + 16 : HD + 32], zero16], axis=0)
            high = unskew(high, row_shift, (1, 2, 4))
            wide = unskew(wide, col_shift, (1, 2, 4, 8))
            stack = [high, zero24, wide] if tile == 0 else [zero24, high, wide]
            tables.append(jnp.concatenate(stack, axis=0))
        table = tables[0] if len(tables) == 1 else jnp.concatenate(tables, axis=1)
        return table.astype(BF)

    def all_heads(lanes):
        count = HEADS // 2
        dvs, dks, dqs, drs = [], [], [], []

        def last_part(head, score_grad, both):
            rel = rel_odd if head % 2 else rel_even
            table = rel_table(both, lanes)
            queries = qkv[0, 0, 0:lanes, shifted(head, 0)]
            grads = dot(jnp.concatenate([score_grad, table], axis=0), queries)
            dks.append(grads[0:KEYS])
            drs.append(grads[KEYS:])
            from_rel = dot(rel[...], table, TN)
            side = head % 2 * HD
            dqs.append(both[0:HD] + from_rel[side : side + HD])
            if head % 2:
                d_out[0, 0, 0:lanes, shifted(head, 0)] = jnp.concatenate(dqs[-2:], axis=0).astype(BF).T
                d_out[0, 0, 0:KEYS, shifted(head, 1)] = (jnp.where(even, dks[-2], dks[-1]) * HD ** (-0.5)).astype(BF)

        prob_grad = prob_grads(0, lanes)
        before = None
        for head in range(count):
            ahead = prob_grads(head + 1, lanes) if head + 1 < count else None
            probs_low = p[0, 0, head, :, 0:lanes]
            probs = probs_low.astype(F32)
            total = jnp.sum(prob_grad * probs, axis=0, keepdims=True)
            score_grad = (probs * (prob_grad - total)).astype(BF)
            dvs.append(dot(probs_low, upstream[window, 0:lanes, shifted(head, 0)]))
            left = jnp.concatenate([kt[head * HD : head * HD + HD, 0:KEYS], fold[...]], axis=0)
            both = dot(left, score_grad)
            if head % 2:
                d_out[0, 0, 0:KEYS, shifted(head, 2)] = jnp.where(even, dvs[-2], dvs[-1]).astype(BF)
            if before is not None:
                last_part(head - 1, *before)
            before, prob_grad = (score_grad, both), ahead
        last_part(count - 1, *before)
        evens = drs[0] + drs[2] + drs[4]
        odds = drs[1] + drs[3] + drs[5]
        rel_grad[...] += jnp.where(even, evens, odds)

    d_out[0, 0, KEYS:, HALF:] = jnp.zeros((SLOTS - KEYS, 2 * HALF), BF)

    @pl.when(band < 2)
    def _():
        all_heads(256)

    @pl.when(band == 2)
    def _():
        all_heads(128)
        d_out[0, 0, 128:, 0:HALF] = jnp.zeros((128, HALF), BF)

    sums[0:1, :] += jnp.sum(d_out[...].reshape(SLOTS, TRIO).astype(F32), axis=0, keepdims=True)


def fold_table():
    table = np.zeros((32, WIN, 16), np.float32)
    for k in range(WIN):
        for l in range(WIN):
            table[k, k, l] = 1
            table[16 + l, k, l] = 1
    return table.reshape(32, KEYS)


def attend_back(spot, qkv, p, ctx_grad, side, spread, rel_even, rel_odd, fold, bands, *d_in):
    first, last = bands
    block = pl.BlockSpec((1, 1, SLOTS, TRIO), lambda s, w, *_: (s + first, w, 0, 0))
    share = (last - first) / 3
    return pl.pallas_call(
        lambda *refs: attend_back_kernel(first, *refs),
        grid_spec=pltpu.PrefetchScalarGridSpec(
            num_scalar_prefetch=1,
            grid=(last - first, NWIN),
            in_specs=[
                block,
                pl.BlockSpec((1, 1, HEADS // 2, KEYS, SLOTS), lambda s, w, *_: (s + first, w, 0, 0, 0)),
                pl.BlockSpec((OWN, HALF), lambda *_: (0, side), pipeline_mode=pl.Buffered(1)),
                whole((NWIN * 32, PAIR)),
                whole((GREL, 128)),
                whole((GREL, 128)),
                whole((32, KEYS)),
            ]
            + [pl.BlockSpec(memory_space=pl.ANY)] * len(d_in),
            out_specs=[
                pl.BlockSpec((1, 1, SLOTS, TRIO), lambda s, w, *_: (s + first, w, 0, side)),
                pl.BlockSpec((GREL, 128), lambda s, w, *_: (0, 0)),
                pl.BlockSpec((8, TRIO), lambda s, w, *_: (0, 0)),
            ],
            scratch_shapes=[pltpu.VMEM((NWIN, SLOTS, HALF), BF), pltpu.VMEM((HALF, SLOTS), BF)],
        ),
        out_shape=[
            jax.ShapeDtypeStruct((3, NWIN, SLOTS, 2 * TRIO), BF),
            jax.ShapeDtypeStruct((GREL, 128), F32),
            jax.ShapeDtypeStruct((8, TRIO), F32),
        ],
        input_output_aliases={8: 0} if d_in else {},
        compiler_params=params(),
        cost_estimate=cost(20e9 * share, 45e6 * share),
    )(spot, qkv, p, ctx_grad, spread, rel_even, rel_odd, fold, *d_in)


def norm_grad_kernel(d, weights_own, spot, mine, theirs, gather, *refs):
    out, joined = refs[-2:]

    @pl.when((pl.program_id(0) == 0) & (pl.program_id(1) == 0))
    def _():
        for s in range(3):
            joined[:, s * HALF : s * HALF + HALF] = weights_own[s]
        join_pieces(spot[1], mine, theirs, joined, TRIO)

    rows = NWIN * 128
    total = dot(d[...].reshape(rows, 2 * TRIO), joined[...], NT).astype(BF).reshape(NWIN, 4, 32, D)
    for t in range(4):
        moved = dot(gather[...], total[:, t].reshape(NWIN * 32, D)).astype(BF)
        out[:, t * PAIR : t * PAIR + PAIR, :] = moved.reshape(1, PAIR, D)


def norm_grad(d, weights_own, core, mine, theirs, gather, bands, *before):
    first, last = bands
    share = (last - first) / 3
    block = pl.BlockSpec((1, NWIN, 128, 2 * TRIO), lambda s, t: (s + first, 0, t, 0))
    return pl.pallas_call(
        norm_grad_kernel,
        grid=(last - first, 2),
        in_specs=[block, whole((3, D, HALF)), SCALAR]
        + [whole((3, HALF, HALF)), whole((3, HALF, HALF)), whole((PAIR, NWIN * 32))]
        + [pl.BlockSpec(memory_space=pl.ANY)] * len(before),
        out_specs=pl.BlockSpec((1, 4 * PAIR, D), lambda s, t: (s + first, t, 0)),
        out_shape=jax.ShapeDtypeStruct((3, 8 * PAIR, D), BF),
        input_output_aliases={6: 0} if before else {},
        scratch_shapes=[pltpu.VMEM((D, 2 * TRIO), BF)],
        compiler_params=params(),
        cost_estimate=cost(14e9 * share, 30e6 * share),
    )(d, weights_own, core, mine, theirs, gather, *before)


def qkv_grad_kernel(spot, xt, d, proj, kept, sent, total):
    step = pl.program_id(0)
    for col in range(0, TRIO, 256):
        cols = slice(col, min(col + 256, TRIO))
        part = dot(xt[...], d[:, cols])
        total[:, cols] = jnp.where(step == 0, part, total[:, cols] + part)

    @pl.when(step == pl.num_programs(0) - 1)
    def _():
        first = spot[1] == 0
        values = [total[:, s * HALF : s * HALF + HALF].astype(BF) for s in range(3)] + [proj[...]]
        for k in range(2):
            kept[k] = jnp.where(first, values[k], values[2 + k])
            sent[k] = jnp.where(first, values[2 + k], values[k])


def qkv_grad(core, xt, d, side, proj):
    rows = NWIN * SLOTS
    block = pl.BlockSpec((2, D, HALF), lambda i: (0, 0, 0))
    shape = jax.ShapeDtypeStruct((2, D, HALF), BF)
    return pl.pallas_call(
        qkv_grad_kernel,
        grid=(3,),
        in_specs=[
            SCALAR,
            pl.BlockSpec((D, rows), lambda i: (0, i)),
            pl.BlockSpec((rows, TRIO), lambda i: (i, side)),
            whole((D, HALF)),
        ],
        out_specs=[block, block],
        out_shape=[shape, shape],
        scratch_shapes=[pltpu.VMEM((D, TRIO), F32)],
        compiler_params=params(),
        cost_estimate=cost(7e9, 16e6),
    )(core, xt, d.reshape(3 * rows, 2 * TRIO), proj)


EARLY = 3


def input_kernel(
    spot, x, middle_grad, up_a, up_b, early_a, early_b, late_a, late_b, gain,
    one_mine, one_theirs, two_mine, two_theirs, out, sums, one_out, two_out,
):
    step = pl.program_id(0)
    first = spot[1] == 0
    mine, theirs = one_mine[...].astype(F32), one_theirs[...].astype(F32)
    one_out[0] = jnp.where(first, mine, theirs)
    one_out[1] = jnp.where(first, theirs, mine)
    mine, theirs = two_mine[...].astype(F32), two_theirs[...].astype(F32)
    two_out[:, 0:HALF] = jnp.where(first, mine, theirs)
    two_out[:, HALF:] = jnp.where(first, theirs, mine)

    @pl.when(step == 0)
    def _():
        sums[...] = jnp.zeros_like(sums)

    for k, (up, early, late) in enumerate(((up_a, early_a, late_a), (up_b, early_b, late_b))):
        rows = slice(k * PAIR, k * PAIR + PAIR)
        scaled, inverse = norm_parts(x[rows, :].astype(F32))
        at, some = taken_pair(spot[0], 2 * step + k)
        shared = jnp.where(at < EARLY, early[...].astype(F32), late[...].astype(F32)) * some.astype(F32)
        upstream = up[0].astype(F32) + shared
        scaled_up = upstream * vec(gain)
        mean = jnp.mean(scaled_up, axis=-1, keepdims=True)
        second = jnp.mean(scaled_up * scaled, axis=-1, keepdims=True)
        out[rows, :] = (middle_grad[rows, :].astype(F32) + inverse * (scaled_up - mean - scaled * second)).astype(BF)
        add_row(sums, 0, upstream * scaled)
        add_row(sums, 1, upstream)


def input_of(spot, x, middle_grad, up, early, late, gain, ones, twos):
    rows = 2 * PAIR
    row_block = pl.BlockSpec((rows, D), lambda i, *_: (i, 0))
    up_at = lambda k: lambda i, spot: band_step(spot[0], 2 * i + k) + (0,)
    early_at = lambda k: lambda i, spot: (jnp.minimum(taken_pair(spot[0], 2 * i + k)[0], EARLY - 1), 0)
    late_at = lambda k: lambda i, spot: (jnp.maximum(taken_pair(spot[0], 2 * i + k)[0] - EARLY, 0), 0)
    steps = OWN // rows
    one_rows, two_rows = HALF // steps, FF // 2 // steps
    return pl.pallas_call(
        input_kernel,
        grid_spec=pltpu.PrefetchScalarGridSpec(
            num_scalar_prefetch=1,
            grid=(steps,),
            in_specs=[
                pl.BlockSpec((rows, D), lambda i, spot: (spot[0] * steps + i, 0)),
                row_block,
                pl.BlockSpec((1, PAIR, D), up_at(0)),
                pl.BlockSpec((1, PAIR, D), up_at(1)),
                pl.BlockSpec((PAIR, D), early_at(0)),
                pl.BlockSpec((PAIR, D), early_at(1)),
                pl.BlockSpec((PAIR, D), late_at(0)),
                pl.BlockSpec((PAIR, D), late_at(1)),
                whole((D,)),
            ]
            + [pl.BlockSpec((one_rows, FF // 2), lambda i, *_: (i, 0))] * 2
            + [pl.BlockSpec((two_rows, HALF), lambda i, *_: (i, 0))] * 2,
            out_specs=[
                row_block,
                pl.BlockSpec((8, D), lambda i, *_: (0, 0)),
                pl.BlockSpec((2, one_rows, FF // 2), lambda i, *_: (0, i, 0)),
                pl.BlockSpec((two_rows, D), lambda i, *_: (i, 0)),
            ],
        ),
        out_shape=[
            jax.ShapeDtypeStruct((OWN, D), BF),
            jax.ShapeDtypeStruct((8, D), F32),
            jax.ShapeDtypeStruct((2, HALF, FF // 2), F32),
            jax.ShapeDtypeStruct((FF // 2, D), F32),
        ],
        compiler_params=params(),
        cost_estimate=cost(1e8, 35e6),
    )(spot, x, middle_grad, up, up, early, early, late, late, gain, *ones, *twos)


MESH = pl.DeviceIdType.MESH
SMALL = 24


def bits_of(size):
    return size.bit_length() - 1


def line_plan(order, rows):
    plan, doubles = [], [("double", order[0], rows)]
    for bit in order[1:]:
        if rows % 32 == 0:
            doubles.append(("double", bit, rows))
            rows //= 2
            plan.append(("halve", bit, rows))
        else:
            plan.append(("both", bit, rows))
    return plan + doubles[::-1]


PARTS = 2
PART_ROWS = D // 2 // PARTS


def last_kernel(bits, plans, orders, *refs):
    (line_a, line_b, one_sums, two_sums, fc1_sums, sums_a, sums_c, sums_b) = refs[:8]
    rel_a, rel_b, rel_c, hots, out, small, rel = refs[8:15]
    small_landed, rel_landed, sends, recvs = refs[15:19]
    rooms = list(refs[19:])
    dp, mp = lax.axis_index("dp"), lax.axis_index("mp")
    bit_at = lambda bit: mp if bit == 0 else (dp // bit) % 2

    def partner(bit):
        if bit == 0:
            return (dp, 1 - mp)
        return (jnp.where(bit_at(bit) == 0, dp + bit, dp - bit), mp)

    barrier = pltpu.get_barrier_semaphore()
    every = [1] + bits + [0]
    for bit in every:
        pl.semaphore_signal(barrier, inc=1, device_id=partner(bit), device_id_type=MESH)

    count = [0]

    def send(src, dst, bit):
        at = count[0]
        count[0] += 1
        copy = pltpu.make_async_remote_copy(
            src_ref=src,
            dst_ref=dst,
            send_sem=sends.at[at],
            recv_sem=recvs.at[at],
            device_id=partner(bit),
            device_id_type=MESH,
        )
        copy.start()
        return copy

    def line(k, part):
        order, value = orders[k], (line_a, line_b)[k].at[pl.ds(part * PART_ROWS, PART_ROWS)]
        slot = dp % 2 * 2 + k
        first = bit_at(order[0]) * (D // 2) + part * PART_ROWS
        start, size, placed = first, PART_ROWS, False
        for kind, bit, after in plans[k]:
            if kind == "double":
                here = pl.ds(pl.multiple_of(start, 16), size)
                if not placed:
                    out[slot, here, :] = value[...]
                    placed = True
                copy = send(out.at[slot, here], out.at[slot, here], bit)
                yield
                copy.wait()
                if after != size or bit != order[0]:
                    start, size = start - bit_at(bit) * size, 2 * size
                continue
            mine = bit_at(bit) if kind == "halve" else 0
            gone = 1 - mine if kind == "halve" else 0
            room, total = rooms.pop(0), rooms.pop(0)
            copy = send(value.at[pl.ds(pl.multiple_of(gone * after, 16), after)], room, bit)
            yield
            copy.wait()
            rows = pl.ds(pl.multiple_of(mine * after, 16), after)
            total[...] = (value[rows, :].astype(F32) + room[...].astype(F32)).astype(BF)
            value = total
            start, size = start + mine * after, after
        copies = []
        for half in range(2):
            rows = pl.ds(half * (D // 2) + part * PART_ROWS, PART_ROWS)
            copies.append(send(out.at[slot, rows], out.at[slot, rows], 1))
        yield
        for copy in copies:
            copy.wait()

    def vectors():
        for at, bit in enumerate(bits + [0, 1]):
            copies = [send(small, small_landed.at[at], bit), send(rel, rel_landed.at[at], bit)]
            yield
            for copy in copies:
                copy.wait()
            small[...] += small_landed[at]
            rel[...] += rel_landed[at]

    lines = [line(k, part) for part in range(PARTS) for k in range(2)]
    pl.semaphore_wait(barrier, len(every))
    for one in lines:
        next(one)

    small[...] = jnp.zeros_like(small)
    small[0:2, :] = one_sums[0:2, :]
    small[2:6, :] = two_sums[0:4, :]
    first = mp == 0
    own = [sums_a[0:1, :] + sums_c[0:1, :], fc1_sums[0:1, 0 : FF // 2]]
    other = [sums_b[0:1, :], fc1_sums[0:1, FF // 2 :]]
    for row, flip in ((6, False), (9, True)):
        picked = [jnp.where(first != flip, a, b) for a, b in zip(own, other)]
        small[row : row + 1, 0:HALF] = picked[0][:, 0:HALF]
        small[row : row + 1, HALF:] = picked[0][:, 2 * HALF :]
        small[row + 1 : row + 2, :] = picked[1][:, 0:D]
        small[row + 2 : row + 3, :] = picked[1][:, D:]
    table = rel_a[...] + rel_b[...] + rel_c[...]
    table = lax.dot_general(hots[...], table, TN, precision=lax.Precision.HIGHEST, preferred_element_type=F32)
    rel[...] = table + pltpu.roll(table, HD, 1)

    active = lines + [vectors()]
    while active:
        for one in list(active):
            if next(one, "end") == "end":
                active.remove(one)


def last_sums(bits, orders, lines, sums, rels, hots):
    vmem = pl.BlockSpec(memory_space=pltpu.VMEM)
    rounds = len(bits) + 2
    copies = 2 * rounds + 2 * PARTS * (2 * len(bits) + 2)
    plans = [line_plan(order, PART_ROWS) for order in orders]
    rooms = []
    for at in range(len(plans[0])):
        for part in range(PARTS):
            for plan in plans:
                if plan[at][0] != "double":
                    rooms += [pltpu.VMEM((plan[at][2], HALF), BF)] * 2
    return pl.pallas_call(
        lambda *refs: last_kernel(bits, plans, orders, *refs),
        in_specs=[vmem] * (2 + len(sums) + len(rels) + 1),
        out_specs=[vmem] * 3,
        out_shape=[
            jax.ShapeDtypeStruct((4, D, HALF), BF),
            jax.ShapeDtypeStruct((SMALL, D), F32),
            jax.ShapeDtypeStruct((56, 128), F32),
        ],
        scratch_shapes=[
            pltpu.VMEM((rounds, SMALL, D), F32),
            pltpu.VMEM((rounds, 56, 128), F32),
            pltpu.SemaphoreType.DMA((copies,)),
            pltpu.SemaphoreType.DMA((copies,)),
        ]
        + rooms,
        compiler_params=pltpu.CompilerParams(
            collective_id=0, has_side_effects=True, vmem_limit_bytes=40 * 2**20
        ),
    )(*lines, *sums, *rels, hots)


CORE, PAIRED = 1, 0


def bit_of(bit):
    return lax.axis_index("mp") if bit == PAIRED else (lax.axis_index("dp") // bit) % 2


def exchange(value, bit):
    if bit == PAIRED:
        return lax.ppermute(value, "mp", [(0, 1), (1, 0)])
    return lax.ppermute(value, "dp", [(i, i ^ bit) for i in range(lax.axis_size("dp"))])


class Line:
    def __init__(self, value, places, rank, steps, sent=None):
        self.terms = [(value, tuple(places))]
        self.fixed = {}
        self.rank = list(rank)
        self.steps = list(steps)
        self.sent, self.taken = sent, None
        self.value = None

    def part(self, changes):
        fixed = {**self.fixed, **changes}
        total = None
        for term, places in self.terms:
            starts, sizes, shape = [], [], []
            for bit in places:
                starts.append(fixed.get(bit, 0))
                sizes.append(1 if bit in fixed else 2)
                if bit not in fixed:
                    shape.append(2)
            rest = term.shape[len(places) :]
            if places:
                starts = [jnp.asarray(at, jnp.int32) for at in starts + [0] * len(rest)]
                term = lax.dynamic_slice(term, starts, tuple(sizes) + rest).reshape(tuple(shape) + rest)
            total = term.astype(F32) if total is None else total + term.astype(F32)
        return total.astype(BF)

    def prepare(self):
        kind, bit = self.steps[0]
        if kind == "halve":
            mine = 0 if bit == PAIRED else bit_of(bit)
            self.sent = self.part({bit: 1 - mine})
            self.fixed[bit] = mine
        elif kind == "double":
            if self.value is None:
                self.value, self.done = self.part({}), []
            self.sent = self.value
        elif kind == "pass":
            self.sent = self.part({})

    def launch(self):
        self.taken = exchange(self.sent, self.steps[0][1])

    def land(self):
        kind, bit = self.steps.pop(0)
        if kind in ("halve", "give"):
            places = [p for p in self.terms[0][1] if p not in self.fixed]
            self.terms.append((self.taken, tuple(places)))
        elif kind == "pass":
            self.terms = [(self.taken, tuple(p for p in self.terms[0][1] if p not in self.fixed))]
        else:
            if not self.steps:
                self.value, self.taken_last, self.taken = self.sent, self.taken, None
                return
            self.done = sorted(self.done + [bit], key=self.rank.index)
            axis = self.done.index(bit)
            shape = [1] * (self.value.ndim + 1)
            shape[axis] = 2
            mine = jnp.arange(2).reshape(shape) == bit_of(bit)
            wide = lambda v: jnp.expand_dims(v, axis)
            self.value = jnp.where(mine, wide(self.sent), wide(self.taken))
        self.taken = None


def advance(anchor, lines):
    flying = [line for line in lines if line.taken is not None]
    anchor, taken = lax.optimization_barrier((anchor, [line.taken for line in flying]))
    for line, value in zip(flying, taken):
        line.taken = value
        line.land()
    going = [line for line in lines if line.steps]
    for line in going:
        line.prepare()
    anchor, sent = lax.optimization_barrier((anchor, [line.sent for line in going]))
    for line, value in zip(going, sent):
        line.sent = value
        line.launch()
    return anchor


def finish(lines):
    while any(line.steps for line in lines):
        for line in lines:
            if not line.steps:
                continue
            if line.taken is None:
                line.prepare()
                line.launch()
        for line in lines:
            if line.taken is not None:
                line.land()


def on_device(
    image_tokens,
    norm1_gain,
    norm1_shift,
    qkv_weight,
    qv_bias,
    rel_rows,
    rel_cols,
    proj_weight,
    proj_bias,
    norm2_gain,
    norm2_shift,
    fc1_weight,
    fc1_bias,
    fc2_weight,
    fc2_bias,
    out_cotangent,
):
    place = lax.axis_index("mp")
    core = lax.axis_index("dp") % 2
    swap = lambda value: lax.ppermute(value, "mp", [(0, 1), (1, 0)])
    size = lax.axis_size("dp")
    core_swap = lambda value: lax.ppermute(value, "dp", [(i, i ^ 1) for i in range(size)])

    def by_core(weight, axis, mine):
        return lax.dynamic_slice_in_dim(weight, (core if mine else 1 - core) * HALF, HALF, axis)

    spot = jnp.stack([place, core]).astype(jnp.int32)
    spread = jnp.asarray(spread_rows(), BF)
    gather = jnp.asarray(spread_rows().T, BF)
    fold = jnp.asarray(fold_table(), BF)
    high_hot, wide_hot = rel_onehots()
    hots = jnp.asarray(np.pad(np.concatenate([high_hot, wide_hot], axis=1), ((0, 0), (0, 2))), F32)
    high_hot, wide_hot = jnp.asarray(high_hot, BF), jnp.asarray(wide_hot, BF)
    qkv_mine = swap(by_core(qkv_weight, 1, True))
    bias_other = swap(qv_bias)
    fc1_bias_other = swap(fc1_bias)
    x_windows = windows_of(spot, image_tokens, norm1_gain, norm1_shift, spread)
    cot_t = turned_of(out_cotangent)
    x_windows, cot_t, qkv_mine = lax.optimization_barrier((x_windows, cot_t, qkv_mine))
    late = (by_core(fc1_weight, 0, True), by_core(fc2_weight, 1, True), proj_weight)
    x_windows, qkv_mine, late = lax.optimization_barrier((x_windows, qkv_mine, late))
    qkv_theirs = exchange(qkv_mine, CORE)
    one_mine, two_mine, proj_other = (swap(w) for w in late)
    qkv_a, p_a, ctx_a, xt, rel_even, rel_odd = attend(
        x_windows, qv_bias, True, qkv_weight, high_hot, wide_hot, rel_rows, rel_cols
    )
    qkv_b, p_b, ctx_b = attend(
        x_windows, bias_other, False, spot, qkv_mine, qkv_theirs, rel_even, rel_odd
    )
    ctx_b, one_mine, two_mine, proj_other = lax.optimization_barrier((ctx_b, one_mine, two_mine, proj_other))
    one_theirs, two_theirs = exchange(one_mine, CORE), exchange(two_mine, CORE)
    middle, normed, normed_t, context = middle_of(
        spot, ctx_a, ctx_b, image_tokens, proj_weight, proj_other, proj_bias, norm2_gain, norm2_shift, gather
    )
    forward, back, one_kept, one_sent, two_kept, two_sent, fc1_sums = feed(
        spot, normed, normed_t, out_cotangent, cot_t, fc1_weight, (one_mine, one_theirs), fc1_bias,
        fc1_bias_other, fc2_weight, (two_mine, two_theirs),
    )
    bits = [2**k for k in range(1, bits_of(size))]
    turned = bits[1:2] + bits[0:1] + bits[2:]
    halves = lambda order: [("halve", bit) for bit in order]
    doubles = lambda order: [("double", bit) for bit in order]

    def cut(value, axis, places):
        shape = value.shape[:axis] + (2,) * len(places) + (value.shape[axis] // 2 ** len(places),)
        return value.reshape(shape + value.shape[axis + 1 :])

    def feed_line(kept, sent, order, back):
        steps = [("give", CORE)] + halves(order) + doubles(back) + [("double", CORE)]
        rank = [CORE] + bits
        return Line(cut(kept, 1, bits), [PAIRED] + bits, rank, steps, cut(sent, 1, bits))

    one_line = feed_line(one_kept, one_sent, [PAIRED] + bits, bits[::-1])
    two_line = feed_line(two_kept, two_sent, bits[:2] + [PAIRED] + bits[2:], turned[::-1])
    feed_lines = [one_line, two_line]

    middle = advance(middle, feed_lines)
    block_out, middle_grad, ctx_grad, proj_own, proj_oth, two_sums = resid_of(
        middle, forward, back, out_cotangent, context, proj_weight, proj_other, fc2_bias, norm2_gain
    )
    back_of = lambda qkv, p, side, grad, bands, *d: attend_back(
        spot, qkv, p, grad, side, spread, rel_even, rel_odd, fold, bands, *d
    )
    ctx_grad = advance(ctx_grad, feed_lines)
    d, rel_b, sums_b = back_of(qkv_b, p_b, 1, ctx_grad, (0, 3))
    d = advance(d, feed_lines)
    kept_b, sent_b = qkv_grad(spot, xt, d, 1, proj_oth)
    line_b = Line(kept_b, [], [], [("give", CORE)], sent_b)
    lines = feed_lines + [line_b]
    ctx_grad, kept_b, d = lax.optimization_barrier((ctx_grad, kept_b, d))
    ctx_grad = advance(ctx_grad, lines)
    d, rel_a0, sums_a0 = back_of(qkv_a, p_a, 0, ctx_grad, (0, 1), d)
    d = advance(d, lines)
    passes = []
    for k in range(2):
        line = Line(None, [], [], [("pass", PAIRED)])
        line.terms = [(term[k], ()) for term, _ in line_b.terms]
        passes.append(line)
    d = advance(d, passes[:1])
    d, rel_a, sums_a = back_of(qkv_a, p_a, 0, ctx_grad, (1, 3), d)
    d = advance(d, feed_lines + passes[:1])
    d = advance(d, passes[1:])
    up = norm_grad(d, qkv_weight, spot, qkv_mine, qkv_theirs, gather, (1, 3))
    at = [2 - place, (1 - place) * 4 * SIDE, jnp.zeros_like(place)]
    shares = []
    for first, count in ((0, 2 * EARLY), (2 * EARLY, 10 - 2 * EARLY)):
        start = [at[0], at[1] + first * SIDE, at[2]]
        part = lax.dynamic_slice(up, start, (1, count * SIDE, D)).reshape(count * SIDE, D)
        shares.append(Line(part, [], [], [("pass", PAIRED)]))
    d = advance(d, feed_lines + passes[1:])
    d = advance(d, shares[:1])
    kept_a, sent_a = qkv_grad(spot, xt, d, 0, proj_own)
    line_a = Line(kept_a, [], [], [("give", CORE)], sent_a)
    kept_a, d = lax.optimization_barrier((kept_a, d))
    d = advance(d, feed_lines + [line_a] + shares[:1])
    d = advance(d, shares[1:])
    up = norm_grad(d, qkv_weight, spot, qkv_mine, qkv_theirs, gather, (0, 1), up)
    up = advance(up, feed_lines + [line_a] + shares[1:])
    early, late = (line.terms[0][0] for line in shares)
    q_lines = []
    for k, order in enumerate((bits, turned)):
        line = Line(None, [], [], halves(order[:1]))
        line.terms = [(part.reshape(2, 2, D // 2, HALF), ("line", order[0])) for part, _ in line_a.terms]
        line.terms += [(part.reshape(2, D // 2, HALF), (order[0],)) for part, _ in passes[k].terms]
        line.fixed = {"line": k}
        q_lines.append(line)
    up = advance(up, q_lines)
    finish(feed_lines)
    flat = lambda line, rows: (line.value.reshape(rows, -1), line.taken_last.reshape(rows, -1))
    input_grad, one_sums, one_sum, two_sum = input_of(
        spot, image_tokens, middle_grad, up, early, late, norm1_gain, flat(one_line, HALF), flat(two_line, FF // 2)
    )
    one_sums = advance(one_sums, q_lines)
    four, small, rel = last_sums(
        bits,
        [bits, turned],
        [line.part({}) for line in q_lines],
        [one_sums, two_sums, fc1_sums, sums_a, sums_a0, sums_b],
        [rel_a, rel_a0, rel_b],
        hots,
    )
    one_sum = one_sum.reshape(D, FF // 2)
    mine = jnp.where(place == 0, small[6:9], small[9:12])
    return (
        block_out,
        input_grad,
        small[0],
        small[1],
        four[0:3].astype(F32),
        mine[0].reshape(2, HALF),
        rel[:RELS, :HD],
        rel[RELS : 2 * RELS, :HD],
        jnp.concatenate([four[3, :HALF], four[3, HALF:]], axis=1).astype(F32),
        small[5],
        small[2],
        small[3],
        one_sum,
        mine[1:3].reshape(-1),
        two_sum,
        small[4],
    )


def solution(mesh):
    in_specs = (
        P("dp", None),
        P(),
        P(),
        P(None, None, "mp"),
        P(None, "mp"),
        P(),
        P(),
        P("mp", None),
        P(),
        P(),
        P(),
        P(None, "mp"),
        P("mp"),
        P("mp", None),
        P(),
        P(("dp", "mp"), None),
    )
    out_specs = (
        P(("dp", "mp"), None),
        P(("dp", "mp"), None),
        P(),
        P(),
        P(None, None, "mp"),
        P(None, "mp"),
        P(),
        P(),
        P("mp", None),
        P(),
        P(),
        P(),
        P(None, "mp"),
        P("mp"),
        P("mp", None),
        P(),
    )
    return jax.shard_map(
        on_device, mesh=mesh, in_specs=in_specs, out_specs=out_specs, check_vma=False
    )
```

```python
import jax
import jax.numpy as jnp
import numpy as np
from jax import lax
from jax.experimental import pallas as pl
from jax.experimental.pallas import tpu as pltpu
from jax.sharding import PartitionSpec as P

D = 768
HEADS = 12
HD = 64
FF = 3072
WIN = 14
SIDE = 64
NWIN = 5
RELS = 27
EPSILON = 1e-06
F32 = jnp.float32
BF = jnp.bfloat16

SLOTS = 256
KEYS = WIN * 16
PAIR = 2 * SIDE
GREL = 80
OWN = SIDE * SIDE // 2

HALF = D // 2
TRIO = 3 * HALF
PAIRS = HEADS // 4

NN = (((1,), (0,)), ((), ()))
NT = (((1,), (1,)), ((), ()))
TN = (((0,), (0,)), ((), ()))


def dot(left, right, dims=NN):
    return lax.dot_general(left, right, dims, preferred_element_type=F32)


def params(limit=60):
    return pltpu.CompilerParams(vmem_limit_bytes=limit * 2**20)


def cost(flops, moved, exps=0):
    return pl.CostEstimate(flops=int(flops), bytes_accessed=int(moved), transcendentals=int(exps))


def whole(shape):
    return pl.BlockSpec(shape, lambda *_: (0,) * len(shape), pipeline_mode=pl.Buffered(1))


def band_start(place, band):
    return (1 - place) * (14 * band) + place * (42 - 14 * band + 21 * band * (band - 1))


def image_pair(place, band, step):
    pair = band_start(place, band) // 2 + step
    return jnp.minimum(pair, SIDE // 2 - 1), pair < SIDE // 2


def owned_pair(place, band, step):
    pair = band_start(place, band) // 2 + step - 16 * place
    return jnp.clip(pair, 0, 15), (pair >= 0) & (pair < 16)


def band_step(place, pair):
    first = pair // 7, pair % 7
    band = jnp.where(pair < 5, 1, jnp.where(pair < 12, 0, 2))
    second = band, jnp.where(pair < 5, pair + 2, jnp.where(pair < 12, pair - 5, pair - 12))
    return tuple(jnp.where(place == 0, a, b) for a, b in zip(first, second))


def taken_pair(place, pair):
    return (
        jnp.where(place == 0, jnp.maximum(pair - 14, 0), jnp.minimum(pair, 4)),
        jnp.where(place == 0, pair >= 14, pair < 5),
    )


def spread_rows():
    table = np.zeros((NWIN, 2, 16, PAIR), np.float32)
    for w in range(NWIN):
        for r in range(2):
            for j in range(WIN):
                if WIN * w + j < SIDE:
                    table[w, r, j, r * SIDE + WIN * w + j] = 1
    return table.reshape(NWIN * 32, PAIR)


def rel_order():
    rows = np.full(GREL, -1)
    for m in range(21):
        rows[m] = 26 - (m + 6)
        rows[24 + m] = 26 - m
    cols = np.full(GREL, -1)
    for m in range(RELS):
        cols[48 + m] = 26 - m
    return rows, cols


def rel_onehots():
    rows, cols = rel_order()
    high = (rows[:, None] == np.arange(RELS)[None, :]).astype(np.float32)
    wide = (cols[:, None] == np.arange(RELS)[None, :]).astype(np.float32)
    return high, wide


def norm_parts(values):
    average = jnp.mean(values, axis=-1, keepdims=True)
    centred = values - average
    inverse = lax.rsqrt(jnp.mean(centred * centred, axis=-1, keepdims=True) + EPSILON)
    return centred * inverse, inverse


def vec(ref):
    return ref[...].astype(F32).reshape(1, D)


def window_kernel(spot, *refs):
    xs, (gain, shift, spread, out) = refs[:7], refs[7:]
    band = pl.program_id(0)
    for t in range(7):
        scaled, _ = norm_parts(xs[t][...].astype(F32))
        normed = scaled * vec(gain) + vec(shift)
        valid = image_pair(spot[0], band, t)[1]
        normed = (normed * valid.astype(F32)).astype(BF)
        moved = dot(spread[...], normed).astype(BF)
        out[:, :, 32 * t : 32 * t + 32, :] = moved.reshape(1, NWIN, 32, D)
    out[:, :, 224:, :] = jnp.zeros((1, NWIN, 32, D), BF)


def windows_of(spot, x, gain, shift, spread):
    at = lambda t: lambda s, spot: (image_pair(spot[0], s, t)[0], 0)
    return pl.pallas_call(
        window_kernel,
        grid_spec=pltpu.PrefetchScalarGridSpec(
            num_scalar_prefetch=1,
            grid=(3,),
            in_specs=[pl.BlockSpec((PAIR, D), at(t)) for t in range(7)]
            + [whole((D,)), whole((D,)), whole((NWIN * 32, PAIR))],
            out_specs=pl.BlockSpec((1, NWIN, SLOTS, D), lambda s, *_: (s, 0, 0, 0)),
        ),
        out_shape=jax.ShapeDtypeStruct((3, NWIN, SLOTS, D), BF),
        compiler_params=params(),
        cost_estimate=cost(3 * 7 * 160 * 128 * 768 * 2, 10e6),
    )(spot, *([x] * 7), gain, shift, spread)


def shift_masks(lanes_from):
    lane = lax.broadcasted_iota(jnp.int32, (1, 128), 1) + lanes_from
    high = lane // 16
    row_shift = jnp.where(lane < 128, 7 - high, jnp.maximum(13 - high, 0))
    col_shift = jnp.maximum(13 - lane % 16, 0)
    return row_shift, col_shift


def skew(table, shift, bits):
    size = table.shape[0]
    for bit in bits:
        moved = pltpu.roll(table, size - bit, 0)
        table = jnp.where((shift & bit) != 0, moved, table)
    return table


def unskew(table, shift, bits):
    for bit in bits:
        moved = pltpu.roll(table, bit, 0)
        table = jnp.where((shift & bit) != 0, moved, table)
    return table


def start_own(weights, bias, high_hot, wide_hot, rel_rows, rel_cols, rel_even, rel_odd, joined):
    for s in range(3):
        joined[:, s * HALF : s * HALF + HALF] = weights[s]
    table = (dot(high_hot[...], rel_rows[...]) + dot(wide_hot[...], rel_cols[...])).astype(BF)
    blank = jnp.zeros_like(table)
    rel_even[...] = jnp.concatenate([table, blank], axis=1)
    rel_odd[...] = jnp.concatenate([blank, table], axis=1)


def join_pieces(core, mine, theirs, joined, col):
    for piece, at in ((mine, core), (theirs, 1 - core)):
        rows = pl.ds(pl.multiple_of(at * HALF, HALF), HALF)
        for s in range(3):
            joined[rows, col + s * HALF : col + s * HALF + HALF] = piece[s]


def attend_own(
    x, bias, weights, high_hot, wide_hot, rel_rows, rel_cols,
    qkv_out, p_out, ctx_out, xt_out, rel_even, rel_odd, joined, vt,
):
    @pl.when((pl.program_id(0) == 0) & (pl.program_id(1) == 0))
    def _():
        start_own(weights, bias, high_hot, wide_hot, rel_rows, rel_cols, rel_even, rel_odd, joined)

    attend_window(x, bias, rel_even, rel_odd, qkv_out, p_out, ctx_out, xt_out, joined, vt)


def attend_other(x, bias, spot, mine, theirs, rel_even, rel_odd, qkv_out, p_out, ctx_out, joined, vt):
    @pl.when((pl.program_id(0) == 0) & (pl.program_id(1) == 0))
    def _():
        join_pieces(spot[1], mine, theirs, joined, 0)

    attend_window(x, bias, rel_even, rel_odd, qkv_out, p_out, ctx_out, None, joined, vt)


def attend_window(x, bias, rel_even, rel_odd, qkv_out, p_out, ctx_out, xt_out, joined, vt):
    band = pl.program_id(0)
    biases = bias[...].astype(F32)
    biases = jnp.concatenate([biases[0:1], jnp.zeros((1, HALF), F32), biases[1:2]], axis=1)
    block = x[...].reshape(SLOTS, D)
    if xt_out is not None:
        xt_out[...] = block.T
    scales = jnp.where(lax.broadcasted_iota(jnp.int32, (1, TRIO), 1) // HALF == 1, HD ** (-0.5), 1.0)
    low = ((dot(block, joined[...]) + biases) * scales).astype(BF)
    qkv_out[0, 0] = low
    vt[...] = low[:, 2 * HALF :].T

    even = lax.broadcasted_iota(jnp.int32, (1, 128), 1) < HD

    def raw_scores(head, lanes):
        col = head // 2 * 128
        keys = qkv_out[0, 0, 0:KEYS, HALF + col : HALF + col + 128]
        kept = jnp.where(even != (head % 2 == 1), keys, jnp.zeros_like(keys))
        rel = rel_odd if head % 2 else rel_even
        left = jnp.concatenate([kept, rel[...]], axis=0)
        return dot(left, qkv_out[0, 0, 0:lanes, col : col + 128], NT)

    def soft(head, raw, lanes):
        parts = []
        for tile in range(lanes // 128):
            row_shift, col_shift = shift_masks(tile * 128)
            raw_t = raw[:, tile * 128 : tile * 128 + 128]
            base = raw_t[0:KEYS]
            high = skew(raw_t[KEYS + 24 * tile : KEYS + 24 * tile + 24], row_shift, (4, 2, 1))[0:16]
            wide = skew(raw_t[KEYS + 48 : KEYS + 80], col_shift, (8, 4, 2, 1))[0:16]
            place = lax.broadcasted_iota(jnp.int32, (16, 128), 0)
            wide = jnp.where(place < WIN, wide, -1e30)
            scores = base.reshape(WIN, 16, 128) + wide[None] + high[0:WIN][:, None, :]
            scores = scores.reshape(KEYS, 128)
            peak = jnp.max(scores, axis=0, keepdims=True)
            grown = jnp.exp(scores - peak)
            total = jnp.sum(grown, axis=0, keepdims=True)
            parts.append((grown * (1.0 / total)).astype(BF))
        probs = parts[0] if len(parts) == 1 else jnp.concatenate(parts, axis=1)
        p_out[0, 0, head, :, 0:lanes] = probs
        return probs

    def all_heads(lanes):
        count = HEADS // 2
        raw = raw_scores(0, lanes)
        contexts = []
        for head in range(count):
            ahead = raw_scores(head + 1, lanes) if head + 1 < count else None
            probs = soft(head, raw, lanes)
            if head:
                contexts.append(dot(vt[(head - 1) * HD : head * HD, 0:KEYS], before).astype(BF))
            if head and head % 2 == 0:
                col = (head - 2) * HD
                ctx_out[0, 0, 0:lanes, col : col + 128] = jnp.concatenate(contexts[-2:], axis=0).T
            before, raw = probs, ahead
        contexts.append(dot(vt[(count - 1) * HD :, 0:KEYS], before).astype(BF))
        ctx_out[0, 0, 0:lanes, HALF - 128 :] = jnp.concatenate(contexts[-2:], axis=0).T

    @pl.when(band < 2)
    def _():
        all_heads(256)

    @pl.when(band == 2)
    def _():
        all_heads(128)


SCALAR = pl.BlockSpec(memory_space=pltpu.SMEM)


def attend(x, bias, first, *operands):
    block = lambda width: pl.BlockSpec((1, 1, SLOTS, width), lambda s, w: (s, w, 0, 0))
    shape = lambda width: jax.ShapeDtypeStruct((3, NWIN, SLOTS, width), BF)
    out_specs = [
        block(TRIO),
        pl.BlockSpec((1, 1, HEADS // 2, KEYS, SLOTS), lambda s, w: (s, w, 0, 0, 0)),
        block(HALF),
    ]
    out_shape = [
        shape(TRIO),
        jax.ShapeDtypeStruct((3, NWIN, HEADS // 2, KEYS, SLOTS), BF),
        shape(HALF),
    ]
    rel = pl.BlockSpec((GREL, 128), lambda s, w: (0, 0))
    if first:
        in_specs = [whole((3, D, HALF)), whole((GREL, RELS)), whole((GREL, RELS)), whole((RELS, HD)), whole((RELS, HD))]
        out_specs += [pl.BlockSpec((D, SLOTS), lambda s, w: (0, s * NWIN + w)), rel, rel]
        out_shape += [jax.ShapeDtypeStruct((D, 3 * NWIN * SLOTS), BF)] + [jax.ShapeDtypeStruct((GREL, 128), BF)] * 2
    else:
        in_specs = [SCALAR, whole((3, HALF, HALF)), whole((3, HALF, HALF)), whole((GREL, 128)), whole((GREL, 128))]
    return pl.pallas_call(
        attend_own if first else attend_other,
        grid=(3, NWIN),
        in_specs=[block(D), whole((2, HALF))] + in_specs,
        out_specs=out_specs,
        out_shape=out_shape,
        scratch_shapes=[pltpu.VMEM((D, TRIO), BF), pltpu.VMEM((HALF, SLOTS), BF)],
        compiler_params=params(),
        cost_estimate=cost(15e9, 45e6, 4e6),
    )(x, bias, *operands)


def middle_kernel(
    spot, own_a, own_b, other_a, other_b, x, proj_own, proj_other, bias, gain, shift, gather,
    middle, normed, normed_t, ctx_out, proj,
):
    @pl.when(pl.program_id(0) == 0)
    def _():
        proj[0:HALF, :] = proj_own[...]
        proj[HALF:, :] = proj_other[...]

    for row, parts in ((0, (own_a, other_a)), (PAIR, (own_b, other_b))):
        for side in range(2):
            moved = dot(gather[...], parts[side][...].reshape(NWIN * 32, HALF)).astype(BF)
            ctx_out[row : row + PAIR, side * HALF : side * HALF + HALF] = moved
    value = x[...].astype(F32) + (dot(ctx_out[...], proj[...]) + vec(bias))
    middle[...] = value.astype(BF)
    scaled, _ = norm_parts(value)
    low = (scaled * vec(gain) + vec(shift)).astype(BF)
    normed[...] = low
    normed_t[...] = low.T


def middle_of(spot, ctx_own, ctx_other, x, proj_own, proj_other, bias, gain, shift, gather):
    rows = 2 * PAIR

    def at(k):
        def place(i, spot):
            band, step = band_step(spot[0], 2 * i + k)
            return band, 0, step, 0

        return pl.BlockSpec((1, NWIN, 32, HALF), place)

    row_block = pl.BlockSpec((rows, D), lambda i, *_: (i, 0))
    col_block = pl.BlockSpec((D, rows), lambda i, *_: (0, i))
    low = jax.ShapeDtypeStruct((OWN, D), BF)
    return pl.pallas_call(
        middle_kernel,
        grid_spec=pltpu.PrefetchScalarGridSpec(
            num_scalar_prefetch=1,
            grid=(OWN // rows,),
            in_specs=[
                at(0),
                at(1),
                at(0),
                at(1),
                pl.BlockSpec((rows, D), lambda i, spot: (spot[0] * (OWN // rows) + i, 0)),
                whole((HALF, D)),
                whole((HALF, D)),
                whole((D,)),
                whole((D,)),
                whole((D,)),
                whole((PAIR, NWIN * 32)),
            ],
            out_specs=[row_block, row_block, col_block, row_block],
            scratch_shapes=[pltpu.VMEM((D, D), BF)],
        ),
        out_shape=[low, low, jax.ShapeDtypeStruct((D, OWN), BF), low],
        compiler_params=params(),
        cost_estimate=cost(3e9, 25e6),
    )(spot, ctx_own, ctx_own, ctx_other, ctx_other, x, proj_own, proj_other, bias, gain, shift, gather)


def turn_kernel(value, out):
    out[...] = value[...].T


def turned_of(value):
    rows = 512
    return pl.pallas_call(
        turn_kernel,
        grid=(OWN // rows,),
        in_specs=[pl.BlockSpec((rows, D), lambda i: (i, 0))],
        out_specs=pl.BlockSpec((D, rows), lambda i: (0, i)),
        out_shape=jax.ShapeDtypeStruct((D, OWN), BF),
        compiler_params=params(),
        cost_estimate=cost(1e6, 6e6),
    )(value)


CHUNK = 512
CHUNKS = FF // CHUNK


def feed_kernel(
    spot, normed, normed_t, cot, cot_t, one_a, one_b, one_c, bias_a, bias_b, two_a, two_b, two_c,
    forward_out, back_out, one_kept, one_sent, two_kept, two_sent, sums,
    forward, back, one, two, bias, hidden, grads,
):
    step = pl.program_id(0)

    @pl.when(step == 0)
    def _():
        forward[...] = jnp.zeros_like(forward)
        back[...] = jnp.zeros_like(back)

    @pl.when(step < CHUNKS // 2)
    def _():
        bias[...] = bias_a[...].astype(F32).reshape(1, CHUNK)
        one[...] = one_a[...]
        two[...] = two_a[...]

    @pl.when(step >= CHUNKS // 2)
    def _():
        bias[...] = bias_b[...].astype(F32).reshape(1, CHUNK)
        mine = pl.multiple_of(spot[1] * HALF, HALF)
        theirs = pl.multiple_of((1 - spot[1]) * HALF, HALF)
        one[pl.ds(mine, HALF), :] = one_b[...]
        one[pl.ds(theirs, HALF), :] = one_c[...]
        two[:, pl.ds(mine, HALF)] = two_b[...]
        two[:, pl.ds(theirs, HALF)] = two_c[...]

    total = jnp.zeros((1, CHUNK), F32)
    def starts(t):
        rows = slice(t * 256, t * 256 + 256)
        return dot(normed[rows, :], one[...]), dot(cot[rows, :], two[...], NT)

    now = starts(0)
    for t in range(OWN // 256):
        rows = slice(t * 256, t * 256 + 256)
        ahead = starts(t + 1) if t + 1 < OWN // 256 else None
        pre = now[0] + bias[...]
        phi = 0.5 * (1.0 + lax.erf(pre * 0.7071067811865476))
        slope = phi + pre * (jnp.exp(-0.5 * pre * pre) * 0.3989422804014327)
        low = (pre * phi).astype(BF)
        grad = (now[1] * slope).astype(BF)
        hidden[rows, :] = low
        grads[rows, :] = grad
        total += jnp.sum(grad.astype(F32), axis=0, keepdims=True)
        if t:
            before = slice(t * 256 - 256, t * 256)
            forward[before, :] += dot(last[0], two[...])
            back[before, :] += dot(last[1], one[...], NT)
        last, now = (low, grad), ahead
    forward[OWN - 256 :, :] += dot(last[0], two[...])
    back[OWN - 256 :, :] += dot(last[1], one[...], NT)
    sums[...] = total

    first = spot[1] == 0
    one_grad = dot(normed_t[...], grads[...]).astype(BF)
    low, high = one_grad[:HALF], one_grad[HALF:]
    one_kept[0] = jnp.where(first, low, high)
    one_sent[0] = jnp.where(first, high, low)
    two_grad = dot(cot_t[...], hidden[...]).astype(BF)
    low, high = two_grad[:HALF], two_grad[HALF:]
    two_kept[0] = jnp.where(first, low, high).T
    two_sent[0] = jnp.where(first, high, low).T

    @pl.when(step == pl.num_programs(0) - 1)
    def _():
        forward_out[...] = forward[...].astype(BF)
        back_out[...] = back[...].astype(BF)


def feed(spot, normed, normed_t, cot, cot_t, one_a, ones, bias_a, bias_b, two_a, twos):
    half = CHUNKS // 2
    own = lambda j: jnp.minimum(j, half - 1)
    other = lambda j: jnp.maximum(j - half, 0)
    one_block = pl.BlockSpec((1, HALF, CHUNK), lambda j, *_: (j // half, 0, j % half))
    two_block = pl.BlockSpec((1, CHUNK, HALF), lambda j, *_: (j // half, j % half, 0))
    one_piece = pl.BlockSpec((HALF, CHUNK), lambda j, *_: (0, other(j)))
    two_piece = pl.BlockSpec((CHUNK, HALF), lambda j, *_: (other(j), 0))
    one_shape = jax.ShapeDtypeStruct((2, HALF, FF // 2), BF)
    two_shape = jax.ShapeDtypeStruct((2, FF // 2, HALF), BF)
    sum_block = pl.BlockSpec((OWN, D), lambda j, *_: (0, 0))
    bias_block = pl.BlockSpec((1, CHUNK), lambda j, *_: (0, j))
    return pl.pallas_call(
        feed_kernel,
        grid_spec=pltpu.PrefetchScalarGridSpec(
            num_scalar_prefetch=1,
            grid=(CHUNKS,),
            in_specs=[
                whole((OWN, D)),
                whole((D, OWN)),
                whole((OWN, D)),
                whole((D, OWN)),
                pl.BlockSpec((D, CHUNK), lambda j, *_: (0, own(j))),
                one_piece,
                one_piece,
                pl.BlockSpec((CHUNK,), lambda j, *_: (own(j),)),
                pl.BlockSpec((CHUNK,), lambda j, *_: (other(j),)),
                pl.BlockSpec((CHUNK, D), lambda j, *_: (own(j), 0)),
                two_piece,
                two_piece,
            ],
            out_specs=[sum_block, sum_block, one_block, one_block, two_block, two_block, bias_block],
            scratch_shapes=[
                pltpu.VMEM((OWN, D), F32),
                pltpu.VMEM((OWN, D), F32),
                pltpu.VMEM((D, CHUNK), BF),
                pltpu.VMEM((CHUNK, D), BF),
                pltpu.VMEM((1, CHUNK), F32),
                pltpu.VMEM((OWN, CHUNK), BF),
                pltpu.VMEM((OWN, CHUNK), BF),
            ],
        ),
        out_shape=[
            jax.ShapeDtypeStruct((OWN, D), BF),
            jax.ShapeDtypeStruct((OWN, D), BF),
            one_shape,
            one_shape,
            two_shape,
            two_shape,
            jax.ShapeDtypeStruct((1, FF), F32),
        ],
        compiler_params=params(62),
        cost_estimate=cost(58e9, 60e6, 12e6),
    )(spot, normed, normed_t, cot, cot_t, one_a, *ones, bias_a, bias_b, two_a, *twos)


def add_row(sums, row, values):
    sums[row : row + 1, :] += jnp.sum(values, axis=0, keepdims=True)


def resid_kernel(
    middle, forward, back, cot, context, proj_own, proj_other, bias, gain,
    block_out, grad_out, ctx_grad, grad_own, grad_other, sums, proj, proj_grad,
):
    step = pl.program_id(0)

    @pl.when(step == 0)
    def _():
        proj[0:HALF, :] = proj_own[...]
        proj[HALF:, :] = proj_other[...]
        proj_grad[...] = jnp.zeros_like(proj_grad)
        sums[...] = jnp.zeros_like(sums)

    value = middle[...].astype(F32)
    block_out[...] = (value + (forward[...].astype(F32) + vec(bias))).astype(BF)
    scaled, inverse = norm_parts(value)
    upstream = back[...].astype(F32)
    scaled_up = upstream * vec(gain)
    first = jnp.mean(scaled_up, axis=-1, keepdims=True)
    second = jnp.mean(scaled_up * scaled, axis=-1, keepdims=True)
    cotangent = cot[...].astype(F32)
    grad = cotangent + inverse * (scaled_up - first - scaled * second)
    low = grad.astype(BF)
    grad_out[...] = low
    ctx_grad[...] = dot(low, proj[...], NT).astype(BF)
    proj_grad[...] += dot(context[...], low, TN)
    add_row(sums, 0, upstream * scaled)
    add_row(sums, 1, upstream)
    add_row(sums, 2, cotangent)
    add_row(sums, 3, low.astype(F32))

    @pl.when(step == pl.num_programs(0) - 1)
    def _():
        for out, row in ((grad_own, 0), (grad_other, HALF)):
            for col in (0, HALF):
                out[col : col + HALF, :] = proj_grad[row : row + HALF, col : col + HALF].astype(BF)


def resid_of(middle, forward, back, cot, context, proj_own, proj_other, bias, gain):
    rows = 512
    row_block = pl.BlockSpec((rows, D), lambda i: (i, 0))
    half_block = pl.BlockSpec((D, HALF), lambda i: (0, 0))
    return pl.pallas_call(
        resid_kernel,
        grid=(OWN // rows,),
        in_specs=[row_block] * 5 + [whole((HALF, D)), whole((HALF, D)), whole((D,)), whole((D,))],
        out_specs=[
            row_block,
            row_block,
            row_block,
            half_block,
            half_block,
            pl.BlockSpec((8, D), lambda i: (0, 0)),
        ],
        out_shape=[
            jax.ShapeDtypeStruct((OWN, D), BF),
            jax.ShapeDtypeStruct((OWN, D), BF),
            jax.ShapeDtypeStruct((OWN, D), BF),
            jax.ShapeDtypeStruct((D, HALF), BF),
            jax.ShapeDtypeStruct((D, HALF), BF),
            jax.ShapeDtypeStruct((8, D), F32),
        ],
        scratch_shapes=[pltpu.VMEM((D, D), BF), pltpu.VMEM((D, D), F32)],
        compiler_params=params(),
        cost_estimate=cost(5e9, 40e6),
    )(middle, forward, back, cot, context, proj_own, proj_other, bias, gain)


def attend_back_kernel(first, spot, qkv, p, ctx_grad, spread, rel_even, rel_odd, fold, *refs):
    d_out, rel_grad, sums, upstream, kt = refs[-5:]
    band = pl.program_id(0) + first
    window = pl.program_id(1)

    @pl.when((band == first) & (window == 0))
    def _():
        rel_grad[...] = jnp.zeros_like(rel_grad)
        sums[...] = jnp.zeros_like(sums)

    @pl.when(window == 0)
    def _():
        for t in range(7):
            at, owned = owned_pair(spot[0], band, t)
            rows = pl.ds(pl.multiple_of(at * PAIR, PAIR), PAIR)
            moved = dot(spread[...], ctx_grad[rows, :])
            moved = moved * owned.astype(F32)
            upstream[:, 32 * t : 32 * t + 32, :] = moved.astype(BF).reshape(NWIN, 32, HALF)
        upstream[:, 224:256, :] = jnp.zeros((NWIN, 32, HALF), BF)

    kt[...] = qkv[0, 0, :, HALF : 2 * HALF].T
    even = lax.broadcasted_iota(jnp.int32, (1, 128), 1) < HD

    def shifted(head, by):
        return slice(by * HALF + head // 2 * 128, by * HALF + head // 2 * 128 + 128)

    def prob_grads(head, lanes):
        values = qkv[0, 0, 0:KEYS, shifted(head, 2)]
        kept = jnp.where(even != (head % 2 == 1), values, jnp.zeros_like(values))
        return dot(kept, upstream[window, 0:lanes, shifted(head, 0)], NT)

    def rel_table(both, lanes):
        tables = []
        zero8 = jnp.zeros((8, 128), F32)
        zero24 = jnp.zeros((24, 128), F32)
        zero16 = jnp.zeros((16, 128), F32)
        for tile in range(lanes // 128):
            row_shift, col_shift = shift_masks(tile * 128)
            part = both[:, tile * 128 : tile * 128 + 128]
            high = jnp.concatenate([part[HD : HD + 16], zero8], axis=0)
            wide = jnp.concatenate([part[HD + 16 : HD + 32], zero16], axis=0)
            high = unskew(high, row_shift, (1, 2, 4))
            wide = unskew(wide, col_shift, (1, 2, 4, 8))
            stack = [high, zero24, wide] if tile == 0 else [zero24, high, wide]
            tables.append(jnp.concatenate(stack, axis=0))
        table = tables[0] if len(tables) == 1 else jnp.concatenate(tables, axis=1)
        return table.astype(BF)

    def all_heads(lanes):
        count = HEADS // 2
        dvs, dks, dqs, drs = [], [], [], []

        def last_part(head, score_grad, both):
            rel = rel_odd if head % 2 else rel_even
            table = rel_table(both, lanes)
            queries = qkv[0, 0, 0:lanes, shifted(head, 0)]
            grads = dot(jnp.concatenate([score_grad, table], axis=0), queries)
            dks.append(grads[0:KEYS])
            drs.append(grads[KEYS:])
            from_rel = dot(rel[...], table, TN)
            side = head % 2 * HD
            dqs.append(both[0:HD] + from_rel[side : side + HD])
            if head % 2:
                d_out[0, 0, 0:lanes, shifted(head, 0)] = jnp.concatenate(dqs[-2:], axis=0).astype(BF).T
                d_out[0, 0, 0:KEYS, shifted(head, 1)] = (jnp.where(even, dks[-2], dks[-1]) * HD ** (-0.5)).astype(BF)

        prob_grad = prob_grads(0, lanes)
        before = None
        for head in range(count):
            ahead = prob_grads(head + 1, lanes) if head + 1 < count else None
            probs_low = p[0, 0, head, :, 0:lanes]
            probs = probs_low.astype(F32)
            total = jnp.sum(prob_grad * probs, axis=0, keepdims=True)
            score_grad = (probs * (prob_grad - total)).astype(BF)
            dvs.append(dot(probs_low, upstream[window, 0:lanes, shifted(head, 0)]))
            left = jnp.concatenate([kt[head * HD : head * HD + HD, 0:KEYS], fold[...]], axis=0)
            both = dot(left, score_grad)
            if head % 2:
                d_out[0, 0, 0:KEYS, shifted(head, 2)] = jnp.where(even, dvs[-2], dvs[-1]).astype(BF)
            if before is not None:
                last_part(head - 1, *before)
            before, prob_grad = (score_grad, both), ahead
        last_part(count - 1, *before)
        evens = drs[0] + drs[2] + drs[4]
        odds = drs[1] + drs[3] + drs[5]
        rel_grad[...] += jnp.where(even, evens, odds)

    d_out[0, 0, KEYS:, HALF:] = jnp.zeros((SLOTS - KEYS, 2 * HALF), BF)

    @pl.when(band < 2)
    def _():
        all_heads(256)

    @pl.when(band == 2)
    def _():
        all_heads(128)
        d_out[0, 0, 128:, 0:HALF] = jnp.zeros((128, HALF), BF)

    sums[0:1, :] += jnp.sum(d_out[...].reshape(SLOTS, TRIO).astype(F32), axis=0, keepdims=True)


def fold_table():
    table = np.zeros((32, WIN, 16), np.float32)
    for k in range(WIN):
        for l in range(WIN):
            table[k, k, l] = 1
            table[16 + l, k, l] = 1
    return table.reshape(32, KEYS)


def attend_back(spot, qkv, p, ctx_grad, side, spread, rel_even, rel_odd, fold, bands, *d_in):
    first, last = bands
    block = pl.BlockSpec((1, 1, SLOTS, TRIO), lambda s, w, *_: (s + first, w, 0, 0))
    share = (last - first) / 3
    return pl.pallas_call(
        lambda *refs: attend_back_kernel(first, *refs),
        grid_spec=pltpu.PrefetchScalarGridSpec(
            num_scalar_prefetch=1,
            grid=(last - first, NWIN),
            in_specs=[
                block,
                pl.BlockSpec((1, 1, HEADS // 2, KEYS, SLOTS), lambda s, w, *_: (s + first, w, 0, 0, 0)),
                pl.BlockSpec((OWN, HALF), lambda *_: (0, side), pipeline_mode=pl.Buffered(1)),
                whole((NWIN * 32, PAIR)),
                whole((GREL, 128)),
                whole((GREL, 128)),
                whole((32, KEYS)),
            ]
            + [pl.BlockSpec(memory_space=pl.ANY)] * len(d_in),
            out_specs=[
                pl.BlockSpec((1, 1, SLOTS, TRIO), lambda s, w, *_: (s + first, w, 0, side)),
                pl.BlockSpec((GREL, 128), lambda s, w, *_: (0, 0)),
                pl.BlockSpec((8, TRIO), lambda s, w, *_: (0, 0)),
            ],
            scratch_shapes=[pltpu.VMEM((NWIN, SLOTS, HALF), BF), pltpu.VMEM((HALF, SLOTS), BF)],
        ),
        out_shape=[
            jax.ShapeDtypeStruct((3, NWIN, SLOTS, 2 * TRIO), BF),
            jax.ShapeDtypeStruct((GREL, 128), F32),
            jax.ShapeDtypeStruct((8, TRIO), F32),
        ],
        input_output_aliases={8: 0} if d_in else {},
        compiler_params=params(),
        cost_estimate=cost(20e9 * share, 45e6 * share),
    )(spot, qkv, p, ctx_grad, spread, rel_even, rel_odd, fold, *d_in)


def norm_grad_kernel(d, weights_own, spot, mine, theirs, gather, *refs):
    out, joined = refs[-2:]

    @pl.when((pl.program_id(0) == 0) & (pl.program_id(1) == 0))
    def _():
        for s in range(3):
            joined[:, s * HALF : s * HALF + HALF] = weights_own[s]
        join_pieces(spot[1], mine, theirs, joined, TRIO)

    rows = NWIN * 128
    total = dot(d[...].reshape(rows, 2 * TRIO), joined[...], NT).astype(BF).reshape(NWIN, 4, 32, D)
    for t in range(4):
        moved = dot(gather[...], total[:, t].reshape(NWIN * 32, D)).astype(BF)
        out[:, t * PAIR : t * PAIR + PAIR, :] = moved.reshape(1, PAIR, D)


def norm_grad(d, weights_own, core, mine, theirs, gather, bands, *before):
    first, last = bands
    share = (last - first) / 3
    block = pl.BlockSpec((1, NWIN, 128, 2 * TRIO), lambda s, t: (s + first, 0, t, 0))
    return pl.pallas_call(
        norm_grad_kernel,
        grid=(last - first, 2),
        in_specs=[block, whole((3, D, HALF)), SCALAR]
        + [whole((3, HALF, HALF)), whole((3, HALF, HALF)), whole((PAIR, NWIN * 32))]
        + [pl.BlockSpec(memory_space=pl.ANY)] * len(before),
        out_specs=pl.BlockSpec((1, 4 * PAIR, D), lambda s, t: (s + first, t, 0)),
        out_shape=jax.ShapeDtypeStruct((3, 8 * PAIR, D), BF),
        input_output_aliases={6: 0} if before else {},
        scratch_shapes=[pltpu.VMEM((D, 2 * TRIO), BF)],
        compiler_params=params(),
        cost_estimate=cost(14e9 * share, 30e6 * share),
    )(d, weights_own, core, mine, theirs, gather, *before)


def qkv_grad_kernel(spot, xt, d, proj, kept, sent, total):
    step = pl.program_id(0)
    for col in range(0, TRIO, 256):
        cols = slice(col, min(col + 256, TRIO))
        part = dot(xt[...], d[:, cols])
        total[:, cols] = jnp.where(step == 0, part, total[:, cols] + part)

    @pl.when(step == pl.num_programs(0) - 1)
    def _():
        first = spot[1] == 0
        values = [total[:, s * HALF : s * HALF + HALF].astype(BF) for s in range(3)] + [proj[...]]
        for k in range(2):
            kept[k] = jnp.where(first, values[k], values[2 + k])
            sent[k] = jnp.where(first, values[2 + k], values[k])


def qkv_grad(core, xt, d, side, proj):
    rows = NWIN * SLOTS
    block = pl.BlockSpec((2, D, HALF), lambda i: (0, 0, 0))
    shape = jax.ShapeDtypeStruct((2, D, HALF), BF)
    return pl.pallas_call(
        qkv_grad_kernel,
        grid=(3,),
        in_specs=[
            SCALAR,
            pl.BlockSpec((D, rows), lambda i: (0, i)),
            pl.BlockSpec((rows, TRIO), lambda i: (i, side)),
            whole((D, HALF)),
        ],
        out_specs=[block, block],
        out_shape=[shape, shape],
        scratch_shapes=[pltpu.VMEM((D, TRIO), F32)],
        compiler_params=params(),
        cost_estimate=cost(7e9, 16e6),
    )(core, xt, d.reshape(3 * rows, 2 * TRIO), proj)


EARLY = 3


def input_kernel(
    spot, x, middle_grad, up_a, up_b, early_a, early_b, late_a, late_b, gain,
    one_mine, one_theirs, two_mine, two_theirs, out, sums, one_out, two_out,
):
    step = pl.program_id(0)
    first = spot[1] == 0
    mine, theirs = one_mine[...].astype(F32), one_theirs[...].astype(F32)
    one_out[0] = jnp.where(first, mine, theirs)
    one_out[1] = jnp.where(first, theirs, mine)
    mine, theirs = two_mine[...].astype(F32), two_theirs[...].astype(F32)
    two_out[:, 0:HALF] = jnp.where(first, mine, theirs)
    two_out[:, HALF:] = jnp.where(first, theirs, mine)

    @pl.when(step == 0)
    def _():
        sums[...] = jnp.zeros_like(sums)

    for k, (up, early, late) in enumerate(((up_a, early_a, late_a), (up_b, early_b, late_b))):
        rows = slice(k * PAIR, k * PAIR + PAIR)
        scaled, inverse = norm_parts(x[rows, :].astype(F32))
        at, some = taken_pair(spot[0], 2 * step + k)
        shared = jnp.where(at < EARLY, early[...].astype(F32), late[...].astype(F32)) * some.astype(F32)
        upstream = up[0].astype(F32) + shared
        scaled_up = upstream * vec(gain)
        mean = jnp.mean(scaled_up, axis=-1, keepdims=True)
        second = jnp.mean(scaled_up * scaled, axis=-1, keepdims=True)
        out[rows, :] = (middle_grad[rows, :].astype(F32) + inverse * (scaled_up - mean - scaled * second)).astype(BF)
        add_row(sums, 0, upstream * scaled)
        add_row(sums, 1, upstream)


def input_of(spot, x, middle_grad, up, early, late, gain, ones, twos):
    rows = 2 * PAIR
    row_block = pl.BlockSpec((rows, D), lambda i, *_: (i, 0))
    up_at = lambda k: lambda i, spot: band_step(spot[0], 2 * i + k) + (0,)
    early_at = lambda k: lambda i, spot: (jnp.minimum(taken_pair(spot[0], 2 * i + k)[0], EARLY - 1), 0)
    late_at = lambda k: lambda i, spot: (jnp.maximum(taken_pair(spot[0], 2 * i + k)[0] - EARLY, 0), 0)
    steps = OWN // rows
    one_rows, two_rows = HALF // steps, FF // 2 // steps
    return pl.pallas_call(
        input_kernel,
        grid_spec=pltpu.PrefetchScalarGridSpec(
            num_scalar_prefetch=1,
            grid=(steps,),
            in_specs=[
                pl.BlockSpec((rows, D), lambda i, spot: (spot[0] * steps + i, 0)),
                row_block,
                pl.BlockSpec((1, PAIR, D), up_at(0)),
                pl.BlockSpec((1, PAIR, D), up_at(1)),
                pl.BlockSpec((PAIR, D), early_at(0)),
                pl.BlockSpec((PAIR, D), early_at(1)),
                pl.BlockSpec((PAIR, D), late_at(0)),
                pl.BlockSpec((PAIR, D), late_at(1)),
                whole((D,)),
            ]
            + [pl.BlockSpec((one_rows, FF // 2), lambda i, *_: (i, 0))] * 2
            + [pl.BlockSpec((two_rows, HALF), lambda i, *_: (i, 0))] * 2,
            out_specs=[
                row_block,
                pl.BlockSpec((8, D), lambda i, *_: (0, 0)),
                pl.BlockSpec((2, one_rows, FF // 2), lambda i, *_: (0, i, 0)),
                pl.BlockSpec((two_rows, D), lambda i, *_: (i, 0)),
            ],
        ),
        out_shape=[
            jax.ShapeDtypeStruct((OWN, D), BF),
            jax.ShapeDtypeStruct((8, D), F32),
            jax.ShapeDtypeStruct((2, HALF, FF // 2), F32),
            jax.ShapeDtypeStruct((FF // 2, D), F32),
        ],
        compiler_params=params(),
        cost_estimate=cost(1e8, 35e6),
    )(spot, x, middle_grad, up, up, early, early, late, late, gain, *ones, *twos)


MESH = pl.DeviceIdType.MESH
SMALL = 24


def bits_of(size):
    return size.bit_length() - 1


def line_plan(order, rows):
    plan, doubles = [], [("double", order[0], rows)]
    for bit in order[1:]:
        if rows % 32 == 0:
            doubles.append(("double", bit, rows))
            rows //= 2
            plan.append(("halve", bit, rows))
        else:
            plan.append(("both", bit, rows))
    return plan + doubles[::-1]


PARTS = 3
PART_ROWS = D // 2 // PARTS


def last_kernel(bits, plans, orders, *refs):
    (line_a, line_b, one_sums, two_sums, fc1_sums, sums_a, sums_c, sums_b) = refs[:8]
    rel_a, rel_b, rel_c, hots, out, small, rel = refs[8:15]
    small_landed, rel_landed, sends, recvs = refs[15:19]
    rooms = list(refs[19:])
    dp, mp = lax.axis_index("dp"), lax.axis_index("mp")
    bit_at = lambda bit: mp if bit == 0 else (dp // bit) % 2

    def partner(bit):
        if bit == 0:
            return (dp, 1 - mp)
        return (jnp.where(bit_at(bit) == 0, dp + bit, dp - bit), mp)

    barrier = pltpu.get_barrier_semaphore()
    every = [1] + bits + [0]
    for bit in every:
        pl.semaphore_signal(barrier, inc=1, device_id=partner(bit), device_id_type=MESH)

    count = [0]

    def send(src, dst, bit):
        at = count[0]
        count[0] += 1
        copy = pltpu.make_async_remote_copy(
            src_ref=src,
            dst_ref=dst,
            send_sem=sends.at[at],
            recv_sem=recvs.at[at],
            device_id=partner(bit),
            device_id_type=MESH,
        )
        copy.start()
        return copy

    def line(k, part):
        order, value = orders[k], (line_a, line_b)[k].at[pl.ds(part * PART_ROWS, PART_ROWS)]
        slot = dp % 2 * 2 + k
        first = bit_at(order[0]) * (D // 2) + part * PART_ROWS
        start, size, placed = first, PART_ROWS, False
        for kind, bit, after in plans[k]:
            if kind == "double":
                here = pl.ds(pl.multiple_of(start, 16), size)
                if not placed:
                    out[slot, here, :] = value[...]
                    placed = True
                copy = send(out.at[slot, here], out.at[slot, here], bit)
                yield
                copy.wait()
                if after != size or bit != order[0]:
                    start, size = start - bit_at(bit) * size, 2 * size
                continue
            mine = bit_at(bit) if kind == "halve" else 0
            gone = 1 - mine if kind == "halve" else 0
            room, total = rooms.pop(0), rooms.pop(0)
            copy = send(value.at[pl.ds(pl.multiple_of(gone * after, 16), after)], room, bit)
            yield
            copy.wait()
            rows = pl.ds(pl.multiple_of(mine * after, 16), after)
            total[...] = (value[rows, :].astype(F32) + room[...].astype(F32)).astype(BF)
            value = total
            start, size = start + mine * after, after
        copies = []
        for half in range(2):
            rows = pl.ds(half * (D // 2) + part * PART_ROWS, PART_ROWS)
            copies.append(send(out.at[slot, rows], out.at[slot, rows], 1))
        yield
        for copy in copies:
            copy.wait()

    def vectors():
        for at, bit in enumerate(bits + [0, 1]):
            copies = [send(small, small_landed.at[at], bit), send(rel, rel_landed.at[at], bit)]
            yield
            for copy in copies:
                copy.wait()
            small[...] += small_landed[at]
            rel[...] += rel_landed[at]

    lines = [line(k, part) for part in range(PARTS) for k in range(2)]
    pl.semaphore_wait(barrier, len(every))
    for one in lines:
        next(one)

    small[...] = jnp.zeros_like(small)
    small[0:2, :] = one_sums[0:2, :]
    small[2:6, :] = two_sums[0:4, :]
    first = mp == 0
    own = [sums_a[0:1, :] + sums_c[0:1, :], fc1_sums[0:1, 0 : FF // 2]]
    other = [sums_b[0:1, :], fc1_sums[0:1, FF // 2 :]]
    for row, flip in ((6, False), (9, True)):
        picked = [jnp.where(first != flip, a, b) for a, b in zip(own, other)]
        small[row : row + 1, 0:HALF] = picked[0][:, 0:HALF]
        small[row : row + 1, HALF:] = picked[0][:, 2 * HALF :]
        small[row + 1 : row + 2, :] = picked[1][:, 0:D]
        small[row + 2 : row + 3, :] = picked[1][:, D:]
    table = rel_a[...] + rel_b[...] + rel_c[...]
    table = lax.dot_general(hots[...], table, TN, precision=lax.Precision.HIGHEST, preferred_element_type=F32)
    rel[...] = table + pltpu.roll(table, HD, 1)

    active = lines + [vectors()]
    while active:
        for one in list(active):
            if next(one, "end") == "end":
                active.remove(one)


def last_sums(bits, orders, lines, sums, rels, hots):
    vmem = pl.BlockSpec(memory_space=pltpu.VMEM)
    rounds = len(bits) + 2
    copies = 2 * rounds + 2 * PARTS * (2 * len(bits) + 2)
    plans = [line_plan(order, PART_ROWS) for order in orders]
    rooms = []
    for at in range(len(plans[0])):
        for part in range(PARTS):
            for plan in plans:
                if plan[at][0] != "double":
                    rooms += [pltpu.VMEM((plan[at][2], HALF), BF)] * 2
    return pl.pallas_call(
        lambda *refs: last_kernel(bits, plans, orders, *refs),
        in_specs=[vmem] * (2 + len(sums) + len(rels) + 1),
        out_specs=[vmem] * 3,
        out_shape=[
            jax.ShapeDtypeStruct((4, D, HALF), BF),
            jax.ShapeDtypeStruct((SMALL, D), F32),
            jax.ShapeDtypeStruct((56, 128), F32),
        ],
        scratch_shapes=[
            pltpu.VMEM((rounds, SMALL, D), F32),
            pltpu.VMEM((rounds, 56, 128), F32),
            pltpu.SemaphoreType.DMA((copies,)),
            pltpu.SemaphoreType.DMA((copies,)),
        ]
        + rooms,
        compiler_params=pltpu.CompilerParams(
            collective_id=0, has_side_effects=True, vmem_limit_bytes=40 * 2**20
        ),
    )(*lines, *sums, *rels, hots)


CORE, PAIRED = 1, 0


def bit_of(bit):
    return lax.axis_index("mp") if bit == PAIRED else (lax.axis_index("dp") // bit) % 2


def exchange(value, bit):
    if bit == PAIRED:
        return lax.ppermute(value, "mp", [(0, 1), (1, 0)])
    return lax.ppermute(value, "dp", [(i, i ^ bit) for i in range(lax.axis_size("dp"))])


class Line:
    def __init__(self, value, places, rank, steps, sent=None):
        self.terms = [(value, tuple(places))]
        self.fixed = {}
        self.rank = list(rank)
        self.steps = list(steps)
        self.sent, self.taken = sent, None
        self.value = None

    def part(self, changes):
        fixed = {**self.fixed, **changes}
        total = None
        for term, places in self.terms:
            starts, sizes, shape = [], [], []
            for bit in places:
                starts.append(fixed.get(bit, 0))
                sizes.append(1 if bit in fixed else 2)
                if bit not in fixed:
                    shape.append(2)
            rest = term.shape[len(places) :]
            if places:
                starts = [jnp.asarray(at, jnp.int32) for at in starts + [0] * len(rest)]
                term = lax.dynamic_slice(term, starts, tuple(sizes) + rest).reshape(tuple(shape) + rest)
            total = term.astype(F32) if total is None else total + term.astype(F32)
        return total.astype(BF)

    def prepare(self):
        kind, bit = self.steps[0]
        if kind == "halve":
            mine = 0 if bit == PAIRED else bit_of(bit)
            self.sent = self.part({bit: 1 - mine})
            self.fixed[bit] = mine
        elif kind == "double":
            if self.value is None:
                self.value, self.done = self.part({}), []
            self.sent = self.value
        elif kind == "pass":
            self.sent = self.part({})

    def launch(self):
        self.taken = exchange(self.sent, self.steps[0][1])

    def land(self):
        kind, bit = self.steps.pop(0)
        if kind in ("halve", "give"):
            places = [p for p in self.terms[0][1] if p not in self.fixed]
            self.terms.append((self.taken, tuple(places)))
        elif kind == "pass":
            self.terms = [(self.taken, tuple(p for p in self.terms[0][1] if p not in self.fixed))]
        else:
            if not self.steps:
                self.value, self.taken_last, self.taken = self.sent, self.taken, None
                return
            self.done = sorted(self.done + [bit], key=self.rank.index)
            axis = self.done.index(bit)
            shape = [1] * (self.value.ndim + 1)
            shape[axis] = 2
            mine = jnp.arange(2).reshape(shape) == bit_of(bit)
            wide = lambda v: jnp.expand_dims(v, axis)
            self.value = jnp.where(mine, wide(self.sent), wide(self.taken))
        self.taken = None


def advance(anchor, lines):
    flying = [line for line in lines if line.taken is not None]
    anchor, taken = lax.optimization_barrier((anchor, [line.taken for line in flying]))
    for line, value in zip(flying, taken):
        line.taken = value
        line.land()
    going = [line for line in lines if line.steps]
    for line in going:
        line.prepare()
    anchor, sent = lax.optimization_barrier((anchor, [line.sent for line in going]))
    for line, value in zip(going, sent):
        line.sent = value
        line.launch()
    return anchor


def finish(lines):
    while any(line.steps for line in lines):
        for line in lines:
            if not line.steps:
                continue
            if line.taken is None:
                line.prepare()
                line.launch()
        for line in lines:
            if line.taken is not None:
                line.land()


def on_device(
    image_tokens,
    norm1_gain,
    norm1_shift,
    qkv_weight,
    qv_bias,
    rel_rows,
    rel_cols,
    proj_weight,
    proj_bias,
    norm2_gain,
    norm2_shift,
    fc1_weight,
    fc1_bias,
    fc2_weight,
    fc2_bias,
    out_cotangent,
):
    place = lax.axis_index("mp")
    core = lax.axis_index("dp") % 2
    swap = lambda value: lax.ppermute(value, "mp", [(0, 1), (1, 0)])
    size = lax.axis_size("dp")
    core_swap = lambda value: lax.ppermute(value, "dp", [(i, i ^ 1) for i in range(size)])

    def by_core(weight, axis, mine):
        return lax.dynamic_slice_in_dim(weight, (core if mine else 1 - core) * HALF, HALF, axis)

    spot = jnp.stack([place, core]).astype(jnp.int32)
    spread = jnp.asarray(spread_rows(), BF)
    gather = jnp.asarray(spread_rows().T, BF)
    fold = jnp.asarray(fold_table(), BF)
    high_hot, wide_hot = rel_onehots()
    hots = jnp.asarray(np.pad(np.concatenate([high_hot, wide_hot], axis=1), ((0, 0), (0, 2))), F32)
    high_hot, wide_hot = jnp.asarray(high_hot, BF), jnp.asarray(wide_hot, BF)
    qkv_mine = swap(by_core(qkv_weight, 1, True))
    bias_other = swap(qv_bias)
    fc1_bias_other = swap(fc1_bias)
    x_windows = windows_of(spot, image_tokens, norm1_gain, norm1_shift, spread)
    cot_t = turned_of(out_cotangent)
    x_windows, cot_t, qkv_mine = lax.optimization_barrier((x_windows, cot_t, qkv_mine))
    late = (by_core(fc1_weight, 0, True), by_core(fc2_weight, 1, True), proj_weight)
    x_windows, qkv_mine, late = lax.optimization_barrier((x_windows, qkv_mine, late))
    qkv_theirs = exchange(qkv_mine, CORE)
    one_mine, two_mine, proj_other = (swap(w) for w in late)
    qkv_a, p_a, ctx_a, xt, rel_even, rel_odd = attend(
        x_windows, qv_bias, True, qkv_weight, high_hot, wide_hot, rel_rows, rel_cols
    )
    qkv_b, p_b, ctx_b = attend(
        x_windows, bias_other, False, spot, qkv_mine, qkv_theirs, rel_even, rel_odd
    )
    ctx_b, one_mine, two_mine, proj_other = lax.optimization_barrier((ctx_b, one_mine, two_mine, proj_other))
    one_theirs, two_theirs = exchange(one_mine, CORE), exchange(two_mine, CORE)
    middle, normed, normed_t, context = middle_of(
        spot, ctx_a, ctx_b, image_tokens, proj_weight, proj_other, proj_bias, norm2_gain, norm2_shift, gather
    )
    forward, back, one_kept, one_sent, two_kept, two_sent, fc1_sums = feed(
        spot, normed, normed_t, out_cotangent, cot_t, fc1_weight, (one_mine, one_theirs), fc1_bias,
        fc1_bias_other, fc2_weight, (two_mine, two_theirs),
    )
    bits = [2**k for k in range(1, bits_of(size))]
    turned = bits[1:2] + bits[0:1] + bits[2:]
    halves = lambda order: [("halve", bit) for bit in order]
    doubles = lambda order: [("double", bit) for bit in order]

    def cut(value, axis, places):
        shape = value.shape[:axis] + (2,) * len(places) + (value.shape[axis] // 2 ** len(places),)
        return value.reshape(shape + value.shape[axis + 1 :])

    def feed_line(kept, sent, order, back):
        steps = [("give", CORE)] + halves(order) + doubles(back) + [("double", CORE)]
        rank = [CORE] + bits
        return Line(cut(kept, 1, bits), [PAIRED] + bits, rank, steps, cut(sent, 1, bits))

    one_line = feed_line(one_kept, one_sent, [PAIRED] + bits, bits[::-1])
    two_line = feed_line(two_kept, two_sent, bits[:2] + [PAIRED] + bits[2:], turned[::-1])
    feed_lines = [one_line, two_line]

    middle = advance(middle, feed_lines)
    block_out, middle_grad, ctx_grad, proj_own, proj_oth, two_sums = resid_of(
        middle, forward, back, out_cotangent, context, proj_weight, proj_other, fc2_bias, norm2_gain
    )
    back_of = lambda qkv, p, side, grad, bands, *d: attend_back(
        spot, qkv, p, grad, side, spread, rel_even, rel_odd, fold, bands, *d
    )
    ctx_grad = advance(ctx_grad, feed_lines)
    d, rel_b, sums_b = back_of(qkv_b, p_b, 1, ctx_grad, (0, 3))
    d = advance(d, feed_lines)
    kept_b, sent_b = qkv_grad(spot, xt, d, 1, proj_oth)
    line_b = Line(kept_b, [], [], [("give", CORE)], sent_b)
    lines = feed_lines + [line_b]
    ctx_grad, kept_b, d = lax.optimization_barrier((ctx_grad, kept_b, d))
    ctx_grad = advance(ctx_grad, lines)
    d, rel_a0, sums_a0 = back_of(qkv_a, p_a, 0, ctx_grad, (0, 1), d)
    d = advance(d, lines)
    passes = []
    for k in range(2):
        line = Line(None, [], [], [("pass", PAIRED)])
        line.terms = [(term[k], ()) for term, _ in line_b.terms]
        passes.append(line)
    d = advance(d, passes[:1])
    d, rel_a, sums_a = back_of(qkv_a, p_a, 0, ctx_grad, (1, 3), d)
    d = advance(d, feed_lines + passes[:1])
    d = advance(d, passes[1:])
    up = norm_grad(d, qkv_weight, spot, qkv_mine, qkv_theirs, gather, (1, 3))
    at = [2 - place, (1 - place) * 4 * SIDE, jnp.zeros_like(place)]
    shares = []
    for first, count in ((0, 2 * EARLY), (2 * EARLY, 10 - 2 * EARLY)):
        start = [at[0], at[1] + first * SIDE, at[2]]
        part = lax.dynamic_slice(up, start, (1, count * SIDE, D)).reshape(count * SIDE, D)
        shares.append(Line(part, [], [], [("pass", PAIRED)]))
    d = advance(d, feed_lines + passes[1:])
    d = advance(d, shares[:1])
    kept_a, sent_a = qkv_grad(spot, xt, d, 0, proj_own)
    line_a = Line(kept_a, [], [], [("give", CORE)], sent_a)
    kept_a, d = lax.optimization_barrier((kept_a, d))
    d = advance(d, feed_lines + [line_a] + shares[:1])
    d = advance(d, shares[1:])
    up = norm_grad(d, qkv_weight, spot, qkv_mine, qkv_theirs, gather, (0, 1), up)
    up = advance(up, feed_lines + [line_a] + shares[1:])
    early, late = (line.terms[0][0] for line in shares)
    q_lines = []
    for k, order in enumerate((bits, turned)):
        line = Line(None, [], [], halves(order[:1]))
        line.terms = [(part.reshape(2, 2, D // 2, HALF), ("line", order[0])) for part, _ in line_a.terms]
        line.terms += [(part.reshape(2, D // 2, HALF), (order[0],)) for part, _ in passes[k].terms]
        line.fixed = {"line": k}
        q_lines.append(line)
    up = advance(up, q_lines)
    finish(feed_lines)
    flat = lambda line, rows: (line.value.reshape(rows, -1), line.taken_last.reshape(rows, -1))
    input_grad, one_sums, one_sum, two_sum = input_of(
        spot, image_tokens, middle_grad, up, early, late, norm1_gain, flat(one_line, HALF), flat(two_line, FF // 2)
    )
    one_sums = advance(one_sums, q_lines)
    four, small, rel = last_sums(
        bits,
        [bits, turned],
        [line.part({}) for line in q_lines],
        [one_sums, two_sums, fc1_sums, sums_a, sums_a0, sums_b],
        [rel_a, rel_a0, rel_b],
        hots,
    )
    one_sum = one_sum.reshape(D, FF // 2)
    mine = jnp.where(place == 0, small[6:9], small[9:12])
    return (
        block_out,
        input_grad,
        small[0],
        small[1],
        four[0:3].astype(F32),
        mine[0].reshape(2, HALF),
        rel[:RELS, :HD],
        rel[RELS : 2 * RELS, :HD],
        jnp.concatenate([four[3, :HALF], four[3, HALF:]], axis=1).astype(F32),
        small[5],
        small[2],
        small[3],
        one_sum,
        mine[1:3].reshape(-1),
        two_sum,
        small[4],
    )


def solution(mesh):
    in_specs = (
        P("dp", None),
        P(),
        P(),
        P(None, None, "mp"),
        P(None, "mp"),
        P(),
        P(),
        P("mp", None),
        P(),
        P(),
        P(),
        P(None, "mp"),
        P("mp"),
        P("mp", None),
        P(),
        P(("dp", "mp"), None),
    )
    out_specs = (
        P(("dp", "mp"), None),
        P(("dp", "mp"), None),
        P(),
        P(),
        P(None, None, "mp"),
        P(None, "mp"),
        P(),
        P(),
        P("mp", None),
        P(),
        P(),
        P(),
        P(None, "mp"),
        P("mp"),
        P("mp", None),
        P(),
    )
    return jax.shard_map(
        on_device, mesh=mesh, in_specs=in_specs, out_specs=out_specs, check_vma=False
    )
```
